32 devices in a mesh: grp: 4 (over x, core), fsdp: 8 (over z, y).
Axes of the slice: x: 2, y: 2, z: 4, core: 2. Of those that a mesh axis runs over, the one named last changes fastest.
Arguments:
- caption_states: bfloat16 [8, 128, 4096], P('fsdp'), may hold values from -6 to 6
- caption_lens: int32 [8], replicated, may hold values from 4 to 128
- text_gain: float32 [4096], replicated, may hold values from 0.25 to 1.75
- text_query: bfloat16 [4096, 2048], P(None, 'grp'), may hold values from -0.01171875 to 0.01171875
- text_key: bfloat16 [4096, 2048], P(None, 'grp'), may hold values from -0.09375 to 0.09375
- text_value: bfloat16 [4096, 2048], P(None, 'grp'), may hold values from -0.09375 to 0.09375
- text_bias: float32 [32, 128, 128], P('grp'), may hold values from -4 to 4
- text_out: bfloat16 [2048, 4096], P('grp'), may hold values from -0.125 to 0.125
- final_gain: float32 [4096], replicated, may hold values from 0.25 to 1.75
- cross_key: bfloat16 [4096, 1536], P('fsdp', 'grp'), may hold values from -0.09375 to 0.09375
- cross_value: bfloat16 [4096, 1536], P('fsdp', 'grp'), may hold values from -0.09375 to 0.09375
- video_states: bfloat16 [2048, 3072], P('fsdp'), may hold values from -6 to 6
- video_counts: int32 [8], replicated, may hold values from 128 to 1024, as said below
- sample_caption: int32 [8], replicated, may hold values from 0 to 7, each once
- cross_query: bfloat16 [3072, 1536], P('fsdp', 'grp'), may hold values from -0.109375 to 0.109375
- cross_out: bfloat16 [1536, 3072], P('grp', 'fsdp'), may hold values from -0.15625 to 0.15625
- out_grad: bfloat16 [2048, 3072], P('fsdp'), may hold values from -6 to 6
Outputs:
- updated: bfloat16 [2048, 3072], P('fsdp', 'grp')
- input_grad: bfloat16 [2048, 3072], P('fsdp', 'grp')
- query_grad: float32 [3072, 1536], P('fsdp', 'grp')
- out_weight_grad: float32 [1536, 3072], P('grp', 'fsdp')
- key_grad: bfloat16 [8, 128, 1536], P('fsdp', None, 'grp')
- value_grad: bfloat16 [8, 128, 1536], P('fsdp', None, 'grp')
The draws below stay inside these ranges and needn't reach their ends.
Inputs may be any that keep to these rules, and one draw needn't show every extreme that they name: `video_counts`: counts of the samples in order, summing to 2048. `sample_caption`: each caption belongs to exactly one sample.
All inputs are finite; a program needn't handle non-finite values.
Results may differ from the reference program's by a relative error of at most 0.04.
Values may be sent and summed in bfloat16 or wider, within the bound.
No kernel may reach another device: no remote copies, remote signals or barrier semaphores. Data moves between devices by JAX's collectives and lax.ppermute only.
A program may use at most 128 MiB of HBM per device.

```python
import math
import jax
import jax.numpy as jnp
from jax import lax

TEXT_WIDTH = 4096
TEXT_HEADS = 32
TEXT_HEADDIM = 64
MODEL_WIDTH = 3072
CROSS_HEADS = 12
HEAD_SIZE = 128
CAPTION_LEN = 128
VIDEO_DEV = 256
CAPTIONS = 8
VIDEO_TOKENS = 2048
VIDEO_MOST = 1024
N_FSDP = 8


def draw_video_counts(key, part):
    key = jax.random.fold_in(key, 11)
    key_weights, key_order, key_place = jax.random.split(key, 3)
    half = VIDEO_DEV // 2
    others = CAPTIONS - 2
    extra = VIDEO_TOKENS - VIDEO_MOST - half - others * half
    weights = jax.random.randint(key_weights, (others,), 1, 5).astype(jnp.int32)
    total = jnp.sum(weights).astype(jnp.int32)
    share = (extra * weights // total).astype(jnp.int32)
    left = (extra - jnp.sum(share)).astype(jnp.int32)
    order = jax.random.permutation(key_order, others).astype(jnp.int32)
    share = share + (order < left).astype(jnp.int32)
    counts = jnp.concatenate([jnp.full((1,), VIDEO_MOST, jnp.int32), jnp.full((1,), half, jnp.int32), (half + share).astype(jnp.int32)])
    place = jax.random.permutation(key_place, CAPTIONS).astype(jnp.int32)
    return counts[place].astype(jnp.int32)


def touch_ends(values, key, low, largest):
    longest = values.shape.index(max(values.shape))
    spots = []
    for shift in (0, 1):
        where = [jax.random.randint(jax.random.fold_in(key, axis), (), 0, length) for axis, length in enumerate(values.shape)]
        where[longest] = (where[longest] + shift) % values.shape[longest]
        spots.append(tuple(where))
    return values.at[spots[0]].set(low).at[spots[1]].set(largest)


def block_scale(key, dims, shards, low, largest):
    loudness = 1.0
    for dim, shards_of in shards:
        draws = jax.random.uniform(jax.random.fold_in(jax.random.fold_in(key, 6), dim), (shards_of,), jnp.float32, low / len(shards), largest / len(shards))
        loudness = loudness * jnp.repeat(jnp.exp(draws), dims[dim] // shards_of).reshape((-1,) + (1,) * (len(dims) - 1 - dim))
    return loudness


def gaussian(rng, dims, scale, most, cuts=(), held_as=jnp.bfloat16):
    array = jax.random.normal(rng, dims, jnp.float32) * scale
    if len(cuts) > 0:
        array = block_scale(rng, dims, cuts, -0.22, 0.18) * array
    return jnp.clip(array, min=-most, max=most).astype(held_as)


def setup_inputs(seed: int = 0) -> dict:
    streams_of = jax.random.split(jax.random.key(seed), 18)
    return {
        "caption_states": gaussian(streams_of[0], (CAPTIONS, CAPTION_LEN, TEXT_WIDTH), 1.0, 6.0, ((0, 8),)),
        "caption_lens": touch_ends(jax.random.randint(streams_of[1], (CAPTIONS,), 4, CAPTION_LEN + 1), jax.random.fold_in(streams_of[1], 1), 4, CAPTION_LEN).astype(jnp.int32),
        "text_gain": jnp.clip(1.0 + 0.15 * jax.random.normal(streams_of[2], (TEXT_WIDTH,), jnp.float32), 0.25, 1.75),
        "text_query": gaussian(streams_of[3], (TEXT_WIDTH, TEXT_HEADS * TEXT_HEADDIM), (TEXT_WIDTH * TEXT_HEADDIM) ** -0.5, 0.01171875, ((1, 4),)),
        "text_key": gaussian(streams_of[4], (TEXT_WIDTH, TEXT_HEADS * TEXT_HEADDIM), TEXT_WIDTH ** -0.5, 0.09375, ((1, 4),)),
        "text_value": gaussian(streams_of[5], (TEXT_WIDTH, TEXT_HEADS * TEXT_HEADDIM), TEXT_WIDTH ** -0.5, 0.09375, ((1, 4),)),
        "text_bias": gaussian(streams_of[6], (TEXT_HEADS, CAPTION_LEN, CAPTION_LEN), 1.0, 4.0, ((0, 4),), jnp.float32),
        "text_out": gaussian(streams_of[7], (TEXT_HEADS * TEXT_HEADDIM, TEXT_WIDTH), (TEXT_HEADS * TEXT_HEADDIM) ** -0.5, 0.125, ((0, 4),)),
        "final_gain": jnp.clip(1.0 + 0.15 * jax.random.normal(streams_of[8], (TEXT_WIDTH,), jnp.float32), 0.25, 1.75),
        "cross_key": gaussian(streams_of[9], (TEXT_WIDTH, CROSS_HEADS * HEAD_SIZE), TEXT_WIDTH ** -0.5, 0.09375, ((0, 8), (1, 4))),
        "cross_value": gaussian(streams_of[10], (TEXT_WIDTH, CROSS_HEADS * HEAD_SIZE), TEXT_WIDTH ** -0.5, 0.09375, ((0, 8), (1, 4))),
        "video_states": gaussian(streams_of[11], (VIDEO_TOKENS, MODEL_WIDTH), 1.0, 6.0, ((0, 8),)),
        "video_counts": draw_video_counts(jax.random.fold_in(streams_of[17], 71), 0),
        "sample_caption": jax.random.permutation(streams_of[13], CAPTIONS).astype(jnp.int32),
        "cross_query": gaussian(streams_of[14], (MODEL_WIDTH, CROSS_HEADS * HEAD_SIZE), MODEL_WIDTH ** -0.5, 0.109375, ((0, 8), (1, 4))),
        "cross_out": gaussian(streams_of[15], (CROSS_HEADS * HEAD_SIZE, MODEL_WIDTH), (CROSS_HEADS * HEAD_SIZE) ** -0.5, 0.15625, ((0, 4), (1, 8))),
        "out_grad": gaussian(streams_of[16], (VIDEO_TOKENS, MODEL_WIDTH), 1.0, 6.0, ((0, 8),)),
    }


def rms_scale(values, gain):
    mean_square = lax.optimization_barrier(jnp.mean(values * values, axis=-1, keepdims=True))
    return values * lax.rsqrt(mean_square + 1e-06) * gain

def token_captions(video_counts, sample_caption, positions):
    sample_end = jnp.cumsum(video_counts).astype(jnp.int32)
    token_sample = lax.optimization_barrier(jnp.sum((sample_end[None, :] <= positions[:, None]).astype(jnp.int32), axis=1))
    numbers = jnp.arange(sample_caption.shape[0], dtype=jnp.int32)
    picked = token_sample[:, None] == numbers[None, :]
    return lax.optimization_barrier(jnp.sum(jnp.where(picked, sample_caption[None, :], 0), axis=1)).astype(jnp.int32)

def text_encoder(caption_states, caption_lens, text_gain, text_query, text_key, text_value, text_bias, text_out, final_gain):
    flat_states = caption_states.astype(jnp.float32).reshape(CAPTIONS * CAPTION_LEN, TEXT_WIDTH)
    normed = rms_scale(flat_states, text_gain).astype(jnp.bfloat16)

    def heads_of(weight):
        product = jnp.dot(normed, weight, preferred_element_type=jnp.float32).astype(jnp.bfloat16)
        return product.reshape(CAPTIONS, CAPTION_LEN, TEXT_HEADS, TEXT_HEADDIM)
    text_queries = heads_of(text_query)
    text_keys = heads_of(text_key)
    text_values = heads_of(text_value)
    text_scores = jnp.einsum('cihd,cjhd->chij', text_queries.astype(jnp.float32), text_keys.astype(jnp.float32)) + text_bias[None]
    key_valid = jnp.arange(CAPTION_LEN, dtype=jnp.int32)[None, :] < caption_lens[:, None]
    exp_scores = jnp.where(key_valid[:, None, None, :], jnp.exp(text_scores), 0.0)
    text_weights = (exp_scores / lax.optimization_barrier(jnp.sum(exp_scores, axis=-1, keepdims=True))).astype(jnp.bfloat16)
    text_mixed = jnp.einsum('chij,cjhd->cihd', text_weights.astype(jnp.float32), text_values.astype(jnp.float32))
    text_mixed = text_mixed.astype(jnp.bfloat16).reshape(CAPTIONS * CAPTION_LEN, TEXT_HEADS * TEXT_HEADDIM)
    text_sum = flat_states + jnp.dot(text_mixed, text_out, preferred_element_type=jnp.float32)
    return rms_scale(text_sum, final_gain).astype(jnp.bfloat16)

def reference(caption_states, caption_lens, text_gain, text_query, text_key, text_value, text_bias, text_out, final_gain, cross_key, cross_value, video_states, video_counts, sample_caption, cross_query, cross_out, out_grad):
    encoded = text_encoder(caption_states, caption_lens, text_gain, text_query, text_key, text_value, text_bias, text_out, final_gain)
    width = CROSS_HEADS * HEAD_SIZE
    keys_all = jnp.dot(encoded, cross_key, preferred_element_type=jnp.float32).astype(jnp.bfloat16).reshape(CAPTIONS, CAPTION_LEN, width)
    values_all = jnp.dot(encoded, cross_value, preferred_element_type=jnp.float32).astype(jnp.bfloat16).reshape(CAPTIONS, CAPTION_LEN, width)
    positions = jnp.arange(VIDEO_TOKENS, dtype=jnp.int32)
    token_cap = token_captions(video_counts, sample_caption, positions).reshape(N_FSDP, VIDEO_DEV)
    score_scale = 1.0 / math.sqrt(HEAD_SIZE)

    def column_step(carry, inputs):
        key_sum, value_sum, query_sum, outw_sum = carry
        video_col, grad_col, cap_col = inputs
        video = video_col.astype(jnp.float32)
        center = video - lax.optimization_barrier(jnp.mean(video, axis=-1, keepdims=True))
        inverse = lax.rsqrt(lax.optimization_barrier(jnp.mean(center * center, axis=-1, keepdims=True)) + 1e-06)
        video_hat = center * inverse
        video_normed = video_hat.astype(jnp.bfloat16)
        queries = jnp.dot(video_normed, cross_query, preferred_element_type=jnp.float32).astype(jnp.bfloat16)
        queries = queries.reshape(VIDEO_DEV, CROSS_HEADS, HEAD_SIZE)
        chosen_keys = jnp.take(keys_all, cap_col, axis=0).reshape(VIDEO_DEV, CAPTION_LEN, CROSS_HEADS, HEAD_SIZE)
        chosen_values = jnp.take(values_all, cap_col, axis=0).reshape(VIDEO_DEV, CAPTION_LEN, CROSS_HEADS, HEAD_SIZE)
        scores = jnp.einsum('thd,tjhd->thj', queries.astype(jnp.float32), chosen_keys.astype(jnp.float32)) * score_scale
        token_lens = jnp.take(caption_lens, cap_col, axis=0)
        key_valid = (jnp.arange(CAPTION_LEN, dtype=jnp.int32)[None, :] < token_lens[:, None])[:, None, :]
        exp_scores = jnp.where(key_valid, jnp.exp(scores), 0.0)
        weights = exp_scores / lax.optimization_barrier(jnp.sum(exp_scores, axis=-1, keepdims=True))
        probs = weights.astype(jnp.bfloat16)
        attended = jnp.einsum('thj,tjhd->thd', probs.astype(jnp.float32), chosen_values.astype(jnp.float32))
        attended = attended.astype(jnp.bfloat16).reshape(VIDEO_DEV, width)
        updated_col = (video + jnp.dot(attended, cross_out, preferred_element_type=jnp.float32)).astype(jnp.bfloat16)
        d_attended = jnp.dot(grad_col, cross_out.T, preferred_element_type=jnp.float32).astype(jnp.bfloat16)
        d_attended = d_attended.reshape(VIDEO_DEV, CROSS_HEADS, HEAD_SIZE)
        d_probs = jnp.einsum('thd,tjhd->thj', d_attended.astype(jnp.float32), chosen_values.astype(jnp.float32))
        d_scores = (weights * (d_probs - lax.optimization_barrier(jnp.sum(weights * d_probs, axis=-1, keepdims=True))) * score_scale).astype(jnp.bfloat16)
        d_queries = jnp.einsum('thj,tjhd->thd', d_scores.astype(jnp.float32), chosen_keys.astype(jnp.float32))
        d_queries = d_queries.astype(jnp.bfloat16).reshape(VIDEO_DEV, width)
        owners = (cap_col[None, :] == jnp.arange(CAPTIONS, dtype=jnp.int32)[:, None]).astype(jnp.float32)
        key_term = jnp.einsum('ct,thj,thd->cjhd', owners, d_scores.astype(jnp.float32), queries.astype(jnp.float32))
        value_term = jnp.einsum('ct,thj,thd->cjhd', owners, probs.astype(jnp.float32), d_attended.astype(jnp.float32))
        key_term = lax.optimization_barrier(key_term.reshape(CAPTIONS, CAPTION_LEN, width).astype(jnp.bfloat16))
        value_term = lax.optimization_barrier(value_term.reshape(CAPTIONS, CAPTION_LEN, width).astype(jnp.bfloat16))
        d_normed = jnp.dot(d_queries, cross_query.T, preferred_element_type=jnp.float32)
        first_mean = lax.optimization_barrier(jnp.mean(d_normed, axis=-1, keepdims=True))
        second_mean = lax.optimization_barrier(jnp.mean(d_normed * video_hat, axis=-1, keepdims=True))
        input_col = (grad_col.astype(jnp.float32) + inverse * (d_normed - first_mean - video_hat * second_mean)).astype(jnp.bfloat16)
        query_term = lax.optimization_barrier(jnp.dot(video_normed.T, d_queries, preferred_element_type=jnp.float32).astype(jnp.bfloat16))
        outw_term = lax.optimization_barrier(jnp.dot(attended.T, grad_col, preferred_element_type=jnp.float32).astype(jnp.bfloat16))
        carry = (key_sum + key_term.astype(jnp.float32), value_sum + value_term.astype(jnp.float32), query_sum + query_term.astype(jnp.float32), outw_sum + outw_term.astype(jnp.float32))
        return (carry, (updated_col, input_col))
    start_carry = (jnp.zeros((CAPTIONS, CAPTION_LEN, width), jnp.float32), jnp.zeros((CAPTIONS, CAPTION_LEN, width), jnp.float32), jnp.zeros((MODEL_WIDTH, width), jnp.float32), jnp.zeros((width, MODEL_WIDTH), jnp.float32))
    inputs = (video_states.reshape(N_FSDP, VIDEO_DEV, MODEL_WIDTH), out_grad.reshape(N_FSDP, VIDEO_DEV, MODEL_WIDTH), token_cap)
    final_carry, outputs = lax.scan(column_step, start_carry, inputs)
    key_sum, value_sum, query_grad, out_weight_grad = final_carry
    updated = outputs[0].reshape(VIDEO_TOKENS, MODEL_WIDTH)
    input_grad = outputs[1].reshape(VIDEO_TOKENS, MODEL_WIDTH)
    return (updated, input_grad, query_grad, out_weight_grad, key_sum.astype(jnp.bfloat16), value_sum.astype(jnp.bfloat16))
```

```python
import math

import jax
import jax.numpy as jnp
from jax import lax
from jax.sharding import PartitionSpec as P

HEAD_SIZE = 128
BF = jnp.bfloat16
F32 = jnp.float32


def rms_scale(values, gain):
    mean_square = jnp.mean(values * values, axis=-1, keepdims=True)
    return values * lax.rsqrt(mean_square + 1e-06) * gain


def mm(left, right):
    return jnp.dot(left, right, preferred_element_type=F32)


def contract_last(left, right):
    return lax.dot_general(left, right, (((1,), (1,)), ((), ())), preferred_element_type=F32)


def contract_first(left, right):
    return lax.dot_general(left, right, (((0,), (0,)), ((), ())), preferred_element_type=F32)


def fsend(block, far, side):
    size = lax.axis_size("fsdp")
    pairs = size // 2
    perm = [(s, ((s // 2 + far) % pairs) * 2 + ((s % 2) ^ side)) for s in range(size)]
    return lax.ppermute(block, "fsdp", perm)


def gsend(block, flip):
    return lax.ppermute(block, "grp", [(s, s ^ flip) for s in range(lax.axis_size("grp"))])


def gather_ring(block):
    blocks = []
    current = block
    for far in range(lax.axis_size("fsdp") // 2):
        if far:
            current = fsend(current, 1, 0)
        blocks += [current, fsend(current, 0, 1)]
    return blocks


def gather_direct(block):
    blocks = []
    for far in range(lax.axis_size("fsdp") // 2):
        current = fsend(block, far, 0) if far else block
        blocks += [current, fsend(current, 0, 1)]
    return blocks


def quarter(array, index, axis=0):
    size = array.shape[axis] // 4
    return lax.dynamic_slice_in_dim(array, index * size, size, axis)


def grp_scatter(partial, g, axis):
    away = [quarter(partial, g ^ 1, axis), quarter(partial, g ^ 3, axis)]
    kept = [quarter(partial, g, axis), quarter(partial, g ^ 2, axis)]
    got = gsend(jnp.stack(away).astype(BF), 1)
    far = gsend((kept[1] + got[1].astype(F32)).astype(BF), 2)
    return kept[0] + got[0].astype(F32) + far.astype(F32)


def local(
    caption_states,
    caption_lens,
    text_gain,
    text_query,
    text_key,
    text_value,
    text_bias,
    text_out,
    final_gain,
    cross_key,
    cross_value,
    video_states,
    video_counts,
    sample_caption,
    cross_query,
    cross_out,
    out_grad,
):
    column = lax.axis_index("fsdp")
    g = lax.axis_index("grp")
    fsdp = lax.axis_size("fsdp")
    pairs = fsdp // 2
    z, y = column // 2, column % 2
    caps_local, cap_len, text_width = caption_states.shape
    tokens, model_width = video_states.shape
    width_local = cross_key.shape[1]
    cross_local = width_local // HEAD_SIZE
    query_rows = cross_query.shape[0]

    def source(far, side):
        return ((z - far) % pairs) * 2 + (y ^ side)

    def target(far, side):
        return ((z + far) % pairs) * 2 + (y ^ side)

    query_blocks = gather_ring(cross_query)
    out_blocks = gather_ring(cross_out)
    full_query = jnp.zeros((model_width, width_local), BF)
    full_out = jnp.zeros((width_local, model_width), BF)
    for far in range(pairs):
        for side in range(2):
            start = source(far, side) * query_rows
            full_query = lax.dynamic_update_slice(
                full_query, query_blocks[2 * far + side], (start, jnp.int32(0))
            )
            full_out = lax.dynamic_update_slice(
                full_out, out_blocks[2 * far + side], (jnp.int32(0), start)
            )

    own_kv = jnp.concatenate([cross_key, cross_value], axis=1)
    other_kv = fsend(own_kv, 0, 1)
    pair_kv = jnp.concatenate(
        [jnp.where(y == 0, own_kv, other_kv), jnp.where(y == 0, other_kv, own_kv)], axis=0
    )

    local_lens = lax.dynamic_slice_in_dim(caption_lens, column * caps_local, caps_local)
    flat_states = caption_states.reshape(caps_local * cap_len, text_width).astype(F32)
    text_normed = rms_scale(flat_states, text_gain).astype(BF)
    local_heads = text_bias.shape[0]
    head_width = text_query.shape[1] // local_heads

    def heads_of(weight):
        return mm(text_normed, weight).astype(BF).reshape(
            caps_local, cap_len, local_heads, head_width
        )

    text_queries = heads_of(text_query)
    text_keys = heads_of(text_key)
    text_values = heads_of(text_value)
    text_scores = (
        jnp.einsum("cihd,cjhd->chij", text_queries, text_keys, preferred_element_type=F32)
        + text_bias[None]
    )
    key_valid = jnp.arange(cap_len, dtype=jnp.int32)[None, :] < local_lens[:, None]
    exp_scores = jnp.where(key_valid[:, None, None, :], jnp.exp(text_scores), 0.0)
    text_weights = (exp_scores / jnp.sum(exp_scores, axis=-1, keepdims=True)).astype(BF)
    text_mixed = jnp.einsum(
        "chij,cjhd->cihd", text_weights, text_values, preferred_element_type=F32
    )
    text_mixed = text_mixed.astype(BF).reshape(caps_local * cap_len, local_heads * head_width)
    partial_text = mm(text_mixed, text_out)
    text_rows = grp_scatter(partial_text, g, 0)
    encoded = rms_scale(quarter(flat_states, g) + text_rows, final_gain).astype(BF)

    part = text_width // pairs
    pieces = [
        lax.dynamic_slice_in_dim(encoded, ((z + far) % pairs) * part, part, 1)
        for far in range(pairs)
    ]
    mine = jnp.stack([fsend(p, far, 0) if far else p for far, p in enumerate(pieces)])
    over_x = jnp.concatenate([mine[:, None], gsend(mine, 2)[:, None]], axis=1)
    over_core = jnp.stack([over_x, gsend(over_x, 1)], axis=2)
    kv_partial = mm(over_core.reshape(-1, part), pair_kv).reshape(pairs, cap_len, 2 * width_local)
    kv_sum = kv_partial[0]
    for far in range(1, pairs):
        kv_sum += fsend(kv_partial[far].astype(BF), pairs - far, 0).astype(F32)
    kv_rows = kv_sum.astype(BF).reshape(4, cap_len // 4, 2 * width_local)
    order = jnp.arange(4, dtype=jnp.int32) ^ g
    cap_kv = jnp.concatenate(
        [lax.dynamic_slice_in_dim(kv_rows, order[k], 1, 0) for k in range(4)], axis=0
    ).reshape(cap_len, 2 * width_local)
    all_kv = jnp.stack(gather_direct(cap_kv))

    video = video_states.astype(F32)
    center = video - jnp.mean(video, axis=-1, keepdims=True)
    inverse = lax.rsqrt(jnp.mean(center * center, axis=-1, keepdims=True) + 1e-06)
    video_hat = center * inverse
    video_normed = video_hat.astype(BF)

    both = jnp.stack([quarter(video_normed, g), quarter(out_grad, g)])
    tiles = []
    for far in range(pairs):
        for side in range(2):
            tile = lax.dynamic_slice_in_dim(both, target(far, side) * query_rows, query_rows, 2)
            tiles.append(fsend(tile, far, side) if far or side else tile)
    tiles = jnp.stack(tiles)
    tiles_x = jnp.stack([tiles, gsend(tiles, 2)], axis=2)
    tiles_all = jnp.stack([tiles_x, gsend(tiles_x, 1)], axis=3)
    normed_tile = tiles_all[:, 0].reshape(-1, query_rows)
    grad_tile = tiles_all[:, 1].reshape(-1, query_rows)

    caption_total = all_kv.shape[0]
    positions = column * tokens + jnp.arange(tokens, dtype=jnp.int32)
    sample_end = jnp.cumsum(video_counts)
    token_sample = jnp.sum((sample_end[None, :] <= positions[:, None]).astype(jnp.int32), axis=1)
    slot_count = 3
    slot_sample = token_sample[0] + jnp.arange(slot_count, dtype=jnp.int32)
    slot_valid = slot_sample < caption_total
    slot_clipped = jnp.minimum(slot_sample, caption_total - 1)
    numbers = jnp.arange(caption_total, dtype=jnp.int32)
    slot_pick = slot_clipped[:, None] == numbers[None, :]
    slot_caption = jnp.sum(jnp.where(slot_pick, sample_caption[None, :], 0), axis=1)
    caption_pick = slot_caption[:, None] == numbers[None, :]
    slot_lens = jnp.sum(jnp.where(caption_pick, caption_lens[None, :], 0), axis=1)
    slot_member = token_sample[None, :] == slot_sample[:, None]
    member_float = slot_member.astype(F32)
    member_half = slot_member.astype(BF)
    slot_entry = ((z - slot_caption // 2) % pairs) * 2 + ((slot_caption % 2) ^ y)
    slot_kv = jnp.take(all_kv, slot_entry, axis=0)
    slot_keys = slot_kv[..., :width_local].reshape(slot_count, cap_len, cross_local, HEAD_SIZE)
    slot_values = slot_kv[..., width_local:].reshape(slot_count, cap_len, cross_local, HEAD_SIZE)
    token_lens = jnp.sum(jnp.where(slot_member, slot_lens[:, None], 0), axis=0)

    query_sum = mm(video_normed, full_query)
    queries = query_sum.astype(BF)
    d_attended = contract_last(out_grad, full_out).astype(BF).reshape(
        tokens, cross_local, HEAD_SIZE
    )
    score_scale = 1.0 / math.sqrt(HEAD_SIZE)
    query_heads = queries.reshape(tokens, cross_local, HEAD_SIZE)
    slot_scores = jnp.einsum("thd,kjhd->kthj", query_heads, slot_keys, preferred_element_type=F32)
    scores = jnp.sum(member_float[:, :, None, None] * slot_scores, axis=0) * score_scale
    token_valid = (jnp.arange(cap_len, dtype=jnp.int32)[None, :] < token_lens[:, None])[:, None, :]
    exp_video = jnp.where(token_valid, jnp.exp(scores), 0.0)
    weights = exp_video / jnp.sum(exp_video, axis=-1, keepdims=True)
    probs = weights.astype(BF)
    masked_probs = member_half[:, :, None, None] * probs[None]
    attended = jnp.einsum("kthj,kjhd->thd", masked_probs, slot_values, preferred_element_type=F32)
    attended = attended.astype(BF).reshape(tokens, width_local)

    def reorder(array):
        return jnp.concatenate([quarter(array, order[k]) for k in range(4)], axis=0)

    all_attended = jnp.concatenate(gather_direct(reorder(attended)), axis=0)
    out_weight_grad = contract_first(all_attended, grad_tile)

    out_share = grp_scatter(mm(attended, full_out), g, 1)
    updated = (quarter(video, g, 1) + out_share).astype(BF)

    slot_dprobs = jnp.einsum("thd,kjhd->kthj", d_attended, slot_values, preferred_element_type=F32)
    d_probs = jnp.sum(member_float[:, :, None, None] * slot_dprobs, axis=0)
    d_scores = (
        weights * (d_probs - jnp.sum(weights * d_probs, axis=-1, keepdims=True)) * score_scale
    ).astype(BF)
    masked_scores = member_half[:, :, None, None] * d_scores[None]
    d_queries = jnp.einsum("kthj,kjhd->thd", masked_scores, slot_keys, preferred_element_type=F32)
    d_queries = d_queries.astype(BF).reshape(tokens, width_local)
    all_d_queries = jnp.concatenate(gather_direct(reorder(d_queries)), axis=0)
    query_grad = contract_first(normed_tile, all_d_queries)

    key_slots = jnp.einsum("kthj,thd->kjhd", masked_scores, query_heads, preferred_element_type=F32)
    value_slots = jnp.einsum("kthj,thd->kjhd", masked_probs, d_attended, preferred_element_type=F32)
    slot_terms = jnp.concatenate(
        [
            key_slots.reshape(slot_count, cap_len, width_local),
            value_slots.reshape(slot_count, cap_len, width_local),
        ],
        axis=-1,
    )

    def caption_terms(far, side):
        picked = (slot_caption == target(far, side)) & slot_valid
        return jnp.sum(jnp.where(picked[:, None, None], slot_terms, 0.0), axis=0)

    away = jnp.stack([caption_terms(far, 1).astype(BF) for far in range(pairs)])
    got = fsend(away, 0, 1).astype(F32)
    kv_grads = caption_terms(0, 0) + got[0]
    for far in range(1, pairs):
        kv_grads += fsend((caption_terms(far, 0) + got[far]).astype(BF), far, 0).astype(F32)
    kv_grads = kv_grads.astype(BF)[None]
    key_grad = kv_grads[:, :, :width_local]
    value_grad = kv_grads[:, :, width_local:]

    d_wide = d_queries.astype(F32)
    column_sum = jnp.sum(full_query.astype(F32), axis=0)
    row_sums = jnp.stack(
        [jnp.sum(d_wide * column_sum, axis=-1), jnp.sum(d_wide * query_sum, axis=-1)]
    )
    row_sums = row_sums + gsend(row_sums, 1)
    row_sums = (row_sums + gsend(row_sums, 2)) / model_width
    d_share = grp_scatter(contract_last(d_queries, full_query), g, 1)
    input_grad = (
        quarter(out_grad, g, 1).astype(F32)
        + inverse
        * (d_share - row_sums[0][:, None] - quarter(video_hat, g, 1) * row_sums[1][:, None])
    ).astype(BF)
    return (updated, input_grad, query_grad, out_weight_grad, key_grad, value_grad)


def solution(mesh):
    in_specs = (
        P("fsdp", None, None),
        P(),
        P(),
        P(None, "grp"),
        P(None, "grp"),
        P(None, "grp"),
        P("grp", None, None),
        P("grp", None),
        P(),
        P("fsdp", "grp"),
        P("fsdp", "grp"),
        P("fsdp", None),
        P(),
        P(),
        P("fsdp", "grp"),
        P("grp", "fsdp"),
        P("fsdp", None),
    )
    out_specs = (
        P("fsdp", "grp"),
        P("fsdp", "grp"),
        P("fsdp", "grp"),
        P("grp", "fsdp"),
        P("fsdp", None, "grp"),
        P("fsdp", None, "grp"),
    )
    return jax.shard_map(local, mesh=mesh, in_specs=in_specs, out_specs=out_specs, check_vma=False)
```

```python
import math

import jax
import jax.numpy as jnp
from jax import lax
from jax.experimental import pallas as pl
from jax.experimental.pallas import tpu as pltpu
from jax.sharding import PartitionSpec as P

HEAD_SIZE = 128
BF = jnp.bfloat16
F32 = jnp.float32
SLOTS = 3
VMEM_BYTES = 50 * 1024 * 1024


def rms_scale(values, gain):
    mean_square = jnp.mean(values * values, axis=-1, keepdims=True)
    return values * lax.rsqrt(mean_square + 1e-06) * gain


def mm(left, right):
    return jnp.dot(left, right, preferred_element_type=F32)


def contract_last(left, right):
    return lax.dot_general(left, right, (((1,), (1,)), ((), ())), preferred_element_type=F32)


def contract_first(left, right):
    return lax.dot_general(left, right, (((0,), (0,)), ((), ())), preferred_element_type=F32)


def fsend(block, far, side):
    size = lax.axis_size("fsdp")
    pairs = size // 2
    perm = [(s, ((s // 2 + far) % pairs) * 2 + ((s % 2) ^ side)) for s in range(size)]
    return lax.ppermute(block, "fsdp", perm)


def gsend(block, flip):
    return lax.ppermute(block, "grp", [(s, s ^ flip) for s in range(lax.axis_size("grp"))])


def gather_ring(block):
    blocks = []
    current = block
    for far in range(lax.axis_size("fsdp") // 2):
        if far:
            current = fsend(current, 1, 0)
        blocks += [current, fsend(current, 0, 1)]
    return blocks


def gather_direct(block):
    blocks = []
    for far in range(lax.axis_size("fsdp") // 2):
        current = fsend(block, far, 0) if far else block
        blocks += [current, fsend(current, 0, 1)]
    return blocks


def quarter(array, index, axis=0):
    size = array.shape[axis] // 4
    return lax.dynamic_slice_in_dim(array, index * size, size, axis)


def grp_scatter(partial, g, axis):
    away = [quarter(partial, g ^ 1, axis), quarter(partial, g ^ 3, axis)]
    kept = [quarter(partial, g, axis), quarter(partial, g ^ 2, axis)]
    got = gsend(jnp.stack(away).astype(BF), 1)
    far = gsend((kept[1] + got[1].astype(F32)).astype(BF), 2)
    return kept[0] + got[0].astype(F32) + far.astype(F32)


def local_general(
    caption_states,
    caption_lens,
    text_gain,
    text_query,
    text_key,
    text_value,
    text_bias,
    text_out,
    final_gain,
    cross_key,
    cross_value,
    video_states,
    video_counts,
    sample_caption,
    cross_query,
    cross_out,
    out_grad,
):
    column = lax.axis_index("fsdp")
    g = lax.axis_index("grp")
    fsdp = lax.axis_size("fsdp")
    pairs = fsdp // 2
    z, y = column // 2, column % 2
    caps_local, cap_len, text_width = caption_states.shape
    tokens, model_width = video_states.shape
    width_local = cross_key.shape[1]
    cross_local = width_local // HEAD_SIZE
    query_rows = cross_query.shape[0]

    def source(far, side):
        return ((z - far) % pairs) * 2 + (y ^ side)

    def target(far, side):
        return ((z + far) % pairs) * 2 + (y ^ side)

    query_blocks = gather_ring(cross_query)
    out_blocks = gather_ring(cross_out)
    full_query = jnp.zeros((model_width, width_local), BF)
    full_out = jnp.zeros((width_local, model_width), BF)
    for far in range(pairs):
        for side in range(2):
            start = source(far, side) * query_rows
            full_query = lax.dynamic_update_slice(
                full_query, query_blocks[2 * far + side], (start, jnp.int32(0))
            )
            full_out = lax.dynamic_update_slice(
                full_out, out_blocks[2 * far + side], (jnp.int32(0), start)
            )

    own_kv = jnp.concatenate([cross_key, cross_value], axis=1)
    other_kv = fsend(own_kv, 0, 1)
    pair_kv = jnp.concatenate(
        [jnp.where(y == 0, own_kv, other_kv), jnp.where(y == 0, other_kv, own_kv)], axis=0
    )

    local_lens = lax.dynamic_slice_in_dim(caption_lens, column * caps_local, caps_local)
    flat_states = caption_states.reshape(caps_local * cap_len, text_width).astype(F32)
    text_normed = rms_scale(flat_states, text_gain).astype(BF)
    local_heads = text_bias.shape[0]
    head_width = text_query.shape[1] // local_heads

    def heads_of(weight):
        return mm(text_normed, weight).astype(BF).reshape(
            caps_local, cap_len, local_heads, head_width
        )

    text_queries = heads_of(text_query)
    text_keys = heads_of(text_key)
    text_values = heads_of(text_value)
    text_scores = (
        jnp.einsum("cihd,cjhd->chij", text_queries, text_keys, preferred_element_type=F32)
        + text_bias[None]
    )
    key_valid = jnp.arange(cap_len, dtype=jnp.int32)[None, :] < local_lens[:, None]
    exp_scores = jnp.where(key_valid[:, None, None, :], jnp.exp(text_scores), 0.0)
    text_weights = (exp_scores / jnp.sum(exp_scores, axis=-1, keepdims=True)).astype(BF)
    text_mixed = jnp.einsum(
        "chij,cjhd->cihd", text_weights, text_values, preferred_element_type=F32
    )
    text_mixed = text_mixed.astype(BF).reshape(caps_local * cap_len, local_heads * head_width)
    partial_text = mm(text_mixed, text_out)
    text_rows = grp_scatter(partial_text, g, 0)
    encoded = rms_scale(quarter(flat_states, g) + text_rows, final_gain).astype(BF)

    part = text_width // pairs
    pieces = [
        lax.dynamic_slice_in_dim(encoded, ((z + far) % pairs) * part, part, 1)
        for far in range(pairs)
    ]
    mine = jnp.stack([fsend(p, far, 0) if far else p for far, p in enumerate(pieces)])
    over_x = jnp.concatenate([mine[:, None], gsend(mine, 2)[:, None]], axis=1)
    over_core = jnp.stack([over_x, gsend(over_x, 1)], axis=2)
    kv_partial = mm(over_core.reshape(-1, part), pair_kv).reshape(pairs, cap_len, 2 * width_local)
    kv_sum = kv_partial[0]
    for far in range(1, pairs):
        kv_sum += fsend(kv_partial[far].astype(BF), pairs - far, 0).astype(F32)
    kv_rows = kv_sum.astype(BF).reshape(4, cap_len // 4, 2 * width_local)
    order = jnp.arange(4, dtype=jnp.int32) ^ g
    cap_kv = jnp.concatenate(
        [lax.dynamic_slice_in_dim(kv_rows, order[k], 1, 0) for k in range(4)], axis=0
    ).reshape(cap_len, 2 * width_local)
    all_kv = jnp.stack(gather_direct(cap_kv))

    video = video_states.astype(F32)
    center = video - jnp.mean(video, axis=-1, keepdims=True)
    inverse = lax.rsqrt(jnp.mean(center * center, axis=-1, keepdims=True) + 1e-06)
    video_hat = center * inverse
    video_normed = video_hat.astype(BF)

    both = jnp.stack([quarter(video_normed, g), quarter(out_grad, g)])
    tiles = []
    for far in range(pairs):
        for side in range(2):
            tile = lax.dynamic_slice_in_dim(both, target(far, side) * query_rows, query_rows, 2)
            tiles.append(fsend(tile, far, side) if far or side else tile)
    tiles = jnp.stack(tiles)
    tiles_x = jnp.stack([tiles, gsend(tiles, 2)], axis=2)
    tiles_all = jnp.stack([tiles_x, gsend(tiles_x, 1)], axis=3)
    normed_tile = tiles_all[:, 0].reshape(-1, query_rows)
    grad_tile = tiles_all[:, 1].reshape(-1, query_rows)

    caption_total = all_kv.shape[0]
    positions = column * tokens + jnp.arange(tokens, dtype=jnp.int32)
    sample_end = jnp.cumsum(video_counts)
    token_sample = jnp.sum((sample_end[None, :] <= positions[:, None]).astype(jnp.int32), axis=1)
    slot_count = 3
    slot_sample = token_sample[0] + jnp.arange(slot_count, dtype=jnp.int32)
    slot_valid = slot_sample < caption_total
    slot_clipped = jnp.minimum(slot_sample, caption_total - 1)
    numbers = jnp.arange(caption_total, dtype=jnp.int32)
    slot_pick = slot_clipped[:, None] == numbers[None, :]
    slot_caption = jnp.sum(jnp.where(slot_pick, sample_caption[None, :], 0), axis=1)
    caption_pick = slot_caption[:, None] == numbers[None, :]
    slot_lens = jnp.sum(jnp.where(caption_pick, caption_lens[None, :], 0), axis=1)
    slot_member = token_sample[None, :] == slot_sample[:, None]
    member_float = slot_member.astype(F32)
    member_half = slot_member.astype(BF)
    slot_entry = ((z - slot_caption // 2) % pairs) * 2 + ((slot_caption % 2) ^ y)
    slot_kv = jnp.take(all_kv, slot_entry, axis=0)
    slot_keys = slot_kv[..., :width_local].reshape(slot_count, cap_len, cross_local, HEAD_SIZE)
    slot_values = slot_kv[..., width_local:].reshape(slot_count, cap_len, cross_local, HEAD_SIZE)
    token_lens = jnp.sum(jnp.where(slot_member, slot_lens[:, None], 0), axis=0)

    query_sum = mm(video_normed, full_query)
    queries = query_sum.astype(BF)
    d_attended = contract_last(out_grad, full_out).astype(BF).reshape(
        tokens, cross_local, HEAD_SIZE
    )
    score_scale = 1.0 / math.sqrt(HEAD_SIZE)
    query_heads = queries.reshape(tokens, cross_local, HEAD_SIZE)
    slot_scores = jnp.einsum("thd,kjhd->kthj", query_heads, slot_keys, preferred_element_type=F32)
    scores = jnp.sum(member_float[:, :, None, None] * slot_scores, axis=0) * score_scale
    token_valid = (jnp.arange(cap_len, dtype=jnp.int32)[None, :] < token_lens[:, None])[:, None, :]
    exp_video = jnp.where(token_valid, jnp.exp(scores), 0.0)
    weights = exp_video / jnp.sum(exp_video, axis=-1, keepdims=True)
    probs = weights.astype(BF)
    masked_probs = member_half[:, :, None, None] * probs[None]
    attended = jnp.einsum("kthj,kjhd->thd", masked_probs, slot_values, preferred_element_type=F32)
    attended = attended.astype(BF).reshape(tokens, width_local)

    def reorder(array):
        return jnp.concatenate([quarter(array, order[k]) for k in range(4)], axis=0)

    all_attended = jnp.concatenate(gather_direct(reorder(attended)), axis=0)
    out_weight_grad = contract_first(all_attended, grad_tile)

    out_share = grp_scatter(mm(attended, full_out), g, 1)
    updated = (quarter(video, g, 1) + out_share).astype(BF)

    slot_dprobs = jnp.einsum("thd,kjhd->kthj", d_attended, slot_values, preferred_element_type=F32)
    d_probs = jnp.sum(member_float[:, :, None, None] * slot_dprobs, axis=0)
    d_scores = (
        weights * (d_probs - jnp.sum(weights * d_probs, axis=-1, keepdims=True)) * score_scale
    ).astype(BF)
    masked_scores = member_half[:, :, None, None] * d_scores[None]
    d_queries = jnp.einsum("kthj,kjhd->thd", masked_scores, slot_keys, preferred_element_type=F32)
    d_queries = d_queries.astype(BF).reshape(tokens, width_local)
    all_d_queries = jnp.concatenate(gather_direct(reorder(d_queries)), axis=0)
    query_grad = contract_first(normed_tile, all_d_queries)

    key_slots = jnp.einsum("kthj,thd->kjhd", masked_scores, query_heads, preferred_element_type=F32)
    value_slots = jnp.einsum("kthj,thd->kjhd", masked_probs, d_attended, preferred_element_type=F32)
    slot_terms = jnp.concatenate(
        [
            key_slots.reshape(slot_count, cap_len, width_local),
            value_slots.reshape(slot_count, cap_len, width_local),
        ],
        axis=-1,
    )

    def caption_terms(far, side):
        picked = (slot_caption == target(far, side)) & slot_valid
        return jnp.sum(jnp.where(picked[:, None, None], slot_terms, 0.0), axis=0)

    away = jnp.stack([caption_terms(far, 1).astype(BF) for far in range(pairs)])
    got = fsend(away, 0, 1).astype(F32)
    kv_grads = caption_terms(0, 0) + got[0]
    for far in range(1, pairs):
        kv_grads += fsend((caption_terms(far, 0) + got[far]).astype(BF), far, 0).astype(F32)
    kv_grads = kv_grads.astype(BF)[None]
    key_grad = kv_grads[:, :, :width_local]
    value_grad = kv_grads[:, :, width_local:]

    d_wide = d_queries.astype(F32)
    column_sum = jnp.sum(full_query.astype(F32), axis=0)
    row_sums = jnp.stack(
        [jnp.sum(d_wide * column_sum, axis=-1), jnp.sum(d_wide * query_sum, axis=-1)]
    )
    row_sums = row_sums + gsend(row_sums, 1)
    row_sums = (row_sums + gsend(row_sums, 2)) / model_width
    d_share = grp_scatter(contract_last(d_queries, full_query), g, 1)
    input_grad = (
        quarter(out_grad, g, 1).astype(F32)
        + inverse
        * (d_share - row_sums[0][:, None] - quarter(video_hat, g, 1) * row_sums[1][:, None])
    ).astype(BF)
    return (updated, input_grad, query_grad, out_weight_grad, key_grad, value_grad)


def after(value, *others):
    return lax.optimization_barrier((value, *others))[0]


def call(body, out_shape, operands, scalars, scratch=(), flops=0):
    shapes = jax.tree.leaves(out_shape)
    moved = sum(math.prod(a.shape) * a.dtype.itemsize for a in (*operands, *shapes))
    specs = [pl.BlockSpec(memory_space=pltpu.SMEM)] * scalars
    specs += [pl.BlockSpec(memory_space=pltpu.VMEM)] * (len(operands) - scalars)
    return pl.pallas_call(
        body,
        out_shape=out_shape,
        in_specs=specs,
        out_specs=jax.tree.map(lambda _: pl.BlockSpec(memory_space=pltpu.VMEM), out_shape),
        scratch_shapes=list(scratch),
        compiler_params=pltpu.CompilerParams(vmem_limit_bytes=VMEM_BYTES),
        cost_estimate=pl.CostEstimate(flops=flops, bytes_accessed=moved, transcendentals=0),
    )(*operands)


def shaped(shape, dtype=BF):
    return jax.ShapeDtypeStruct(shape, dtype)


def aligned(start, unit):
    return pl.multiple_of(start, unit)


def prepare_video(video_states, out_grad, place, pairs, part):
    tokens, model_width = video_states.shape
    rows = tokens // 4

    def body(place_ref, video_ref, grad_ref, normed_ref, mean_ref, inverse_ref, *tile_refs):
        @pl.loop(0, tokens // 32)
        def _(step):
            here = pl.ds(aligned(step * 32, 32), 32)
            values = video_ref[here, :].astype(F32)
            mean = jnp.mean(values, axis=-1, keepdims=True)
            center = values - mean
            inverse = lax.rsqrt(jnp.mean(center * center, axis=-1, keepdims=True) + 1e-06)
            normed_ref[here, :] = (center * inverse).astype(BF)
            mean_ref[here, :] = mean
            inverse_ref[here, :] = inverse

        z, y, g = place_ref[0], place_ref[1], place_ref[2]
        mine = pl.ds(aligned(g * rows, rows), rows)
        for far in range(pairs):
            for side in range(2):
                to = lax.rem(z + far, pairs) * 2 + (y ^ side)
                columns = pl.ds(aligned(to * part, 128), part)
                tile_refs[far][side, 0] = normed_ref[mine, columns]
                tile_refs[far][side, 1] = grad_ref[mine, columns]

    out = [shaped((tokens, model_width)), shaped((tokens, 1), F32), shaped((tokens, 1), F32)]
    out += [shaped((2, 2, rows, part))] * pairs
    normed, mean, inverse, *tiles = call(body, out, (place, video_states, out_grad), 1)
    return normed, mean, inverse, tiles


def project_rows(normed, out_grad, blocks, place, pairs, part):
    tokens = normed.shape[0]
    width = blocks[0].shape[1]

    def body(place_ref, normed_ref, grad_ref, *refs):
        block_refs, (query_ref, d_ref, sum_ref) = refs[:-3], refs[-3:]
        z, y = place_ref[0], place_ref[1]
        query = jnp.zeros((tokens, width), F32)
        d_attended = jnp.zeros((tokens, width), F32)
        total = jnp.zeros((1, width), F32)
        for far in range(pairs):
            for side in range(2):
                block = block_refs[2 * far + side]
                origin = lax.rem(z - far + pairs, pairs) * 2 + (y ^ side)
                columns = pl.ds(aligned(origin * part, 128), part)
                weight = block[:part, :]
                query += mm(normed_ref[:, columns], weight)
                d_attended += contract_last(grad_ref[:, columns], block[part : part + width, :])
                total += jnp.sum(weight.astype(F32), axis=0, keepdims=True)
        query_ref[...] = query.astype(BF)
        d_ref[...] = d_attended.astype(BF)
        sum_ref[...] = total

    out = [shaped((tokens, width)), shaped((tokens, width)), shaped((1, width), F32)]
    flops = 4 * tokens * width * normed.shape[1]
    return call(body, out, (place, normed, out_grad, *blocks), 1, flops=flops)


def project_captions(parts, own_key, own_value, side_block, place, pairs, skip):
    quarter_rows, depth = parts[0].shape[1:]
    half = depth // 2
    width = own_key.shape[1]

    def body(place_ref, *refs):
        part_refs = refs[:4]
        key_ref, value_ref, side_ref = refs[4:7]
        out_refs = refs[7:]
        y = place_ref[1]
        mine = pl.ds(aligned(y * half, 128), half)
        theirs = pl.ds(aligned((1 - y) * half, 128), half)
        own = jnp.concatenate([r[far, :, mine] for far in range(pairs) for r in part_refs], 0)
        other = jnp.concatenate([r[far, :, theirs] for far in range(pairs) for r in part_refs], 0)
        keys = mm(own, key_ref[...]) + mm(other, side_ref[skip : skip + half, :])
        values = mm(own, value_ref[...]) + mm(other, side_ref[skip + half : skip + 2 * half, :])
        for far in range(pairs):
            rows = slice(far * 4 * quarter_rows, (far + 1) * 4 * quarter_rows)
            out_refs[far][:, :width] = keys[rows].astype(BF)
            out_refs[far][:, width:] = values[rows].astype(BF)

    out = [shaped((4 * quarter_rows, 2 * width))] * pairs
    flops = 4 * pairs * 4 * quarter_rows * depth * width
    operands = (place, *parts, own_key, own_value, side_block)
    return call(body, out, operands, 1, flops=flops)


def attend(queries, d_attended, column_sum, kv_blocks, place, counts, sample_caption, lens, pairs):
    tokens, width = queries.shape
    cap_len = kv_blocks[0].shape[0]
    heads = width // HEAD_SIZE
    captions = counts.shape[0]
    keys_wide = SLOTS * cap_len
    cap_quarter, row_quarter = cap_len // 4, tokens // 4
    scale = 1.0 / math.sqrt(HEAD_SIZE)

    def body(place_ref, count_ref, caption_ref, len_ref, q_ref, da_ref, sum_ref, *refs):
        block_refs = refs[: len(kv_blocks)]
        both_ref, att_ref, dq_ref, rows_ref, own_ref, away_ref, kv_ref = refs[len(kv_blocks) :]
        z, y, g = place_ref[0], place_ref[1], place_ref[2]
        base = (z * 2 + y) * tokens

        def find(sample, carry):
            total, first, start = carry
            total = total + count_ref[sample]
            past = total <= base
            return total, first + past.astype(jnp.int32), jnp.where(past, total, start)

        zero = jnp.int32(0)
        _, first, start = lax.fori_loop(0, captions, find, (zero, zero, zero))
        low, high, length, far_to, side_to, valid = [], [], [], [], [], []
        edge = start - base
        for slot in range(SLOTS):
            ok = first + slot < captions
            sample = jnp.minimum(first + slot, captions - 1)
            caption = caption_ref[sample]
            low.append(edge)
            edge = edge + jnp.where(ok, count_ref[sample], 0)
            high.append(edge)
            length.append(len_ref[caption])
            far_to.append(lax.rem(caption // 2 - z + pairs, pairs))
            side_to.append(lax.rem(caption, 2) ^ y)
            valid.append(ok)
            entry = lax.rem(z - caption // 2 + pairs, pairs) * 2 + side_to[slot]
            for number, block in enumerate(block_refs):

                @pl.when(entry == number)
                def _(slot=slot, block=block):
                    kv_ref[slot * cap_len : (slot + 1) * cap_len, :] = block[...]

        token = lax.broadcasted_iota(jnp.int32, (tokens, keys_wide), 0)
        column = lax.broadcasted_iota(jnp.int32, (tokens, keys_wide), 1)
        slot_of = column // cap_len
        inside = column % cap_len
        key = ((inside // cap_quarter) ^ g) * cap_quarter + inside % cap_quarter

        def of_slot(values):
            return jnp.where(slot_of == 0, values[0], jnp.where(slot_of == 1, values[1], values[2]))

        live = (token >= of_slot(low)) & (token < of_slot(high)) & (key < of_slot(length))
        own_ref[...] = jnp.zeros_like(own_ref)
        away_ref[...] = jnp.zeros_like(away_ref)
        first_sum = jnp.zeros((tokens, 1), F32)
        second_sum = jnp.zeros((tokens, 1), F32)
        for head in range(heads):
            at = slice(head * HEAD_SIZE, (head + 1) * HEAD_SIZE)
            at_value = slice(width + head * HEAD_SIZE, width + (head + 1) * HEAD_SIZE)
            query, d_att = q_ref[:, at], da_ref[:, at]
            keys, values = kv_ref[:, at], kv_ref[:, at_value]
            grown = jnp.where(live, jnp.exp(contract_last(query, keys) * scale), 0.0)
            weights = grown * (1.0 / jnp.sum(grown, axis=-1, keepdims=True))
            probs = weights.astype(BF)
            d_probs = contract_last(d_att, values)
            mixed = jnp.sum(weights * d_probs, axis=-1, keepdims=True)
            d_scores = (weights * (d_probs - mixed) * scale).astype(BF)
            att_ref[:, at] = mm(probs, values).astype(BF)
            d_query = mm(d_scores, keys).astype(BF)
            dq_ref[:, at] = d_query
            d_wide = d_query.astype(F32)
            first_sum += jnp.sum(d_wide * sum_ref[:, at], axis=-1, keepdims=True)
            second_sum += jnp.sum(d_wide * query.astype(F32), axis=-1, keepdims=True)
            key_grad = contract_first(d_scores, query).astype(BF)
            value_grad = contract_first(probs, d_att).astype(BF)
            for slot in range(SLOTS):
                for part in range(4):
                    held = slice(
                        slot * cap_len + part * cap_quarter, slot * cap_len + (part + 1) * cap_quarter
                    )
                    to = pl.ds(aligned((part ^ g) * cap_quarter, cap_quarter), cap_quarter)
                    for side, target_ref in enumerate((own_ref, away_ref)):

                        @pl.when(valid[slot] & (side_to[slot] == side))
                        def _(slot=slot, held=held, to=to, target_ref=target_ref):
                            target_ref[far_to[slot], to, at] = key_grad[held]
                            target_ref[far_to[slot], to, at_value] = value_grad[held]

        rows_ref[:, 0:1] = first_sum
        rows_ref[:, 1:2] = second_sum
        for part in range(4):
            rows = pl.ds(aligned((part ^ g) * row_quarter, row_quarter), row_quarter)
            to = slice(part * row_quarter, (part + 1) * row_quarter)
            both_ref[0, to, :] = att_ref[rows, :]
            both_ref[1, to, :] = dq_ref[rows, :]

    out = [
        shaped((2, tokens, width)),
        shaped((tokens, width)),
        shaped((tokens, width)),
        shaped((tokens, 2), F32),
        shaped((pairs, cap_len, 2 * width)),
        shaped((pairs, cap_len, 2 * width)),
    ]
    operands = (place, counts, sample_caption, lens, queries, d_attended, column_sum, *kv_blocks)
    scratch = [pltpu.VMEM((keys_wide, 2 * width), BF)]
    return call(body, out, operands, 4, scratch, flops=12 * tokens * keys_wide * width)


def project_back(attended, d_queries, blocks, place, pairs, part):
    tokens, width = attended.shape
    model_width = 2 * pairs * part
    per_piece = 2 * pairs // 4

    def body(place_ref, att_ref, dq_ref, *refs):
        block_refs = refs[: len(blocks)]
        halves = (refs[len(blocks) : len(blocks) + 2], refs[len(blocks) + 2 :])
        z, y, g = place_ref[0], place_ref[1], place_ref[2]
        att, d_query = att_ref[...], dq_ref[...]
        for far in range(pairs):
            for side in range(2):
                block = block_refs[2 * far + side]
                origin = lax.rem(z - far + pairs, pairs) * 2 + (y ^ side)
                flip = (origin // per_piece) ^ g
                start = ((flip // 2) * per_piece + lax.rem(origin, per_piece)) * part
                columns = pl.ds(aligned(start, 128), part)
                added = mm(att, block[part : part + width, :]).astype(BF)
                d_normed = contract_last(d_query, block[:part, :]).astype(BF)
                for number, (out_ref, d_ref) in enumerate(halves):

                    @pl.when(lax.rem(flip, 2) == number)
                    def _(out_ref=out_ref, d_ref=d_ref, added=added, d_normed=d_normed):
                        out_ref[:, columns] = added
                        d_ref[:, columns] = d_normed

    out = [shaped((tokens, model_width // 2))] * 4
    flops = 4 * tokens * width * model_width
    return call(body, out, (place, attended, d_queries, *blocks), 1, flops=flops)


def weight_grads(tiles, both_blocks, pairs):
    part = tiles[0].shape[-1]
    width = both_blocks[0].shape[-1]

    def body(*refs):
        tile_refs, block_refs, (query_ref, out_ref) = refs[:4], refs[4:-2], refs[-2:]
        query_grad = jnp.zeros((part, width), F32)
        out_grad = jnp.zeros((width, part), F32)
        for far in range(pairs):
            for side in range(2):
                block = block_refs[2 * far + side]
                normed, grad = (
                    jnp.concatenate([r[far, side, which] for r in tile_refs], axis=0)
                    for which in range(2)
                )
                out_grad += contract_first(block[0], grad)
                query_grad += contract_first(normed, block[1])
        query_ref[...] = query_grad
        out_ref[...] = out_grad

    out = [shaped((part, width), F32), shaped((width, part), F32)]
    flops = 4 * 2 * pairs * both_blocks[0].shape[1] * part * width
    return call(body, out, (*tiles, *both_blocks), 0, flops=flops)


def local(
    caption_states,
    caption_lens,
    text_gain,
    text_query,
    text_key,
    text_value,
    text_bias,
    text_out,
    final_gain,
    cross_key,
    cross_value,
    video_states,
    video_counts,
    sample_caption,
    cross_query,
    cross_out,
    out_grad,
):
    column = lax.axis_index("fsdp")
    g = lax.axis_index("grp")
    pairs = lax.axis_size("fsdp") // 2
    z, y = column // 2, column % 2
    place = jnp.stack([z, y, g]).astype(jnp.int32)
    caps_local, cap_len, text_width = caption_states.shape
    tokens, model_width = video_states.shape
    width_local = cross_key.shape[1]
    part = cross_query.shape[0]

    own_weights = jnp.concatenate([cross_query, cross_out], axis=0)
    ring = [own_weights, fsend(own_weights, 1, 0)]
    side_block = fsend(jnp.concatenate([own_weights, cross_key, cross_value], axis=0), 0, 1)

    local_lens = lax.dynamic_slice_in_dim(caption_lens, column * caps_local, caps_local)
    flat_states = caption_states.reshape(caps_local * cap_len, text_width).astype(F32)
    text_normed = rms_scale(flat_states, text_gain).astype(BF)
    local_heads = text_bias.shape[0]
    head_width = text_query.shape[1] // local_heads

    def heads_of(weight):
        return mm(text_normed, weight).astype(BF).reshape(
            caps_local, cap_len, local_heads, head_width
        )

    text_queries = heads_of(text_query)
    text_keys = heads_of(text_key)
    text_values = heads_of(text_value)
    text_scores = (
        jnp.einsum("cihd,cjhd->chij", text_queries, text_keys, preferred_element_type=F32)
        + text_bias[None]
    )
    key_valid = jnp.arange(cap_len, dtype=jnp.int32)[None, :] < local_lens[:, None]
    exp_scores = jnp.where(key_valid[:, None, None, :], jnp.exp(text_scores), 0.0)
    text_weights = (exp_scores / jnp.sum(exp_scores, axis=-1, keepdims=True)).astype(BF)
    text_mixed = jnp.einsum(
        "chij,cjhd->cihd", text_weights, text_values, preferred_element_type=F32
    )
    text_mixed = text_mixed.astype(BF).reshape(caps_local * cap_len, local_heads * head_width)
    text_mixed = jnp.concatenate([quarter(text_mixed, g ^ k) for k in (0, 2, 1, 3)], axis=0)
    partial_text = mm(text_mixed, text_out).astype(BF)
    partial_text = after(partial_text, ring[1])
    half_rows = partial_text.shape[0] // 2
    quarter_rows = half_rows // 2
    got = gsend(partial_text[half_rows:], 1).astype(F32)
    normed, mean, inverse, tiles = prepare_video(
        after(video_states, partial_text), out_grad, place, pairs, part
    )
    ring.append(fsend(after(ring[1], partial_text), 1, 0))
    kept = partial_text[:half_rows].astype(F32) + got
    text_rows = kept[:quarter_rows] + gsend(kept[quarter_rows:].astype(BF), 2).astype(F32)
    encoded = rms_scale(quarter(flat_states, g) + text_rows, final_gain).astype(BF)
    encoded = after(encoded, ring[2], normed)

    depth = text_width // pairs
    pieces = [
        lax.dynamic_slice_in_dim(encoded, ((z + far) % pairs) * depth, depth, 1)
        for far in range(pairs)
    ]
    mine = jnp.stack([fsend(p, far, 0) if far else p for far, p in enumerate(pieces)])
    over_x = gsend(mine, 2)
    parts = [mine, gsend(mine, 1), over_x, gsend(over_x, 1)]
    current = after(ring[2], mine)
    for far in range(3, pairs):
        current = fsend(current, 1, 0)
        ring.append(current)
    blocks = [own_weights, side_block]
    for block in ring[1:]:
        blocks += [block, fsend(block, 0, 1)]

    kv_partial = project_captions(
        parts, cross_key, cross_value, side_block, place, pairs, own_weights.shape[0]
    )
    kv_partial = after(tuple(kv_partial), ring[-1])
    kv_sum = kv_partial[0].astype(F32)
    for far in range(1, pairs):
        kv_sum += fsend(kv_partial[far], pairs - far, 0).astype(F32)
    kv_blocks = gather_direct(kv_sum.astype(BF))

    queries, d_attended, column_sum = project_rows(normed, out_grad, blocks, place, pairs, part)

    tiles = after(tuple(tiles), kv_blocks[-2])
    over_z = [fsend(t, far, 0) if far else t for far, t in enumerate(tiles)]
    over_y = fsend(jnp.stack([t[1] for t in over_z]), 0, 1)
    tiles = jnp.stack([jnp.stack([t[0] for t in over_z]), over_y], axis=1)
    tiles_x = gsend(tiles, 2)
    tiles = [tiles, gsend(tiles, 1), tiles_x, gsend(tiles_x, 1)]

    both, attended, d_queries, row_sums, kv_own, kv_away = attend(
        queries,
        d_attended,
        column_sum,
        kv_blocks,
        place,
        video_counts,
        sample_caption,
        caption_lens,
        pairs,
    )
    kv_side = fsend(kv_away, 0, 1)
    both_blocks = gather_ring(both)
    row_sums = row_sums + gsend(row_sums, 1)
    row_sums = (row_sums + gsend(row_sums, 2)) / model_width

    out_kept, d_kept, out_away, d_away = project_back(
        attended, d_queries, blocks, place, pairs, part
    )
    slice_width = model_width // 4

    def finish(kept, away):
        kept = kept.astype(F32) + gsend(away, 1).astype(F32)
        sent = gsend(kept[:, slice_width:].astype(BF), 2)
        return kept[:, :slice_width] + sent.astype(F32)

    video = quarter(video_states, g, 1).astype(F32)
    updated = (video + finish(out_kept, out_away)).astype(BF)
    video_hat = (video - mean) * inverse
    d_share = finish(d_kept, d_away)
    input_grad = (
        quarter(out_grad, g, 1).astype(F32)
        + inverse * (d_share - row_sums[:, 0:1] - video_hat * row_sums[:, 1:2])
    ).astype(BF)

    kv_terms = kv_own.astype(F32) + kv_side.astype(F32)
    kv_grads = kv_terms[0]
    for far in range(1, pairs):
        kv_grads += fsend(kv_terms[far].astype(BF), far, 0).astype(F32)
    kv_grads = kv_grads.astype(BF)[None]
    key_grad = kv_grads[:, :, :width_local]
    value_grad = kv_grads[:, :, width_local:]

    query_grad, out_weight_grad = weight_grads(tiles, both_blocks, pairs)
    return (updated, input_grad, query_grad, out_weight_grad, key_grad, value_grad)


def local_of(*arrays):
    cross_query = arrays[14]
    return local_general(*arrays) if cross_query.shape[0] % 128 else local(*arrays)


def solution(mesh):
    in_specs = (
        P("fsdp", None, None),
        P(),
        P(),
        P(None, "grp"),
        P(None, "grp"),
        P(None, "grp"),
        P("grp", None, None),
        P("grp", None),
        P(),
        P("fsdp", "grp"),
        P("fsdp", "grp"),
        P("fsdp", None),
        P(),
        P(),
        P("fsdp", "grp"),
        P("grp", "fsdp"),
        P("fsdp", None),
    )
    out_specs = (
        P("fsdp", "grp"),
        P("fsdp", "grp"),
        P("fsdp", "grp"),
        P("grp", "fsdp"),
        P("fsdp", None, "grp"),
        P("fsdp", None, "grp"),
    )
    return jax.shard_map(
        local_of, mesh=mesh, in_specs=in_specs, out_specs=out_specs, check_vma=False
    )
```

```python
import math

import jax
import jax.numpy as jnp
from jax import lax
from jax.experimental import pallas as pl
from jax.experimental.pallas import tpu as pltpu
from jax.sharding import PartitionSpec as P

HEAD_SIZE = 128
BF = jnp.bfloat16
F32 = jnp.float32
SLOTS = 3
VMEM_BYTES = 50 * 1024 * 1024
SMALL = pl.CostEstimate(flops=1, bytes_accessed=1, transcendentals=0)


def rms_scale(values, gain):
    mean_square = jnp.mean(values * values, axis=-1, keepdims=True)
    return values * lax.rsqrt(mean_square + 1e-06) * gain


def mm(left, right):
    return jnp.dot(left, right, preferred_element_type=F32)


def contract_last(left, right):
    return lax.dot_general(left, right, (((1,), (1,)), ((), ())), preferred_element_type=F32)


def contract_first(left, right):
    return lax.dot_general(left, right, (((0,), (0,)), ((), ())), preferred_element_type=F32)


def fsend(block, far, side):
    size = lax.axis_size("fsdp")
    pairs = size // 2
    perm = [(s, ((s // 2 + far) % pairs) * 2 + ((s % 2) ^ side)) for s in range(size)]
    return lax.ppermute(block, "fsdp", perm)


def gsend(block, flip):
    return lax.ppermute(block, "grp", [(s, s ^ flip) for s in range(lax.axis_size("grp"))])


def gather_ring(block):
    blocks = []
    current = block
    for far in range(lax.axis_size("fsdp") // 2):
        if far:
            current = fsend(current, 1, 0)
        blocks += [current, fsend(current, 0, 1)]
    return blocks


def gather_direct(block):
    blocks = []
    for far in range(lax.axis_size("fsdp") // 2):
        current = fsend(block, far, 0) if far else block
        blocks += [current, fsend(current, 0, 1)]
    return blocks


def quarter(array, index, axis=0):
    size = array.shape[axis] // 4
    return lax.dynamic_slice_in_dim(array, index * size, size, axis)


def grp_scatter(partial, g, axis):
    away = [quarter(partial, g ^ 1, axis), quarter(partial, g ^ 3, axis)]
    kept = [quarter(partial, g, axis), quarter(partial, g ^ 2, axis)]
    got = gsend(jnp.stack(away).astype(BF), 1)
    far = gsend((kept[1] + got[1].astype(F32)).astype(BF), 2)
    return kept[0] + got[0].astype(F32) + far.astype(F32)


def local_general(
    caption_states,
    caption_lens,
    text_gain,
    text_query,
    text_key,
    text_value,
    text_bias,
    text_out,
    final_gain,
    cross_key,
    cross_value,
    video_states,
    video_counts,
    sample_caption,
    cross_query,
    cross_out,
    out_grad,
):
    column = lax.axis_index("fsdp")
    g = lax.axis_index("grp")
    fsdp = lax.axis_size("fsdp")
    pairs = fsdp // 2
    z, y = column // 2, column % 2
    caps_local, cap_len, text_width = caption_states.shape
    tokens, model_width = video_states.shape
    width_local = cross_key.shape[1]
    cross_local = width_local // HEAD_SIZE
    query_rows = cross_query.shape[0]

    def source(far, side):
        return ((z - far) % pairs) * 2 + (y ^ side)

    def target(far, side):
        return ((z + far) % pairs) * 2 + (y ^ side)

    query_blocks = gather_ring(cross_query)
    out_blocks = gather_ring(cross_out)
    full_query = jnp.zeros((model_width, width_local), BF)
    full_out = jnp.zeros((width_local, model_width), BF)
    for far in range(pairs):
        for side in range(2):
            start = source(far, side) * query_rows
            full_query = lax.dynamic_update_slice(
                full_query, query_blocks[2 * far + side], (start, jnp.int32(0))
            )
            full_out = lax.dynamic_update_slice(
                full_out, out_blocks[2 * far + side], (jnp.int32(0), start)
            )

    own_kv = jnp.concatenate([cross_key, cross_value], axis=1)
    other_kv = fsend(own_kv, 0, 1)
    pair_kv = jnp.concatenate(
        [jnp.where(y == 0, own_kv, other_kv), jnp.where(y == 0, other_kv, own_kv)], axis=0
    )

    local_lens = lax.dynamic_slice_in_dim(caption_lens, column * caps_local, caps_local)
    flat_states = caption_states.reshape(caps_local * cap_len, text_width).astype(F32)
    text_normed = rms_scale(flat_states, text_gain).astype(BF)
    local_heads = text_bias.shape[0]
    head_width = text_query.shape[1] // local_heads

    def heads_of(weight):
        return mm(text_normed, weight).astype(BF).reshape(
            caps_local, cap_len, local_heads, head_width
        )

    text_queries = heads_of(text_query)
    text_keys = heads_of(text_key)
    text_values = heads_of(text_value)
    text_scores = (
        jnp.einsum("cihd,cjhd->chij", text_queries, text_keys, preferred_element_type=F32)
        + text_bias[None]
    )
    key_valid = jnp.arange(cap_len, dtype=jnp.int32)[None, :] < local_lens[:, None]
    exp_scores = jnp.where(key_valid[:, None, None, :], jnp.exp(text_scores), 0.0)
    text_weights = (exp_scores / jnp.sum(exp_scores, axis=-1, keepdims=True)).astype(BF)
    text_mixed = jnp.einsum(
        "chij,cjhd->cihd", text_weights, text_values, preferred_element_type=F32
    )
    text_mixed = text_mixed.astype(BF).reshape(caps_local * cap_len, local_heads * head_width)
    partial_text = mm(text_mixed, text_out)
    text_rows = grp_scatter(partial_text, g, 0)
    encoded = rms_scale(quarter(flat_states, g) + text_rows, final_gain).astype(BF)

    part = text_width // pairs
    pieces = [
        lax.dynamic_slice_in_dim(encoded, ((z + far) % pairs) * part, part, 1)
        for far in range(pairs)
    ]
    mine = jnp.stack([fsend(p, far, 0) if far else p for far, p in enumerate(pieces)])
    over_x = jnp.concatenate([mine[:, None], gsend(mine, 2)[:, None]], axis=1)
    over_core = jnp.stack([over_x, gsend(over_x, 1)], axis=2)
    kv_partial = mm(over_core.reshape(-1, part), pair_kv).reshape(pairs, cap_len, 2 * width_local)
    kv_sum = kv_partial[0]
    for far in range(1, pairs):
        kv_sum += fsend(kv_partial[far].astype(BF), pairs - far, 0).astype(F32)
    kv_rows = kv_sum.astype(BF).reshape(4, cap_len // 4, 2 * width_local)
    order = jnp.arange(4, dtype=jnp.int32) ^ g
    cap_kv = jnp.concatenate(
        [lax.dynamic_slice_in_dim(kv_rows, order[k], 1, 0) for k in range(4)], axis=0
    ).reshape(cap_len, 2 * width_local)
    all_kv = jnp.stack(gather_direct(cap_kv))

    video = video_states.astype(F32)
    center = video - jnp.mean(video, axis=-1, keepdims=True)
    inverse = lax.rsqrt(jnp.mean(center * center, axis=-1, keepdims=True) + 1e-06)
    video_hat = center * inverse
    video_normed = video_hat.astype(BF)

    both = jnp.stack([quarter(video_normed, g), quarter(out_grad, g)])
    tiles = []
    for far in range(pairs):
        for side in range(2):
            tile = lax.dynamic_slice_in_dim(both, target(far, side) * query_rows, query_rows, 2)
            tiles.append(fsend(tile, far, side) if far or side else tile)
    tiles = jnp.stack(tiles)
    tiles_x = jnp.stack([tiles, gsend(tiles, 2)], axis=2)
    tiles_all = jnp.stack([tiles_x, gsend(tiles_x, 1)], axis=3)
    normed_tile = tiles_all[:, 0].reshape(-1, query_rows)
    grad_tile = tiles_all[:, 1].reshape(-1, query_rows)

    caption_total = all_kv.shape[0]
    positions = column * tokens + jnp.arange(tokens, dtype=jnp.int32)
    sample_end = jnp.cumsum(video_counts)
    token_sample = jnp.sum((sample_end[None, :] <= positions[:, None]).astype(jnp.int32), axis=1)
    slot_count = 3
    slot_sample = token_sample[0] + jnp.arange(slot_count, dtype=jnp.int32)
    slot_valid = slot_sample < caption_total
    slot_clipped = jnp.minimum(slot_sample, caption_total - 1)
    numbers = jnp.arange(caption_total, dtype=jnp.int32)
    slot_pick = slot_clipped[:, None] == numbers[None, :]
    slot_caption = jnp.sum(jnp.where(slot_pick, sample_caption[None, :], 0), axis=1)
    caption_pick = slot_caption[:, None] == numbers[None, :]
    slot_lens = jnp.sum(jnp.where(caption_pick, caption_lens[None, :], 0), axis=1)
    slot_member = token_sample[None, :] == slot_sample[:, None]
    member_float = slot_member.astype(F32)
    member_half = slot_member.astype(BF)
    slot_entry = ((z - slot_caption // 2) % pairs) * 2 + ((slot_caption % 2) ^ y)
    slot_kv = jnp.take(all_kv, slot_entry, axis=0)
    slot_keys = slot_kv[..., :width_local].reshape(slot_count, cap_len, cross_local, HEAD_SIZE)
    slot_values = slot_kv[..., width_local:].reshape(slot_count, cap_len, cross_local, HEAD_SIZE)
    token_lens = jnp.sum(jnp.where(slot_member, slot_lens[:, None], 0), axis=0)

    query_sum = mm(video_normed, full_query)
    queries = query_sum.astype(BF)
    d_attended = contract_last(out_grad, full_out).astype(BF).reshape(
        tokens, cross_local, HEAD_SIZE
    )
    score_scale = 1.0 / math.sqrt(HEAD_SIZE)
    query_heads = queries.reshape(tokens, cross_local, HEAD_SIZE)
    slot_scores = jnp.einsum("thd,kjhd->kthj", query_heads, slot_keys, preferred_element_type=F32)
    scores = jnp.sum(member_float[:, :, None, None] * slot_scores, axis=0) * score_scale
    token_valid = (jnp.arange(cap_len, dtype=jnp.int32)[None, :] < token_lens[:, None])[:, None, :]
    exp_video = jnp.where(token_valid, jnp.exp(scores), 0.0)
    weights = exp_video / jnp.sum(exp_video, axis=-1, keepdims=True)
    probs = weights.astype(BF)
    masked_probs = member_half[:, :, None, None] * probs[None]
    attended = jnp.einsum("kthj,kjhd->thd", masked_probs, slot_values, preferred_element_type=F32)
    attended = attended.astype(BF).reshape(tokens, width_local)

    def reorder(array):
        return jnp.concatenate([quarter(array, order[k]) for k in range(4)], axis=0)

    all_attended = jnp.concatenate(gather_direct(reorder(attended)), axis=0)
    out_weight_grad = contract_first(all_attended, grad_tile)

    out_share = grp_scatter(mm(attended, full_out), g, 1)
    updated = (quarter(video, g, 1) + out_share).astype(BF)

    slot_dprobs = jnp.einsum("thd,kjhd->kthj", d_attended, slot_values, preferred_element_type=F32)
    d_probs = jnp.sum(member_float[:, :, None, None] * slot_dprobs, axis=0)
    d_scores = (
        weights * (d_probs - jnp.sum(weights * d_probs, axis=-1, keepdims=True)) * score_scale
    ).astype(BF)
    masked_scores = member_half[:, :, None, None] * d_scores[None]
    d_queries = jnp.einsum("kthj,kjhd->thd", masked_scores, slot_keys, preferred_element_type=F32)
    d_queries = d_queries.astype(BF).reshape(tokens, width_local)
    all_d_queries = jnp.concatenate(gather_direct(reorder(d_queries)), axis=0)
    query_grad = contract_first(normed_tile, all_d_queries)

    key_slots = jnp.einsum("kthj,thd->kjhd", masked_scores, query_heads, preferred_element_type=F32)
    value_slots = jnp.einsum("kthj,thd->kjhd", masked_probs, d_attended, preferred_element_type=F32)
    slot_terms = jnp.concatenate(
        [
            key_slots.reshape(slot_count, cap_len, width_local),
            value_slots.reshape(slot_count, cap_len, width_local),
        ],
        axis=-1,
    )

    def caption_terms(far, side):
        picked = (slot_caption == target(far, side)) & slot_valid
        return jnp.sum(jnp.where(picked[:, None, None], slot_terms, 0.0), axis=0)

    away = jnp.stack([caption_terms(far, 1).astype(BF) for far in range(pairs)])
    got = fsend(away, 0, 1).astype(F32)
    kv_grads = caption_terms(0, 0) + got[0]
    for far in range(1, pairs):
        kv_grads += fsend((caption_terms(far, 0) + got[far]).astype(BF), far, 0).astype(F32)
    kv_grads = kv_grads.astype(BF)[None]
    key_grad = kv_grads[:, :, :width_local]
    value_grad = kv_grads[:, :, width_local:]

    d_wide = d_queries.astype(F32)
    column_sum = jnp.sum(full_query.astype(F32), axis=0)
    row_sums = jnp.stack(
        [jnp.sum(d_wide * column_sum, axis=-1), jnp.sum(d_wide * query_sum, axis=-1)]
    )
    row_sums = row_sums + gsend(row_sums, 1)
    row_sums = (row_sums + gsend(row_sums, 2)) / model_width
    d_share = grp_scatter(contract_last(d_queries, full_query), g, 1)
    input_grad = (
        quarter(out_grad, g, 1).astype(F32)
        + inverse
        * (d_share - row_sums[0][:, None] - quarter(video_hat, g, 1) * row_sums[1][:, None])
    ).astype(BF)
    return (updated, input_grad, query_grad, out_weight_grad, key_grad, value_grad)


def after(value, *others):
    return lax.optimization_barrier((value, *others))[0]


def call(body, out_shape, operands, scalars, scratch=()):
    specs = [pl.BlockSpec(memory_space=pltpu.SMEM)] * scalars
    specs += [pl.BlockSpec(memory_space=pltpu.VMEM)] * (len(operands) - scalars)
    return pl.pallas_call(
        body,
        out_shape=out_shape,
        in_specs=specs,
        out_specs=jax.tree.map(lambda _: pl.BlockSpec(memory_space=pltpu.VMEM), out_shape),
        scratch_shapes=list(scratch),
        compiler_params=pltpu.CompilerParams(vmem_limit_bytes=VMEM_BYTES),
        cost_estimate=SMALL,
    )(*operands)


def shaped(shape, dtype=BF):
    return jax.ShapeDtypeStruct(shape, dtype)


def aligned(start, unit):
    return pl.multiple_of(start, unit)


def project_text(states, gain, weights, sent, steps=4):
    rows, depth = states.shape
    width = weights[0].shape[1]
    chunk = depth // steps
    starts = [sum(a.shape[0] for a in sent[:k]) for k in range(len(sent) + 1)]

    def body(states_ref, gain_ref, wq_ref, wk_ref, wv_ref, *refs):
        sent_refs = refs[: len(sent)]
        out_ref, few_ref, all_ref, normed_ref, total_ref, sems = refs[len(sent) :]
        step = pl.program_id(0)

        def copies():
            made = []
            for k, source in enumerate(sent_refs):
                to = slice(starts[k], starts[k + 1])
                made.append(pltpu.make_async_copy(source, all_ref.at[to], sems.at[k]))
                if k < 2:
                    made.append(
                        pltpu.make_async_copy(source, few_ref.at[to], sems.at[len(sent) + k])
                    )
            return made

        @pl.when(step == 0)
        def _():
            for copy in copies():
                copy.start()
            for at in range(0, rows, 16):
                values = states_ref[at : at + 16, :].astype(F32)
                normed_ref[at : at + 16, :] = rms_scale(values, gain_ref[...]).astype(BF)
            total_ref[...] = jnp.zeros_like(total_ref)

        here = normed_ref[:, pl.ds(aligned(step * chunk, chunk), chunk)]
        for k, weight_ref in enumerate((wq_ref, wk_ref, wv_ref)):
            total_ref[:, k * width : (k + 1) * width] += mm(here, weight_ref[...])

        @pl.when(step == steps - 1)
        def _():
            out_ref[...] = total_ref[...].astype(BF)
            for copy in copies():
                copy.wait()

    whole = lambda shape: pl.BlockSpec(shape, lambda i: (0,) * len(shape))
    wide = sent[0].shape[1]
    out = [shaped((rows, 3 * width)), shaped((starts[2], wide)), shaped((starts[-1], wide))]
    return pl.pallas_call(
        body,
        grid=(steps,),
        out_shape=out,
        in_specs=[whole((rows, depth)), whole((1, depth))]
        + [pl.BlockSpec((chunk, width), lambda i: (i, 0))] * 3
        + [pl.BlockSpec(memory_space=pl.ANY)] * len(sent),
        out_specs=[whole(out[0].shape)] + [pl.BlockSpec(memory_space=pl.ANY)] * 2,
        scratch_shapes=[
            pltpu.VMEM((rows, depth), BF),
            pltpu.VMEM((rows, 3 * width), F32),
            pltpu.SemaphoreType.DMA((len(sent) + 2,)),
        ],
        compiler_params=pltpu.CompilerParams(vmem_limit_bytes=VMEM_BYTES),
        cost_estimate=SMALL,
    )(states, gain.reshape(1, -1), *weights, *sent)


def attend_text(projected, bias, text_out, place, lens, steps=4):
    rows = projected.shape[0]
    heads = bias.shape[0]
    inner, depth = text_out.shape
    size = inner // heads
    quarter_rows = rows // 4
    chunk = depth // steps

    def body(place_ref, len_ref, qkv_ref, bias_ref, out_ref, kept_ref, away_ref, held_ref, mixed_ref):
        @pl.when(pl.program_id(0) == 0)
        def _():
            g = place_ref[2]
            length = len_ref[place_ref[0] * 2 + place_ref[1]]
            live = lax.broadcasted_iota(jnp.int32, (rows, rows), 1) < length
            for head in range(heads):
                query, key, value = (
                    qkv_ref[:, k * inner + head * size : k * inner + (head + 1) * size]
                    for k in range(3)
                )
                grown = jnp.where(live, jnp.exp(contract_last(query, key) + bias_ref[head]), 0.0)
                weights = grown * (1.0 / jnp.sum(grown, axis=-1, keepdims=True))
                held_ref[:, head * size : (head + 1) * size] = mm(weights.astype(BF), value).astype(BF)
            for k, to in ((0, 0), (2, 1), (1, 2), (3, 3)):
                rows_from = pl.ds(aligned((g ^ k) * quarter_rows, quarter_rows), quarter_rows)
                mixed_ref[to * quarter_rows : (to + 1) * quarter_rows, :] = held_ref[rows_from, :]

        product = mm(mixed_ref[...], out_ref[...]).astype(BF)
        kept_ref[...] = product[: rows // 2]
        away_ref[...] = product[rows // 2 :]

    whole = lambda shape: pl.BlockSpec(shape, lambda i: (0,) * len(shape))
    return pl.pallas_call(
        body,
        grid=(steps,),
        out_shape=[shaped((rows // 2, depth))] * 2,
        in_specs=[pl.BlockSpec(memory_space=pltpu.SMEM)] * 2
        + [whole(projected.shape), whole(bias.shape)]
        + [pl.BlockSpec((inner, chunk), lambda i: (0, i))],
        out_specs=[pl.BlockSpec((rows // 2, chunk), lambda i: (0, i))] * 2,
        scratch_shapes=[pltpu.VMEM((rows, inner), BF), pltpu.VMEM((rows, inner), BF)],
        compiler_params=pltpu.CompilerParams(vmem_limit_bytes=VMEM_BYTES),
        cost_estimate=SMALL,
    )(place, lens, projected, bias, text_out)


def encode_rows(states, kept, got, far, gain, place, pairs):
    quarter_rows = states.shape[0] // 4
    width = states.shape[1]
    depth = width // pairs

    def body(place_ref, states_ref, kept_ref, got_ref, far_ref, gain_ref, *refs):
        piece_refs, encoded_ref = refs[:-1], refs[-1]
        z, g = place_ref[0], place_ref[2]
        mine = pl.ds(aligned(g * quarter_rows, quarter_rows), quarter_rows)
        total = states_ref[mine, :].astype(F32) + far_ref[...].astype(F32)
        total += kept_ref[:quarter_rows, :].astype(F32) + got_ref[:quarter_rows, :].astype(F32)
        encoded_ref[...] = rms_scale(total, gain_ref[...]).astype(BF)
        for far_by, piece in enumerate(piece_refs):
            to = lax.rem(z + far_by, pairs)
            piece[...] = encoded_ref[:, pl.ds(aligned(to * depth, 128), depth)]

    out = [shaped((quarter_rows, depth))] * pairs
    operands = (place, states, kept, got, far, gain.reshape(1, -1))
    return call(body, out, operands, 1, [pltpu.VMEM((quarter_rows, width), BF)])


def prepare_video(video_states, out_grad, place, pairs, part):
    tokens, model_width = video_states.shape
    rows = tokens // 4

    def body(place_ref, video_ref, grad_ref, normed_ref, mean_ref, inverse_ref, *tile_refs):
        @pl.loop(0, tokens // 32)
        def _(step):
            here = pl.ds(aligned(step * 32, 32), 32)
            values = video_ref[here, :].astype(F32)
            mean = jnp.mean(values, axis=-1, keepdims=True)
            center = values - mean
            inverse = lax.rsqrt(jnp.mean(center * center, axis=-1, keepdims=True) + 1e-06)
            normed_ref[here, :] = (center * inverse).astype(BF)
            mean_ref[here, :] = mean
            inverse_ref[here, :] = inverse

        z, y, g = place_ref[0], place_ref[1], place_ref[2]
        mine = pl.ds(aligned(g * rows, rows), rows)
        for far in range(pairs):
            for side in range(2):
                to = lax.rem(z + far, pairs) * 2 + (y ^ side)
                columns = pl.ds(aligned(to * part, 128), part)
                tile_refs[side][far, 0] = normed_ref[mine, columns]
                tile_refs[side][far, 1] = grad_ref[mine, columns]

    out = [shaped((tokens, model_width)), shaped((tokens, 1), F32), shaped((tokens, 1), F32)]
    out += [shaped((pairs, 2, rows, part))] * 2
    return call(body, out, (place, video_states, out_grad), 1)


def project_rows(normed, out_grad, blocks, place, pairs, part):
    tokens = normed.shape[0]
    width = blocks[0].shape[1]

    def body(place_ref, normed_ref, grad_ref, *refs):
        block_refs, (query_ref, d_ref, sum_ref) = refs[:-3], refs[-3:]
        z, y = place_ref[0], place_ref[1]
        query = jnp.zeros((tokens, width), F32)
        d_attended = jnp.zeros((tokens, width), F32)
        total = jnp.zeros((1, width), F32)
        for far in range(pairs):
            for side in range(2):
                block = block_refs[2 * far + side]
                origin = lax.rem(z - far + pairs, pairs) * 2 + (y ^ side)
                columns = pl.ds(aligned(origin * part, 128), part)
                weight = block[:part, :]
                query += mm(normed_ref[:, columns], weight)
                d_attended += contract_last(grad_ref[:, columns], block[part : part + width, :])
                total += jnp.sum(weight.astype(F32), axis=0, keepdims=True)
        query_ref[...] = query.astype(BF)
        d_ref[...] = d_attended.astype(BF)
        sum_ref[...] = total

    out = [shaped((tokens, width)), shaped((tokens, width)), shaped((1, width), F32)]
    return call(body, out, (place, normed, out_grad, *blocks), 1)


def project_captions(parts, own_key, own_value, side_block, place, pairs, skip):
    quarter_rows, depth = parts[0].shape[1:]
    half = depth // 2
    width = own_key.shape[1]

    def body(place_ref, *refs):
        part_refs = refs[:4]
        key_ref, value_ref, side_ref = refs[4:7]
        out_refs = refs[7:]
        y = place_ref[1]
        mine = pl.ds(aligned(y * half, 128), half)
        theirs = pl.ds(aligned((1 - y) * half, 128), half)
        own = jnp.concatenate([r[far, :, mine] for far in range(pairs) for r in part_refs], 0)
        other = jnp.concatenate([r[far, :, theirs] for far in range(pairs) for r in part_refs], 0)
        keys = mm(own, key_ref[...]) + mm(other, side_ref[skip : skip + half, :])
        values = mm(own, value_ref[...]) + mm(other, side_ref[skip + half : skip + 2 * half, :])
        for far in range(pairs):
            rows = slice(far * 4 * quarter_rows, (far + 1) * 4 * quarter_rows)
            out_refs[far][:, :width] = keys[rows].astype(BF)
            out_refs[far][:, width:] = values[rows].astype(BF)

    out = [shaped((4 * quarter_rows, 2 * width))] * pairs
    operands = (place, *parts, own_key, own_value, side_block)
    return call(body, out, operands, 1)


def attend(queries, d_attended, column_sum, kv_blocks, place, counts, sample_caption, lens, pairs):
    tokens, width = queries.shape
    cap_len = kv_blocks[0].shape[0]
    heads = width // HEAD_SIZE
    captions = counts.shape[0]
    keys_wide = SLOTS * cap_len
    cap_quarter, row_quarter = cap_len // 4, tokens // 4
    scale = 1.0 / math.sqrt(HEAD_SIZE)

    def body(place_ref, count_ref, caption_ref, len_ref, q_ref, da_ref, sum_ref, *refs):
        block_refs = refs[: len(kv_blocks)]
        both_ref, att_ref, dq_ref, rows_ref, own_ref, away_ref, kv_ref = refs[len(kv_blocks) :]
        z, y, g = place_ref[0], place_ref[1], place_ref[2]
        base = (z * 2 + y) * tokens

        def find(sample, carry):
            total, first, start = carry
            total = total + count_ref[sample]
            past = total <= base
            return total, first + past.astype(jnp.int32), jnp.where(past, total, start)

        zero = jnp.int32(0)
        _, first, start = lax.fori_loop(0, captions, find, (zero, zero, zero))
        low, high, length, far_to, side_to, valid = [], [], [], [], [], []
        edge = start - base
        for slot in range(SLOTS):
            ok = first + slot < captions
            sample = jnp.minimum(first + slot, captions - 1)
            caption = caption_ref[sample]
            low.append(edge)
            edge = edge + jnp.where(ok, count_ref[sample], 0)
            high.append(edge)
            length.append(len_ref[caption])
            far_to.append(lax.rem(caption // 2 - z + pairs, pairs))
            side_to.append(lax.rem(caption, 2) ^ y)
            valid.append(ok)
            entry = lax.rem(z - caption // 2 + pairs, pairs) * 2 + side_to[slot]
            for number, block in enumerate(block_refs):

                @pl.when(entry == number)
                def _(slot=slot, block=block):
                    kv_ref[slot * cap_len : (slot + 1) * cap_len, :] = block[...]

        token = lax.broadcasted_iota(jnp.int32, (tokens, keys_wide), 0)
        column = lax.broadcasted_iota(jnp.int32, (tokens, keys_wide), 1)
        slot_of = column // cap_len
        inside = column % cap_len
        key = ((inside // cap_quarter) ^ g) * cap_quarter + inside % cap_quarter

        def of_slot(values):
            return jnp.where(slot_of == 0, values[0], jnp.where(slot_of == 1, values[1], values[2]))

        live = (token >= of_slot(low)) & (token < of_slot(high)) & (key < of_slot(length))
        own_ref[...] = jnp.zeros_like(own_ref)
        away_ref[...] = jnp.zeros_like(away_ref)
        first_sum = jnp.zeros((tokens, 1), F32)
        second_sum = jnp.zeros((tokens, 1), F32)
        for head in range(heads):
            at = slice(head * HEAD_SIZE, (head + 1) * HEAD_SIZE)
            at_value = slice(width + head * HEAD_SIZE, width + (head + 1) * HEAD_SIZE)
            query, d_att = q_ref[:, at], da_ref[:, at]
            keys, values = kv_ref[:, at], kv_ref[:, at_value]
            grown = jnp.where(live, jnp.exp(contract_last(query, keys) * scale), 0.0)
            weights = grown * (1.0 / jnp.sum(grown, axis=-1, keepdims=True))
            probs = weights.astype(BF)
            d_probs = contract_last(d_att, values)
            mixed = jnp.sum(weights * d_probs, axis=-1, keepdims=True)
            d_scores = (weights * (d_probs - mixed) * scale).astype(BF)
            att_ref[:, at] = mm(probs, values).astype(BF)
            d_query = mm(d_scores, keys).astype(BF)
            dq_ref[:, at] = d_query
            d_wide = d_query.astype(F32)
            first_sum += jnp.sum(d_wide * sum_ref[:, at], axis=-1, keepdims=True)
            second_sum += jnp.sum(d_wide * query.astype(F32), axis=-1, keepdims=True)
            key_grad = contract_first(d_scores, query).astype(BF)
            value_grad = contract_first(probs, d_att).astype(BF)
            for slot in range(SLOTS):
                for part in range(4):
                    held = slice(
                        slot * cap_len + part * cap_quarter, slot * cap_len + (part + 1) * cap_quarter
                    )
                    to = pl.ds(aligned((part ^ g) * cap_quarter, cap_quarter), cap_quarter)
                    for side, target_ref in enumerate((own_ref, away_ref)):

                        @pl.when(valid[slot] & (side_to[slot] == side))
                        def _(slot=slot, held=held, to=to, target_ref=target_ref):
                            target_ref[far_to[slot], to, at] = key_grad[held]
                            target_ref[far_to[slot], to, at_value] = value_grad[held]

        rows_ref[:, 0:1] = first_sum
        rows_ref[:, 1:2] = second_sum
        for part in range(4):
            rows = pl.ds(aligned((part ^ g) * row_quarter, row_quarter), row_quarter)
            to = slice(part * row_quarter, (part + 1) * row_quarter)
            both_ref[0, to, :] = att_ref[rows, :]
            both_ref[1, to, :] = dq_ref[rows, :]

    out = [
        shaped((2, tokens, width)),
        shaped((tokens, width)),
        shaped((tokens, width)),
        shaped((tokens, 2), F32),
        shaped((pairs, cap_len, 2 * width)),
        shaped((pairs, cap_len, 2 * width)),
    ]
    operands = (place, counts, sample_caption, lens, queries, d_attended, column_sum, *kv_blocks)
    scratch = [pltpu.VMEM((keys_wide, 2 * width), BF)]
    return call(body, out, operands, 4, scratch)


def project_back(attended, d_queries, blocks, place, pairs, part):
    tokens, width = attended.shape
    model_width = 2 * pairs * part
    per_piece = 2 * pairs // 4
    piece = model_width // 4

    def body(place_ref, att_ref, dq_ref, *refs):
        block_refs = refs[: len(blocks)]
        own_ref, far_ref, away_ref = refs[len(blocks) :]
        z, y, g = place_ref[0], place_ref[1], place_ref[2]
        att, d_query = att_ref[...], dq_ref[...]
        for far in range(pairs):
            for side in range(2):
                block = block_refs[2 * far + side]
                origin = lax.rem(z - far + pairs, pairs) * 2 + (y ^ side)
                flip = (origin // per_piece) ^ g
                start = lax.rem(origin, per_piece) * part
                columns = pl.ds(aligned(start, 128), part)
                beyond = pl.ds(aligned(start + piece, 128), part)
                added = mm(att, block[part : part + width, :]).astype(BF)
                d_normed = contract_last(d_query, block[:part, :]).astype(BF)
                places = ((own_ref, columns), (away_ref, columns), (far_ref, columns), (away_ref, beyond))
                for number, (target_ref, to) in enumerate(places):

                    @pl.when(flip == number)
                    def _(target_ref=target_ref, to=to, added=added, d_normed=d_normed):
                        target_ref[0, :, to] = added
                        target_ref[1, :, to] = d_normed

    out = [shaped((2, tokens, piece)), shaped((2, tokens, piece)), shaped((2, tokens, 2 * piece))]
    return call(body, out, (place, attended, d_queries, *blocks), 1)


def weight_grads(tiles, both_blocks, pairs):
    part = tiles[0].shape[-1]
    width = both_blocks[0].shape[-1]

    def body(*refs):
        tile_refs, block_refs, (query_ref, out_ref) = refs[:4], refs[4:-2], refs[-2:]
        query_grad = jnp.zeros((part, width), F32)
        out_grad = jnp.zeros((width, part), F32)
        for far in range(pairs):
            for side in range(2):
                block = block_refs[2 * far + side]
                normed, grad = (
                    jnp.concatenate([r[far, side, which] for r in tile_refs], axis=0)
                    for which in range(2)
                )
                out_grad += contract_first(block[0], grad)
                query_grad += contract_first(normed, block[1])
        query_ref[...] = query_grad
        out_ref[...] = out_grad

    out = [shaped((part, width), F32), shaped((width, part), F32)]
    return call(body, out, (*tiles, *both_blocks), 0)


def local(
    caption_states,
    caption_lens,
    text_gain,
    text_query,
    text_key,
    text_value,
    text_bias,
    text_out,
    final_gain,
    cross_key,
    cross_value,
    video_states,
    video_counts,
    sample_caption,
    cross_query,
    cross_out,
    out_grad,
):
    column = lax.axis_index("fsdp")
    g = lax.axis_index("grp")
    pairs = lax.axis_size("fsdp") // 2
    z, y = column // 2, column % 2
    place = jnp.stack([z, y, g]).astype(jnp.int32)
    caps_local, cap_len, text_width = caption_states.shape
    tokens, model_width = video_states.shape
    width_local = cross_key.shape[1]
    part = cross_query.shape[0]

    weights = (cross_query, cross_out, cross_key, cross_value)
    states = caption_states.reshape(cap_len, text_width)

    projected, own_weights, own_blocks = project_text(
        states, text_gain, (text_query, text_key, text_value), weights
    )
    ring = [own_weights, fsend(own_weights, 1, 0)]
    side_block = fsend(own_blocks, 0, 1)
    kept, away = attend_text(projected, text_bias, text_out, place, caption_lens)
    quarter_rows = cap_len // 4
    got = gsend(away, 1)
    normed, mean, inverse, own_tiles, other_tiles = prepare_video(
        after(video_states, kept), out_grad, place, pairs, part
    )
    over_core = after(got, ring[1], normed)
    sent = (kept[quarter_rows:].astype(F32) + over_core[quarter_rows:].astype(F32)).astype(BF)
    ring.append(fsend(after(ring[1], over_core), 1, 0))
    over_x = gsend(sent, 2)
    pieces = encode_rows(
        states, kept, over_core, after(over_x, ring[2]), final_gain, place, pairs
    )

    mine = jnp.stack([fsend(p, far, 0) if far else p for far, p in enumerate(pieces)])
    over_x = gsend(mine, 2)
    parts = [mine, gsend(mine, 1), over_x, gsend(over_x, 1)]
    current = after(ring[2], pieces[0])
    for far in range(3, pairs):
        current = fsend(current, 1, 0)
        ring.append(current)
    blocks = [own_weights, side_block]
    for block in ring[1:]:
        blocks += [block, fsend(block, 0, 1)]
    other_tiles = fsend(other_tiles, 0, 1)

    parts[3] = after(parts[3], ring[-1], blocks[3])
    kv_partial = project_captions(
        parts, cross_key, cross_value, side_block, place, pairs, own_weights.shape[0]
    )
    kv_sum = kv_partial[0].astype(F32)
    for far in range(1, pairs):
        kv_sum += fsend(kv_partial[far], pairs - far, 0).astype(F32)
    kv_sum = after(kv_sum.astype(BF), blocks[5], other_tiles)
    kv_blocks = gather_direct(kv_sum)
    for k in range(7, len(blocks), 2):
        kv_blocks[2] = after(kv_blocks[2], blocks[k])

    queries, d_attended, column_sum = project_rows(
        normed, after(out_grad, kv_blocks[2]), blocks, place, pairs, part
    )

    tiles = jnp.stack([own_tiles, other_tiles], axis=1)
    over_z = [fsend(after(tiles[far], kv_blocks[4]), far, 0) for far in range(1, pairs)]
    over_z = [tiles[0]] + over_z

    both, attended, d_queries, row_sums, kv_own, kv_away = attend(
        queries,
        d_attended,
        column_sum,
        kv_blocks,
        place,
        video_counts,
        sample_caption,
        caption_lens,
        pairs,
    )
    kv_away, both = after((kv_away, both), over_z[1:-1])
    kv_side = fsend(kv_away, 0, 1)
    both_blocks = [both, fsend(both, 0, 1)]
    waits = [kv_side, both_blocks[1]]
    current = after(both, over_z[-1])
    for far in range(1, pairs):
        current = fsend(current, 1, 0)
        side = fsend(after(current, waits[far - 1]), 0, 1)
        both_blocks += [current, side]
        waits.append(side)
    tiles = jnp.stack(over_z)
    tiles_x = gsend(tiles, 2)
    tiles_core = gsend(tiles, 1)
    row_sums = row_sums + gsend(row_sums, 1)
    row_sums = (row_sums + gsend(row_sums, 2)) / model_width

    attended = after(attended, kv_side, tiles_x, both_blocks[1], both_blocks[4])
    own, far_piece, away = project_back(attended, d_queries, blocks, place, pairs, part)
    width = model_width // 4
    got = gsend(away, 1)
    sent = (far_piece.astype(F32) + got[:, :, width:].astype(F32)).astype(BF)
    far_sum = gsend(sent, 2)
    total = own.astype(F32) + got[:, :, :width].astype(F32) + far_sum.astype(F32)
    video = quarter(video_states, g, 1).astype(F32)
    updated = (video + total[0]).astype(BF)
    video_hat = (video - mean) * inverse
    input_grad = (
        quarter(out_grad, g, 1).astype(F32)
        + inverse * (total[1] - row_sums[:, 0:1] - video_hat * row_sums[:, 1:2])
    ).astype(BF)

    def kv_term(far):
        return kv_own[far].astype(F32) + kv_side[far].astype(F32)

    kv_grads = kv_term(0)
    for far in range(1, pairs):
        kv_grads += fsend(kv_term(far).astype(BF), far, 0).astype(F32)
    kv_grads = kv_grads.astype(BF)[None]
    key_grad = kv_grads[:, :, :width_local]
    value_grad = kv_grads[:, :, width_local:]

    tiles = [tiles, tiles_core, tiles_x, gsend(tiles_x, 1)]
    query_grad, out_weight_grad = weight_grads(tiles, both_blocks, pairs)
    return (updated, input_grad, query_grad, out_weight_grad, key_grad, value_grad)


def local_of(*arrays):
    whole_tiles = arrays[14].shape[0] % 128 == 0 and arrays[0].shape[0] == 1
    return local(*arrays) if whole_tiles else local_general(*arrays)


def solution(mesh):
    in_specs = (
        P("fsdp", None, None),
        P(),
        P(),
        P(None, "grp"),
        P(None, "grp"),
        P(None, "grp"),
        P("grp", None, None),
        P("grp", None),
        P(),
        P("fsdp", "grp"),
        P("fsdp", "grp"),
        P("fsdp", None),
        P(),
        P(),
        P("fsdp", "grp"),
        P("grp", "fsdp"),
        P("fsdp", None),
    )
    out_specs = (
        P("fsdp", "grp"),
        P("fsdp", "grp"),
        P("fsdp", "grp"),
        P("grp", "fsdp"),
        P("fsdp", None, "grp"),
        P("fsdp", None, "grp"),
    )
    return jax.shard_map(
        local_of, mesh=mesh, in_specs=in_specs, out_specs=out_specs, check_vma=False
    )
```

```python
import math

import jax
import jax.numpy as jnp
from jax import lax
from jax.experimental import pallas as pl
from jax.experimental.pallas import tpu as pltpu
from jax.sharding import PartitionSpec as P

HEAD_SIZE = 128
BF = jnp.bfloat16
F32 = jnp.float32
SLOTS = 3
VMEM_BYTES = 60 * 1024 * 1024
SMALL = pl.CostEstimate(flops=1, bytes_accessed=1, transcendentals=0)


def rms_scale(values, gain):
    mean_square = jnp.mean(values * values, axis=-1, keepdims=True)
    return values * lax.rsqrt(mean_square + 1e-06) * gain


def mm(left, right):
    return jnp.dot(left, right, preferred_element_type=F32)


def contract_last(left, right):
    return lax.dot_general(left, right, (((1,), (1,)), ((), ())), preferred_element_type=F32)


def contract_first(left, right):
    return lax.dot_general(left, right, (((0,), (0,)), ((), ())), preferred_element_type=F32)


def fsend(block, far, side):
    size = lax.axis_size("fsdp")
    pairs = size // 2
    perm = [(s, ((s // 2 + far) % pairs) * 2 + ((s % 2) ^ side)) for s in range(size)]
    return lax.ppermute(block, "fsdp", perm)


def gsend(block, flip):
    return lax.ppermute(block, "grp", [(s, s ^ flip) for s in range(lax.axis_size("grp"))])


def gather_ring(block):
    blocks = []
    current = block
    for far in range(lax.axis_size("fsdp") // 2):
        if far:
            current = fsend(current, 1, 0)
        blocks += [current, fsend(current, 0, 1)]
    return blocks


def gather_direct(block):
    blocks = []
    for far in range(lax.axis_size("fsdp") // 2):
        current = fsend(block, far, 0) if far else block
        blocks += [current, fsend(current, 0, 1)]
    return blocks


def quarter(array, index, axis=0):
    size = array.shape[axis] // 4
    return lax.dynamic_slice_in_dim(array, index * size, size, axis)


def grp_scatter(partial, g, axis):
    away = [quarter(partial, g ^ 1, axis), quarter(partial, g ^ 3, axis)]
    kept = [quarter(partial, g, axis), quarter(partial, g ^ 2, axis)]
    got = gsend(jnp.stack(away).astype(BF), 1)
    far = gsend((kept[1] + got[1].astype(F32)).astype(BF), 2)
    return kept[0] + got[0].astype(F32) + far.astype(F32)


def local_general(
    caption_states,
    caption_lens,
    text_gain,
    text_query,
    text_key,
    text_value,
    text_bias,
    text_out,
    final_gain,
    cross_key,
    cross_value,
    video_states,
    video_counts,
    sample_caption,
    cross_query,
    cross_out,
    out_grad,
):
    column = lax.axis_index("fsdp")
    g = lax.axis_index("grp")
    fsdp = lax.axis_size("fsdp")
    pairs = fsdp // 2
    z, y = column // 2, column % 2
    caps_local, cap_len, text_width = caption_states.shape
    tokens, model_width = video_states.shape
    width_local = cross_key.shape[1]
    cross_local = width_local // HEAD_SIZE
    query_rows = cross_query.shape[0]

    def source(far, side):
        return ((z - far) % pairs) * 2 + (y ^ side)

    def target(far, side):
        return ((z + far) % pairs) * 2 + (y ^ side)

    query_blocks = gather_ring(cross_query)
    out_blocks = gather_ring(cross_out)
    full_query = jnp.zeros((model_width, width_local), BF)
    full_out = jnp.zeros((width_local, model_width), BF)
    for far in range(pairs):
        for side in range(2):
            start = source(far, side) * query_rows
            full_query = lax.dynamic_update_slice(
                full_query, query_blocks[2 * far + side], (start, jnp.int32(0))
            )
            full_out = lax.dynamic_update_slice(
                full_out, out_blocks[2 * far + side], (jnp.int32(0), start)
            )

    own_kv = jnp.concatenate([cross_key, cross_value], axis=1)
    other_kv = fsend(own_kv, 0, 1)
    pair_kv = jnp.concatenate(
        [jnp.where(y == 0, own_kv, other_kv), jnp.where(y == 0, other_kv, own_kv)], axis=0
    )

    local_lens = lax.dynamic_slice_in_dim(caption_lens, column * caps_local, caps_local)
    flat_states = caption_states.reshape(caps_local * cap_len, text_width).astype(F32)
    text_normed = rms_scale(flat_states, text_gain).astype(BF)
    local_heads = text_bias.shape[0]
    head_width = text_query.shape[1] // local_heads

    def heads_of(weight):
        return mm(text_normed, weight).astype(BF).reshape(
            caps_local, cap_len, local_heads, head_width
        )

    text_queries = heads_of(text_query)
    text_keys = heads_of(text_key)
    text_values = heads_of(text_value)
    text_scores = (
        jnp.einsum("cihd,cjhd->chij", text_queries, text_keys, preferred_element_type=F32)
        + text_bias[None]
    )
    key_valid = jnp.arange(cap_len, dtype=jnp.int32)[None, :] < local_lens[:, None]
    exp_scores = jnp.where(key_valid[:, None, None, :], jnp.exp(text_scores), 0.0)
    text_weights = (exp_scores / jnp.sum(exp_scores, axis=-1, keepdims=True)).astype(BF)
    text_mixed = jnp.einsum(
        "chij,cjhd->cihd", text_weights, text_values, preferred_element_type=F32
    )
    text_mixed = text_mixed.astype(BF).reshape(caps_local * cap_len, local_heads * head_width)
    partial_text = mm(text_mixed, text_out)
    text_rows = grp_scatter(partial_text, g, 0)
    encoded = rms_scale(quarter(flat_states, g) + text_rows, final_gain).astype(BF)

    part = text_width // pairs
    pieces = [
        lax.dynamic_slice_in_dim(encoded, ((z + far) % pairs) * part, part, 1)
        for far in range(pairs)
    ]
    mine = jnp.stack([fsend(p, far, 0) if far else p for far, p in enumerate(pieces)])
    over_x = jnp.concatenate([mine[:, None], gsend(mine, 2)[:, None]], axis=1)
    over_core = jnp.stack([over_x, gsend(over_x, 1)], axis=2)
    kv_partial = mm(over_core.reshape(-1, part), pair_kv).reshape(pairs, cap_len, 2 * width_local)
    kv_sum = kv_partial[0]
    for far in range(1, pairs):
        kv_sum += fsend(kv_partial[far].astype(BF), pairs - far, 0).astype(F32)
    kv_rows = kv_sum.astype(BF).reshape(4, cap_len // 4, 2 * width_local)
    order = jnp.arange(4, dtype=jnp.int32) ^ g
    cap_kv = jnp.concatenate(
        [lax.dynamic_slice_in_dim(kv_rows, order[k], 1, 0) for k in range(4)], axis=0
    ).reshape(cap_len, 2 * width_local)
    all_kv = jnp.stack(gather_direct(cap_kv))

    video = video_states.astype(F32)
    center = video - jnp.mean(video, axis=-1, keepdims=True)
    inverse = lax.rsqrt(jnp.mean(center * center, axis=-1, keepdims=True) + 1e-06)
    video_hat = center * inverse
    video_normed = video_hat.astype(BF)

    both = jnp.stack([quarter(video_normed, g), quarter(out_grad, g)])
    tiles = []
    for far in range(pairs):
        for side in range(2):
            tile = lax.dynamic_slice_in_dim(both, target(far, side) * query_rows, query_rows, 2)
            tiles.append(fsend(tile, far, side) if far or side else tile)
    tiles = jnp.stack(tiles)
    tiles_x = jnp.stack([tiles, gsend(tiles, 2)], axis=2)
    tiles_all = jnp.stack([tiles_x, gsend(tiles_x, 1)], axis=3)
    normed_tile = tiles_all[:, 0].reshape(-1, query_rows)
    grad_tile = tiles_all[:, 1].reshape(-1, query_rows)

    caption_total = all_kv.shape[0]
    positions = column * tokens + jnp.arange(tokens, dtype=jnp.int32)
    sample_end = jnp.cumsum(video_counts)
    token_sample = jnp.sum((sample_end[None, :] <= positions[:, None]).astype(jnp.int32), axis=1)
    slot_count = 3
    slot_sample = token_sample[0] + jnp.arange(slot_count, dtype=jnp.int32)
    slot_valid = slot_sample < caption_total
    slot_clipped = jnp.minimum(slot_sample, caption_total - 1)
    numbers = jnp.arange(caption_total, dtype=jnp.int32)
    slot_pick = slot_clipped[:, None] == numbers[None, :]
    slot_caption = jnp.sum(jnp.where(slot_pick, sample_caption[None, :], 0), axis=1)
    caption_pick = slot_caption[:, None] == numbers[None, :]
    slot_lens = jnp.sum(jnp.where(caption_pick, caption_lens[None, :], 0), axis=1)
    slot_member = token_sample[None, :] == slot_sample[:, None]
    member_float = slot_member.astype(F32)
    member_half = slot_member.astype(BF)
    slot_entry = ((z - slot_caption // 2) % pairs) * 2 + ((slot_caption % 2) ^ y)
    slot_kv = jnp.take(all_kv, slot_entry, axis=0)
    slot_keys = slot_kv[..., :width_local].reshape(slot_count, cap_len, cross_local, HEAD_SIZE)
    slot_values = slot_kv[..., width_local:].reshape(slot_count, cap_len, cross_local, HEAD_SIZE)
    token_lens = jnp.sum(jnp.where(slot_member, slot_lens[:, None], 0), axis=0)

    query_sum = mm(video_normed, full_query)
    queries = query_sum.astype(BF)
    d_attended = contract_last(out_grad, full_out).astype(BF).reshape(
        tokens, cross_local, HEAD_SIZE
    )
    score_scale = 1.0 / math.sqrt(HEAD_SIZE)
    query_heads = queries.reshape(tokens, cross_local, HEAD_SIZE)
    slot_scores = jnp.einsum("thd,kjhd->kthj", query_heads, slot_keys, preferred_element_type=F32)
    scores = jnp.sum(member_float[:, :, None, None] * slot_scores, axis=0) * score_scale
    token_valid = (jnp.arange(cap_len, dtype=jnp.int32)[None, :] < token_lens[:, None])[:, None, :]
    exp_video = jnp.where(token_valid, jnp.exp(scores), 0.0)
    weights = exp_video / jnp.sum(exp_video, axis=-1, keepdims=True)
    probs = weights.astype(BF)
    masked_probs = member_half[:, :, None, None] * probs[None]
    attended = jnp.einsum("kthj,kjhd->thd", masked_probs, slot_values, preferred_element_type=F32)
    attended = attended.astype(BF).reshape(tokens, width_local)

    def reorder(array):
        return jnp.concatenate([quarter(array, order[k]) for k in range(4)], axis=0)

    all_attended = jnp.concatenate(gather_direct(reorder(attended)), axis=0)
    out_weight_grad = contract_first(all_attended, grad_tile)

    out_share = grp_scatter(mm(attended, full_out), g, 1)
    updated = (quarter(video, g, 1) + out_share).astype(BF)

    slot_dprobs = jnp.einsum("thd,kjhd->kthj", d_attended, slot_values, preferred_element_type=F32)
    d_probs = jnp.sum(member_float[:, :, None, None] * slot_dprobs, axis=0)
    d_scores = (
        weights * (d_probs - jnp.sum(weights * d_probs, axis=-1, keepdims=True)) * score_scale
    ).astype(BF)
    masked_scores = member_half[:, :, None, None] * d_scores[None]
    d_queries = jnp.einsum("kthj,kjhd->thd", masked_scores, slot_keys, preferred_element_type=F32)
    d_queries = d_queries.astype(BF).reshape(tokens, width_local)
    all_d_queries = jnp.concatenate(gather_direct(reorder(d_queries)), axis=0)
    query_grad = contract_first(normed_tile, all_d_queries)

    key_slots = jnp.einsum("kthj,thd->kjhd", masked_scores, query_heads, preferred_element_type=F32)
    value_slots = jnp.einsum("kthj,thd->kjhd", masked_probs, d_attended, preferred_element_type=F32)
    slot_terms = jnp.concatenate(
        [
            key_slots.reshape(slot_count, cap_len, width_local),
            value_slots.reshape(slot_count, cap_len, width_local),
        ],
        axis=-1,
    )

    def caption_terms(far, side):
        picked = (slot_caption == target(far, side)) & slot_valid
        return jnp.sum(jnp.where(picked[:, None, None], slot_terms, 0.0), axis=0)

    away = jnp.stack([caption_terms(far, 1).astype(BF) for far in range(pairs)])
    got = fsend(away, 0, 1).astype(F32)
    kv_grads = caption_terms(0, 0) + got[0]
    for far in range(1, pairs):
        kv_grads += fsend((caption_terms(far, 0) + got[far]).astype(BF), far, 0).astype(F32)
    kv_grads = kv_grads.astype(BF)[None]
    key_grad = kv_grads[:, :, :width_local]
    value_grad = kv_grads[:, :, width_local:]

    d_wide = d_queries.astype(F32)
    column_sum = jnp.sum(full_query.astype(F32), axis=0)
    row_sums = jnp.stack(
        [jnp.sum(d_wide * column_sum, axis=-1), jnp.sum(d_wide * query_sum, axis=-1)]
    )
    row_sums = row_sums + gsend(row_sums, 1)
    row_sums = (row_sums + gsend(row_sums, 2)) / model_width
    d_share = grp_scatter(contract_last(d_queries, full_query), g, 1)
    input_grad = (
        quarter(out_grad, g, 1).astype(F32)
        + inverse
        * (d_share - row_sums[0][:, None] - quarter(video_hat, g, 1) * row_sums[1][:, None])
    ).astype(BF)
    return (updated, input_grad, query_grad, out_weight_grad, key_grad, value_grad)


def after(value, *others):
    return lax.optimization_barrier((value, *others))[0]


def call(body, out_shape, operands, scalars, scratch=()):
    specs = [pl.BlockSpec(memory_space=pltpu.SMEM)] * scalars
    specs += [pl.BlockSpec(memory_space=pltpu.VMEM)] * (len(operands) - scalars)
    return pl.pallas_call(
        body,
        out_shape=out_shape,
        in_specs=specs,
        out_specs=jax.tree.map(lambda _: pl.BlockSpec(memory_space=pltpu.VMEM), out_shape),
        scratch_shapes=list(scratch),
        compiler_params=pltpu.CompilerParams(vmem_limit_bytes=VMEM_BYTES),
        cost_estimate=SMALL,
    )(*operands)


def shaped(shape, dtype=BF):
    return jax.ShapeDtypeStruct(shape, dtype)


def aligned(start, unit):
    return pl.multiple_of(start, unit)


def project_text(states, gain, weights, steps=4):
    rows, depth = states.shape
    width = weights[0].shape[1]
    chunk = depth // steps

    def body(states_ref, gain_ref, wq_ref, wk_ref, wv_ref, out_ref, normed_ref, total_ref):
        step = pl.program_id(0)

        @pl.when(step == 0)
        def _():
            for at in range(0, rows, 16):
                values = states_ref[at : at + 16, :].astype(F32)
                normed_ref[at : at + 16, :] = rms_scale(values, gain_ref[...]).astype(BF)
            total_ref[...] = jnp.zeros_like(total_ref)

        here = normed_ref[:, pl.ds(aligned(step * chunk, chunk), chunk)]
        for k, weight_ref in enumerate((wq_ref, wk_ref, wv_ref)):
            total_ref[:, k * width : (k + 1) * width] += mm(here, weight_ref[...])

        @pl.when(step == steps - 1)
        def _():
            out_ref[...] = total_ref[...].astype(BF)

    whole = lambda shape: pl.BlockSpec(shape, lambda i: (0,) * len(shape))
    return pl.pallas_call(
        body,
        grid=(steps,),
        out_shape=shaped((rows, 3 * width)),
        in_specs=[whole((rows, depth)), whole((1, depth))]
        + [pl.BlockSpec((chunk, width), lambda i: (i, 0))] * 3,
        out_specs=whole((rows, 3 * width)),
        scratch_shapes=[pltpu.VMEM((rows, depth), BF), pltpu.VMEM((rows, 3 * width), F32)],
        compiler_params=pltpu.CompilerParams(vmem_limit_bytes=VMEM_BYTES),
        cost_estimate=SMALL,
    )(states, gain.reshape(1, -1), *weights)


def attend_text(projected, bias, text_out, place, lens, steps=4):
    rows = projected.shape[0]
    heads = bias.shape[0]
    inner, depth = text_out.shape
    size = inner // heads
    quarter_rows = rows // 4
    chunk = depth // steps

    def body(place_ref, len_ref, qkv_ref, bias_ref, out_ref, kept_ref, away_ref, held_ref, mixed_ref):
        @pl.when(pl.program_id(0) == 0)
        def _():
            g = place_ref[2]
            length = len_ref[place_ref[0] * 2 + place_ref[1]]
            live = lax.broadcasted_iota(jnp.int32, (rows, rows), 1) < length
            for head in range(heads):
                query, key, value = (
                    qkv_ref[:, k * inner + head * size : k * inner + (head + 1) * size]
                    for k in range(3)
                )
                grown = jnp.where(live, jnp.exp(contract_last(query, key) + bias_ref[head]), 0.0)
                weights = grown * (1.0 / jnp.sum(grown, axis=-1, keepdims=True))
                held_ref[:, head * size : (head + 1) * size] = mm(weights.astype(BF), value).astype(BF)
            for k, to in ((0, 0), (2, 1), (1, 2), (3, 3)):
                rows_from = pl.ds(aligned((g ^ k) * quarter_rows, quarter_rows), quarter_rows)
                mixed_ref[to * quarter_rows : (to + 1) * quarter_rows, :] = held_ref[rows_from, :]

        product = mm(mixed_ref[...], out_ref[...]).astype(BF)
        kept_ref[...] = product[: rows // 2]
        away_ref[...] = product[rows // 2 :]

    whole = lambda shape: pl.BlockSpec(shape, lambda i: (0,) * len(shape))
    return pl.pallas_call(
        body,
        grid=(steps,),
        out_shape=[shaped((rows // 2, depth))] * 2,
        in_specs=[pl.BlockSpec(memory_space=pltpu.SMEM)] * 2
        + [whole(projected.shape), whole(bias.shape)]
        + [pl.BlockSpec((inner, chunk), lambda i: (0, i))],
        out_specs=[pl.BlockSpec((rows // 2, chunk), lambda i: (0, i))] * 2,
        scratch_shapes=[pltpu.VMEM((rows, inner), BF), pltpu.VMEM((rows, inner), BF)],
        compiler_params=pltpu.CompilerParams(vmem_limit_bytes=VMEM_BYTES),
        cost_estimate=SMALL,
    )(place, lens, projected, bias, text_out)


def encode_rows(states, kept, got, far, gain, place, pairs):
    quarter_rows = states.shape[0] // 4
    width = states.shape[1]
    depth = width // pairs

    def body(place_ref, states_ref, kept_ref, got_ref, far_ref, gain_ref, *refs):
        piece_refs, encoded_ref = refs[:-1], refs[-1]
        z, g = place_ref[0], place_ref[2]
        mine = pl.ds(aligned(g * quarter_rows, quarter_rows), quarter_rows)
        total = states_ref[mine, :].astype(F32) + far_ref[...].astype(F32)
        total += kept_ref[:quarter_rows, :].astype(F32) + got_ref[:quarter_rows, :].astype(F32)
        encoded_ref[...] = rms_scale(total, gain_ref[...]).astype(BF)
        for far_by, piece in enumerate(piece_refs):
            to = lax.rem(z + far_by, pairs)
            piece[...] = encoded_ref[:, pl.ds(aligned(to * depth, 128), depth)]

    out = [shaped((quarter_rows, depth))] * pairs
    operands = (place, states, kept, got, far, gain.reshape(1, -1))
    return call(body, out, operands, 1, [pltpu.VMEM((quarter_rows, width), BF)])


def pieces_of(pairs_of_blocks):
    arrays, listed = [], []
    for entry in pairs_of_blocks:
        numbers = []
        for array, start in entry:
            if not any(array is held for held in arrays):
                arrays.append(array)
            numbers.append((next(k for k, held in enumerate(arrays) if held is array), start))
        listed.append(numbers)
    return arrays, listed


def prepare_video(video_states, out_grad, place, pairs, part):
    tokens, model_width = video_states.shape
    rows = tokens // 4

    def body(place_ref, video_ref, grad_ref, normed_ref, mean_ref, inverse_ref, *tile_refs):
        @pl.loop(0, tokens // 32)
        def _(step):
            here = pl.ds(aligned(step * 32, 32), 32)
            values = video_ref[here, :].astype(F32)
            mean = jnp.mean(values, axis=-1, keepdims=True)
            center = values - mean
            inverse = lax.rsqrt(jnp.mean(center * center, axis=-1, keepdims=True) + 1e-06)
            normed_ref[here, :] = (center * inverse).astype(BF)
            mean_ref[here, :] = mean
            inverse_ref[here, :] = inverse

        z, y, g = place_ref[0], place_ref[1], place_ref[2]
        mine = pl.ds(aligned(g * rows, rows), rows)
        for far in range(pairs):
            for side in range(2):
                to = lax.rem(z + far, pairs) * 2 + (y ^ side)
                columns = pl.ds(aligned(to * part, 128), part)
                tile_refs[side][far, 0] = normed_ref[mine, columns]
                tile_refs[side][far, 1] = grad_ref[mine, columns]

    out = [shaped((tokens, model_width)), shaped((tokens, 1), F32), shaped((tokens, 1), F32)]
    out += [shaped((pairs, 2, rows, part))] * 2
    return call(body, out, (place, video_states, out_grad), 1)


def project_rows(normed, out_grad, blocks, place, pairs, part):
    tokens = normed.shape[0]
    arrays, blocks = pieces_of(blocks)
    width = arrays[0].shape[1]

    def body(place_ref, normed_ref, grad_ref, *refs):
        block_refs, (query_ref, d_ref, sum_ref) = refs[:-3], refs[-3:]
        z, y = place_ref[0], place_ref[1]
        query = jnp.zeros((tokens, width), F32)
        d_attended = jnp.zeros((tokens, width), F32)
        total = jnp.zeros((1, width), F32)
        for far in range(pairs):
            for side in range(2):
                (of_query, query_at), (of_out, out_at) = blocks[2 * far + side]
                origin = lax.rem(z - far + pairs, pairs) * 2 + (y ^ side)
                columns = pl.ds(aligned(origin * part, 128), part)
                weight = block_refs[of_query][query_at : query_at + part, :]
                out_weight = block_refs[of_out][out_at : out_at + width, :]
                query += mm(normed_ref[:, columns], weight)
                d_attended += contract_last(grad_ref[:, columns], out_weight)
                total += jnp.sum(weight.astype(F32), axis=0, keepdims=True)
        query_ref[...] = query.astype(BF)
        d_ref[...] = d_attended.astype(BF)
        sum_ref[...] = total

    out = [shaped((tokens, width)), shaped((tokens, width)), shaped((1, width), F32)]
    return call(body, out, (place, normed, out_grad, *arrays), 1)


def project_captions(parts, own_key, own_value, side_key, side_value, place, pairs):
    quarter_rows, depth = parts[0].shape[1:]
    half = depth // 2
    width = own_key.shape[1]

    def body(place_ref, *refs):
        part_refs = refs[:4]
        key_ref, value_ref, side_key_ref, side_value_ref = refs[4:8]
        out_refs = refs[8:]
        y = place_ref[1]
        mine = pl.ds(aligned(y * half, 128), half)
        theirs = pl.ds(aligned((1 - y) * half, 128), half)
        own = jnp.concatenate([r[far, :, mine] for far in range(pairs) for r in part_refs], 0)
        other = jnp.concatenate([r[far, :, theirs] for far in range(pairs) for r in part_refs], 0)
        keys = mm(own, key_ref[...]) + mm(other, side_key_ref[...])
        values = mm(own, value_ref[...]) + mm(other, side_value_ref[...])
        for far in range(pairs):
            rows = slice(far * 4 * quarter_rows, (far + 1) * 4 * quarter_rows)
            out_refs[far][:, :width] = keys[rows].astype(BF)
            out_refs[far][:, width:] = values[rows].astype(BF)

    out = [shaped((4 * quarter_rows, 2 * width))] * pairs
    operands = (place, *parts, own_key, own_value, side_key, side_value)
    return call(body, out, operands, 1)


def attend(queries, d_attended, column_sum, kv_blocks, place, counts, sample_caption, lens, pairs):
    tokens, width = queries.shape
    cap_len = kv_blocks[0].shape[0]
    heads = width // HEAD_SIZE
    captions = counts.shape[0]
    keys_wide = SLOTS * cap_len
    cap_quarter, row_quarter = cap_len // 4, tokens // 4
    scale = 1.0 / math.sqrt(HEAD_SIZE)

    def body(place_ref, count_ref, caption_ref, len_ref, q_ref, da_ref, sum_ref, *refs):
        block_refs = refs[: len(kv_blocks)]
        both_ref, att_ref, dq_ref, rows_ref, own_ref, away_ref, kv_ref = refs[len(kv_blocks) :]
        z, y, g = place_ref[0], place_ref[1], place_ref[2]
        base = (z * 2 + y) * tokens

        def find(sample, carry):
            total, first, start = carry
            total = total + count_ref[sample]
            past = total <= base
            return total, first + past.astype(jnp.int32), jnp.where(past, total, start)

        zero = jnp.int32(0)
        _, first, start = lax.fori_loop(0, captions, find, (zero, zero, zero))
        low, high, length, far_to, side_to, valid = [], [], [], [], [], []
        edge = start - base
        for slot in range(SLOTS):
            ok = first + slot < captions
            sample = jnp.minimum(first + slot, captions - 1)
            caption = caption_ref[sample]
            low.append(edge)
            edge = edge + jnp.where(ok, count_ref[sample], 0)
            high.append(edge)
            length.append(len_ref[caption])
            far_to.append(lax.rem(caption // 2 - z + pairs, pairs))
            side_to.append(lax.rem(caption, 2) ^ y)
            valid.append(ok)
            entry = lax.rem(z - caption // 2 + pairs, pairs) * 2 + side_to[slot]
            for number, block in enumerate(block_refs):

                @pl.when(entry == number)
                def _(slot=slot, block=block):
                    kv_ref[slot * cap_len : (slot + 1) * cap_len, :] = block[...]

        token = lax.broadcasted_iota(jnp.int32, (tokens, keys_wide), 0)
        column = lax.broadcasted_iota(jnp.int32, (tokens, keys_wide), 1)
        slot_of = column // cap_len
        inside = column % cap_len
        key = ((inside // cap_quarter) ^ g) * cap_quarter + inside % cap_quarter

        def of_slot(values):
            return jnp.where(slot_of == 0, values[0], jnp.where(slot_of == 1, values[1], values[2]))

        live = (token >= of_slot(low)) & (token < of_slot(high)) & (key < of_slot(length))
        own_ref[...] = jnp.zeros_like(own_ref)
        away_ref[...] = jnp.zeros_like(away_ref)
        first_sum = jnp.zeros((tokens, 1), F32)
        second_sum = jnp.zeros((tokens, 1), F32)
        for head in range(heads):
            at = slice(head * HEAD_SIZE, (head + 1) * HEAD_SIZE)
            at_value = slice(width + head * HEAD_SIZE, width + (head + 1) * HEAD_SIZE)
            query, d_att = q_ref[:, at], da_ref[:, at]
            keys, values = kv_ref[:, at], kv_ref[:, at_value]
            grown = jnp.where(live, jnp.exp(contract_last(query, keys) * scale), 0.0)
            weights = grown * (1.0 / jnp.sum(grown, axis=-1, keepdims=True))
            probs = weights.astype(BF)
            d_probs = contract_last(d_att, values)
            mixed = jnp.sum(weights * d_probs, axis=-1, keepdims=True)
            d_scores = (weights * (d_probs - mixed) * scale).astype(BF)
            att_ref[:, at] = mm(probs, values).astype(BF)
            d_query = mm(d_scores, keys).astype(BF)
            dq_ref[:, at] = d_query
            d_wide = d_query.astype(F32)
            first_sum += jnp.sum(d_wide * sum_ref[:, at], axis=-1, keepdims=True)
            second_sum += jnp.sum(d_wide * query.astype(F32), axis=-1, keepdims=True)
            key_grad = contract_first(d_scores, query).astype(BF)
            value_grad = contract_first(probs, d_att).astype(BF)
            for slot in range(SLOTS):
                for part in range(4):
                    held = slice(
                        slot * cap_len + part * cap_quarter, slot * cap_len + (part + 1) * cap_quarter
                    )
                    to = pl.ds(aligned((part ^ g) * cap_quarter, cap_quarter), cap_quarter)
                    for side, target_ref in enumerate((own_ref, away_ref)):

                        @pl.when(valid[slot] & (side_to[slot] == side))
                        def _(slot=slot, held=held, to=to, target_ref=target_ref):
                            target_ref[far_to[slot], to, at] = key_grad[held]
                            target_ref[far_to[slot], to, at_value] = value_grad[held]

        rows_ref[:, 0:1] = first_sum
        rows_ref[:, 1:2] = second_sum
        for part in range(4):
            rows = pl.ds(aligned((part ^ g) * row_quarter, row_quarter), row_quarter)
            to = slice(part * row_quarter, (part + 1) * row_quarter)
            both_ref[0, to, :] = att_ref[rows, :]
            both_ref[1, to, :] = dq_ref[rows, :]

    out = [
        shaped((2, tokens, width)),
        shaped((tokens, width)),
        shaped((tokens, width)),
        shaped((tokens, 2), F32),
        shaped((pairs, cap_len, 2 * width)),
        shaped((pairs, cap_len, 2 * width)),
    ]
    operands = (place, counts, sample_caption, lens, queries, d_attended, column_sum, *kv_blocks)
    scratch = [pltpu.VMEM((keys_wide, 2 * width), BF)]
    return call(body, out, operands, 4, scratch)


def project_back(attended, d_queries, blocks, place, pairs, part):
    tokens, width = attended.shape
    arrays, blocks = pieces_of(blocks)
    model_width = 2 * pairs * part
    per_piece = 2 * pairs // 4
    piece = model_width // 4

    def body(place_ref, att_ref, dq_ref, *refs):
        block_refs = refs[: len(arrays)]
        own_ref, far_ref, away_ref = refs[len(arrays) :]
        z, y, g = place_ref[0], place_ref[1], place_ref[2]
        att, d_query = att_ref[...], dq_ref[...]
        for far in range(pairs):
            for side in range(2):
                (of_query, query_at), (of_out, out_at) = blocks[2 * far + side]
                weight = block_refs[of_query][query_at : query_at + part, :]
                out_weight = block_refs[of_out][out_at : out_at + width, :]
                origin = lax.rem(z - far + pairs, pairs) * 2 + (y ^ side)
                flip = (origin // per_piece) ^ g
                start = lax.rem(origin, per_piece) * part
                columns = pl.ds(aligned(start, 128), part)
                beyond = pl.ds(aligned(start + piece, 128), part)
                added = mm(att, out_weight).astype(BF)
                d_normed = contract_last(d_query, weight).astype(BF)
                places = ((own_ref, columns), (away_ref, columns), (far_ref, columns), (away_ref, beyond))
                for number, (target_ref, to) in enumerate(places):

                    @pl.when(flip == number)
                    def _(target_ref=target_ref, to=to, added=added, d_normed=d_normed):
                        target_ref[0, :, to] = added
                        target_ref[1, :, to] = d_normed

    out = [shaped((2, tokens, piece)), shaped((2, tokens, piece)), shaped((2, tokens, 2 * piece))]
    return call(body, out, (place, attended, d_queries, *arrays), 1)


def weight_grads(tiles, both_blocks, pairs):
    part = tiles[0].shape[-1]
    arrays, blocks = pieces_of(both_blocks)
    width = arrays[0].shape[-1]

    def body(*refs):
        tile_refs, block_refs, (query_ref, out_ref) = refs[:4], refs[4:-2], refs[-2:]
        query_grad = jnp.zeros((part, width), F32)
        out_grad = jnp.zeros((width, part), F32)
        for far in range(pairs):
            for side in range(2):
                ((number, at),) = blocks[2 * far + side]
                block = block_refs[number]
                normed, grad = (
                    jnp.concatenate([r[far, side, which] for r in tile_refs], axis=0)
                    for which in range(2)
                )
                out_grad += contract_first(block[at], grad)
                query_grad += contract_first(normed, block[at + 1])
        query_ref[...] = query_grad
        out_ref[...] = out_grad

    out = [shaped((part, width), F32), shaped((width, part), F32)]
    return call(body, out, (*tiles, *arrays), 0)


def local(
    caption_states,
    caption_lens,
    text_gain,
    text_query,
    text_key,
    text_value,
    text_bias,
    text_out,
    final_gain,
    cross_key,
    cross_value,
    video_states,
    video_counts,
    sample_caption,
    cross_query,
    cross_out,
    out_grad,
):
    column = lax.axis_index("fsdp")
    g = lax.axis_index("grp")
    pairs = lax.axis_size("fsdp") // 2
    z, y = column // 2, column % 2
    place = jnp.stack([z, y, g]).astype(jnp.int32)
    caps_local, cap_len, text_width = caption_states.shape
    tokens, model_width = video_states.shape
    width_local = cross_key.shape[1]
    part = cross_query.shape[0]

    states = caption_states.reshape(cap_len, text_width)
    quarter_rows = cap_len // 4

    first = [fsend(cross_query, 1, 0), fsend(cross_out, 1, 0)]
    side_key, side_value = fsend(cross_key, 0, 1), fsend(cross_value, 0, 1)
    projected = project_text(states, text_gain, (text_query, text_key, text_value))
    kept, away = attend_text(projected, text_bias, text_out, place, caption_lens)
    kept, away = after((kept, away), first, side_key, side_value)
    got = gsend(away, 1)
    ring = [None, jnp.concatenate(first, axis=0)]
    side_first = fsend(jnp.concatenate([cross_query, cross_out, *first], axis=0), 0, 1)
    ring.append(fsend(ring[1], 1, 0))
    sent = (kept[quarter_rows:].astype(F32) + got[quarter_rows:].astype(F32)).astype(BF)
    over_x = gsend(sent, 2)
    normed, mean, inverse, own_tiles, other_tiles = prepare_video(
        after(video_states, sent), out_grad, place, pairs, part
    )
    pieces = encode_rows(states, kept, got, over_x, final_gain, place, pairs)

    mine = jnp.stack([fsend(p, far, 0) if far else p for far, p in enumerate(pieces)])
    mine = after(mine, ring[2])
    over_x = gsend(mine, 2)
    parts = [mine, gsend(mine, 1), over_x, gsend(over_x, 1)]
    current = after(ring[2], mine)
    for far in range(3, pairs):
        current = fsend(current, 1, 0)
        ring.append(current)
    parts[3] = after(parts[3], side_first)
    kv_partial = project_captions(
        parts, cross_key, cross_value, side_key, side_value, place, pairs
    )
    kv_partial = after(tuple(kv_partial), ring[-1])
    kv_sum = kv_partial[0].astype(F32)
    for far in range(1, pairs):
        kv_sum += fsend(kv_partial[far], pairs - far, 0).astype(F32)
    side_later = [fsend(w, 0, 1) for w in ring[2:]]
    other_tiles = fsend(other_tiles, 0, 1)
    kv_sum = after(kv_sum.astype(BF), side_later[0])
    kv_blocks = gather_direct(kv_sum)
    kv_blocks[4] = after(kv_blocks[4], side_later, other_tiles)

    step = part + width_local
    blocks = []
    for far, held in enumerate(ring):
        side, start = (side_first, far * step) if far < 2 else (side_later[far - 2], 0)
        here = ((held, 0), (held, part)) if far else ((cross_query, 0), (cross_out, 0))
        blocks += [here, ((side, start), (side, start + part))]
    queries, d_attended, column_sum = project_rows(
        normed, after(out_grad, kv_blocks[4]), blocks, place, pairs, part
    )

    tiles = jnp.stack([own_tiles, other_tiles], axis=1)
    over_z = [fsend(after(tiles[far], kv_blocks[4]), far, 0) for far in range(1, pairs)]
    over_z = [tiles[0]] + over_z

    both, attended, d_queries, row_sums, kv_own, kv_away = attend(
        queries,
        d_attended,
        column_sum,
        kv_blocks,
        place,
        video_counts,
        sample_caption,
        caption_lens,
        pairs,
    )
    kv_away, both, row_sums = after((kv_away, both, row_sums), over_z[1:-1])

    kv_side = fsend(kv_away, 0, 1)
    late = [both, fsend(both, 1, 0)]
    sums_core = gsend(row_sums, 1)
    tiles = jnp.stack(over_z)
    attended = after(attended, late[1])
    own, far_piece, away = project_back(attended, d_queries, blocks, place, pairs, part)
    kv_side, late, sums_core, tiles, away = after((kv_side, late, sums_core, tiles, away))

    sides = [fsend(jnp.stack(late[:2]).reshape(4, tokens, width_local), 0, 1)]
    late = list(late)
    for far in range(2, pairs):
        late.append(fsend(late[-1], 1, 0))
    tiles_x = gsend(tiles, 2)
    tiles_core = gsend(tiles, 1)
    row_sums = row_sums + sums_core
    sums_x = gsend(row_sums, 2)
    got = gsend(away, 1)
    done = after((sides[0], late, tiles_x, tiles_core, sums_x, got, kv_side))
    sides[0], late, tiles_x, tiles_core, sums_x, got, kv_side = done

    for far in range(2, pairs, 2):
        stacked = jnp.stack(late[far : far + 2])
        sides.append(fsend(stacked.reshape(-1, tokens, width_local), 0, 1))
    both_blocks = []
    for far in range(pairs):
        both_blocks += [((late[far], 0),), ((sides[far // 2], far % 2 * 2),)]
    width = model_width // 4
    sent = (far_piece.astype(F32) + got[:, :, width:].astype(F32)).astype(BF)
    far_sum = gsend(sent, 2)
    total = own.astype(F32) + got[:, :, :width].astype(F32) + far_sum.astype(F32)
    row_sums = (row_sums + sums_x) / model_width
    video = quarter(video_states, g, 1).astype(F32)
    updated = (video + total[0]).astype(BF)
    video_hat = (video - mean) * inverse
    input_grad = (
        quarter(out_grad, g, 1).astype(F32)
        + inverse * (total[1] - row_sums[:, 0:1] - video_hat * row_sums[:, 1:2])
    ).astype(BF)

    def kv_term(far):
        return kv_own[far].astype(F32) + kv_side[far].astype(F32)

    kv_grads = kv_term(0)
    for far in range(1, pairs):
        kv_grads += fsend(kv_term(far).astype(BF), far, 0).astype(F32)
    kv_grads = kv_grads.astype(BF)[None]
    key_grad = kv_grads[:, :, :width_local]
    value_grad = kv_grads[:, :, width_local:]

    tiles = [tiles, tiles_core, tiles_x, gsend(tiles_x, 1)]
    query_grad, out_weight_grad = weight_grads(tiles, both_blocks, pairs)
    return (updated, input_grad, query_grad, out_weight_grad, key_grad, value_grad)


def local_of(*arrays):
    whole_tiles = arrays[14].shape[0] % 128 == 0 and arrays[0].shape[0] == 1
    return local(*arrays) if whole_tiles else local_general(*arrays)


def solution(mesh):
    in_specs = (
        P("fsdp", None, None),
        P(),
        P(),
        P(None, "grp"),
        P(None, "grp"),
        P(None, "grp"),
        P("grp", None, None),
        P("grp", None),
        P(),
        P("fsdp", "grp"),
        P("fsdp", "grp"),
        P("fsdp", None),
        P(),
        P(),
        P("fsdp", "grp"),
        P("grp", "fsdp"),
        P("fsdp", None),
    )
    out_specs = (
        P("fsdp", "grp"),
        P("fsdp", "grp"),
        P("fsdp", "grp"),
        P("grp", "fsdp"),
        P("fsdp", None, "grp"),
        P("fsdp", None, "grp"),
    )
    return jax.shard_map(
        local_of, mesh=mesh, in_specs=in_specs, out_specs=out_specs, check_vma=False
    )
```

```python
import math

import jax
import jax.numpy as jnp
from jax import lax
from jax.experimental import pallas as pl
from jax.experimental.pallas import tpu as pltpu
from jax.sharding import PartitionSpec as P

HEAD_SIZE = 128
BF = jnp.bfloat16
F32 = jnp.float32
SLOTS = 3
VMEM_BYTES = 20 * 1024 * 1024
SPARE_BYTES = 8 * 1024 * 1024
SMALL = pl.CostEstimate(flops=1, bytes_accessed=1, transcendentals=0)


def rms_scale(values, gain):
    mean_square = jnp.mean(values * values, axis=-1, keepdims=True)
    return values * lax.rsqrt(mean_square + 1e-06) * gain


def mm(left, right):
    return jnp.dot(left, right, preferred_element_type=F32)


def contract_last(left, right):
    return lax.dot_general(left, right, (((1,), (1,)), ((), ())), preferred_element_type=F32)


def contract_first(left, right):
    return lax.dot_general(left, right, (((0,), (0,)), ((), ())), preferred_element_type=F32)


def fsend(block, far, side):
    size = lax.axis_size("fsdp")
    pairs = size // 2
    perm = [(s, ((s // 2 + far) % pairs) * 2 + ((s % 2) ^ side)) for s in range(size)]
    return lax.ppermute(block, "fsdp", perm)


def gsend(block, flip):
    return lax.ppermute(block, "grp", [(s, s ^ flip) for s in range(lax.axis_size("grp"))])


def gather_ring(block):
    blocks = []
    current = block
    for far in range(lax.axis_size("fsdp") // 2):
        if far:
            current = fsend(current, 1, 0)
        blocks += [current, fsend(current, 0, 1)]
    return blocks


def gather_direct(block):
    blocks = []
    for far in range(lax.axis_size("fsdp") // 2):
        current = fsend(block, far, 0) if far else block
        blocks += [current, fsend(current, 0, 1)]
    return blocks


def quarter(array, index, axis=0):
    size = array.shape[axis] // 4
    return lax.dynamic_slice_in_dim(array, index * size, size, axis)


def grp_scatter(partial, g, axis):
    away = [quarter(partial, g ^ 1, axis), quarter(partial, g ^ 3, axis)]
    kept = [quarter(partial, g, axis), quarter(partial, g ^ 2, axis)]
    got = gsend(jnp.stack(away).astype(BF), 1)
    far = gsend((kept[1] + got[1].astype(F32)).astype(BF), 2)
    return kept[0] + got[0].astype(F32) + far.astype(F32)


def local_general(
    caption_states,
    caption_lens,
    text_gain,
    text_query,
    text_key,
    text_value,
    text_bias,
    text_out,
    final_gain,
    cross_key,
    cross_value,
    video_states,
    video_counts,
    sample_caption,
    cross_query,
    cross_out,
    out_grad,
):
    column = lax.axis_index("fsdp")
    g = lax.axis_index("grp")
    fsdp = lax.axis_size("fsdp")
    pairs = fsdp // 2
    z, y = column // 2, column % 2
    caps_local, cap_len, text_width = caption_states.shape
    tokens, model_width = video_states.shape
    width_local = cross_key.shape[1]
    cross_local = width_local // HEAD_SIZE
    query_rows = cross_query.shape[0]

    def source(far, side):
        return ((z - far) % pairs) * 2 + (y ^ side)

    def target(far, side):
        return ((z + far) % pairs) * 2 + (y ^ side)

    query_blocks = gather_ring(cross_query)
    out_blocks = gather_ring(cross_out)
    full_query = jnp.zeros((model_width, width_local), BF)
    full_out = jnp.zeros((width_local, model_width), BF)
    for far in range(pairs):
        for side in range(2):
            start = source(far, side) * query_rows
            full_query = lax.dynamic_update_slice(
                full_query, query_blocks[2 * far + side], (start, jnp.int32(0))
            )
            full_out = lax.dynamic_update_slice(
                full_out, out_blocks[2 * far + side], (jnp.int32(0), start)
            )

    own_kv = jnp.concatenate([cross_key, cross_value], axis=1)
    other_kv = fsend(own_kv, 0, 1)
    pair_kv = jnp.concatenate(
        [jnp.where(y == 0, own_kv, other_kv), jnp.where(y == 0, other_kv, own_kv)], axis=0
    )

    local_lens = lax.dynamic_slice_in_dim(caption_lens, column * caps_local, caps_local)
    flat_states = caption_states.reshape(caps_local * cap_len, text_width).astype(F32)
    text_normed = rms_scale(flat_states, text_gain).astype(BF)
    local_heads = text_bias.shape[0]
    head_width = text_query.shape[1] // local_heads

    def heads_of(weight):
        return mm(text_normed, weight).astype(BF).reshape(
            caps_local, cap_len, local_heads, head_width
        )

    text_queries = heads_of(text_query)
    text_keys = heads_of(text_key)
    text_values = heads_of(text_value)
    text_scores = (
        jnp.einsum("cihd,cjhd->chij", text_queries, text_keys, preferred_element_type=F32)
        + text_bias[None]
    )
    key_valid = jnp.arange(cap_len, dtype=jnp.int32)[None, :] < local_lens[:, None]
    exp_scores = jnp.where(key_valid[:, None, None, :], jnp.exp(text_scores), 0.0)
    text_weights = (exp_scores / jnp.sum(exp_scores, axis=-1, keepdims=True)).astype(BF)
    text_mixed = jnp.einsum(
        "chij,cjhd->cihd", text_weights, text_values, preferred_element_type=F32
    )
    text_mixed = text_mixed.astype(BF).reshape(caps_local * cap_len, local_heads * head_width)
    partial_text = mm(text_mixed, text_out)
    text_rows = grp_scatter(partial_text, g, 0)
    encoded = rms_scale(quarter(flat_states, g) + text_rows, final_gain).astype(BF)

    part = text_width // pairs
    pieces = [
        lax.dynamic_slice_in_dim(encoded, ((z + far) % pairs) * part, part, 1)
        for far in range(pairs)
    ]
    mine = jnp.stack([fsend(p, far, 0) if far else p for far, p in enumerate(pieces)])
    over_x = jnp.concatenate([mine[:, None], gsend(mine, 2)[:, None]], axis=1)
    over_core = jnp.stack([over_x, gsend(over_x, 1)], axis=2)
    kv_partial = mm(over_core.reshape(-1, part), pair_kv).reshape(pairs, cap_len, 2 * width_local)
    kv_sum = kv_partial[0]
    for far in range(1, pairs):
        kv_sum += fsend(kv_partial[far].astype(BF), pairs - far, 0).astype(F32)
    kv_rows = kv_sum.astype(BF).reshape(4, cap_len // 4, 2 * width_local)
    order = jnp.arange(4, dtype=jnp.int32) ^ g
    cap_kv = jnp.concatenate(
        [lax.dynamic_slice_in_dim(kv_rows, order[k], 1, 0) for k in range(4)], axis=0
    ).reshape(cap_len, 2 * width_local)
    all_kv = jnp.stack(gather_direct(cap_kv))

    video = video_states.astype(F32)
    center = video - jnp.mean(video, axis=-1, keepdims=True)
    inverse = lax.rsqrt(jnp.mean(center * center, axis=-1, keepdims=True) + 1e-06)
    video_hat = center * inverse
    video_normed = video_hat.astype(BF)

    both = jnp.stack([quarter(video_normed, g), quarter(out_grad, g)])
    tiles = []
    for far in range(pairs):
        for side in range(2):
            tile = lax.dynamic_slice_in_dim(both, target(far, side) * query_rows, query_rows, 2)
            tiles.append(fsend(tile, far, side) if far or side else tile)
    tiles = jnp.stack(tiles)
    tiles_x = jnp.stack([tiles, gsend(tiles, 2)], axis=2)
    tiles_all = jnp.stack([tiles_x, gsend(tiles_x, 1)], axis=3)
    normed_tile = tiles_all[:, 0].reshape(-1, query_rows)
    grad_tile = tiles_all[:, 1].reshape(-1, query_rows)

    caption_total = all_kv.shape[0]
    positions = column * tokens + jnp.arange(tokens, dtype=jnp.int32)
    sample_end = jnp.cumsum(video_counts)
    token_sample = jnp.sum((sample_end[None, :] <= positions[:, None]).astype(jnp.int32), axis=1)
    slot_count = 3
    slot_sample = token_sample[0] + jnp.arange(slot_count, dtype=jnp.int32)
    slot_valid = slot_sample < caption_total
    slot_clipped = jnp.minimum(slot_sample, caption_total - 1)
    numbers = jnp.arange(caption_total, dtype=jnp.int32)
    slot_pick = slot_clipped[:, None] == numbers[None, :]
    slot_caption = jnp.sum(jnp.where(slot_pick, sample_caption[None, :], 0), axis=1)
    caption_pick = slot_caption[:, None] == numbers[None, :]
    slot_lens = jnp.sum(jnp.where(caption_pick, caption_lens[None, :], 0), axis=1)
    slot_member = token_sample[None, :] == slot_sample[:, None]
    member_float = slot_member.astype(F32)
    member_half = slot_member.astype(BF)
    slot_entry = ((z - slot_caption // 2) % pairs) * 2 + ((slot_caption % 2) ^ y)
    slot_kv = jnp.take(all_kv, slot_entry, axis=0)
    slot_keys = slot_kv[..., :width_local].reshape(slot_count, cap_len, cross_local, HEAD_SIZE)
    slot_values = slot_kv[..., width_local:].reshape(slot_count, cap_len, cross_local, HEAD_SIZE)
    token_lens = jnp.sum(jnp.where(slot_member, slot_lens[:, None], 0), axis=0)

    query_sum = mm(video_normed, full_query)
    queries = query_sum.astype(BF)
    d_attended = contract_last(out_grad, full_out).astype(BF).reshape(
        tokens, cross_local, HEAD_SIZE
    )
    score_scale = 1.0 / math.sqrt(HEAD_SIZE)
    query_heads = queries.reshape(tokens, cross_local, HEAD_SIZE)
    slot_scores = jnp.einsum("thd,kjhd->kthj", query_heads, slot_keys, preferred_element_type=F32)
    scores = jnp.sum(member_float[:, :, None, None] * slot_scores, axis=0) * score_scale
    token_valid = (jnp.arange(cap_len, dtype=jnp.int32)[None, :] < token_lens[:, None])[:, None, :]
    exp_video = jnp.where(token_valid, jnp.exp(scores), 0.0)
    weights = exp_video / jnp.sum(exp_video, axis=-1, keepdims=True)
    probs = weights.astype(BF)
    masked_probs = member_half[:, :, None, None] * probs[None]
    attended = jnp.einsum("kthj,kjhd->thd", masked_probs, slot_values, preferred_element_type=F32)
    attended = attended.astype(BF).reshape(tokens, width_local)

    def reorder(array):
        return jnp.concatenate([quarter(array, order[k]) for k in range(4)], axis=0)

    all_attended = jnp.concatenate(gather_direct(reorder(attended)), axis=0)
    out_weight_grad = contract_first(all_attended, grad_tile)

    out_share = grp_scatter(mm(attended, full_out), g, 1)
    updated = (quarter(video, g, 1) + out_share).astype(BF)

    slot_dprobs = jnp.einsum("thd,kjhd->kthj", d_attended, slot_values, preferred_element_type=F32)
    d_probs = jnp.sum(member_float[:, :, None, None] * slot_dprobs, axis=0)
    d_scores = (
        weights * (d_probs - jnp.sum(weights * d_probs, axis=-1, keepdims=True)) * score_scale
    ).astype(BF)
    masked_scores = member_half[:, :, None, None] * d_scores[None]
    d_queries = jnp.einsum("kthj,kjhd->thd", masked_scores, slot_keys, preferred_element_type=F32)
    d_queries = d_queries.astype(BF).reshape(tokens, width_local)
    all_d_queries = jnp.concatenate(gather_direct(reorder(d_queries)), axis=0)
    query_grad = contract_first(normed_tile, all_d_queries)

    key_slots = jnp.einsum("kthj,thd->kjhd", masked_scores, query_heads, preferred_element_type=F32)
    value_slots = jnp.einsum("kthj,thd->kjhd", masked_probs, d_attended, preferred_element_type=F32)
    slot_terms = jnp.concatenate(
        [
            key_slots.reshape(slot_count, cap_len, width_local),
            value_slots.reshape(slot_count, cap_len, width_local),
        ],
        axis=-1,
    )

    def caption_terms(far, side):
        picked = (slot_caption == target(far, side)) & slot_valid
        return jnp.sum(jnp.where(picked[:, None, None], slot_terms, 0.0), axis=0)

    away = jnp.stack([caption_terms(far, 1).astype(BF) for far in range(pairs)])
    got = fsend(away, 0, 1).astype(F32)
    kv_grads = caption_terms(0, 0) + got[0]
    for far in range(1, pairs):
        kv_grads += fsend((caption_terms(far, 0) + got[far]).astype(BF), far, 0).astype(F32)
    kv_grads = kv_grads.astype(BF)[None]
    key_grad = kv_grads[:, :, :width_local]
    value_grad = kv_grads[:, :, width_local:]

    d_wide = d_queries.astype(F32)
    column_sum = jnp.sum(full_query.astype(F32), axis=0)
    row_sums = jnp.stack(
        [jnp.sum(d_wide * column_sum, axis=-1), jnp.sum(d_wide * query_sum, axis=-1)]
    )
    row_sums = row_sums + gsend(row_sums, 1)
    row_sums = (row_sums + gsend(row_sums, 2)) / model_width
    d_share = grp_scatter(contract_last(d_queries, full_query), g, 1)
    input_grad = (
        quarter(out_grad, g, 1).astype(F32)
        + inverse
        * (d_share - row_sums[0][:, None] - quarter(video_hat, g, 1) * row_sums[1][:, None])
    ).astype(BF)
    return (updated, input_grad, query_grad, out_weight_grad, key_grad, value_grad)


def after(value, *others):
    return lax.optimization_barrier((value, *others))[0]


def call(body, out_shape, operands, scalars, scratch=()):
    specs = [pl.BlockSpec(memory_space=pltpu.SMEM)] * scalars
    specs += [pl.BlockSpec(memory_space=pltpu.VMEM)] * (len(operands) - scalars)
    held = (*operands[scalars:], *jax.tree.leaves(out_shape), *scratch)
    held_bytes = sum(math.prod(a.shape) * jnp.dtype(a.dtype).itemsize for a in held)
    return pl.pallas_call(
        body,
        out_shape=out_shape,
        in_specs=specs,
        out_specs=jax.tree.map(lambda _: pl.BlockSpec(memory_space=pltpu.VMEM), out_shape),
        scratch_shapes=list(scratch),
        compiler_params=pltpu.CompilerParams(vmem_limit_bytes=held_bytes + SPARE_BYTES),
        cost_estimate=SMALL,
    )(*operands)


def shaped(shape, dtype=BF):
    return jax.ShapeDtypeStruct(shape, dtype)


def aligned(start, unit):
    return pl.multiple_of(start, unit)


def project_text(states, gain, weights, steps=4):
    rows, depth = states.shape
    width = weights[0].shape[1]
    chunk = depth // steps

    def body(states_ref, gain_ref, wq_ref, wk_ref, wv_ref, out_ref, normed_ref, total_ref):
        step = pl.program_id(0)

        @pl.when(step == 0)
        def _():
            for at in range(0, rows, 16):
                values = states_ref[at : at + 16, :].astype(F32)
                normed_ref[at : at + 16, :] = rms_scale(values, gain_ref[...]).astype(BF)
            total_ref[...] = jnp.zeros_like(total_ref)

        here = normed_ref[:, pl.ds(aligned(step * chunk, chunk), chunk)]
        for k, weight_ref in enumerate((wq_ref, wk_ref, wv_ref)):
            total_ref[:, k * width : (k + 1) * width] += mm(here, weight_ref[...])

        @pl.when(step == steps - 1)
        def _():
            out_ref[...] = total_ref[...].astype(BF)

    whole = lambda shape: pl.BlockSpec(shape, lambda i: (0,) * len(shape))
    return pl.pallas_call(
        body,
        grid=(steps,),
        out_shape=shaped((rows, 3 * width)),
        in_specs=[whole((rows, depth)), whole((1, depth))]
        + [pl.BlockSpec((chunk, width), lambda i: (i, 0))] * 3,
        out_specs=whole((rows, 3 * width)),
        scratch_shapes=[pltpu.VMEM((rows, depth), BF), pltpu.VMEM((rows, 3 * width), F32)],
        compiler_params=pltpu.CompilerParams(vmem_limit_bytes=VMEM_BYTES),
        cost_estimate=SMALL,
    )(states, gain.reshape(1, -1), *weights)


def attend_text(projected, bias, text_out, place, lens, steps=4):
    rows = projected.shape[0]
    heads = bias.shape[0]
    inner, depth = text_out.shape
    size = inner // heads
    quarter_rows = rows // 4
    chunk = depth // steps

    def body(place_ref, len_ref, qkv_ref, bias_ref, out_ref, kept_ref, away_ref, held_ref, mixed_ref):
        @pl.when(pl.program_id(0) == 0)
        def _():
            g = place_ref[2]
            length = len_ref[place_ref[0] * 2 + place_ref[1]]
            live = lax.broadcasted_iota(jnp.int32, (rows, rows), 1) < length
            for head in range(heads):
                query, key, value = (
                    qkv_ref[:, k * inner + head * size : k * inner + (head + 1) * size]
                    for k in range(3)
                )
                grown = jnp.where(live, jnp.exp(contract_last(query, key) + bias_ref[head]), 0.0)
                weights = grown * (1.0 / jnp.sum(grown, axis=-1, keepdims=True))
                held_ref[:, head * size : (head + 1) * size] = mm(weights.astype(BF), value).astype(BF)
            for k, to in ((0, 0), (2, 1), (1, 2), (3, 3)):
                rows_from = pl.ds(aligned((g ^ k) * quarter_rows, quarter_rows), quarter_rows)
                mixed_ref[to * quarter_rows : (to + 1) * quarter_rows, :] = held_ref[rows_from, :]

        product = mm(mixed_ref[...], out_ref[...]).astype(BF)
        kept_ref[...] = product[: rows // 2]
        away_ref[...] = product[rows // 2 :]

    whole = lambda shape: pl.BlockSpec(shape, lambda i: (0,) * len(shape))
    return pl.pallas_call(
        body,
        grid=(steps,),
        out_shape=[shaped((rows // 2, depth))] * 2,
        in_specs=[pl.BlockSpec(memory_space=pltpu.SMEM)] * 2
        + [whole(projected.shape), whole(bias.shape)]
        + [pl.BlockSpec((inner, chunk), lambda i: (0, i))],
        out_specs=[pl.BlockSpec((rows // 2, chunk), lambda i: (0, i))] * 2,
        scratch_shapes=[pltpu.VMEM((rows, inner), BF), pltpu.VMEM((rows, inner), BF)],
        compiler_params=pltpu.CompilerParams(vmem_limit_bytes=VMEM_BYTES),
        cost_estimate=SMALL,
    )(place, lens, projected, bias, text_out)


def encode_rows(states, kept, got, far, gain, place, pairs):
    quarter_rows = states.shape[0] // 4
    width = states.shape[1]
    depth = width // pairs

    def body(place_ref, states_ref, kept_ref, got_ref, far_ref, gain_ref, *refs):
        piece_refs, encoded_ref = refs[:-1], refs[-1]
        z, g = place_ref[0], place_ref[2]
        mine = pl.ds(aligned(g * quarter_rows, quarter_rows), quarter_rows)
        total = states_ref[mine, :].astype(F32) + far_ref[...].astype(F32)
        total += kept_ref[:quarter_rows, :].astype(F32) + got_ref[:quarter_rows, :].astype(F32)
        encoded_ref[...] = rms_scale(total, gain_ref[...]).astype(BF)
        for far_by, piece in enumerate(piece_refs):
            to = lax.rem(z + far_by, pairs)
            piece[...] = encoded_ref[:, pl.ds(aligned(to * depth, 128), depth)]

    out = [shaped((quarter_rows, depth))] * pairs
    operands = (place, states, kept, got, far, gain.reshape(1, -1))
    return call(body, out, operands, 1, [pltpu.VMEM((quarter_rows, width), BF)])


def pieces_of(pairs_of_blocks):
    arrays, listed = [], []
    for entry in pairs_of_blocks:
        numbers = []
        for array, start in entry:
            if not any(array is held for held in arrays):
                arrays.append(array)
            numbers.append((next(k for k, held in enumerate(arrays) if held is array), start))
        listed.append(numbers)
    return arrays, listed


def prepare_video(video_states, out_grad, place, pairs, part):
    tokens, model_width = video_states.shape
    rows = tokens // 4

    def body(place_ref, video_ref, grad_ref, normed_ref, mean_ref, inverse_ref, *tile_refs):
        @pl.loop(0, tokens // 32)
        def _(step):
            here = pl.ds(aligned(step * 32, 32), 32)
            values = video_ref[here, :].astype(F32)
            mean = jnp.mean(values, axis=-1, keepdims=True)
            center = values - mean
            inverse = lax.rsqrt(jnp.mean(center * center, axis=-1, keepdims=True) + 1e-06)
            normed_ref[here, :] = (center * inverse).astype(BF)
            mean_ref[here, :] = mean
            inverse_ref[here, :] = inverse

        z, y, g = place_ref[0], place_ref[1], place_ref[2]
        mine = pl.ds(aligned(g * rows, rows), rows)
        for far in range(pairs):
            for side in range(2):
                to = lax.rem(z + far, pairs) * 2 + (y ^ side)
                columns = pl.ds(aligned(to * part, 128), part)
                tile_refs[side][far, 0] = normed_ref[mine, columns]
                tile_refs[side][far, 1] = grad_ref[mine, columns]

    out = [shaped((tokens, model_width)), shaped((tokens, 1), F32), shaped((tokens, 1), F32)]
    out += [shaped((pairs, 2, rows, part))] * 2
    return call(body, out, (place, video_states, out_grad), 1)


def project_rows(normed, out_grad, blocks, place, pairs, part):
    tokens = normed.shape[0]
    arrays, blocks = pieces_of(blocks)
    width = arrays[0].shape[1]

    def body(place_ref, normed_ref, grad_ref, *refs):
        block_refs, (query_ref, d_ref, sum_ref) = refs[:-3], refs[-3:]
        z, y = place_ref[0], place_ref[1]
        query = jnp.zeros((tokens, width), F32)
        d_attended = jnp.zeros((tokens, width), F32)
        total = jnp.zeros((1, width), F32)
        for far in range(pairs):
            for side in range(2):
                (of_query, query_at), (of_out, out_at) = blocks[2 * far + side]
                origin = lax.rem(z - far + pairs, pairs) * 2 + (y ^ side)
                columns = pl.ds(aligned(origin * part, 128), part)
                weight = block_refs[of_query][query_at : query_at + part, :]
                out_weight = block_refs[of_out][out_at : out_at + width, :]
                query += mm(normed_ref[:, columns], weight)
                d_attended += contract_last(grad_ref[:, columns], out_weight)
                total += jnp.sum(weight.astype(F32), axis=0, keepdims=True)
        query_ref[...] = query.astype(BF)
        d_ref[...] = d_attended.astype(BF)
        sum_ref[...] = total

    out = [shaped((tokens, width)), shaped((tokens, width)), shaped((1, width), F32)]
    return call(body, out, (place, normed, out_grad, *arrays), 1)


def project_captions(parts, own_key, own_value, side_key, side_value, place, pairs):
    quarter_rows, depth = parts[0].shape[1:]
    half = depth // 2
    width = own_key.shape[1]

    def body(place_ref, *refs):
        part_refs = refs[:4]
        key_ref, value_ref, side_key_ref, side_value_ref = refs[4:8]
        out_refs = refs[8:]
        y = place_ref[1]
        mine = pl.ds(aligned(y * half, 128), half)
        theirs = pl.ds(aligned((1 - y) * half, 128), half)
        own = jnp.concatenate([r[far, :, mine] for far in range(pairs) for r in part_refs], 0)
        other = jnp.concatenate([r[far, :, theirs] for far in range(pairs) for r in part_refs], 0)
        keys = mm(own, key_ref[...]) + mm(other, side_key_ref[...])
        values = mm(own, value_ref[...]) + mm(other, side_value_ref[...])
        for far in range(pairs):
            rows = slice(far * 4 * quarter_rows, (far + 1) * 4 * quarter_rows)
            out_refs[far][:, :width] = keys[rows].astype(BF)
            out_refs[far][:, width:] = values[rows].astype(BF)

    out = [shaped((4 * quarter_rows, 2 * width))] * pairs
    operands = (place, *parts, own_key, own_value, side_key, side_value)
    return call(body, out, operands, 1)


def attend(queries, d_attended, column_sum, kv_blocks, place, counts, sample_caption, lens, pairs):
    tokens, width = queries.shape
    cap_len = kv_blocks[0].shape[0]
    heads = width // HEAD_SIZE
    captions = counts.shape[0]
    keys_wide = SLOTS * cap_len
    cap_quarter, row_quarter = cap_len // 4, tokens // 4
    scale = 1.0 / math.sqrt(HEAD_SIZE)

    def body(place_ref, count_ref, caption_ref, len_ref, q_ref, da_ref, sum_ref, *refs):
        block_refs = refs[: len(kv_blocks)]
        both_ref, att_ref, dq_ref, rows_ref, own_ref, away_ref, kv_ref = refs[len(kv_blocks) :]
        z, y, g = place_ref[0], place_ref[1], place_ref[2]
        base = (z * 2 + y) * tokens

        def find(sample, carry):
            total, first, start = carry
            total = total + count_ref[sample]
            past = total <= base
            return total, first + past.astype(jnp.int32), jnp.where(past, total, start)

        zero = jnp.int32(0)
        _, first, start = lax.fori_loop(0, captions, find, (zero, zero, zero))
        low, high, length, far_to, side_to, valid = [], [], [], [], [], []
        edge = start - base
        for slot in range(SLOTS):
            ok = first + slot < captions
            sample = jnp.minimum(first + slot, captions - 1)
            caption = caption_ref[sample]
            low.append(edge)
            edge = edge + jnp.where(ok, count_ref[sample], 0)
            high.append(edge)
            length.append(len_ref[caption])
            far_to.append(lax.rem(caption // 2 - z + pairs, pairs))
            side_to.append(lax.rem(caption, 2) ^ y)
            valid.append(ok)
            entry = lax.rem(z - caption // 2 + pairs, pairs) * 2 + side_to[slot]
            for number, block in enumerate(block_refs):

                @pl.when(entry == number)
                def _(slot=slot, block=block):
                    kv_ref[slot * cap_len : (slot + 1) * cap_len, :] = block[...]

        token = lax.broadcasted_iota(jnp.int32, (tokens, keys_wide), 0)
        column = lax.broadcasted_iota(jnp.int32, (tokens, keys_wide), 1)
        slot_of = column // cap_len
        inside = column % cap_len
        key = ((inside // cap_quarter) ^ g) * cap_quarter + inside % cap_quarter

        def of_slot(values):
            return jnp.where(slot_of == 0, values[0], jnp.where(slot_of == 1, values[1], values[2]))

        live = (token >= of_slot(low)) & (token < of_slot(high)) & (key < of_slot(length))
        own_ref[...] = jnp.zeros_like(own_ref)
        away_ref[...] = jnp.zeros_like(away_ref)
        first_sum = jnp.zeros((tokens, 1), F32)
        second_sum = jnp.zeros((tokens, 1), F32)
        for head in range(heads):
            at = slice(head * HEAD_SIZE, (head + 1) * HEAD_SIZE)
            at_value = slice(width + head * HEAD_SIZE, width + (head + 1) * HEAD_SIZE)
            query, d_att = q_ref[:, at], da_ref[:, at]
            keys, values = kv_ref[:, at], kv_ref[:, at_value]
            grown = jnp.where(live, jnp.exp(contract_last(query, keys) * scale), 0.0)
            weights = grown * (1.0 / jnp.sum(grown, axis=-1, keepdims=True))
            probs = weights.astype(BF)
            d_probs = contract_last(d_att, values)
            mixed = jnp.sum(weights * d_probs, axis=-1, keepdims=True)
            d_scores = (weights * (d_probs - mixed) * scale).astype(BF)
            att_ref[:, at] = mm(probs, values).astype(BF)
            d_query = mm(d_scores, keys).astype(BF)
            dq_ref[:, at] = d_query
            d_wide = d_query.astype(F32)
            first_sum += jnp.sum(d_wide * sum_ref[:, at], axis=-1, keepdims=True)
            second_sum += jnp.sum(d_wide * query.astype(F32), axis=-1, keepdims=True)
            key_grad = contract_first(d_scores, query).astype(BF)
            value_grad = contract_first(probs, d_att).astype(BF)
            for slot in range(SLOTS):
                for part in range(4):
                    held = slice(
                        slot * cap_len + part * cap_quarter, slot * cap_len + (part + 1) * cap_quarter
                    )
                    to = pl.ds(aligned((part ^ g) * cap_quarter, cap_quarter), cap_quarter)
                    for side, target_ref in enumerate((own_ref, away_ref)):

                        @pl.when(valid[slot] & (side_to[slot] == side))
                        def _(slot=slot, held=held, to=to, target_ref=target_ref):
                            target_ref[far_to[slot], to, at] = key_grad[held]
                            target_ref[far_to[slot], to, at_value] = value_grad[held]

        rows_ref[:, 0:1] = first_sum
        rows_ref[:, 1:2] = second_sum
        for part in range(4):
            rows = pl.ds(aligned((part ^ g) * row_quarter, row_quarter), row_quarter)
            to = slice(part * row_quarter, (part + 1) * row_quarter)
            both_ref[0, to, :] = att_ref[rows, :]
            both_ref[1, to, :] = dq_ref[rows, :]

    out = [
        shaped((2, tokens, width)),
        shaped((tokens, width)),
        shaped((tokens, width)),
        shaped((tokens, 2), F32),
        shaped((pairs, cap_len, 2 * width)),
        shaped((pairs, cap_len, 2 * width)),
    ]
    operands = (place, counts, sample_caption, lens, queries, d_attended, column_sum, *kv_blocks)
    scratch = [pltpu.VMEM((keys_wide, 2 * width), BF)]
    return call(body, out, operands, 4, scratch)


def project_back(attended, d_queries, blocks, place, pairs, part):
    tokens, width = attended.shape
    arrays, blocks = pieces_of(blocks)
    model_width = 2 * pairs * part
    per_piece = 2 * pairs // 4
    piece = model_width // 4

    def body(place_ref, att_ref, dq_ref, *refs):
        block_refs = refs[: len(arrays)]
        own_ref, far_ref, away_ref = refs[len(arrays) :]
        z, y, g = place_ref[0], place_ref[1], place_ref[2]
        att, d_query = att_ref[...], dq_ref[...]
        for far in range(pairs):
            for side in range(2):
                (of_query, query_at), (of_out, out_at) = blocks[2 * far + side]
                weight = block_refs[of_query][query_at : query_at + part, :]
                out_weight = block_refs[of_out][out_at : out_at + width, :]
                origin = lax.rem(z - far + pairs, pairs) * 2 + (y ^ side)
                flip = (origin // per_piece) ^ g
                start = lax.rem(origin, per_piece) * part
                columns = pl.ds(aligned(start, 128), part)
                beyond = pl.ds(aligned(start + piece, 128), part)
                added = mm(att, out_weight).astype(BF)
                d_normed = contract_last(d_query, weight).astype(BF)
                places = ((own_ref, columns), (away_ref, columns), (far_ref, columns), (away_ref, beyond))
                for number, (target_ref, to) in enumerate(places):

                    @pl.when(flip == number)
                    def _(target_ref=target_ref, to=to, added=added, d_normed=d_normed):
                        target_ref[0, :, to] = added
                        target_ref[1, :, to] = d_normed

    out = [shaped((2, tokens, piece)), shaped((2, tokens, piece)), shaped((2, tokens, 2 * piece))]
    return call(body, out, (place, attended, d_queries, *arrays), 1)


def weight_grads(tiles, both_blocks, known, pairs):
    part = tiles[0].shape[-1]
    given = [k for k, block in enumerate(both_blocks) if block is not None]
    arrays, blocks = pieces_of([both_blocks[k] for k in given])
    width = arrays[0].shape[-1]
    known = known or []

    def body(*refs):
        tile_refs, known_refs = refs[:4], refs[4 : 4 + len(known)]
        block_refs, (query_ref, out_ref) = refs[4 + len(known) : -2], refs[-2:]
        query_grad = known_refs[0][...] if known else jnp.zeros((part, width), F32)
        out_grad = known_refs[1][...] if known else jnp.zeros((width, part), F32)
        for k, ((number, at),) in zip(given, blocks):
            side, far = divmod(k, pairs)
            block = block_refs[number]
            normed, grad = (
                jnp.concatenate([r[far, side, which] for r in tile_refs], axis=0)
                for which in range(2)
            )
            out_grad += contract_first(block[at], grad)
            query_grad += contract_first(normed, block[at + 1])
        query_ref[...] = query_grad
        out_ref[...] = out_grad

    out = [shaped((part, width), F32), shaped((width, part), F32)]
    return call(body, out, (*tiles, *known, *arrays), 0)


def local(
    caption_states,
    caption_lens,
    text_gain,
    text_query,
    text_key,
    text_value,
    text_bias,
    text_out,
    final_gain,
    cross_key,
    cross_value,
    video_states,
    video_counts,
    sample_caption,
    cross_query,
    cross_out,
    out_grad,
):
    column = lax.axis_index("fsdp")
    g = lax.axis_index("grp")
    pairs = lax.axis_size("fsdp") // 2
    z, y = column // 2, column % 2
    place = jnp.stack([z, y, g]).astype(jnp.int32)
    caps_local, cap_len, text_width = caption_states.shape
    tokens, model_width = video_states.shape
    width_local = cross_key.shape[1]
    part = cross_query.shape[0]

    states = caption_states.reshape(cap_len, text_width)
    quarter_rows = cap_len // 4

    first = [fsend(cross_query, 1, 0), fsend(cross_out, 1, 0)]
    side_key, side_value = fsend(cross_key, 0, 1), fsend(cross_value, 0, 1)
    projected = project_text(states, text_gain, (text_query, text_key, text_value))
    kept, away = attend_text(projected, text_bias, text_out, place, caption_lens)
    kept, away = after((kept, away), first, side_key, side_value)
    got = gsend(away, 1)
    ring = [None, jnp.concatenate(first, axis=0)]
    side_first = fsend(jnp.concatenate([cross_query, cross_out, *first], axis=0), 0, 1)
    ring.append(fsend(ring[1], 1, 0))
    sent = (kept[quarter_rows:].astype(F32) + got[quarter_rows:].astype(F32)).astype(BF)
    over_x = gsend(sent, 2)
    normed, mean, inverse, own_tiles, other_tiles = prepare_video(
        after(video_states, sent), out_grad, place, pairs, part
    )
    other_tiles = fsend(other_tiles, 0, 1)
    pieces = encode_rows(
        states, kept, got, after(over_x, normed), final_gain, place, pairs
    )

    mine = jnp.stack([fsend(p, far, 0) if far else p for far, p in enumerate(pieces)])
    mine = after(mine, ring[2])
    over_x = gsend(mine, 2)
    parts = [mine, gsend(mine, 1), over_x, gsend(over_x, 1)]
    current = after(ring[2], mine)
    for far in range(3, pairs):
        current = fsend(current, 1, 0)
        ring.append(current)
    parts[3] = after(parts[3], side_first, other_tiles)
    kv_partial = project_captions(
        parts, cross_key, cross_value, side_key, side_value, place, pairs
    )
    kv_partial = after(tuple(kv_partial), ring[-1])
    kv_sum = kv_partial[0].astype(F32)
    for far in range(1, pairs):
        kv_sum += fsend(kv_partial[far], pairs - far, 0).astype(F32)
    side_later = [fsend(w, 0, 1) for w in ring[2:]]
    kv_sum = after(kv_sum.astype(BF), side_later)
    kv_blocks = gather_direct(kv_sum)

    step = part + width_local
    blocks = []
    for far, held in enumerate(ring):
        side, start = (side_first, far * step) if far < 2 else (side_later[far - 2], 0)
        here = ((held, 0), (held, part)) if far else ((cross_query, 0), (cross_out, 0))
        blocks += [here, ((side, start), (side, start + part))]
    queries, d_attended, column_sum = project_rows(
        normed, after(out_grad, kv_blocks[4]), blocks, place, pairs, part
    )

    tiles = jnp.stack([own_tiles, other_tiles], axis=1)
    over_z = [fsend(after(tiles[far], kv_blocks[4]), far, 0) for far in range(1, pairs)]
    over_z = [tiles[0]] + over_z

    both, attended, d_queries, row_sums, kv_own, kv_away = attend(
        queries,
        d_attended,
        column_sum,
        kv_blocks,
        place,
        video_counts,
        sample_caption,
        caption_lens,
        pairs,
    )
    kv_away, both, row_sums, over_z = after((kv_away, both, row_sums, over_z))
    tiles = jnp.stack(over_z)

    def chain(blocks, steps):
        for _ in range(steps):
            blocks.append(fsend(blocks[-1], 1, 0))
        return blocks

    def joined(two):
        return jnp.stack(two).reshape(-1, tokens, width_local)

    kv_side = fsend(kv_away, 0, 1)
    late = chain([both], pairs // 2)
    sums_core = gsend(row_sums, 1)
    attended, tiles = after((attended, tiles), sums_core)
    tiles_x = gsend(tiles, 2)
    tiles_core = gsend(tiles, 1)
    own, far_piece, away = project_back(attended, d_queries, blocks, place, pairs, part)
    stage = (kv_side, late, sums_core, tiles_x, tiles_core, joined(late[:2]), away)
    kv_side, late, sums_core, tiles_x, tiles_core, first_two, away = after(stage)

    sides = [fsend(first_two, 0, 1)]
    late = chain(list(late), pairs - 1 - pairs // 2)
    row_sums = row_sums + sums_core
    sums_x = gsend(row_sums, 2)
    got = gsend(away, 1)
    width = model_width // 4
    sent = (far_piece.astype(F32) + got[:, :, width:].astype(F32)).astype(BF)
    far_sum = gsend(sent, 2)
    tiles = [tiles, tiles_core, tiles_x, gsend(tiles_x, 1)]

    def kv_term(far):
        return kv_own[far].astype(F32) + kv_side[far].astype(F32)

    kv_grads = kv_term(0)
    for far in range(1, pairs, 2):
        kv_grads += fsend(kv_term(far).astype(BF), far, 0).astype(F32)
    kv_rest = [kv_term(far).astype(BF) for far in range(2, pairs, 2)]
    others = [joined(late[far : far + 2]) for far in range(2, pairs, 2)]
    stage = (sides[0], late, sums_x, sent, tiles, kv_grads, kv_rest, others)
    sides[0], late, sums_x, _, tiles, kv_grads, kv_rest, others = after(stage)

    sides += [fsend(two, 0, 1) for two in others]
    here = [((block, 0),) for block in late]
    there = [((sides[far // 2], far % 2 * 2),) for far in range(pairs)]
    known = weight_grads(tiles, here + there[:2], None, pairs)
    total = own.astype(F32) + got[:, :, :width].astype(F32) + far_sum.astype(F32)
    row_sums = (row_sums + sums_x) / model_width
    video = quarter(video_states, g, 1).astype(F32)
    updated = (video + total[0]).astype(BF)
    video_hat = (video - mean) * inverse
    input_grad = (
        quarter(out_grad, g, 1).astype(F32)
        + inverse * (total[1] - row_sums[:, 0:1] - video_hat * row_sums[:, 1:2])
    ).astype(BF)
    for far in range(2, pairs, 2):
        kv_grads += fsend(kv_rest[far // 2 - 1], far, 0).astype(F32)
    kv_grads = kv_grads.astype(BF)[None]
    key_grad = kv_grads[:, :, :width_local]
    value_grad = kv_grads[:, :, width_local:]
    query_grad, out_weight_grad = weight_grads(tiles, [None] * (pairs + 2) + there[2:], known, pairs)
    return (updated, input_grad, query_grad, out_weight_grad, key_grad, value_grad)


def local_of(*arrays):
    whole_tiles = arrays[14].shape[0] % 128 == 0 and arrays[0].shape[0] == 1
    return local(*arrays) if whole_tiles else local_general(*arrays)


def solution(mesh):
    in_specs = (
        P("fsdp", None, None),
        P(),
        P(),
        P(None, "grp"),
        P(None, "grp"),
        P(None, "grp"),
        P("grp", None, None),
        P("grp", None),
        P(),
        P("fsdp", "grp"),
        P("fsdp", "grp"),
        P("fsdp", None),
        P(),
        P(),
        P("fsdp", "grp"),
        P("grp", "fsdp"),
        P("fsdp", None),
    )
    out_specs = (
        P("fsdp", "grp"),
        P("fsdp", "grp"),
        P("fsdp", "grp"),
        P("grp", "fsdp"),
        P("fsdp", None, "grp"),
        P("fsdp", None, "grp"),
    )
    return jax.shard_map(
        local_of, mesh=mesh, in_specs=in_specs, out_specs=out_specs, check_vma=False
    )
```

```python
import math

import jax
import jax.numpy as jnp
from jax import lax
from jax.experimental import pallas as pl
from jax.experimental.pallas import tpu as pltpu
from jax.sharding import PartitionSpec as P

HEAD_SIZE = 128
BF = jnp.bfloat16
F32 = jnp.float32
SLOTS = 3
VMEM_BYTES = 60 * 1024 * 1024
SPARE_BYTES = 8 * 1024 * 1024
SMALL = pl.CostEstimate(flops=1, bytes_accessed=1, transcendentals=0)


def rms_scale(values, gain):
    mean_square = jnp.mean(values * values, axis=-1, keepdims=True)
    return values * lax.rsqrt(mean_square + 1e-06) * gain


def mm(left, right):
    return jnp.dot(left, right, preferred_element_type=F32)


def contract_last(left, right):
    return lax.dot_general(left, right, (((1,), (1,)), ((), ())), preferred_element_type=F32)


def contract_first(left, right):
    return lax.dot_general(left, right, (((0,), (0,)), ((), ())), preferred_element_type=F32)


def fsend(block, far, side):
    size = lax.axis_size("fsdp")
    pairs = size // 2
    perm = [(s, ((s // 2 + far) % pairs) * 2 + ((s % 2) ^ side)) for s in range(size)]
    return lax.ppermute(block, "fsdp", perm)


def gsend(block, flip):
    return lax.ppermute(block, "grp", [(s, s ^ flip) for s in range(lax.axis_size("grp"))])


def gather_ring(block):
    blocks = []
    current = block
    for far in range(lax.axis_size("fsdp") // 2):
        if far:
            current = fsend(current, 1, 0)
        blocks += [current, fsend(current, 0, 1)]
    return blocks


def gather_direct(block):
    blocks = []
    for far in range(lax.axis_size("fsdp") // 2):
        current = fsend(block, far, 0) if far else block
        blocks += [current, fsend(current, 0, 1)]
    return blocks


def quarter(array, index, axis=0):
    size = array.shape[axis] // 4
    return lax.dynamic_slice_in_dim(array, index * size, size, axis)


def grp_scatter(partial, g, axis):
    away = [quarter(partial, g ^ 1, axis), quarter(partial, g ^ 3, axis)]
    kept = [quarter(partial, g, axis), quarter(partial, g ^ 2, axis)]
    got = gsend(jnp.stack(away).astype(BF), 1)
    far = gsend((kept[1] + got[1].astype(F32)).astype(BF), 2)
    return kept[0] + got[0].astype(F32) + far.astype(F32)


def local_general(
    caption_states,
    caption_lens,
    text_gain,
    text_query,
    text_key,
    text_value,
    text_bias,
    text_out,
    final_gain,
    cross_key,
    cross_value,
    video_states,
    video_counts,
    sample_caption,
    cross_query,
    cross_out,
    out_grad,
):
    column = lax.axis_index("fsdp")
    g = lax.axis_index("grp")
    fsdp = lax.axis_size("fsdp")
    pairs = fsdp // 2
    z, y = column // 2, column % 2
    caps_local, cap_len, text_width = caption_states.shape
    tokens, model_width = video_states.shape
    width_local = cross_key.shape[1]
    cross_local = width_local // HEAD_SIZE
    query_rows = cross_query.shape[0]

    def source(far, side):
        return ((z - far) % pairs) * 2 + (y ^ side)

    def target(far, side):
        return ((z + far) % pairs) * 2 + (y ^ side)

    query_blocks = gather_ring(cross_query)
    out_blocks = gather_ring(cross_out)
    full_query = jnp.zeros((model_width, width_local), BF)
    full_out = jnp.zeros((width_local, model_width), BF)
    for far in range(pairs):
        for side in range(2):
            start = source(far, side) * query_rows
            full_query = lax.dynamic_update_slice(
                full_query, query_blocks[2 * far + side], (start, jnp.int32(0))
            )
            full_out = lax.dynamic_update_slice(
                full_out, out_blocks[2 * far + side], (jnp.int32(0), start)
            )

    own_kv = jnp.concatenate([cross_key, cross_value], axis=1)
    other_kv = fsend(own_kv, 0, 1)
    pair_kv = jnp.concatenate(
        [jnp.where(y == 0, own_kv, other_kv), jnp.where(y == 0, other_kv, own_kv)], axis=0
    )

    local_lens = lax.dynamic_slice_in_dim(caption_lens, column * caps_local, caps_local)
    flat_states = caption_states.reshape(caps_local * cap_len, text_width).astype(F32)
    text_normed = rms_scale(flat_states, text_gain).astype(BF)
    local_heads = text_bias.shape[0]
    head_width = text_query.shape[1] // local_heads

    def heads_of(weight):
        return mm(text_normed, weight).astype(BF).reshape(
            caps_local, cap_len, local_heads, head_width
        )

    text_queries = heads_of(text_query)
    text_keys = heads_of(text_key)
    text_values = heads_of(text_value)
    text_scores = (
        jnp.einsum("cihd,cjhd->chij", text_queries, text_keys, preferred_element_type=F32)
        + text_bias[None]
    )
    key_valid = jnp.arange(cap_len, dtype=jnp.int32)[None, :] < local_lens[:, None]
    exp_scores = jnp.where(key_valid[:, None, None, :], jnp.exp(text_scores), 0.0)
    text_weights = (exp_scores / jnp.sum(exp_scores, axis=-1, keepdims=True)).astype(BF)
    text_mixed = jnp.einsum(
        "chij,cjhd->cihd", text_weights, text_values, preferred_element_type=F32
    )
    text_mixed = text_mixed.astype(BF).reshape(caps_local * cap_len, local_heads * head_width)
    partial_text = mm(text_mixed, text_out)
    text_rows = grp_scatter(partial_text, g, 0)
    encoded = rms_scale(quarter(flat_states, g) + text_rows, final_gain).astype(BF)

    part = text_width // pairs
    pieces = [
        lax.dynamic_slice_in_dim(encoded, ((z + far) % pairs) * part, part, 1)
        for far in range(pairs)
    ]
    mine = jnp.stack([fsend(p, far, 0) if far else p for far, p in enumerate(pieces)])
    over_x = jnp.concatenate([mine[:, None], gsend(mine, 2)[:, None]], axis=1)
    over_core = jnp.stack([over_x, gsend(over_x, 1)], axis=2)
    kv_partial = mm(over_core.reshape(-1, part), pair_kv).reshape(pairs, cap_len, 2 * width_local)
    kv_sum = kv_partial[0]
    for far in range(1, pairs):
        kv_sum += fsend(kv_partial[far].astype(BF), pairs - far, 0).astype(F32)
    kv_rows = kv_sum.astype(BF).reshape(4, cap_len // 4, 2 * width_local)
    order = jnp.arange(4, dtype=jnp.int32) ^ g
    cap_kv = jnp.concatenate(
        [lax.dynamic_slice_in_dim(kv_rows, order[k], 1, 0) for k in range(4)], axis=0
    ).reshape(cap_len, 2 * width_local)
    all_kv = jnp.stack(gather_direct(cap_kv))

    video = video_states.astype(F32)
    center = video - jnp.mean(video, axis=-1, keepdims=True)
    inverse = lax.rsqrt(jnp.mean(center * center, axis=-1, keepdims=True) + 1e-06)
    video_hat = center * inverse
    video_normed = video_hat.astype(BF)

    both = jnp.stack([quarter(video_normed, g), quarter(out_grad, g)])
    tiles = []
    for far in range(pairs):
        for side in range(2):
            tile = lax.dynamic_slice_in_dim(both, target(far, side) * query_rows, query_rows, 2)
            tiles.append(fsend(tile, far, side) if far or side else tile)
    tiles = jnp.stack(tiles)
    tiles_x = jnp.stack([tiles, gsend(tiles, 2)], axis=2)
    tiles_all = jnp.stack([tiles_x, gsend(tiles_x, 1)], axis=3)
    normed_tile = tiles_all[:, 0].reshape(-1, query_rows)
    grad_tile = tiles_all[:, 1].reshape(-1, query_rows)

    caption_total = all_kv.shape[0]
    positions = column * tokens + jnp.arange(tokens, dtype=jnp.int32)
    sample_end = jnp.cumsum(video_counts)
    token_sample = jnp.sum((sample_end[None, :] <= positions[:, None]).astype(jnp.int32), axis=1)
    slot_count = 3
    slot_sample = token_sample[0] + jnp.arange(slot_count, dtype=jnp.int32)
    slot_valid = slot_sample < caption_total
    slot_clipped = jnp.minimum(slot_sample, caption_total - 1)
    numbers = jnp.arange(caption_total, dtype=jnp.int32)
    slot_pick = slot_clipped[:, None] == numbers[None, :]
    slot_caption = jnp.sum(jnp.where(slot_pick, sample_caption[None, :], 0), axis=1)
    caption_pick = slot_caption[:, None] == numbers[None, :]
    slot_lens = jnp.sum(jnp.where(caption_pick, caption_lens[None, :], 0), axis=1)
    slot_member = token_sample[None, :] == slot_sample[:, None]
    member_float = slot_member.astype(F32)
    member_half = slot_member.astype(BF)
    slot_entry = ((z - slot_caption // 2) % pairs) * 2 + ((slot_caption % 2) ^ y)
    slot_kv = jnp.take(all_kv, slot_entry, axis=0)
    slot_keys = slot_kv[..., :width_local].reshape(slot_count, cap_len, cross_local, HEAD_SIZE)
    slot_values = slot_kv[..., width_local:].reshape(slot_count, cap_len, cross_local, HEAD_SIZE)
    token_lens = jnp.sum(jnp.where(slot_member, slot_lens[:, None], 0), axis=0)

    query_sum = mm(video_normed, full_query)
    queries = query_sum.astype(BF)
    d_attended = contract_last(out_grad, full_out).astype(BF).reshape(
        tokens, cross_local, HEAD_SIZE
    )
    score_scale = 1.0 / math.sqrt(HEAD_SIZE)
    query_heads = queries.reshape(tokens, cross_local, HEAD_SIZE)
    slot_scores = jnp.einsum("thd,kjhd->kthj", query_heads, slot_keys, preferred_element_type=F32)
    scores = jnp.sum(member_float[:, :, None, None] * slot_scores, axis=0) * score_scale
    token_valid = (jnp.arange(cap_len, dtype=jnp.int32)[None, :] < token_lens[:, None])[:, None, :]
    exp_video = jnp.where(token_valid, jnp.exp(scores), 0.0)
    weights = exp_video / jnp.sum(exp_video, axis=-1, keepdims=True)
    probs = weights.astype(BF)
    masked_probs = member_half[:, :, None, None] * probs[None]
    attended = jnp.einsum("kthj,kjhd->thd", masked_probs, slot_values, preferred_element_type=F32)
    attended = attended.astype(BF).reshape(tokens, width_local)

    def reorder(array):
        return jnp.concatenate([quarter(array, order[k]) for k in range(4)], axis=0)

    all_attended = jnp.concatenate(gather_direct(reorder(attended)), axis=0)
    out_weight_grad = contract_first(all_attended, grad_tile)

    out_share = grp_scatter(mm(attended, full_out), g, 1)
    updated = (quarter(video, g, 1) + out_share).astype(BF)

    slot_dprobs = jnp.einsum("thd,kjhd->kthj", d_attended, slot_values, preferred_element_type=F32)
    d_probs = jnp.sum(member_float[:, :, None, None] * slot_dprobs, axis=0)
    d_scores = (
        weights * (d_probs - jnp.sum(weights * d_probs, axis=-1, keepdims=True)) * score_scale
    ).astype(BF)
    masked_scores = member_half[:, :, None, None] * d_scores[None]
    d_queries = jnp.einsum("kthj,kjhd->thd", masked_scores, slot_keys, preferred_element_type=F32)
    d_queries = d_queries.astype(BF).reshape(tokens, width_local)
    all_d_queries = jnp.concatenate(gather_direct(reorder(d_queries)), axis=0)
    query_grad = contract_first(normed_tile, all_d_queries)

    key_slots = jnp.einsum("kthj,thd->kjhd", masked_scores, query_heads, preferred_element_type=F32)
    value_slots = jnp.einsum("kthj,thd->kjhd", masked_probs, d_attended, preferred_element_type=F32)
    slot_terms = jnp.concatenate(
        [
            key_slots.reshape(slot_count, cap_len, width_local),
            value_slots.reshape(slot_count, cap_len, width_local),
        ],
        axis=-1,
    )

    def caption_terms(far, side):
        picked = (slot_caption == target(far, side)) & slot_valid
        return jnp.sum(jnp.where(picked[:, None, None], slot_terms, 0.0), axis=0)

    away = jnp.stack([caption_terms(far, 1).astype(BF) for far in range(pairs)])
    got = fsend(away, 0, 1).astype(F32)
    kv_grads = caption_terms(0, 0) + got[0]
    for far in range(1, pairs):
        kv_grads += fsend((caption_terms(far, 0) + got[far]).astype(BF), far, 0).astype(F32)
    kv_grads = kv_grads.astype(BF)[None]
    key_grad = kv_grads[:, :, :width_local]
    value_grad = kv_grads[:, :, width_local:]

    d_wide = d_queries.astype(F32)
    column_sum = jnp.sum(full_query.astype(F32), axis=0)
    row_sums = jnp.stack(
        [jnp.sum(d_wide * column_sum, axis=-1), jnp.sum(d_wide * query_sum, axis=-1)]
    )
    row_sums = row_sums + gsend(row_sums, 1)
    row_sums = (row_sums + gsend(row_sums, 2)) / model_width
    d_share = grp_scatter(contract_last(d_queries, full_query), g, 1)
    input_grad = (
        quarter(out_grad, g, 1).astype(F32)
        + inverse
        * (d_share - row_sums[0][:, None] - quarter(video_hat, g, 1) * row_sums[1][:, None])
    ).astype(BF)
    return (updated, input_grad, query_grad, out_weight_grad, key_grad, value_grad)


def after(value, *others):
    return lax.optimization_barrier((value, *others))[0]


def call(body, out_shape, operands, scalars, scratch=()):
    specs = [pl.BlockSpec(memory_space=pltpu.SMEM)] * scalars
    specs += [pl.BlockSpec(memory_space=pltpu.VMEM)] * (len(operands) - scalars)
    held = (*operands[scalars:], *jax.tree.leaves(out_shape), *scratch)
    held_bytes = sum(math.prod(a.shape) * jnp.dtype(a.dtype).itemsize for a in held)
    return pl.pallas_call(
        body,
        out_shape=out_shape,
        in_specs=specs,
        out_specs=jax.tree.map(lambda _: pl.BlockSpec(memory_space=pltpu.VMEM), out_shape),
        scratch_shapes=list(scratch),
        compiler_params=pltpu.CompilerParams(vmem_limit_bytes=held_bytes + SPARE_BYTES),
        cost_estimate=SMALL,
    )(*operands)


def shaped(shape, dtype=BF):
    return jax.ShapeDtypeStruct(shape, dtype)


def aligned(start, unit):
    return pl.multiple_of(start, unit)


def project_text(states, gain, weights, steps=4):
    rows, depth = states.shape
    width = weights[0].shape[1]
    chunk = depth // steps

    def body(states_ref, gain_ref, wq_ref, wk_ref, wv_ref, out_ref, normed_ref, total_ref):
        step = pl.program_id(0)

        @pl.when(step == 0)
        def _():
            for at in range(0, rows, 16):
                values = states_ref[at : at + 16, :].astype(F32)
                normed_ref[at : at + 16, :] = rms_scale(values, gain_ref[...]).astype(BF)
            total_ref[...] = jnp.zeros_like(total_ref)

        here = normed_ref[:, pl.ds(aligned(step * chunk, chunk), chunk)]
        for k, weight_ref in enumerate((wq_ref, wk_ref, wv_ref)):
            total_ref[:, k * width : (k + 1) * width] += mm(here, weight_ref[...])

        @pl.when(step == steps - 1)
        def _():
            out_ref[...] = total_ref[...].astype(BF)

    whole = lambda shape: pl.BlockSpec(shape, lambda i: (0,) * len(shape))
    return pl.pallas_call(
        body,
        grid=(steps,),
        out_shape=shaped((rows, 3 * width)),
        in_specs=[whole((rows, depth)), whole((1, depth))]
        + [pl.BlockSpec((chunk, width), lambda i: (i, 0))] * 3,
        out_specs=whole((rows, 3 * width)),
        scratch_shapes=[pltpu.VMEM((rows, depth), BF), pltpu.VMEM((rows, 3 * width), F32)],
        compiler_params=pltpu.CompilerParams(vmem_limit_bytes=VMEM_BYTES),
        cost_estimate=SMALL,
    )(states, gain.reshape(1, -1), *weights)


def attend_text(projected, bias, text_out, place, lens, steps=4):
    rows = projected.shape[0]
    heads = bias.shape[0]
    inner, depth = text_out.shape
    size = inner // heads
    quarter_rows = rows // 4
    chunk = depth // steps

    def body(place_ref, len_ref, qkv_ref, bias_ref, out_ref, kept_ref, away_ref, held_ref, mixed_ref):
        @pl.when(pl.program_id(0) == 0)
        def _():
            g = place_ref[2]
            length = len_ref[place_ref[0] * 2 + place_ref[1]]
            live = lax.broadcasted_iota(jnp.int32, (rows, rows), 1) < length
            for head in range(heads):
                query, key, value = (
                    qkv_ref[:, k * inner + head * size : k * inner + (head + 1) * size]
                    for k in range(3)
                )
                grown = jnp.where(live, jnp.exp(contract_last(query, key) + bias_ref[head]), 0.0)
                weights = grown * (1.0 / jnp.sum(grown, axis=-1, keepdims=True))
                held_ref[:, head * size : (head + 1) * size] = mm(weights.astype(BF), value).astype(BF)
            for k, to in ((0, 0), (2, 1), (1, 2), (3, 3)):
                rows_from = pl.ds(aligned((g ^ k) * quarter_rows, quarter_rows), quarter_rows)
                mixed_ref[to * quarter_rows : (to + 1) * quarter_rows, :] = held_ref[rows_from, :]

        product = mm(mixed_ref[...], out_ref[...]).astype(BF)
        kept_ref[...] = product[: rows // 2]
        away_ref[...] = product[rows // 2 :]

    whole = lambda shape: pl.BlockSpec(shape, lambda i: (0,) * len(shape))
    return pl.pallas_call(
        body,
        grid=(steps,),
        out_shape=[shaped((rows // 2, depth))] * 2,
        in_specs=[pl.BlockSpec(memory_space=pltpu.SMEM)] * 2
        + [whole(projected.shape), whole(bias.shape)]
        + [pl.BlockSpec((inner, chunk), lambda i: (0, i))],
        out_specs=[pl.BlockSpec((rows // 2, chunk), lambda i: (0, i))] * 2,
        scratch_shapes=[pltpu.VMEM((rows, inner), BF), pltpu.VMEM((rows, inner), BF)],
        compiler_params=pltpu.CompilerParams(vmem_limit_bytes=VMEM_BYTES),
        cost_estimate=SMALL,
    )(place, lens, projected, bias, text_out)


def encode_rows(states, kept, got, far, gain, place, pairs):
    quarter_rows = states.shape[0] // 4
    width = states.shape[1]
    depth = width // pairs

    def body(place_ref, states_ref, kept_ref, got_ref, far_ref, gain_ref, *refs):
        piece_refs, encoded_ref = refs[:-1], refs[-1]
        z, g = place_ref[0], place_ref[2]
        mine = pl.ds(aligned(g * quarter_rows, quarter_rows), quarter_rows)
        total = states_ref[mine, :].astype(F32) + far_ref[...].astype(F32)
        total += kept_ref[:quarter_rows, :].astype(F32) + got_ref[:quarter_rows, :].astype(F32)
        encoded_ref[...] = rms_scale(total, gain_ref[...]).astype(BF)
        for far_by, piece in enumerate(piece_refs):
            to = lax.rem(z + far_by, pairs)
            piece[...] = encoded_ref[:, pl.ds(aligned(to * depth, 128), depth)]

    out = [shaped((quarter_rows, depth))] * pairs
    operands = (place, states, kept, got, far, gain.reshape(1, -1))
    return call(body, out, operands, 1, [pltpu.VMEM((quarter_rows, width), BF)])


def pieces_of(pairs_of_blocks):
    arrays, listed = [], []
    for entry in pairs_of_blocks:
        numbers = []
        for array, start in entry:
            if not any(array is held for held in arrays):
                arrays.append(array)
            numbers.append((next(k for k, held in enumerate(arrays) if held is array), start))
        listed.append(numbers)
    return arrays, listed


def prepare_video(video_states, out_grad, place, pairs, part):
    tokens, model_width = video_states.shape
    rows = tokens // 4

    def body(place_ref, video_ref, grad_ref, normed_ref, mean_ref, inverse_ref, *tile_refs):
        @pl.loop(0, tokens // 32)
        def _(step):
            here = pl.ds(aligned(step * 32, 32), 32)
            values = video_ref[here, :].astype(F32)
            mean = jnp.mean(values, axis=-1, keepdims=True)
            center = values - mean
            inverse = lax.rsqrt(jnp.mean(center * center, axis=-1, keepdims=True) + 1e-06)
            normed_ref[here, :] = (center * inverse).astype(BF)
            mean_ref[here, :] = mean
            inverse_ref[here, :] = inverse

        z, y, g = place_ref[0], place_ref[1], place_ref[2]
        mine = pl.ds(aligned(g * rows, rows), rows)
        for far in range(pairs):
            for side in range(2):
                to = lax.rem(z + far, pairs) * 2 + (y ^ side)
                columns = pl.ds(aligned(to * part, 128), part)
                tile_refs[side][far, 0] = normed_ref[mine, columns]
                tile_refs[side][far, 1] = grad_ref[mine, columns]

    out = [shaped((tokens, model_width)), shaped((tokens, 1), F32), shaped((tokens, 1), F32)]
    out += [shaped((pairs, 2, rows, part))] * 2
    return call(body, out, (place, video_states, out_grad), 1)


def project_rows(normed, out_grad, blocks, place, pairs, part):
    tokens = normed.shape[0]
    arrays, blocks = pieces_of(blocks)
    width = arrays[0].shape[1]

    def body(place_ref, normed_ref, grad_ref, *refs):
        block_refs, (query_ref, d_ref, sum_ref) = refs[:-3], refs[-3:]
        z, y = place_ref[0], place_ref[1]
        query = jnp.zeros((tokens, width), F32)
        d_attended = jnp.zeros((tokens, width), F32)
        total = jnp.zeros((1, width), F32)
        for far in range(pairs):
            for side in range(2):
                (of_query, query_at), (of_out, out_at) = blocks[2 * far + side]
                origin = lax.rem(z - far + pairs, pairs) * 2 + (y ^ side)
                columns = pl.ds(aligned(origin * part, 128), part)
                weight = block_refs[of_query][query_at : query_at + part, :]
                out_weight = block_refs[of_out][out_at : out_at + width, :]
                query += mm(normed_ref[:, columns], weight)
                d_attended += contract_last(grad_ref[:, columns], out_weight)
                total += jnp.sum(weight.astype(F32), axis=0, keepdims=True)
        query_ref[...] = query.astype(BF)
        d_ref[...] = d_attended.astype(BF)
        sum_ref[...] = total

    out = [shaped((tokens, width)), shaped((tokens, width)), shaped((1, width), F32)]
    return call(body, out, (place, normed, out_grad, *arrays), 1)


def project_captions(parts, own_key, own_value, side_key, side_value, place, pairs):
    quarter_rows, depth = parts[0].shape[1:]
    half = depth // 2
    width = own_key.shape[1]

    def body(place_ref, *refs):
        part_refs = refs[:4]
        key_ref, value_ref, side_key_ref, side_value_ref = refs[4:8]
        out_refs = refs[8:]
        y = place_ref[1]
        mine = pl.ds(aligned(y * half, 128), half)
        theirs = pl.ds(aligned((1 - y) * half, 128), half)
        own = jnp.concatenate([r[far, :, mine] for far in range(pairs) for r in part_refs], 0)
        other = jnp.concatenate([r[far, :, theirs] for far in range(pairs) for r in part_refs], 0)
        keys = mm(own, key_ref[...]) + mm(other, side_key_ref[...])
        values = mm(own, value_ref[...]) + mm(other, side_value_ref[...])
        for far in range(pairs):
            rows = slice(far * 4 * quarter_rows, (far + 1) * 4 * quarter_rows)
            out_refs[far][:, :width] = keys[rows].astype(BF)
            out_refs[far][:, width:] = values[rows].astype(BF)

    out = [shaped((4 * quarter_rows, 2 * width))] * pairs
    operands = (place, *parts, own_key, own_value, side_key, side_value)
    return call(body, out, operands, 1)


def slots_of(count_ref, caption_ref, base, captions):
    def find(sample, carry):
        total, first, start = carry
        total = total + count_ref[sample]
        past = total <= base
        return total, first + past.astype(jnp.int32), jnp.where(past, total, start)

    zero = jnp.int32(0)
    _, first, start = lax.fori_loop(0, captions, find, (zero, zero, zero))
    found, edge = [], start - base
    for slot in range(SLOTS):
        valid = first + slot < captions
        sample = jnp.minimum(first + slot, captions - 1)
        end = edge + jnp.where(valid, count_ref[sample], 0)
        found.append((edge, end, caption_ref[sample], valid))
        edge = end
    return found


def attend(queries, d_attended, column_sum, kv_blocks, place, counts, sample_caption, lens, pairs):
    tokens, width = queries.shape
    cap_len = kv_blocks[0].shape[0]
    heads = width // HEAD_SIZE
    captions = counts.shape[0]
    keys_wide = SLOTS * cap_len
    cap_quarter, row_quarter = cap_len // 4, tokens // 4
    scale = 1.0 / math.sqrt(HEAD_SIZE)

    def body(place_ref, count_ref, caption_ref, len_ref, q_ref, da_ref, sum_ref, *refs):
        block_refs = refs[: len(kv_blocks)]
        both_ref, att_ref, dq_ref, rows_ref, slot_ref, kv_ref = refs[len(kv_blocks) :]
        z, y, g = place_ref[0], place_ref[1], place_ref[2]
        low, high, length = [], [], []
        found = slots_of(count_ref, caption_ref, (z * 2 + y) * tokens, captions)
        for slot, (start, end, caption, _) in enumerate(found):
            low.append(start)
            high.append(end)
            length.append(len_ref[caption])
            entry = lax.rem(z - caption // 2 + pairs, pairs) * 2 + (lax.rem(caption, 2) ^ y)
            for number, block in enumerate(block_refs):

                @pl.when(entry == number)
                def _(slot=slot, block=block):
                    kv_ref[slot * cap_len : (slot + 1) * cap_len, :] = block[...]

        token = lax.broadcasted_iota(jnp.int32, (tokens, keys_wide), 0)
        column = lax.broadcasted_iota(jnp.int32, (tokens, keys_wide), 1)
        slot_of = column // cap_len
        inside = column % cap_len
        key = ((inside // cap_quarter) ^ g) * cap_quarter + inside % cap_quarter

        def of_slot(values):
            return jnp.where(slot_of == 0, values[0], jnp.where(slot_of == 1, values[1], values[2]))

        live = (token >= of_slot(low)) & (token < of_slot(high)) & (key < of_slot(length))
        first_sum = jnp.zeros((tokens, 1), F32)
        second_sum = jnp.zeros((tokens, 1), F32)
        for head in range(heads):
            at = slice(head * HEAD_SIZE, (head + 1) * HEAD_SIZE)
            at_value = slice(width + head * HEAD_SIZE, width + (head + 1) * HEAD_SIZE)
            query, d_att = q_ref[:, at], da_ref[:, at]
            keys, values = kv_ref[:, at], kv_ref[:, at_value]
            grown = jnp.where(live, jnp.exp(contract_last(query, keys) * scale), 0.0)
            weights = grown * (1.0 / jnp.sum(grown, axis=-1, keepdims=True))
            probs = weights.astype(BF)
            d_probs = contract_last(d_att, values)
            mixed = jnp.sum(weights * d_probs, axis=-1, keepdims=True)
            d_scores = (weights * (d_probs - mixed) * scale).astype(BF)
            att_ref[:, at] = mm(probs, values).astype(BF)
            d_query = mm(d_scores, keys).astype(BF)
            dq_ref[:, at] = d_query
            d_wide = d_query.astype(F32)
            first_sum += jnp.sum(d_wide * sum_ref[:, at], axis=-1, keepdims=True)
            second_sum += jnp.sum(d_wide * query.astype(F32), axis=-1, keepdims=True)
            key_grad = contract_first(d_scores, query).astype(BF)
            value_grad = contract_first(probs, d_att).astype(BF)
            for slot in range(SLOTS):
                for part in range(4):
                    held = slice(
                        slot * cap_len + part * cap_quarter, slot * cap_len + (part + 1) * cap_quarter
                    )
                    to = pl.ds(aligned((part ^ g) * cap_quarter, cap_quarter), cap_quarter)
                    slot_ref[slot, to, at] = key_grad[held]
                    slot_ref[slot, to, at_value] = value_grad[held]

        rows_ref[:, 0:1] = first_sum
        rows_ref[:, 1:2] = second_sum
        for part in range(4):
            rows = pl.ds(aligned((part ^ g) * row_quarter, row_quarter), row_quarter)
            to = slice(part * row_quarter, (part + 1) * row_quarter)
            both_ref[0, to, :] = att_ref[rows, :]
            both_ref[1, to, :] = dq_ref[rows, :]

    out = [
        shaped((2, tokens, width)),
        shaped((tokens, width)),
        shaped((tokens, width)),
        shaped((tokens, 2), F32),
        shaped((SLOTS, cap_len, 2 * width)),
    ]
    operands = (place, counts, sample_caption, lens, queries, d_attended, column_sum, *kv_blocks)
    scratch = [pltpu.VMEM((keys_wide, 2 * width), BF)]
    return call(body, out, operands, 4, scratch)


def caption_terms(slots, side_slots, place, counts, sample_caption, tokens, pairs):
    captions = counts.shape[0]
    shape = slots.shape[1:]

    def body(place_ref, count_ref, caption_ref, own_ref, side_ref, *refs):
        term_refs, total_ref = refs[:-1], refs[-1]
        z, y = place_ref[0], place_ref[1]
        total_ref[...] = jnp.zeros_like(total_ref)
        for side, slot_ref in enumerate((own_ref, side_ref)):
            base = (z * 2 + (y ^ side)) * tokens
            for slot, (_, _, caption, valid) in enumerate(
                slots_of(count_ref, caption_ref, base, captions)
            ):
                far = lax.rem(caption // 2 - z + pairs, pairs)

                @pl.when(valid & (lax.rem(caption, 2) == y))
                def _(slot=slot, far=far, slot_ref=slot_ref):
                    total_ref[far] += slot_ref[slot].astype(F32)

        for far, term_ref in enumerate(term_refs):
            term_ref[...] = total_ref[far].astype(term_ref.dtype)

    out = [shaped(shape, F32 if far == 0 else BF) for far in range(pairs)]
    operands = (place, counts, sample_caption, slots, side_slots)
    return call(body, out, operands, 3, [pltpu.VMEM((pairs, *shape), F32)])


def project_back(attended, d_queries, blocks, place, pairs, part):
    tokens, width = attended.shape
    arrays, blocks = pieces_of(blocks)
    model_width = 2 * pairs * part
    per_piece = 2 * pairs // 4
    piece = model_width // 4

    def body(place_ref, att_ref, dq_ref, *refs):
        block_refs = refs[: len(arrays)]
        own_ref, far_ref, away_ref = refs[len(arrays) :]
        z, y, g = place_ref[0], place_ref[1], place_ref[2]
        att, d_query = att_ref[...], dq_ref[...]
        for far in range(pairs):
            for side in range(2):
                (of_query, query_at), (of_out, out_at) = blocks[2 * far + side]
                weight = block_refs[of_query][query_at : query_at + part, :]
                out_weight = block_refs[of_out][out_at : out_at + width, :]
                origin = lax.rem(z - far + pairs, pairs) * 2 + (y ^ side)
                flip = (origin // per_piece) ^ g
                start = lax.rem(origin, per_piece) * part
                columns = pl.ds(aligned(start, 128), part)
                beyond = pl.ds(aligned(start + piece, 128), part)
                added = mm(att, out_weight).astype(BF)
                d_normed = contract_last(d_query, weight).astype(BF)
                places = ((own_ref, columns), (away_ref, columns), (far_ref, columns), (away_ref, beyond))
                for number, (target_ref, to) in enumerate(places):

                    @pl.when(flip == number)
                    def _(target_ref=target_ref, to=to, added=added, d_normed=d_normed):
                        target_ref[0, :, to] = added
                        target_ref[1, :, to] = d_normed

    out = [shaped((2, tokens, piece)), shaped((2, tokens, piece)), shaped((2, tokens, 2 * piece))]
    return call(body, out, (place, attended, d_queries, *arrays), 1)


def weight_grads(tiles, both_blocks, known, pairs):
    part = tiles[0].shape[-1]
    given = [k for k, block in enumerate(both_blocks) if block is not None]
    arrays, blocks = pieces_of([both_blocks[k] for k in given])
    width = arrays[0].shape[-1]
    known = known or []

    def body(*refs):
        tile_refs, known_refs = refs[:4], refs[4 : 4 + len(known)]
        block_refs, (query_ref, out_ref) = refs[4 + len(known) : -2], refs[-2:]
        query_grad = known_refs[0][...] if known else jnp.zeros((part, width), F32)
        out_grad = known_refs[1][...] if known else jnp.zeros((width, part), F32)
        for k, ((number, at),) in zip(given, blocks):
            side, far = divmod(k, pairs)
            block = block_refs[number]
            normed, grad = (
                jnp.concatenate([r[far, side, which] for r in tile_refs], axis=0)
                for which in range(2)
            )
            out_grad += contract_first(block[at], grad)
            query_grad += contract_first(normed, block[at + 1])
        query_ref[...] = query_grad
        out_ref[...] = out_grad

    out = [shaped((part, width), F32), shaped((width, part), F32)]
    return call(body, out, (*tiles, *known, *arrays), 0)


def local(
    caption_states,
    caption_lens,
    text_gain,
    text_query,
    text_key,
    text_value,
    text_bias,
    text_out,
    final_gain,
    cross_key,
    cross_value,
    video_states,
    video_counts,
    sample_caption,
    cross_query,
    cross_out,
    out_grad,
):
    column = lax.axis_index("fsdp")
    g = lax.axis_index("grp")
    pairs = lax.axis_size("fsdp") // 2
    z, y = column // 2, column % 2
    place = jnp.stack([z, y, g]).astype(jnp.int32)
    caps_local, cap_len, text_width = caption_states.shape
    tokens, model_width = video_states.shape
    width_local = cross_key.shape[1]
    part = cross_query.shape[0]

    states = caption_states.reshape(cap_len, text_width)
    quarter_rows = cap_len // 4

    first = [fsend(cross_query, 1, 0), fsend(cross_out, 1, 0)]
    side_key, side_value = fsend(cross_key, 0, 1), fsend(cross_value, 0, 1)
    projected = project_text(states, text_gain, (text_query, text_key, text_value))
    kept, away = attend_text(projected, text_bias, text_out, place, caption_lens)
    kept, away = after((kept, away), first, side_key, side_value)
    got = gsend(away, 1)
    ring = [None, jnp.concatenate(first, axis=0)]
    side_first = fsend(jnp.concatenate([cross_query, cross_out, *first], axis=0), 0, 1)
    ring.append(fsend(ring[1], 1, 0))
    sent = (kept[quarter_rows:].astype(F32) + got[quarter_rows:].astype(F32)).astype(BF)
    over_x = gsend(sent, 2)
    normed, mean, inverse, own_tiles, other_tiles = prepare_video(
        after(video_states, sent), out_grad, place, pairs, part
    )
    pieces = encode_rows(
        states, kept, got, after(over_x, normed), final_gain, place, pairs
    )

    mine = jnp.stack([fsend(p, far, 0) if far else p for far, p in enumerate(pieces)])
    mine = after(mine, ring[2])
    over_x = gsend(mine, 2)
    parts = [mine, gsend(mine, 1), over_x, gsend(over_x, 1)]
    current = after(ring[2], mine)
    for far in range(3, pairs):
        current = fsend(current, 1, 0)
        ring.append(current)
    parts[3] = after(parts[3], side_first)
    kv_partial = project_captions(
        parts, cross_key, cross_value, side_key, side_value, place, pairs
    )
    kv_partial = after(tuple(kv_partial), ring[-1])
    kv_sum = kv_partial[0].astype(F32)
    for far in range(1, pairs):
        kv_sum += fsend(kv_partial[far], pairs - far, 0).astype(F32)
    side_later = [fsend(w, 0, 1) for w in ring[2:]]
    other_tiles = fsend(other_tiles, 0, 1)
    kv_sum = after(kv_sum.astype(BF), side_later[0])
    kv_blocks = gather_direct(kv_sum)
    kv_blocks[4] = after(kv_blocks[4], side_later, other_tiles)

    step = part + width_local
    blocks = []
    for far, held in enumerate(ring):
        side, start = (side_first, far * step) if far < 2 else (side_later[far - 2], 0)
        here = ((held, 0), (held, part)) if far else ((cross_query, 0), (cross_out, 0))
        blocks += [here, ((side, start), (side, start + part))]
    queries, d_attended, column_sum = project_rows(
        normed, after(out_grad, kv_blocks[4]), blocks, place, pairs, part
    )

    tiles = jnp.stack([own_tiles, other_tiles], axis=1)
    over_z = [fsend(after(tiles[far], kv_blocks[4]), far, 0) for far in range(1, pairs)]
    over_z = [tiles[0]] + over_z

    both, attended, d_queries, row_sums, slots = attend(
        queries,
        d_attended,
        column_sum,
        kv_blocks,
        place,
        video_counts,
        sample_caption,
        caption_lens,
        pairs,
    )
    slots, both, row_sums, over_z = after((slots, both, row_sums, over_z))
    tiles = jnp.stack(over_z)

    def chain(blocks, steps):
        for _ in range(steps):
            blocks.append(fsend(blocks[-1], 1, 0))
        return blocks

    def joined(two):
        return jnp.stack(two).reshape(-1, tokens, width_local)

    side_slots = fsend(slots, 0, 1)
    side_own = fsend(both, 0, 1)
    late = chain([both], 2)
    sums_core = gsend(row_sums, 1)
    attended, tiles = after((attended, tiles), sums_core)
    tiles_x = gsend(tiles, 2)
    own, far_piece, away = project_back(attended, d_queries, blocks, place, pairs, part)
    two = joined(late[1:3])
    stage = (side_slots, side_own, late, sums_core, tiles_x, two, away)
    side_slots, side_own, late, sums_core, tiles_x, two, away = after(stage)

    side_two = fsend(two, 0, 1)
    late = chain(list(late), pairs - 3)
    row_sums = row_sums + sums_core
    sums_x = gsend(row_sums, 2)
    got = gsend(away, 1)
    tiles_core = gsend(tiles, 1)
    width = model_width // 4
    sent = (far_piece.astype(F32) + got[:, :, width:].astype(F32)).astype(BF)
    far_sum = gsend(sent, 2)
    tiles = [tiles, tiles_core, tiles_x, gsend(tiles_x, 1)]
    terms = caption_terms(
        slots, side_slots, place, video_counts, sample_caption, tokens, pairs
    )
    kv_parts = [fsend(terms[far], far, 0) for far in range(1, pairs, 2)]
    stage = (side_two, late, sums_x, sent, tiles, kv_parts, terms)
    side_two, late, sums_x, _, tiles, kv_parts, terms = after(stage)

    here = [((block, 0),) for block in late]
    there = [((side_own, 0),), ((side_two, 0),), ((side_two, 2),)]
    there += [((fsend(block, 0, 1), 0),) for block in late[3:]]
    known = weight_grads(tiles, here + there[:3], None, pairs)
    total = own.astype(F32) + got[:, :, :width].astype(F32) + far_sum.astype(F32)
    row_sums = (row_sums + sums_x) / model_width
    video = quarter(video_states, g, 1).astype(F32)
    updated = (video + total[0]).astype(BF)
    video_hat = (video - mean) * inverse
    input_grad = (
        quarter(out_grad, g, 1).astype(F32)
        + inverse * (total[1] - row_sums[:, 0:1] - video_hat * row_sums[:, 1:2])
    ).astype(BF)
    kv_parts += [fsend(terms[far], far, 0) for far in range(2, pairs, 2)]
    kv_grads = (terms[0] + sum(p.astype(F32) for p in kv_parts)).astype(BF)[None]
    key_grad = kv_grads[:, :, :width_local]
    value_grad = kv_grads[:, :, width_local:]
    query_grad, out_weight_grad = weight_grads(
        tiles, [None] * (pairs + 3) + there[3:], known, pairs
    )
    return (updated, input_grad, query_grad, out_weight_grad, key_grad, value_grad)


def local_of(*arrays):
    whole_tiles = arrays[14].shape[0] % 128 == 0 and arrays[0].shape[0] == 1
    return local(*arrays) if whole_tiles else local_general(*arrays)


def solution(mesh):
    in_specs = (
        P("fsdp", None, None),
        P(),
        P(),
        P(None, "grp"),
        P(None, "grp"),
        P(None, "grp"),
        P("grp", None, None),
        P("grp", None),
        P(),
        P("fsdp", "grp"),
        P("fsdp", "grp"),
        P("fsdp", None),
        P(),
        P(),
        P("fsdp", "grp"),
        P("grp", "fsdp"),
        P("fsdp", None),
    )
    out_specs = (
        P("fsdp", "grp"),
        P("fsdp", "grp"),
        P("fsdp", "grp"),
        P("grp", "fsdp"),
        P("fsdp", None, "grp"),
        P("fsdp", None, "grp"),
    )
    return jax.shard_map(
        local_of, mesh=mesh, in_specs=in_specs, out_specs=out_specs, check_vma=False
    )
```

```python
import math

import jax
import jax.numpy as jnp
from jax import lax
from jax.experimental import pallas as pl
from jax.experimental.pallas import tpu as pltpu
from jax.sharding import PartitionSpec as P

HEAD_SIZE = 128
BF = jnp.bfloat16
F32 = jnp.float32
SLOTS = 3
VMEM_BYTES = 60 * 1024 * 1024
SPARE_BYTES = 8 * 1024 * 1024
SMALL = pl.CostEstimate(flops=1, bytes_accessed=1, transcendentals=0)


def rms_scale(values, gain):
    mean_square = jnp.mean(values * values, axis=-1, keepdims=True)
    return values * lax.rsqrt(mean_square + 1e-06) * gain


def mm(left, right):
    return jnp.dot(left, right, preferred_element_type=F32)


def contract_last(left, right):
    return lax.dot_general(left, right, (((1,), (1,)), ((), ())), preferred_element_type=F32)


def contract_first(left, right):
    return lax.dot_general(left, right, (((0,), (0,)), ((), ())), preferred_element_type=F32)


def fsend(block, far, side):
    size = lax.axis_size("fsdp")
    pairs = size // 2
    perm = [(s, ((s // 2 + far) % pairs) * 2 + ((s % 2) ^ side)) for s in range(size)]
    return lax.ppermute(block, "fsdp", perm)


def gsend(block, flip):
    return lax.ppermute(block, "grp", [(s, s ^ flip) for s in range(lax.axis_size("grp"))])


def gather_ring(block):
    blocks = []
    current = block
    for far in range(lax.axis_size("fsdp") // 2):
        if far:
            current = fsend(current, 1, 0)
        blocks += [current, fsend(current, 0, 1)]
    return blocks


def gather_direct(block):
    blocks = []
    for far in range(lax.axis_size("fsdp") // 2):
        current = fsend(block, far, 0) if far else block
        blocks += [current, fsend(current, 0, 1)]
    return blocks


def quarter(array, index, axis=0):
    size = array.shape[axis] // 4
    return lax.dynamic_slice_in_dim(array, index * size, size, axis)


def grp_scatter(partial, g, axis):
    away = [quarter(partial, g ^ 1, axis), quarter(partial, g ^ 3, axis)]
    kept = [quarter(partial, g, axis), quarter(partial, g ^ 2, axis)]
    got = gsend(jnp.stack(away).astype(BF), 1)
    far = gsend((kept[1] + got[1].astype(F32)).astype(BF), 2)
    return kept[0] + got[0].astype(F32) + far.astype(F32)


def local_general(
    caption_states,
    caption_lens,
    text_gain,
    text_query,
    text_key,
    text_value,
    text_bias,
    text_out,
    final_gain,
    cross_key,
    cross_value,
    video_states,
    video_counts,
    sample_caption,
    cross_query,
    cross_out,
    out_grad,
):
    column = lax.axis_index("fsdp")
    g = lax.axis_index("grp")
    fsdp = lax.axis_size("fsdp")
    pairs = fsdp // 2
    z, y = column // 2, column % 2
    caps_local, cap_len, text_width = caption_states.shape
    tokens, model_width = video_states.shape
    width_local = cross_key.shape[1]
    cross_local = width_local // HEAD_SIZE
    query_rows = cross_query.shape[0]

    def source(far, side):
        return ((z - far) % pairs) * 2 + (y ^ side)

    def target(far, side):
        return ((z + far) % pairs) * 2 + (y ^ side)

    query_blocks = gather_ring(cross_query)
    out_blocks = gather_ring(cross_out)
    full_query = jnp.zeros((model_width, width_local), BF)
    full_out = jnp.zeros((width_local, model_width), BF)
    for far in range(pairs):
        for side in range(2):
            start = source(far, side) * query_rows
            full_query = lax.dynamic_update_slice(
                full_query, query_blocks[2 * far + side], (start, jnp.int32(0))
            )
            full_out = lax.dynamic_update_slice(
                full_out, out_blocks[2 * far + side], (jnp.int32(0), start)
            )

    own_kv = jnp.concatenate([cross_key, cross_value], axis=1)
    other_kv = fsend(own_kv, 0, 1)
    pair_kv = jnp.concatenate(
        [jnp.where(y == 0, own_kv, other_kv), jnp.where(y == 0, other_kv, own_kv)], axis=0
    )

    local_lens = lax.dynamic_slice_in_dim(caption_lens, column * caps_local, caps_local)
    flat_states = caption_states.reshape(caps_local * cap_len, text_width).astype(F32)
    text_normed = rms_scale(flat_states, text_gain).astype(BF)
    local_heads = text_bias.shape[0]
    head_width = text_query.shape[1] // local_heads

    def heads_of(weight):
        return mm(text_normed, weight).astype(BF).reshape(
            caps_local, cap_len, local_heads, head_width
        )

    text_queries = heads_of(text_query)
    text_keys = heads_of(text_key)
    text_values = heads_of(text_value)
    text_scores = (
        jnp.einsum("cihd,cjhd->chij", text_queries, text_keys, preferred_element_type=F32)
        + text_bias[None]
    )
    key_valid = jnp.arange(cap_len, dtype=jnp.int32)[None, :] < local_lens[:, None]
    exp_scores = jnp.where(key_valid[:, None, None, :], jnp.exp(text_scores), 0.0)
    text_weights = (exp_scores / jnp.sum(exp_scores, axis=-1, keepdims=True)).astype(BF)
    text_mixed = jnp.einsum(
        "chij,cjhd->cihd", text_weights, text_values, preferred_element_type=F32
    )
    text_mixed = text_mixed.astype(BF).reshape(caps_local * cap_len, local_heads * head_width)
    partial_text = mm(text_mixed, text_out)
    text_rows = grp_scatter(partial_text, g, 0)
    encoded = rms_scale(quarter(flat_states, g) + text_rows, final_gain).astype(BF)

    part = text_width // pairs
    pieces = [
        lax.dynamic_slice_in_dim(encoded, ((z + far) % pairs) * part, part, 1)
        for far in range(pairs)
    ]
    mine = jnp.stack([fsend(p, far, 0) if far else p for far, p in enumerate(pieces)])
    over_x = jnp.concatenate([mine[:, None], gsend(mine, 2)[:, None]], axis=1)
    over_core = jnp.stack([over_x, gsend(over_x, 1)], axis=2)
    kv_partial = mm(over_core.reshape(-1, part), pair_kv).reshape(pairs, cap_len, 2 * width_local)
    kv_sum = kv_partial[0]
    for far in range(1, pairs):
        kv_sum += fsend(kv_partial[far].astype(BF), pairs - far, 0).astype(F32)
    kv_rows = kv_sum.astype(BF).reshape(4, cap_len // 4, 2 * width_local)
    order = jnp.arange(4, dtype=jnp.int32) ^ g
    cap_kv = jnp.concatenate(
        [lax.dynamic_slice_in_dim(kv_rows, order[k], 1, 0) for k in range(4)], axis=0
    ).reshape(cap_len, 2 * width_local)
    all_kv = jnp.stack(gather_direct(cap_kv))

    video = video_states.astype(F32)
    center = video - jnp.mean(video, axis=-1, keepdims=True)
    inverse = lax.rsqrt(jnp.mean(center * center, axis=-1, keepdims=True) + 1e-06)
    video_hat = center * inverse
    video_normed = video_hat.astype(BF)

    both = jnp.stack([quarter(video_normed, g), quarter(out_grad, g)])
    tiles = []
    for far in range(pairs):
        for side in range(2):
            tile = lax.dynamic_slice_in_dim(both, target(far, side) * query_rows, query_rows, 2)
            tiles.append(fsend(tile, far, side) if far or side else tile)
    tiles = jnp.stack(tiles)
    tiles_x = jnp.stack([tiles, gsend(tiles, 2)], axis=2)
    tiles_all = jnp.stack([tiles_x, gsend(tiles_x, 1)], axis=3)
    normed_tile = tiles_all[:, 0].reshape(-1, query_rows)
    grad_tile = tiles_all[:, 1].reshape(-1, query_rows)

    caption_total = all_kv.shape[0]
    positions = column * tokens + jnp.arange(tokens, dtype=jnp.int32)
    sample_end = jnp.cumsum(video_counts)
    token_sample = jnp.sum((sample_end[None, :] <= positions[:, None]).astype(jnp.int32), axis=1)
    slot_count = 3
    slot_sample = token_sample[0] + jnp.arange(slot_count, dtype=jnp.int32)
    slot_valid = slot_sample < caption_total
    slot_clipped = jnp.minimum(slot_sample, caption_total - 1)
    numbers = jnp.arange(caption_total, dtype=jnp.int32)
    slot_pick = slot_clipped[:, None] == numbers[None, :]
    slot_caption = jnp.sum(jnp.where(slot_pick, sample_caption[None, :], 0), axis=1)
    caption_pick = slot_caption[:, None] == numbers[None, :]
    slot_lens = jnp.sum(jnp.where(caption_pick, caption_lens[None, :], 0), axis=1)
    slot_member = token_sample[None, :] == slot_sample[:, None]
    member_float = slot_member.astype(F32)
    member_half = slot_member.astype(BF)
    slot_entry = ((z - slot_caption // 2) % pairs) * 2 + ((slot_caption % 2) ^ y)
    slot_kv = jnp.take(all_kv, slot_entry, axis=0)
    slot_keys = slot_kv[..., :width_local].reshape(slot_count, cap_len, cross_local, HEAD_SIZE)
    slot_values = slot_kv[..., width_local:].reshape(slot_count, cap_len, cross_local, HEAD_SIZE)
    token_lens = jnp.sum(jnp.where(slot_member, slot_lens[:, None], 0), axis=0)

    query_sum = mm(video_normed, full_query)
    queries = query_sum.astype(BF)
    d_attended = contract_last(out_grad, full_out).astype(BF).reshape(
        tokens, cross_local, HEAD_SIZE
    )
    score_scale = 1.0 / math.sqrt(HEAD_SIZE)
    query_heads = queries.reshape(tokens, cross_local, HEAD_SIZE)
    slot_scores = jnp.einsum("thd,kjhd->kthj", query_heads, slot_keys, preferred_element_type=F32)
    scores = jnp.sum(member_float[:, :, None, None] * slot_scores, axis=0) * score_scale
    token_valid = (jnp.arange(cap_len, dtype=jnp.int32)[None, :] < token_lens[:, None])[:, None, :]
    exp_video = jnp.where(token_valid, jnp.exp(scores), 0.0)
    weights = exp_video / jnp.sum(exp_video, axis=-1, keepdims=True)
    probs = weights.astype(BF)
    masked_probs = member_half[:, :, None, None] * probs[None]
    attended = jnp.einsum("kthj,kjhd->thd", masked_probs, slot_values, preferred_element_type=F32)
    attended = attended.astype(BF).reshape(tokens, width_local)

    def reorder(array):
        return jnp.concatenate([quarter(array, order[k]) for k in range(4)], axis=0)

    all_attended = jnp.concatenate(gather_direct(reorder(attended)), axis=0)
    out_weight_grad = contract_first(all_attended, grad_tile)

    out_share = grp_scatter(mm(attended, full_out), g, 1)
    updated = (quarter(video, g, 1) + out_share).astype(BF)

    slot_dprobs = jnp.einsum("thd,kjhd->kthj", d_attended, slot_values, preferred_element_type=F32)
    d_probs = jnp.sum(member_float[:, :, None, None] * slot_dprobs, axis=0)
    d_scores = (
        weights * (d_probs - jnp.sum(weights * d_probs, axis=-1, keepdims=True)) * score_scale
    ).astype(BF)
    masked_scores = member_half[:, :, None, None] * d_scores[None]
    d_queries = jnp.einsum("kthj,kjhd->thd", masked_scores, slot_keys, preferred_element_type=F32)
    d_queries = d_queries.astype(BF).reshape(tokens, width_local)
    all_d_queries = jnp.concatenate(gather_direct(reorder(d_queries)), axis=0)
    query_grad = contract_first(normed_tile, all_d_queries)

    key_slots = jnp.einsum("kthj,thd->kjhd", masked_scores, query_heads, preferred_element_type=F32)
    value_slots = jnp.einsum("kthj,thd->kjhd", masked_probs, d_attended, preferred_element_type=F32)
    slot_terms = jnp.concatenate(
        [
            key_slots.reshape(slot_count, cap_len, width_local),
            value_slots.reshape(slot_count, cap_len, width_local),
        ],
        axis=-1,
    )

    def caption_terms(far, side):
        picked = (slot_caption == target(far, side)) & slot_valid
        return jnp.sum(jnp.where(picked[:, None, None], slot_terms, 0.0), axis=0)

    away = jnp.stack([caption_terms(far, 1).astype(BF) for far in range(pairs)])
    got = fsend(away, 0, 1).astype(F32)
    kv_grads = caption_terms(0, 0) + got[0]
    for far in range(1, pairs):
        kv_grads += fsend((caption_terms(far, 0) + got[far]).astype(BF), far, 0).astype(F32)
    kv_grads = kv_grads.astype(BF)[None]
    key_grad = kv_grads[:, :, :width_local]
    value_grad = kv_grads[:, :, width_local:]

    d_wide = d_queries.astype(F32)
    column_sum = jnp.sum(full_query.astype(F32), axis=0)
    row_sums = jnp.stack(
        [jnp.sum(d_wide * column_sum, axis=-1), jnp.sum(d_wide * query_sum, axis=-1)]
    )
    row_sums = row_sums + gsend(row_sums, 1)
    row_sums = (row_sums + gsend(row_sums, 2)) / model_width
    d_share = grp_scatter(contract_last(d_queries, full_query), g, 1)
    input_grad = (
        quarter(out_grad, g, 1).astype(F32)
        + inverse
        * (d_share - row_sums[0][:, None] - quarter(video_hat, g, 1) * row_sums[1][:, None])
    ).astype(BF)
    return (updated, input_grad, query_grad, out_weight_grad, key_grad, value_grad)


def after(value, *others):
    return lax.optimization_barrier((value, *others))[0]


def call(body, out_shape, operands, scalars, scratch=()):
    specs = [pl.BlockSpec(memory_space=pltpu.SMEM)] * scalars
    specs += [pl.BlockSpec(memory_space=pltpu.VMEM)] * (len(operands) - scalars)
    held = (*operands[scalars:], *jax.tree.leaves(out_shape), *scratch)
    held_bytes = sum(math.prod(a.shape) * jnp.dtype(a.dtype).itemsize for a in held)
    return pl.pallas_call(
        body,
        out_shape=out_shape,
        in_specs=specs,
        out_specs=jax.tree.map(lambda _: pl.BlockSpec(memory_space=pltpu.VMEM), out_shape),
        scratch_shapes=list(scratch),
        compiler_params=pltpu.CompilerParams(vmem_limit_bytes=held_bytes + SPARE_BYTES),
        cost_estimate=SMALL,
    )(*operands)


def shaped(shape, dtype=BF):
    return jax.ShapeDtypeStruct(shape, dtype)


def aligned(start, unit):
    return pl.multiple_of(start, unit)


def project_text(states, gain, weights, steps=8):
    rows, depth = states.shape
    width = weights[0].shape[1]
    chunk = depth // steps

    def body(states_ref, gain_ref, wq_ref, wk_ref, wv_ref, out_ref, square_ref, total_ref):
        step = pl.program_id(0)

        @pl.when(step == 0)
        def _():
            square_ref[...] = jnp.zeros_like(square_ref)
            total_ref[...] = jnp.zeros_like(total_ref)

        values = states_ref[...].astype(F32)
        square_ref[...] += jnp.sum(values * values, axis=-1, keepdims=True)
        here = (values * gain_ref[...]).astype(BF)
        for k, weight_ref in enumerate((wq_ref, wk_ref, wv_ref)):
            total_ref[:, k * width : (k + 1) * width] += mm(here, weight_ref[...])

        @pl.when(step == steps - 1)
        def _():
            scale = lax.rsqrt(square_ref[...] / depth + 1e-06)
            out_ref[...] = (total_ref[...] * scale).astype(BF)

    return pl.pallas_call(
        body,
        grid=(steps,),
        out_shape=shaped((rows, 3 * width)),
        in_specs=[
            pl.BlockSpec((rows, chunk), lambda i: (0, i)),
            pl.BlockSpec((1, chunk), lambda i: (0, i)),
        ]
        + [pl.BlockSpec((chunk, width), lambda i: (i, 0))] * 3,
        out_specs=pl.BlockSpec((rows, 3 * width), lambda i: (0, 0)),
        scratch_shapes=[pltpu.VMEM((rows, 1), F32), pltpu.VMEM((rows, 3 * width), F32)],
        compiler_params=pltpu.CompilerParams(vmem_limit_bytes=VMEM_BYTES),
        cost_estimate=SMALL,
    )(states, gain.reshape(1, -1), *weights)


def attend_text(projected, bias, text_out, place, lens, steps=4):
    rows = projected.shape[0]
    heads = bias.shape[0]
    inner, depth = text_out.shape
    size = inner // heads
    quarter_rows = rows // 4
    chunk = depth // steps

    def body(place_ref, len_ref, qkv_ref, bias_ref, out_ref, kept_ref, away_ref, held_ref, mixed_ref):
        @pl.when(pl.program_id(0) == 0)
        def _():
            g = place_ref[2]
            length = len_ref[place_ref[0] * 2 + place_ref[1]]
            live = lax.broadcasted_iota(jnp.int32, (rows, rows), 1) < length
            for head in range(heads):
                query, key, value = (
                    qkv_ref[:, k * inner + head * size : k * inner + (head + 1) * size]
                    for k in range(3)
                )
                grown = jnp.where(live, jnp.exp(contract_last(query, key) + bias_ref[head]), 0.0)
                weights = grown * (1.0 / jnp.sum(grown, axis=-1, keepdims=True))
                held_ref[:, head * size : (head + 1) * size] = mm(weights.astype(BF), value).astype(BF)
            for k, to in ((0, 0), (2, 1), (1, 2), (3, 3)):
                rows_from = pl.ds(aligned((g ^ k) * quarter_rows, quarter_rows), quarter_rows)
                mixed_ref[to * quarter_rows : (to + 1) * quarter_rows, :] = held_ref[rows_from, :]

        product = mm(mixed_ref[...], out_ref[...]).astype(BF)
        kept_ref[...] = product[: rows // 2]
        away_ref[...] = product[rows // 2 :]

    whole = lambda shape: pl.BlockSpec(shape, lambda i: (0,) * len(shape))
    return pl.pallas_call(
        body,
        grid=(steps,),
        out_shape=[shaped((rows // 2, depth))] * 2,
        in_specs=[pl.BlockSpec(memory_space=pltpu.SMEM)] * 2
        + [whole(projected.shape), whole(bias.shape)]
        + [pl.BlockSpec((inner, chunk), lambda i: (0, i))],
        out_specs=[pl.BlockSpec((rows // 2, chunk), lambda i: (0, i))] * 2,
        scratch_shapes=[pltpu.VMEM((rows, inner), BF), pltpu.VMEM((rows, inner), BF)],
        compiler_params=pltpu.CompilerParams(vmem_limit_bytes=VMEM_BYTES),
        cost_estimate=SMALL,
    )(place, lens, projected, bias, text_out)


def encode_rows(states, kept, got, far, gain, place, pairs):
    quarter_rows = states.shape[0] // 4
    width = states.shape[1]
    depth = width // pairs

    def body(place_ref, states_ref, kept_ref, got_ref, far_ref, gain_ref, *refs):
        piece_refs, encoded_ref = refs[:-1], refs[-1]
        z, g = place_ref[0], place_ref[2]
        mine = pl.ds(aligned(g * quarter_rows, quarter_rows), quarter_rows)
        total = states_ref[mine, :].astype(F32) + far_ref[...].astype(F32)
        total += kept_ref[:quarter_rows, :].astype(F32) + got_ref[:quarter_rows, :].astype(F32)
        encoded_ref[...] = rms_scale(total, gain_ref[...]).astype(BF)
        for far_by, piece in enumerate(piece_refs):
            to = lax.rem(z + far_by, pairs)
            piece[...] = encoded_ref[:, pl.ds(aligned(to * depth, 128), depth)]

    out = [shaped((quarter_rows, depth))] * pairs
    operands = (place, states, kept, got, far, gain.reshape(1, -1))
    return call(body, out, operands, 1, [pltpu.VMEM((quarter_rows, width), BF)])


def pieces_of(pairs_of_blocks):
    arrays, listed = [], []
    for entry in pairs_of_blocks:
        numbers = []
        for array, start in entry:
            if not any(array is held for held in arrays):
                arrays.append(array)
            numbers.append((next(k for k, held in enumerate(arrays) if held is array), start))
        listed.append(numbers)
    return arrays, listed


def prepare_video(video_states, out_grad, place, pairs, part):
    tokens, model_width = video_states.shape
    rows = tokens // 4

    def body(place_ref, video_ref, grad_ref, normed_ref, mean_ref, inverse_ref, *tile_refs):
        @pl.loop(0, tokens // 32)
        def _(step):
            here = pl.ds(aligned(step * 32, 32), 32)
            values = video_ref[here, :].astype(F32)
            mean = jnp.mean(values, axis=-1, keepdims=True)
            center = values - mean
            inverse = lax.rsqrt(jnp.mean(center * center, axis=-1, keepdims=True) + 1e-06)
            normed_ref[here, :] = (center * inverse).astype(BF)
            mean_ref[here, :] = mean
            inverse_ref[here, :] = inverse

        z, y, g = place_ref[0], place_ref[1], place_ref[2]
        mine = pl.ds(aligned(g * rows, rows), rows)
        for far in range(pairs):
            for side in range(2):
                to = lax.rem(z + far, pairs) * 2 + (y ^ side)
                columns = pl.ds(aligned(to * part, 128), part)
                tile_refs[side][far, 0] = normed_ref[mine, columns]
                tile_refs[side][far, 1] = grad_ref[mine, columns]

    out = [shaped((tokens, model_width)), shaped((tokens, 1), F32), shaped((tokens, 1), F32)]
    out += [shaped((pairs, 2, rows, part))] * 2
    return call(body, out, (place, video_states, out_grad), 1)


def project_rows(normed, out_grad, blocks, place, pairs, part):
    tokens = normed.shape[0]
    arrays, blocks = pieces_of(blocks)
    width = arrays[0].shape[1]

    def body(place_ref, normed_ref, grad_ref, *refs):
        block_refs, (query_ref, d_ref, sum_ref) = refs[:-3], refs[-3:]
        z, y = place_ref[0], place_ref[1]
        query = jnp.zeros((tokens, width), F32)
        d_attended = jnp.zeros((tokens, width), F32)
        total = jnp.zeros((1, width), F32)
        for far in range(pairs):
            for side in range(2):
                (of_query, query_at), (of_out, out_at) = blocks[2 * far + side]
                origin = lax.rem(z - far + pairs, pairs) * 2 + (y ^ side)
                columns = pl.ds(aligned(origin * part, 128), part)
                weight = block_refs[of_query][query_at : query_at + part, :]
                out_weight = block_refs[of_out][out_at : out_at + width, :]
                query += mm(normed_ref[:, columns], weight)
                d_attended += contract_last(grad_ref[:, columns], out_weight)
                total += jnp.sum(weight.astype(F32), axis=0, keepdims=True)
        query_ref[...] = query.astype(BF)
        d_ref[...] = d_attended.astype(BF)
        sum_ref[...] = total

    out = [shaped((tokens, width)), shaped((tokens, width)), shaped((1, width), F32)]
    return call(body, out, (place, normed, out_grad, *arrays), 1)


def project_captions(parts, own_key, own_value, side_both, place, pairs):
    quarter_rows, depth = parts[0].shape[1:]
    half = depth // 2
    width = own_key.shape[1]

    def body(place_ref, *refs):
        part_refs = refs[:4]
        key_ref, value_ref, side_ref = refs[4:7]
        out_refs = refs[7:]
        y = place_ref[1]
        mine = pl.ds(aligned(y * half, 128), half)
        theirs = pl.ds(aligned((1 - y) * half, 128), half)
        own = jnp.concatenate([r[far, :, mine] for far in range(pairs) for r in part_refs], 0)
        other = jnp.concatenate([r[far, :, theirs] for far in range(pairs) for r in part_refs], 0)
        keys = mm(own, key_ref[...]) + mm(other, side_ref[:half, :])
        values = mm(own, value_ref[...]) + mm(other, side_ref[half:, :])
        for far in range(pairs):
            rows = slice(far * 4 * quarter_rows, (far + 1) * 4 * quarter_rows)
            out_refs[far][:, :width] = keys[rows].astype(BF)
            out_refs[far][:, width:] = values[rows].astype(BF)

    out = [shaped((4 * quarter_rows, 2 * width))] * pairs
    operands = (place, *parts, own_key, own_value, side_both)
    return call(body, out, operands, 1)


def slots_of(count_ref, caption_ref, base, captions):
    def find(sample, carry):
        total, first, start = carry
        total = total + count_ref[sample]
        past = total <= base
        return total, first + past.astype(jnp.int32), jnp.where(past, total, start)

    zero = jnp.int32(0)
    _, first, start = lax.fori_loop(0, captions, find, (zero, zero, zero))
    found, edge = [], start - base
    for slot in range(SLOTS):
        valid = first + slot < captions
        sample = jnp.minimum(first + slot, captions - 1)
        end = edge + jnp.where(valid, count_ref[sample], 0)
        found.append((edge, end, caption_ref[sample], valid))
        edge = end
    return found


def attend(queries, d_attended, column_sum, kv_blocks, place, counts, sample_caption, lens, pairs):
    tokens, width = queries.shape
    cap_len = kv_blocks[0].shape[0]
    heads = width // HEAD_SIZE
    captions = counts.shape[0]
    keys_wide = SLOTS * cap_len
    cap_quarter, row_quarter = cap_len // 4, tokens // 4
    scale = 1.0 / math.sqrt(HEAD_SIZE)

    def body(place_ref, count_ref, caption_ref, len_ref, q_ref, da_ref, sum_ref, *refs):
        block_refs = refs[: len(kv_blocks)]
        both_ref, att_ref, dq_ref, rows_ref, slot_ref, kv_ref = refs[len(kv_blocks) :]
        z, y, g = place_ref[0], place_ref[1], place_ref[2]
        low, high, length = [], [], []
        found = slots_of(count_ref, caption_ref, (z * 2 + y) * tokens, captions)
        for slot, (start, end, caption, _) in enumerate(found):
            low.append(start)
            high.append(end)
            length.append(len_ref[caption])
            entry = lax.rem(z - caption // 2 + pairs, pairs) * 2 + (lax.rem(caption, 2) ^ y)
            for number, block in enumerate(block_refs):

                @pl.when(entry == number)
                def _(slot=slot, block=block):
                    kv_ref[slot * cap_len : (slot + 1) * cap_len, :] = block[...]

        token = lax.broadcasted_iota(jnp.int32, (tokens, keys_wide), 0)
        column = lax.broadcasted_iota(jnp.int32, (tokens, keys_wide), 1)
        slot_of = column // cap_len
        inside = column % cap_len
        key = ((inside // cap_quarter) ^ g) * cap_quarter + inside % cap_quarter

        def of_slot(values):
            return jnp.where(slot_of == 0, values[0], jnp.where(slot_of == 1, values[1], values[2]))

        live = (token >= of_slot(low)) & (token < of_slot(high)) & (key < of_slot(length))
        first_sum = jnp.zeros((tokens, 1), F32)
        second_sum = jnp.zeros((tokens, 1), F32)
        for head in range(heads):
            at = slice(head * HEAD_SIZE, (head + 1) * HEAD_SIZE)
            at_value = slice(width + head * HEAD_SIZE, width + (head + 1) * HEAD_SIZE)
            query, d_att = q_ref[:, at], da_ref[:, at]
            keys, values = kv_ref[:, at], kv_ref[:, at_value]
            grown = jnp.where(live, jnp.exp(contract_last(query, keys) * scale), 0.0)
            weights = grown * (1.0 / jnp.sum(grown, axis=-1, keepdims=True))
            probs = weights.astype(BF)
            d_probs = contract_last(d_att, values)
            mixed = jnp.sum(weights * d_probs, axis=-1, keepdims=True)
            d_scores = (weights * (d_probs - mixed) * scale).astype(BF)
            att_ref[:, at] = mm(probs, values).astype(BF)
            d_query = mm(d_scores, keys).astype(BF)
            dq_ref[:, at] = d_query
            d_wide = d_query.astype(F32)
            first_sum += jnp.sum(d_wide * sum_ref[:, at], axis=-1, keepdims=True)
            second_sum += jnp.sum(d_wide * query.astype(F32), axis=-1, keepdims=True)
            key_grad = contract_first(d_scores, query).astype(BF)
            value_grad = contract_first(probs, d_att).astype(BF)
            for slot in range(SLOTS):
                for part in range(4):
                    held = slice(
                        slot * cap_len + part * cap_quarter, slot * cap_len + (part + 1) * cap_quarter
                    )
                    to = pl.ds(aligned((part ^ g) * cap_quarter, cap_quarter), cap_quarter)
                    slot_ref[slot, to, at] = key_grad[held]
                    slot_ref[slot, to, at_value] = value_grad[held]

        rows_ref[:, 0:1] = first_sum
        rows_ref[:, 1:2] = second_sum
        for part in range(4):
            rows = pl.ds(aligned((part ^ g) * row_quarter, row_quarter), row_quarter)
            to = slice(part * row_quarter, (part + 1) * row_quarter)
            both_ref[0, to, :] = att_ref[rows, :]
            both_ref[1, to, :] = dq_ref[rows, :]

    out = [
        shaped((2, tokens, width)),
        shaped((tokens, width)),
        shaped((tokens, width)),
        shaped((tokens, 2), F32),
        shaped((SLOTS, cap_len, 2 * width)),
    ]
    operands = (place, counts, sample_caption, lens, queries, d_attended, column_sum, *kv_blocks)
    scratch = [pltpu.VMEM((keys_wide, 2 * width), BF)]
    return call(body, out, operands, 4, scratch)


def caption_terms(slots, side_slots, place, counts, sample_caption, tokens, pairs):
    captions = counts.shape[0]
    shape = slots.shape[1:]

    def body(place_ref, count_ref, caption_ref, own_ref, side_ref, *refs):
        term_refs, total_ref = refs[:-1], refs[-1]
        z, y = place_ref[0], place_ref[1]
        total_ref[...] = jnp.zeros_like(total_ref)
        for side, slot_ref in enumerate((own_ref, side_ref)):
            base = (z * 2 + (y ^ side)) * tokens
            for slot, (_, _, caption, valid) in enumerate(
                slots_of(count_ref, caption_ref, base, captions)
            ):
                far = lax.rem(caption // 2 - z + pairs, pairs)

                @pl.when(valid & (lax.rem(caption, 2) == y))
                def _(slot=slot, far=far, slot_ref=slot_ref):
                    total_ref[far] += slot_ref[slot].astype(F32)

        for far, term_ref in enumerate(term_refs):
            term_ref[...] = total_ref[far].astype(term_ref.dtype)

    out = [shaped(shape, F32 if far == 0 else BF) for far in range(pairs)]
    operands = (place, counts, sample_caption, slots, side_slots)
    return call(body, out, operands, 3, [pltpu.VMEM((pairs, *shape), F32)])


def project_back(attended, d_queries, blocks, place, pairs, part):
    tokens, width = attended.shape
    arrays, blocks = pieces_of(blocks)
    model_width = 2 * pairs * part
    per_piece = 2 * pairs // 4
    piece = model_width // 4

    def body(place_ref, att_ref, dq_ref, *refs):
        block_refs = refs[: len(arrays)]
        own_ref, far_ref, away_ref = refs[len(arrays) :]
        z, y, g = place_ref[0], place_ref[1], place_ref[2]
        att, d_query = att_ref[...], dq_ref[...]
        for far in range(pairs):
            for side in range(2):
                (of_query, query_at), (of_out, out_at) = blocks[2 * far + side]
                weight = block_refs[of_query][query_at : query_at + part, :]
                out_weight = block_refs[of_out][out_at : out_at + width, :]
                origin = lax.rem(z - far + pairs, pairs) * 2 + (y ^ side)
                flip = (origin // per_piece) ^ g
                start = lax.rem(origin, per_piece) * part
                columns = pl.ds(aligned(start, 128), part)
                beyond = pl.ds(aligned(start + piece, 128), part)
                added = mm(att, out_weight).astype(BF)
                d_normed = contract_last(d_query, weight).astype(BF)
                places = ((own_ref, columns), (away_ref, columns), (far_ref, columns), (away_ref, beyond))
                for number, (target_ref, to) in enumerate(places):

                    @pl.when(flip == number)
                    def _(target_ref=target_ref, to=to, added=added, d_normed=d_normed):
                        target_ref[0, :, to] = added
                        target_ref[1, :, to] = d_normed

    out = [shaped((2, tokens, piece)), shaped((2, tokens, piece)), shaped((2, tokens, 2 * piece))]
    return call(body, out, (place, attended, d_queries, *arrays), 1)


def weight_grads(tiles, both_blocks, known, pairs):
    part = tiles[0].shape[-1]
    given = [k for k, block in enumerate(both_blocks) if block is not None]
    arrays, blocks = pieces_of([both_blocks[k] for k in given])
    width = arrays[0].shape[-1]
    known = known or []

    def body(*refs):
        tile_refs, known_refs = refs[:4], refs[4 : 4 + len(known)]
        block_refs, (query_ref, out_ref) = refs[4 + len(known) : -2], refs[-2:]
        query_grad = known_refs[0][...] if known else jnp.zeros((part, width), F32)
        out_grad = known_refs[1][...] if known else jnp.zeros((width, part), F32)
        for k, ((number, at),) in zip(given, blocks):
            side, far = divmod(k, pairs)
            block = block_refs[number]
            normed, grad = (
                jnp.concatenate([r[far, side, which] for r in tile_refs], axis=0)
                for which in range(2)
            )
            out_grad += contract_first(block[at], grad)
            query_grad += contract_first(normed, block[at + 1])
        query_ref[...] = query_grad
        out_ref[...] = out_grad

    out = [shaped((part, width), F32), shaped((width, part), F32)]
    return call(body, out, (*tiles, *known, *arrays), 0)


def local(
    caption_states,
    caption_lens,
    text_gain,
    text_query,
    text_key,
    text_value,
    text_bias,
    text_out,
    final_gain,
    cross_key,
    cross_value,
    video_states,
    video_counts,
    sample_caption,
    cross_query,
    cross_out,
    out_grad,
):
    column = lax.axis_index("fsdp")
    g = lax.axis_index("grp")
    pairs = lax.axis_size("fsdp") // 2
    z, y = column // 2, column % 2
    place = jnp.stack([z, y, g]).astype(jnp.int32)
    caps_local, cap_len, text_width = caption_states.shape
    tokens, model_width = video_states.shape
    width_local = cross_key.shape[1]
    part = cross_query.shape[0]

    states = caption_states.reshape(cap_len, text_width)
    quarter_rows = cap_len // 4

    ring = [(cross_query, cross_out)]
    ring.append(tuple(fsend(w, 1, 0) for w in ring[0]))
    side_both = fsend(jnp.concatenate([cross_key, cross_value], axis=0), 0, 1)
    side_own = tuple(fsend(w, 0, 1) for w in ring[0])
    projected = project_text(states, text_gain, (text_query, text_key, text_value))
    kept, away = attend_text(projected, text_bias, text_out, place, caption_lens)
    kept, away = after((kept, away), ring[1], side_both)
    got = gsend(away, 1)
    sent = (kept[quarter_rows:].astype(F32) + got[quarter_rows:].astype(F32)).astype(BF)
    sent = after(sent, side_own[0])
    over_x = gsend(sent, 2)
    joint = jnp.concatenate(ring[1], axis=0)
    ring = [ring[0], joint, fsend(joint, 1, 0)]
    side_first = fsend(joint, 0, 1)
    normed, mean, inverse, own_tiles, other_tiles = prepare_video(
        after(video_states, sent), out_grad, place, pairs, part
    )
    pieces = encode_rows(
        states, kept, got, after(over_x, normed, side_own[1]), final_gain, place, pairs
    )

    mine = jnp.stack([fsend(p, far, 0) if far else p for far, p in enumerate(pieces)])
    mine = after(mine, ring[2], side_first)
    over_x = gsend(mine, 2)
    parts = [mine, gsend(mine, 1), over_x, gsend(over_x, 1)]
    current = after(ring[2], mine)
    for far in range(3, pairs):
        current = fsend(current, 1, 0)
        ring.append(current)
    parts[3] = after(parts[3], side_first)
    kv_partial = project_captions(
        parts, cross_key, cross_value, side_both, place, pairs
    )
    kv_partial = after(tuple(kv_partial), ring[-1])
    kv_sum = kv_partial[0].astype(F32)
    for far in range(1, pairs):
        kv_sum += fsend(kv_partial[far], pairs - far, 0).astype(F32)
    side_later = [fsend(w, 0, 1) for w in ring[2:]]
    other_tiles = fsend(other_tiles, 0, 1)
    kv_sum = after(kv_sum.astype(BF), side_later[0])
    kv_blocks = gather_direct(kv_sum)
    kv_blocks[4] = after(kv_blocks[4], side_later, other_tiles)

    blocks = [((cross_query, 0), (cross_out, 0)), ((side_own[0], 0), (side_own[1], 0))]
    for held, side in zip(ring[1:], [side_first, *side_later]):
        blocks += [((held, 0), (held, part)), ((side, 0), (side, part))]
    queries, d_attended, column_sum = project_rows(
        normed, after(out_grad, kv_blocks[4]), blocks, place, pairs, part
    )

    tiles = jnp.stack([own_tiles, other_tiles], axis=1)
    over_z = [fsend(after(tiles[far], kv_blocks[4]), far, 0) for far in range(1, pairs)]
    over_z = [tiles[0]] + over_z

    both, attended, d_queries, row_sums, slots = attend(
        queries,
        d_attended,
        column_sum,
        kv_blocks,
        place,
        video_counts,
        sample_caption,
        caption_lens,
        pairs,
    )
    slots, both, row_sums, over_z = after((slots, both, row_sums, over_z))
    tiles = jnp.stack(over_z)

    def chain(blocks, steps):
        for _ in range(steps):
            blocks.append(fsend(blocks[-1], 1, 0))
        return blocks

    side_slots = fsend(slots, 0, 1)
    side_mine = fsend(both, 0, 1)
    late = chain([both], 2)
    sums_core = gsend(row_sums, 1)
    attended, tiles = after((attended, tiles), sums_core)
    tiles_x = gsend(tiles, 2)
    own, far_piece, away = project_back(attended, d_queries, blocks, place, pairs, part)
    tiles_core = gsend(tiles, 1)
    stage = (side_slots, side_mine, late, sums_core, tiles_x, tiles_core, away)
    side_slots, side_mine, late, sums_core, tiles_x, tiles_core, away = after(stage)

    sides = [fsend(block, 0, 1) for block in late[1:3]]
    late = chain(list(late), pairs - 3)
    row_sums = row_sums + sums_core
    sums_x = gsend(row_sums, 2)
    got = gsend(away, 1)
    width = model_width // 4
    sent = [
        (far_piece[k].astype(F32) + got[k, :, width:].astype(F32)).astype(BF) for k in range(2)
    ]
    far_out = gsend(sent[0], 2)
    terms = caption_terms(
        after(slots, sent[0]), side_slots, place, video_counts, sample_caption, tokens, pairs
    )
    kv_parts = [fsend(terms[far], far, 0) for far in range(1, pairs, 2)]
    stage = (sides, late, sums_x, tiles_x, kv_parts, terms, far_out, sent[1])
    sides, late, sums_x, tiles_x, kv_parts, terms, far_out, sent_d = after(stage)

    here = [((block, 0),) for block in late]
    tiles = [tiles, tiles_core, tiles_x, gsend(tiles_x, 1)]
    there = [((block, 0),) for block in (side_mine, *sides)]
    there += [((fsend(block, 0, 1), 0),) for block in late[3:]]
    known = weight_grads(tiles, here + there[:3], None, pairs)
    total = [
        own[k].astype(F32) + got[k, :, :width].astype(F32) + far.astype(F32)
        for k, far in enumerate((far_out, gsend(sent_d, 2)))
    ]
    row_sums = (row_sums + sums_x) / model_width
    video = quarter(video_states, g, 1).astype(F32)
    updated = (video + total[0]).astype(BF)
    video_hat = (video - mean) * inverse
    input_grad = (
        quarter(out_grad, g, 1).astype(F32)
        + inverse * (total[1] - row_sums[:, 0:1] - video_hat * row_sums[:, 1:2])
    ).astype(BF)
    kv_parts += [fsend(terms[far], far, 0) for far in range(2, pairs, 2)]
    kv_grads = (terms[0] + sum(p.astype(F32) for p in kv_parts)).astype(BF)[None]
    key_grad = kv_grads[:, :, :width_local]
    value_grad = kv_grads[:, :, width_local:]
    query_grad, out_weight_grad = weight_grads(
        tiles, [None] * (pairs + 3) + there[3:], known, pairs
    )
    return (updated, input_grad, query_grad, out_weight_grad, key_grad, value_grad)


def local_of(*arrays):
    whole_tiles = arrays[14].shape[0] % 128 == 0 and arrays[0].shape[0] == 1
    return local(*arrays) if whole_tiles else local_general(*arrays)


def solution(mesh):
    in_specs = (
        P("fsdp", None, None),
        P(),
        P(),
        P(None, "grp"),
        P(None, "grp"),
        P(None, "grp"),
        P("grp", None, None),
        P("grp", None),
        P(),
        P("fsdp", "grp"),
        P("fsdp", "grp"),
        P("fsdp", None),
        P(),
        P(),
        P("fsdp", "grp"),
        P("grp", "fsdp"),
        P("fsdp", None),
    )
    out_specs = (
        P("fsdp", "grp"),
        P("fsdp", "grp"),
        P("fsdp", "grp"),
        P("grp", "fsdp"),
        P("fsdp", None, "grp"),
        P("fsdp", None, "grp"),
    )
    return jax.shard_map(
        local_of, mesh=mesh, in_specs=in_specs, out_specs=out_specs, check_vma=False
    )
```

```python
import math

import jax
import jax.numpy as jnp
from jax import lax
from jax.experimental import pallas as pl
from jax.experimental.pallas import tpu as pltpu
from jax.sharding import PartitionSpec as P

HEAD_SIZE = 128
BF = jnp.bfloat16
F32 = jnp.float32
SLOTS = 3
VMEM_BYTES = 60 * 1024 * 1024
SPARE_BYTES = 8 * 1024 * 1024
SMALL = pl.CostEstimate(flops=1, bytes_accessed=1, transcendentals=0)


def rms_scale(values, gain):
    mean_square = jnp.mean(values * values, axis=-1, keepdims=True)
    return values * lax.rsqrt(mean_square + 1e-06) * gain


def mm(left, right):
    return jnp.dot(left, right, preferred_element_type=F32)


def contract_last(left, right):
    return lax.dot_general(left, right, (((1,), (1,)), ((), ())), preferred_element_type=F32)


def contract_first(left, right):
    return lax.dot_general(left, right, (((0,), (0,)), ((), ())), preferred_element_type=F32)


def fsend(block, far, side):
    size = lax.axis_size("fsdp")
    pairs = size // 2
    perm = [(s, ((s // 2 + far) % pairs) * 2 + ((s % 2) ^ side)) for s in range(size)]
    return lax.ppermute(block, "fsdp", perm)


def gsend(block, flip):
    return lax.ppermute(block, "grp", [(s, s ^ flip) for s in range(lax.axis_size("grp"))])


def gather_ring(block):
    blocks = []
    current = block
    for far in range(lax.axis_size("fsdp") // 2):
        if far:
            current = fsend(current, 1, 0)
        blocks += [current, fsend(current, 0, 1)]
    return blocks


def gather_direct(block):
    blocks = []
    for far in range(lax.axis_size("fsdp") // 2):
        current = fsend(block, far, 0) if far else block
        blocks += [current, fsend(current, 0, 1)]
    return blocks


def quarter(array, index, axis=0):
    size = array.shape[axis] // 4
    return lax.dynamic_slice_in_dim(array, index * size, size, axis)


def grp_scatter(partial, g, axis):
    away = [quarter(partial, g ^ 1, axis), quarter(partial, g ^ 3, axis)]
    kept = [quarter(partial, g, axis), quarter(partial, g ^ 2, axis)]
    got = gsend(jnp.stack(away).astype(BF), 1)
    far = gsend((kept[1] + got[1].astype(F32)).astype(BF), 2)
    return kept[0] + got[0].astype(F32) + far.astype(F32)


def local_general(
    caption_states,
    caption_lens,
    text_gain,
    text_query,
    text_key,
    text_value,
    text_bias,
    text_out,
    final_gain,
    cross_key,
    cross_value,
    video_states,
    video_counts,
    sample_caption,
    cross_query,
    cross_out,
    out_grad,
):
    column = lax.axis_index("fsdp")
    g = lax.axis_index("grp")
    fsdp = lax.axis_size("fsdp")
    pairs = fsdp // 2
    z, y = column // 2, column % 2
    caps_local, cap_len, text_width = caption_states.shape
    tokens, model_width = video_states.shape
    width_local = cross_key.shape[1]
    cross_local = width_local // HEAD_SIZE
    query_rows = cross_query.shape[0]

    def source(far, side):
        return ((z - far) % pairs) * 2 + (y ^ side)

    def target(far, side):
        return ((z + far) % pairs) * 2 + (y ^ side)

    query_blocks = gather_ring(cross_query)
    out_blocks = gather_ring(cross_out)
    full_query = jnp.zeros((model_width, width_local), BF)
    full_out = jnp.zeros((width_local, model_width), BF)
    for far in range(pairs):
        for side in range(2):
            start = source(far, side) * query_rows
            full_query = lax.dynamic_update_slice(
                full_query, query_blocks[2 * far + side], (start, jnp.int32(0))
            )
            full_out = lax.dynamic_update_slice(
                full_out, out_blocks[2 * far + side], (jnp.int32(0), start)
            )

    own_kv = jnp.concatenate([cross_key, cross_value], axis=1)
    other_kv = fsend(own_kv, 0, 1)
    pair_kv = jnp.concatenate(
        [jnp.where(y == 0, own_kv, other_kv), jnp.where(y == 0, other_kv, own_kv)], axis=0
    )

    local_lens = lax.dynamic_slice_in_dim(caption_lens, column * caps_local, caps_local)
    flat_states = caption_states.reshape(caps_local * cap_len, text_width).astype(F32)
    text_normed = rms_scale(flat_states, text_gain).astype(BF)
    local_heads = text_bias.shape[0]
    head_width = text_query.shape[1] // local_heads

    def heads_of(weight):
        return mm(text_normed, weight).astype(BF).reshape(
            caps_local, cap_len, local_heads, head_width
        )

    text_queries = heads_of(text_query)
    text_keys = heads_of(text_key)
    text_values = heads_of(text_value)
    text_scores = (
        jnp.einsum("cihd,cjhd->chij", text_queries, text_keys, preferred_element_type=F32)
        + text_bias[None]
    )
    key_valid = jnp.arange(cap_len, dtype=jnp.int32)[None, :] < local_lens[:, None]
    exp_scores = jnp.where(key_valid[:, None, None, :], jnp.exp(text_scores), 0.0)
    text_weights = (exp_scores / jnp.sum(exp_scores, axis=-1, keepdims=True)).astype(BF)
    text_mixed = jnp.einsum(
        "chij,cjhd->cihd", text_weights, text_values, preferred_element_type=F32
    )
    text_mixed = text_mixed.astype(BF).reshape(caps_local * cap_len, local_heads * head_width)
    partial_text = mm(text_mixed, text_out)
    text_rows = grp_scatter(partial_text, g, 0)
    encoded = rms_scale(quarter(flat_states, g) + text_rows, final_gain).astype(BF)

    part = text_width // pairs
    pieces = [
        lax.dynamic_slice_in_dim(encoded, ((z + far) % pairs) * part, part, 1)
        for far in range(pairs)
    ]
    mine = jnp.stack([fsend(p, far, 0) if far else p for far, p in enumerate(pieces)])
    over_x = jnp.concatenate([mine[:, None], gsend(mine, 2)[:, None]], axis=1)
    over_core = jnp.stack([over_x, gsend(over_x, 1)], axis=2)
    kv_partial = mm(over_core.reshape(-1, part), pair_kv).reshape(pairs, cap_len, 2 * width_local)
    kv_sum = kv_partial[0]
    for far in range(1, pairs):
        kv_sum += fsend(kv_partial[far].astype(BF), pairs - far, 0).astype(F32)
    kv_rows = kv_sum.astype(BF).reshape(4, cap_len // 4, 2 * width_local)
    order = jnp.arange(4, dtype=jnp.int32) ^ g
    cap_kv = jnp.concatenate(
        [lax.dynamic_slice_in_dim(kv_rows, order[k], 1, 0) for k in range(4)], axis=0
    ).reshape(cap_len, 2 * width_local)
    all_kv = jnp.stack(gather_direct(cap_kv))

    video = video_states.astype(F32)
    center = video - jnp.mean(video, axis=-1, keepdims=True)
    inverse = lax.rsqrt(jnp.mean(center * center, axis=-1, keepdims=True) + 1e-06)
    video_hat = center * inverse
    video_normed = video_hat.astype(BF)

    both = jnp.stack([quarter(video_normed, g), quarter(out_grad, g)])
    tiles = []
    for far in range(pairs):
        for side in range(2):
            tile = lax.dynamic_slice_in_dim(both, target(far, side) * query_rows, query_rows, 2)
            tiles.append(fsend(tile, far, side) if far or side else tile)
    tiles = jnp.stack(tiles)
    tiles_x = jnp.stack([tiles, gsend(tiles, 2)], axis=2)
    tiles_all = jnp.stack([tiles_x, gsend(tiles_x, 1)], axis=3)
    normed_tile = tiles_all[:, 0].reshape(-1, query_rows)
    grad_tile = tiles_all[:, 1].reshape(-1, query_rows)

    caption_total = all_kv.shape[0]
    positions = column * tokens + jnp.arange(tokens, dtype=jnp.int32)
    sample_end = jnp.cumsum(video_counts)
    token_sample = jnp.sum((sample_end[None, :] <= positions[:, None]).astype(jnp.int32), axis=1)
    slot_count = 3
    slot_sample = token_sample[0] + jnp.arange(slot_count, dtype=jnp.int32)
    slot_valid = slot_sample < caption_total
    slot_clipped = jnp.minimum(slot_sample, caption_total - 1)
    numbers = jnp.arange(caption_total, dtype=jnp.int32)
    slot_pick = slot_clipped[:, None] == numbers[None, :]
    slot_caption = jnp.sum(jnp.where(slot_pick, sample_caption[None, :], 0), axis=1)
    caption_pick = slot_caption[:, None] == numbers[None, :]
    slot_lens = jnp.sum(jnp.where(caption_pick, caption_lens[None, :], 0), axis=1)
    slot_member = token_sample[None, :] == slot_sample[:, None]
    member_float = slot_member.astype(F32)
    member_half = slot_member.astype(BF)
    slot_entry = ((z - slot_caption // 2) % pairs) * 2 + ((slot_caption % 2) ^ y)
    slot_kv = jnp.take(all_kv, slot_entry, axis=0)
    slot_keys = slot_kv[..., :width_local].reshape(slot_count, cap_len, cross_local, HEAD_SIZE)
    slot_values = slot_kv[..., width_local:].reshape(slot_count, cap_len, cross_local, HEAD_SIZE)
    token_lens = jnp.sum(jnp.where(slot_member, slot_lens[:, None], 0), axis=0)

    query_sum = mm(video_normed, full_query)
    queries = query_sum.astype(BF)
    d_attended = contract_last(out_grad, full_out).astype(BF).reshape(
        tokens, cross_local, HEAD_SIZE
    )
    score_scale = 1.0 / math.sqrt(HEAD_SIZE)
    query_heads = queries.reshape(tokens, cross_local, HEAD_SIZE)
    slot_scores = jnp.einsum("thd,kjhd->kthj", query_heads, slot_keys, preferred_element_type=F32)
    scores = jnp.sum(member_float[:, :, None, None] * slot_scores, axis=0) * score_scale
    token_valid = (jnp.arange(cap_len, dtype=jnp.int32)[None, :] < token_lens[:, None])[:, None, :]
    exp_video = jnp.where(token_valid, jnp.exp(scores), 0.0)
    weights = exp_video / jnp.sum(exp_video, axis=-1, keepdims=True)
    probs = weights.astype(BF)
    masked_probs = member_half[:, :, None, None] * probs[None]
    attended = jnp.einsum("kthj,kjhd->thd", masked_probs, slot_values, preferred_element_type=F32)
    attended = attended.astype(BF).reshape(tokens, width_local)

    def reorder(array):
        return jnp.concatenate([quarter(array, order[k]) for k in range(4)], axis=0)

    all_attended = jnp.concatenate(gather_direct(reorder(attended)), axis=0)
    out_weight_grad = contract_first(all_attended, grad_tile)

    out_share = grp_scatter(mm(attended, full_out), g, 1)
    updated = (quarter(video, g, 1) + out_share).astype(BF)

    slot_dprobs = jnp.einsum("thd,kjhd->kthj", d_attended, slot_values, preferred_element_type=F32)
    d_probs = jnp.sum(member_float[:, :, None, None] * slot_dprobs, axis=0)
    d_scores = (
        weights * (d_probs - jnp.sum(weights * d_probs, axis=-1, keepdims=True)) * score_scale
    ).astype(BF)
    masked_scores = member_half[:, :, None, None] * d_scores[None]
    d_queries = jnp.einsum("kthj,kjhd->thd", masked_scores, slot_keys, preferred_element_type=F32)
    d_queries = d_queries.astype(BF).reshape(tokens, width_local)
    all_d_queries = jnp.concatenate(gather_direct(reorder(d_queries)), axis=0)
    query_grad = contract_first(normed_tile, all_d_queries)

    key_slots = jnp.einsum("kthj,thd->kjhd", masked_scores, query_heads, preferred_element_type=F32)
    value_slots = jnp.einsum("kthj,thd->kjhd", masked_probs, d_attended, preferred_element_type=F32)
    slot_terms = jnp.concatenate(
        [
            key_slots.reshape(slot_count, cap_len, width_local),
            value_slots.reshape(slot_count, cap_len, width_local),
        ],
        axis=-1,
    )

    def caption_terms(far, side):
        picked = (slot_caption == target(far, side)) & slot_valid
        return jnp.sum(jnp.where(picked[:, None, None], slot_terms, 0.0), axis=0)

    away = jnp.stack([caption_terms(far, 1).astype(BF) for far in range(pairs)])
    got = fsend(away, 0, 1).astype(F32)
    kv_grads = caption_terms(0, 0) + got[0]
    for far in range(1, pairs):
        kv_grads += fsend((caption_terms(far, 0) + got[far]).astype(BF), far, 0).astype(F32)
    kv_grads = kv_grads.astype(BF)[None]
    key_grad = kv_grads[:, :, :width_local]
    value_grad = kv_grads[:, :, width_local:]

    d_wide = d_queries.astype(F32)
    column_sum = jnp.sum(full_query.astype(F32), axis=0)
    row_sums = jnp.stack(
        [jnp.sum(d_wide * column_sum, axis=-1), jnp.sum(d_wide * query_sum, axis=-1)]
    )
    row_sums = row_sums + gsend(row_sums, 1)
    row_sums = (row_sums + gsend(row_sums, 2)) / model_width
    d_share = grp_scatter(contract_last(d_queries, full_query), g, 1)
    input_grad = (
        quarter(out_grad, g, 1).astype(F32)
        + inverse
        * (d_share - row_sums[0][:, None] - quarter(video_hat, g, 1) * row_sums[1][:, None])
    ).astype(BF)
    return (updated, input_grad, query_grad, out_weight_grad, key_grad, value_grad)


def after(value, *others):
    return lax.optimization_barrier((value, *others))[0]


def call(body, out_shape, operands, scalars, scratch=()):
    specs = [pl.BlockSpec(memory_space=pltpu.SMEM)] * scalars
    specs += [pl.BlockSpec(memory_space=pltpu.VMEM)] * (len(operands) - scalars)
    held = (*operands[scalars:], *jax.tree.leaves(out_shape), *scratch)
    held_bytes = sum(math.prod(a.shape) * jnp.dtype(a.dtype).itemsize for a in held)
    return pl.pallas_call(
        body,
        out_shape=out_shape,
        in_specs=specs,
        out_specs=jax.tree.map(lambda _: pl.BlockSpec(memory_space=pltpu.VMEM), out_shape),
        scratch_shapes=list(scratch),
        compiler_params=pltpu.CompilerParams(vmem_limit_bytes=held_bytes + SPARE_BYTES),
        cost_estimate=SMALL,
    )(*operands)


def shaped(shape, dtype=BF):
    return jax.ShapeDtypeStruct(shape, dtype)


def aligned(start, unit):
    return pl.multiple_of(start, unit)


def project_text(states, gain, weights, steps=4):
    rows, depth = states.shape
    width = weights[0].shape[1]
    chunk = depth // steps

    def body(states_ref, gain_ref, wq_ref, wk_ref, wv_ref, out_ref, normed_ref, total_ref):
        step = pl.program_id(0)

        @pl.when(step == 0)
        def _():
            for at in range(0, rows, 16):
                values = states_ref[at : at + 16, :].astype(F32)
                normed_ref[at : at + 16, :] = rms_scale(values, gain_ref[...]).astype(BF)
            total_ref[...] = jnp.zeros_like(total_ref)

        here = normed_ref[:, pl.ds(aligned(step * chunk, chunk), chunk)]
        for k, weight_ref in enumerate((wq_ref, wk_ref, wv_ref)):
            total_ref[:, k * width : (k + 1) * width] += mm(here, weight_ref[...])

        @pl.when(step == steps - 1)
        def _():
            out_ref[...] = total_ref[...].astype(BF)

    whole = lambda shape: pl.BlockSpec(shape, lambda i: (0,) * len(shape))
    return pl.pallas_call(
        body,
        grid=(steps,),
        out_shape=shaped((rows, 3 * width)),
        in_specs=[whole((rows, depth)), whole((1, depth))]
        + [pl.BlockSpec((chunk, width), lambda i: (i, 0))] * 3,
        out_specs=whole((rows, 3 * width)),
        scratch_shapes=[pltpu.VMEM((rows, depth), BF), pltpu.VMEM((rows, 3 * width), F32)],
        compiler_params=pltpu.CompilerParams(vmem_limit_bytes=VMEM_BYTES),
        cost_estimate=SMALL,
    )(states, gain.reshape(1, -1), *weights)


def attend_text(projected, bias, text_out, place, lens, steps=4):
    rows = projected.shape[0]
    heads = bias.shape[0]
    inner, depth = text_out.shape
    size = inner // heads
    quarter_rows = rows // 4
    chunk = depth // steps

    def body(place_ref, len_ref, qkv_ref, bias_ref, out_ref, kept_ref, away_ref, held_ref, mixed_ref):
        @pl.when(pl.program_id(0) == 0)
        def _():
            g = place_ref[2]
            length = len_ref[place_ref[0] * 2 + place_ref[1]]
            live = lax.broadcasted_iota(jnp.int32, (rows, rows), 1) < length
            for head in range(heads):
                query, key, value = (
                    qkv_ref[:, k * inner + head * size : k * inner + (head + 1) * size]
                    for k in range(3)
                )
                grown = jnp.where(live, jnp.exp(contract_last(query, key) + bias_ref[head]), 0.0)
                weights = grown * (1.0 / jnp.sum(grown, axis=-1, keepdims=True))
                held_ref[:, head * size : (head + 1) * size] = mm(weights.astype(BF), value).astype(BF)
            for k, to in ((0, 0), (2, 1), (1, 2), (3, 3)):
                rows_from = pl.ds(aligned((g ^ k) * quarter_rows, quarter_rows), quarter_rows)
                mixed_ref[to * quarter_rows : (to + 1) * quarter_rows, :] = held_ref[rows_from, :]

        product = mm(mixed_ref[...], out_ref[...]).astype(BF)
        kept_ref[...] = product[: rows // 2]
        away_ref[...] = product[rows // 2 :]

    whole = lambda shape: pl.BlockSpec(shape, lambda i: (0,) * len(shape))
    return pl.pallas_call(
        body,
        grid=(steps,),
        out_shape=[shaped((rows // 2, depth))] * 2,
        in_specs=[pl.BlockSpec(memory_space=pltpu.SMEM)] * 2
        + [whole(projected.shape), whole(bias.shape)]
        + [pl.BlockSpec((inner, chunk), lambda i: (0, i))],
        out_specs=[pl.BlockSpec((rows // 2, chunk), lambda i: (0, i))] * 2,
        scratch_shapes=[pltpu.VMEM((rows, inner), BF), pltpu.VMEM((rows, inner), BF)],
        compiler_params=pltpu.CompilerParams(vmem_limit_bytes=VMEM_BYTES),
        cost_estimate=SMALL,
    )(place, lens, projected, bias, text_out)


def encode_rows(states, kept, got, far, gain, place, pairs):
    quarter_rows = states.shape[0] // 4
    width = states.shape[1]
    depth = width // pairs

    def body(place_ref, states_ref, kept_ref, got_ref, far_ref, gain_ref, *refs):
        piece_refs, encoded_ref = refs[:-1], refs[-1]
        z, g = place_ref[0], place_ref[2]
        mine = pl.ds(aligned(g * quarter_rows, quarter_rows), quarter_rows)
        total = states_ref[mine, :].astype(F32) + far_ref[...].astype(F32)
        total += kept_ref[:quarter_rows, :].astype(F32) + got_ref[:quarter_rows, :].astype(F32)
        encoded_ref[...] = rms_scale(total, gain_ref[...]).astype(BF)
        for far_by, piece in enumerate(piece_refs):
            to = lax.rem(z + far_by, pairs)
            piece[...] = encoded_ref[:, pl.ds(aligned(to * depth, 128), depth)]

    out = [shaped((quarter_rows, depth))] * pairs
    operands = (place, states, kept, got, far, gain.reshape(1, -1))
    return call(body, out, operands, 1, [pltpu.VMEM((quarter_rows, width), BF)])


def pieces_of(pairs_of_blocks):
    arrays, listed = [], []
    for entry in pairs_of_blocks:
        numbers = []
        for array, start in entry:
            if not any(array is held for held in arrays):
                arrays.append(array)
            numbers.append((next(k for k, held in enumerate(arrays) if held is array), start))
        listed.append(numbers)
    return arrays, listed


def prepare_video(video_states, out_grad, place, pairs, part):
    tokens, model_width = video_states.shape
    rows = tokens // 4

    def body(place_ref, video_ref, grad_ref, normed_ref, mean_ref, inverse_ref, *tile_refs):
        @pl.loop(0, tokens // 32)
        def _(step):
            here = pl.ds(aligned(step * 32, 32), 32)
            values = video_ref[here, :].astype(F32)
            mean = jnp.mean(values, axis=-1, keepdims=True)
            center = values - mean
            inverse = lax.rsqrt(jnp.mean(center * center, axis=-1, keepdims=True) + 1e-06)
            normed_ref[here, :] = (center * inverse).astype(BF)
            mean_ref[here, :] = mean
            inverse_ref[here, :] = inverse

        z, y, g = place_ref[0], place_ref[1], place_ref[2]
        mine = pl.ds(aligned(g * rows, rows), rows)
        for far in range(pairs):
            for side in range(2):
                to = lax.rem(z + far, pairs) * 2 + (y ^ side)
                columns = pl.ds(aligned(to * part, 128), part)
                tile_refs[side][far, 0] = normed_ref[mine, columns]
                tile_refs[side][far, 1] = grad_ref[mine, columns]

    out = [shaped((tokens, model_width)), shaped((tokens, 1), F32), shaped((tokens, 1), F32)]
    out += [shaped((pairs, 2, rows, part))] * 2
    return call(body, out, (place, video_states, out_grad), 1)


def project_rows(normed, out_grad, blocks, place, pairs, part):
    tokens = normed.shape[0]
    arrays, blocks = pieces_of(blocks)
    width = arrays[0].shape[1]

    def body(place_ref, normed_ref, grad_ref, *refs):
        block_refs, (query_ref, d_ref, sum_ref) = refs[:-3], refs[-3:]
        z, y = place_ref[0], place_ref[1]
        query = jnp.zeros((tokens, width), F32)
        d_attended = jnp.zeros((tokens, width), F32)
        total = jnp.zeros((1, width), F32)
        for far in range(pairs):
            for side in range(2):
                (of_query, query_at), (of_out, out_at) = blocks[2 * far + side]
                origin = lax.rem(z - far + pairs, pairs) * 2 + (y ^ side)
                columns = pl.ds(aligned(origin * part, 128), part)
                weight = block_refs[of_query][query_at : query_at + part, :]
                out_weight = block_refs[of_out][out_at : out_at + width, :]
                query += mm(normed_ref[:, columns], weight)
                d_attended += contract_last(grad_ref[:, columns], out_weight)
                total += jnp.sum(weight.astype(F32), axis=0, keepdims=True)
        query_ref[...] = query.astype(BF)
        d_ref[...] = d_attended.astype(BF)
        sum_ref[...] = total

    out = [shaped((tokens, width)), shaped((tokens, width)), shaped((1, width), F32)]
    return call(body, out, (place, normed, out_grad, *arrays), 1)


def project_captions(parts, own_key, own_value, side_key, side_value, place, pairs):
    quarter_rows, depth = parts[0].shape[1:]
    half = depth // 2
    width = own_key.shape[1]

    def body(place_ref, *refs):
        part_refs = refs[:4]
        key_ref, value_ref, side_key_ref, side_value_ref = refs[4:8]
        out_refs = refs[8:]
        y = place_ref[1]
        mine = pl.ds(aligned(y * half, 128), half)
        theirs = pl.ds(aligned((1 - y) * half, 128), half)
        own = jnp.concatenate([r[far, :, mine] for far in range(pairs) for r in part_refs], 0)
        other = jnp.concatenate([r[far, :, theirs] for far in range(pairs) for r in part_refs], 0)
        keys = mm(own, key_ref[...]) + mm(other, side_key_ref[...])
        values = mm(own, value_ref[...]) + mm(other, side_value_ref[...])
        for far in range(pairs):
            rows = slice(far * 4 * quarter_rows, (far + 1) * 4 * quarter_rows)
            out_refs[far][:, :width] = keys[rows].astype(BF)
            out_refs[far][:, width:] = values[rows].astype(BF)

    out = [shaped((4 * quarter_rows, 2 * width))] * pairs
    operands = (place, *parts, own_key, own_value, side_key, side_value)
    return call(body, out, operands, 1)


def slots_of(count_ref, caption_ref, base, captions):
    def find(sample, carry):
        total, first, start = carry
        total = total + count_ref[sample]
        past = total <= base
        return total, first + past.astype(jnp.int32), jnp.where(past, total, start)

    zero = jnp.int32(0)
    _, first, start = lax.fori_loop(0, captions, find, (zero, zero, zero))
    found, edge = [], start - base
    for slot in range(SLOTS):
        valid = first + slot < captions
        sample = jnp.minimum(first + slot, captions - 1)
        end = edge + jnp.where(valid, count_ref[sample], 0)
        found.append((edge, end, caption_ref[sample], valid))
        edge = end
    return found


def attend(queries, d_attended, column_sum, kv_blocks, place, counts, sample_caption, lens, pairs):
    tokens, width = queries.shape
    cap_len = kv_blocks[0].shape[0]
    heads = width // HEAD_SIZE
    captions = counts.shape[0]
    keys_wide = SLOTS * cap_len
    cap_quarter, row_quarter = cap_len // 4, tokens // 4
    scale = 1.0 / math.sqrt(HEAD_SIZE)

    def body(place_ref, count_ref, caption_ref, len_ref, q_ref, da_ref, sum_ref, *refs):
        block_refs = refs[: len(kv_blocks)]
        both_ref, att_ref, dq_ref, rows_ref, slot_ref, kv_ref = refs[len(kv_blocks) :]
        z, y, g = place_ref[0], place_ref[1], place_ref[2]
        low, high, length = [], [], []
        found = slots_of(count_ref, caption_ref, (z * 2 + y) * tokens, captions)
        for slot, (start, end, caption, _) in enumerate(found):
            low.append(start)
            high.append(end)
            length.append(len_ref[caption])
            entry = lax.rem(z - caption // 2 + pairs, pairs) * 2 + (lax.rem(caption, 2) ^ y)
            for number, block in enumerate(block_refs):

                @pl.when(entry == number)
                def _(slot=slot, block=block):
                    kv_ref[slot * cap_len : (slot + 1) * cap_len, :] = block[...]

        token = lax.broadcasted_iota(jnp.int32, (tokens, keys_wide), 0)
        column = lax.broadcasted_iota(jnp.int32, (tokens, keys_wide), 1)
        slot_of = column // cap_len
        inside = column % cap_len
        key = ((inside // cap_quarter) ^ g) * cap_quarter + inside % cap_quarter

        def of_slot(values):
            return jnp.where(slot_of == 0, values[0], jnp.where(slot_of == 1, values[1], values[2]))

        live = (token >= of_slot(low)) & (token < of_slot(high)) & (key < of_slot(length))
        first_sum = jnp.zeros((tokens, 1), F32)
        second_sum = jnp.zeros((tokens, 1), F32)
        for head in range(heads):
            at = slice(head * HEAD_SIZE, (head + 1) * HEAD_SIZE)
            at_value = slice(width + head * HEAD_SIZE, width + (head + 1) * HEAD_SIZE)
            query, d_att = q_ref[:, at], da_ref[:, at]
            keys, values = kv_ref[:, at], kv_ref[:, at_value]
            grown = jnp.where(live, jnp.exp(contract_last(query, keys) * scale), 0.0)
            weights = grown * (1.0 / jnp.sum(grown, axis=-1, keepdims=True))
            probs = weights.astype(BF)
            d_probs = contract_last(d_att, values)
            mixed = jnp.sum(weights * d_probs, axis=-1, keepdims=True)
            d_scores = (weights * (d_probs - mixed) * scale).astype(BF)
            att_ref[:, at] = mm(probs, values).astype(BF)
            d_query = mm(d_scores, keys).astype(BF)
            dq_ref[:, at] = d_query
            d_wide = d_query.astype(F32)
            first_sum += jnp.sum(d_wide * sum_ref[:, at], axis=-1, keepdims=True)
            second_sum += jnp.sum(d_wide * query.astype(F32), axis=-1, keepdims=True)
            key_grad = contract_first(d_scores, query).astype(BF)
            value_grad = contract_first(probs, d_att).astype(BF)
            for slot in range(SLOTS):
                for part in range(4):
                    held = slice(
                        slot * cap_len + part * cap_quarter, slot * cap_len + (part + 1) * cap_quarter
                    )
                    to = pl.ds(aligned((part ^ g) * cap_quarter, cap_quarter), cap_quarter)
                    slot_ref[slot, to, at] = key_grad[held]
                    slot_ref[slot, to, at_value] = value_grad[held]

        rows_ref[:, 0:1] = first_sum
        rows_ref[:, 1:2] = second_sum
        for part in range(4):
            rows = pl.ds(aligned((part ^ g) * row_quarter, row_quarter), row_quarter)
            to = slice(part * row_quarter, (part + 1) * row_quarter)
            both_ref[0, to, :] = att_ref[rows, :]
            both_ref[1, to, :] = dq_ref[rows, :]

    out = [
        shaped((2, tokens, width)),
        shaped((tokens, width)),
        shaped((tokens, width)),
        shaped((tokens, 2), F32),
        shaped((SLOTS, cap_len, 2 * width)),
    ]
    operands = (place, counts, sample_caption, lens, queries, d_attended, column_sum, *kv_blocks)
    scratch = [pltpu.VMEM((keys_wide, 2 * width), BF)]
    return call(body, out, operands, 4, scratch)


def caption_terms(slots, side_slots, place, counts, sample_caption, tokens, pairs):
    captions = counts.shape[0]
    shape = slots.shape[1:]

    def body(place_ref, count_ref, caption_ref, own_ref, side_ref, *refs):
        term_refs, total_ref = refs[:-1], refs[-1]
        z, y = place_ref[0], place_ref[1]
        total_ref[...] = jnp.zeros_like(total_ref)
        for side, slot_ref in enumerate((own_ref, side_ref)):
            base = (z * 2 + (y ^ side)) * tokens
            for slot, (_, _, caption, valid) in enumerate(
                slots_of(count_ref, caption_ref, base, captions)
            ):
                far = lax.rem(caption // 2 - z + pairs, pairs)

                @pl.when(valid & (lax.rem(caption, 2) == y))
                def _(slot=slot, far=far, slot_ref=slot_ref):
                    total_ref[far] += slot_ref[slot].astype(F32)

        for far, term_ref in enumerate(term_refs):
            term_ref[...] = total_ref[far].astype(term_ref.dtype)

    out = [shaped(shape, F32 if far == 0 else BF) for far in range(pairs)]
    operands = (place, counts, sample_caption, slots, side_slots)
    return call(body, out, operands, 3, [pltpu.VMEM((pairs, *shape), F32)])


def project_back(attended, d_queries, blocks, place, pairs, part):
    tokens, width = attended.shape
    arrays, blocks = pieces_of(blocks)
    model_width = 2 * pairs * part
    per_piece = 2 * pairs // 4
    piece = model_width // 4

    def body(place_ref, att_ref, dq_ref, *refs):
        block_refs = refs[: len(arrays)]
        own_ref, far_ref, away_ref = refs[len(arrays) :]
        z, y, g = place_ref[0], place_ref[1], place_ref[2]
        att, d_query = att_ref[...], dq_ref[...]
        for far in range(pairs):
            for side in range(2):
                (of_query, query_at), (of_out, out_at) = blocks[2 * far + side]
                weight = block_refs[of_query][query_at : query_at + part, :]
                out_weight = block_refs[of_out][out_at : out_at + width, :]
                origin = lax.rem(z - far + pairs, pairs) * 2 + (y ^ side)
                flip = (origin // per_piece) ^ g
                start = lax.rem(origin, per_piece) * part
                columns = pl.ds(aligned(start, 128), part)
                beyond = pl.ds(aligned(start + piece, 128), part)
                added = mm(att, out_weight).astype(BF)
                d_normed = contract_last(d_query, weight).astype(BF)
                places = ((own_ref, columns), (away_ref, columns), (far_ref, columns), (away_ref, beyond))
                for number, (target_ref, to) in enumerate(places):

                    @pl.when(flip == number)
                    def _(target_ref=target_ref, to=to, added=added, d_normed=d_normed):
                        target_ref[0, :, to] = added
                        target_ref[1, :, to] = d_normed

    out = [shaped((2, tokens, piece)), shaped((2, tokens, piece)), shaped((2, tokens, 2 * piece))]
    return call(body, out, (place, attended, d_queries, *arrays), 1)


def weight_grads(tiles, both_blocks, known, pairs):
    part = tiles[0].shape[-1]
    given = [k for k, block in enumerate(both_blocks) if block is not None]
    arrays, blocks = pieces_of([both_blocks[k] for k in given])
    width = arrays[0].shape[-1]
    known = known or []

    def body(*refs):
        tile_refs, known_refs = refs[:4], refs[4 : 4 + len(known)]
        block_refs, (query_ref, out_ref) = refs[4 + len(known) : -2], refs[-2:]
        query_grad = known_refs[0][...] if known else jnp.zeros((part, width), F32)
        out_grad = known_refs[1][...] if known else jnp.zeros((width, part), F32)
        for k, ((number, at),) in zip(given, blocks):
            side, far = divmod(k, pairs)
            block = block_refs[number]
            normed, grad = (
                jnp.concatenate([r[far, side, which] for r in tile_refs], axis=0)
                for which in range(2)
            )
            out_grad += contract_first(block[at], grad)
            query_grad += contract_first(normed, block[at + 1])
        query_ref[...] = query_grad
        out_ref[...] = out_grad

    out = [shaped((part, width), F32), shaped((width, part), F32)]
    return call(body, out, (*tiles, *known, *arrays), 0)


def local(
    caption_states,
    caption_lens,
    text_gain,
    text_query,
    text_key,
    text_value,
    text_bias,
    text_out,
    final_gain,
    cross_key,
    cross_value,
    video_states,
    video_counts,
    sample_caption,
    cross_query,
    cross_out,
    out_grad,
):
    column = lax.axis_index("fsdp")
    g = lax.axis_index("grp")
    pairs = lax.axis_size("fsdp") // 2
    z, y = column // 2, column % 2
    place = jnp.stack([z, y, g]).astype(jnp.int32)
    caps_local, cap_len, text_width = caption_states.shape
    tokens, model_width = video_states.shape
    width_local = cross_key.shape[1]
    part = cross_query.shape[0]

    states = caption_states.reshape(cap_len, text_width)
    quarter_rows = cap_len // 4

    first = [fsend(cross_query, 1, 0), fsend(cross_out, 1, 0)]
    side_key, side_value = fsend(cross_key, 0, 1), fsend(cross_value, 0, 1)
    projected = project_text(states, text_gain, (text_query, text_key, text_value))
    kept, away = attend_text(projected, text_bias, text_out, place, caption_lens)
    kept, away = after((kept, away), first, side_key, side_value)
    got = gsend(away, 1)
    ring = [None, jnp.concatenate(first, axis=0)]
    side_first = fsend(jnp.concatenate([cross_query, cross_out, *first], axis=0), 0, 1)
    ring.append(fsend(ring[1], 1, 0))
    sent = (kept[quarter_rows:].astype(F32) + got[quarter_rows:].astype(F32)).astype(BF)
    over_x = gsend(sent, 2)
    normed, mean, inverse, own_tiles, other_tiles = prepare_video(
        after(video_states, sent), out_grad, place, pairs, part
    )
    pieces = encode_rows(
        states, kept, got, after(over_x, normed), final_gain, place, pairs
    )

    mine = jnp.stack([fsend(p, far, 0) if far else p for far, p in enumerate(pieces)])
    mine = after(mine, ring[2])
    over_x = gsend(mine, 2)
    parts = [mine, gsend(mine, 1), over_x, gsend(over_x, 1)]
    current = after(ring[2], mine)
    for far in range(3, pairs):
        current = fsend(current, 1, 0)
        ring.append(current)
    parts[3] = after(parts[3], side_first)
    kv_partial = project_captions(
        parts, cross_key, cross_value, side_key, side_value, place, pairs
    )
    kv_partial = after(tuple(kv_partial), ring[-1])
    kv_sum = kv_partial[0].astype(F32)
    for far in range(1, pairs):
        kv_sum += fsend(kv_partial[far], pairs - far, 0).astype(F32)
    side_later = [fsend(w, 0, 1) for w in ring[2:]]
    other_tiles = fsend(other_tiles, 0, 1)
    kv_sum = after(kv_sum.astype(BF), side_later[0])
    kv_blocks = gather_direct(kv_sum)
    kv_blocks[4] = after(kv_blocks[4], side_later, other_tiles)

    step = part + width_local
    blocks = []
    for far, held in enumerate(ring):
        side, start = (side_first, far * step) if far < 2 else (side_later[far - 2], 0)
        here = ((held, 0), (held, part)) if far else ((cross_query, 0), (cross_out, 0))
        blocks += [here, ((side, start), (side, start + part))]
    queries, d_attended, column_sum = project_rows(
        normed, after(out_grad, kv_blocks[4]), blocks, place, pairs, part
    )

    tiles = jnp.stack([own_tiles, other_tiles], axis=1)
    over_z = [fsend(after(tiles[far], kv_blocks[4]), far, 0) for far in range(1, pairs)]
    over_z = [tiles[0]] + over_z

    both, attended, d_queries, row_sums, slots = attend(
        queries,
        d_attended,
        column_sum,
        kv_blocks,
        place,
        video_counts,
        sample_caption,
        caption_lens,
        pairs,
    )

    def chain(blocks, steps):
        for _ in range(steps):
            blocks.append(fsend(blocks[-1], 1, 0))
        return blocks

    side_slots = fsend(slots, 0, 1)
    side_mine = fsend(both, 0, 1)
    first, over_z = after((both, over_z))
    tiles = jnp.stack(over_z)
    late = chain([first], 2)
    sums_core = gsend(row_sums, 1)
    row_sums = row_sums + sums_core
    attended, tiles = after((attended, tiles), row_sums)
    tiles_x = gsend(tiles, 2)
    own, far_piece, away = project_back(attended, d_queries, blocks, place, pairs, part)
    tiles_core = gsend(tiles, 1)
    stage = (side_slots, side_mine, late, row_sums, tiles_x, tiles_core, away)
    side_slots, side_mine, late, row_sums, tiles_x, tiles_core, away = after(stage)

    sides = [fsend(block, 0, 1) for block in late[1:3]]
    late = chain(list(late), pairs - 3)
    got = gsend(away, 1)
    width = model_width // 4
    sent = [
        (far_piece[k].astype(F32) + got[k, :, width:].astype(F32)).astype(BF) for k in range(2)
    ]
    sums_x = gsend(row_sums, 2)
    far_out = gsend(after(sent[0], sums_x), 2)
    terms = caption_terms(
        after(slots, sent[0]), side_slots, place, video_counts, sample_caption, tokens, pairs
    )
    kv_parts = [fsend(terms[far], far, 0) for far in range(1, pairs, 2)]
    stage = (sides, late, tiles_x, kv_parts, terms, far_out, sent[1])
    sides, late, tiles_x, kv_parts, terms, far_out, sent_d = after(stage)

    here = [((block, 0),) for block in late]
    tiles = [tiles, tiles_core, tiles_x, gsend(tiles_x, 1)]
    there = [((block, 0),) for block in (side_mine, *sides)]
    there += [((fsend(block, 0, 1), 0),) for block in late[3:]]
    known = weight_grads(tiles, here + there[:3], None, pairs)
    total = [
        own[k].astype(F32) + got[k, :, :width].astype(F32) + far.astype(F32)
        for k, far in enumerate((far_out, after(gsend(sent_d, 2), known)))
    ]
    row_sums = (row_sums + sums_x) / model_width
    video = quarter(video_states, g, 1).astype(F32)
    updated = (video + total[0]).astype(BF)
    video_hat = (video - mean) * inverse
    input_grad = (
        quarter(out_grad, g, 1).astype(F32)
        + inverse * (total[1] - row_sums[:, 0:1] - video_hat * row_sums[:, 1:2])
    ).astype(BF)
    kv_parts += [fsend(terms[far], far, 0) for far in range(2, pairs, 2)]
    kv_grads = (terms[0] + sum(p.astype(F32) for p in kv_parts)).astype(BF)[None]
    key_grad = kv_grads[:, :, :width_local]
    value_grad = kv_grads[:, :, width_local:]
    query_grad, out_weight_grad = weight_grads(
        tiles, [None] * (pairs + 3) + there[3:], known, pairs
    )
    return (updated, input_grad, query_grad, out_weight_grad, key_grad, value_grad)


def local_of(*arrays):
    whole_tiles = arrays[14].shape[0] % 128 == 0 and arrays[0].shape[0] == 1
    return local(*arrays) if whole_tiles else local_general(*arrays)


def solution(mesh):
    in_specs = (
        P("fsdp", None, None),
        P(),
        P(),
        P(None, "grp"),
        P(None, "grp"),
        P(None, "grp"),
        P("grp", None, None),
        P("grp", None),
        P(),
        P("fsdp", "grp"),
        P("fsdp", "grp"),
        P("fsdp", None),
        P(),
        P(),
        P("fsdp", "grp"),
        P("grp", "fsdp"),
        P("fsdp", None),
    )
    out_specs = (
        P("fsdp", "grp"),
        P("fsdp", "grp"),
        P("fsdp", "grp"),
        P("grp", "fsdp"),
        P("fsdp", None, "grp"),
        P("fsdp", None, "grp"),
    )
    return jax.shard_map(
        local_of, mesh=mesh, in_specs=in_specs, out_specs=out_specs, check_vma=False
    )
```

```python
import math

import jax
import jax.numpy as jnp
from jax import lax
from jax.experimental import pallas as pl
from jax.experimental.pallas import tpu as pltpu
from jax.sharding import PartitionSpec as P

HEAD_SIZE = 128
BF = jnp.bfloat16
F32 = jnp.float32
SLOTS = 3
VMEM_BYTES = 60 * 1024 * 1024
SPARE_BYTES = 8 * 1024 * 1024
SMALL = pl.CostEstimate(flops=1, bytes_accessed=1, transcendentals=0)


def rms_scale(values, gain):
    mean_square = jnp.mean(values * values, axis=-1, keepdims=True)
    return values * lax.rsqrt(mean_square + 1e-06) * gain


def mm(left, right):
    return jnp.dot(left, right, preferred_element_type=F32)


def contract_last(left, right):
    return lax.dot_general(left, right, (((1,), (1,)), ((), ())), preferred_element_type=F32)


def contract_first(left, right):
    return lax.dot_general(left, right, (((0,), (0,)), ((), ())), preferred_element_type=F32)


def fsend(block, far, side):
    size = lax.axis_size("fsdp")
    pairs = size // 2
    perm = [(s, ((s // 2 + far) % pairs) * 2 + ((s % 2) ^ side)) for s in range(size)]
    return lax.ppermute(block, "fsdp", perm)


def gsend(block, flip):
    return lax.ppermute(block, "grp", [(s, s ^ flip) for s in range(lax.axis_size("grp"))])


def gather_ring(block):
    blocks = []
    current = block
    for far in range(lax.axis_size("fsdp") // 2):
        if far:
            current = fsend(current, 1, 0)
        blocks += [current, fsend(current, 0, 1)]
    return blocks


def gather_direct(block):
    blocks = []
    for far in range(lax.axis_size("fsdp") // 2):
        current = fsend(block, far, 0) if far else block
        blocks += [current, fsend(current, 0, 1)]
    return blocks


def quarter(array, index, axis=0):
    size = array.shape[axis] // 4
    return lax.dynamic_slice_in_dim(array, index * size, size, axis)


def grp_scatter(partial, g, axis):
    away = [quarter(partial, g ^ 1, axis), quarter(partial, g ^ 3, axis)]
    kept = [quarter(partial, g, axis), quarter(partial, g ^ 2, axis)]
    got = gsend(jnp.stack(away).astype(BF), 1)
    far = gsend((kept[1] + got[1].astype(F32)).astype(BF), 2)
    return kept[0] + got[0].astype(F32) + far.astype(F32)


def local_general(
    caption_states,
    caption_lens,
    text_gain,
    text_query,
    text_key,
    text_value,
    text_bias,
    text_out,
    final_gain,
    cross_key,
    cross_value,
    video_states,
    video_counts,
    sample_caption,
    cross_query,
    cross_out,
    out_grad,
):
    column = lax.axis_index("fsdp")
    g = lax.axis_index("grp")
    fsdp = lax.axis_size("fsdp")
    pairs = fsdp // 2
    z, y = column // 2, column % 2
    caps_local, cap_len, text_width = caption_states.shape
    tokens, model_width = video_states.shape
    width_local = cross_key.shape[1]
    cross_local = width_local // HEAD_SIZE
    query_rows = cross_query.shape[0]

    def source(far, side):
        return ((z - far) % pairs) * 2 + (y ^ side)

    def target(far, side):
        return ((z + far) % pairs) * 2 + (y ^ side)

    query_blocks = gather_ring(cross_query)
    out_blocks = gather_ring(cross_out)
    full_query = jnp.zeros((model_width, width_local), BF)
    full_out = jnp.zeros((width_local, model_width), BF)
    for far in range(pairs):
        for side in range(2):
            start = source(far, side) * query_rows
            full_query = lax.dynamic_update_slice(
                full_query, query_blocks[2 * far + side], (start, jnp.int32(0))
            )
            full_out = lax.dynamic_update_slice(
                full_out, out_blocks[2 * far + side], (jnp.int32(0), start)
            )

    own_kv = jnp.concatenate([cross_key, cross_value], axis=1)
    other_kv = fsend(own_kv, 0, 1)
    pair_kv = jnp.concatenate(
        [jnp.where(y == 0, own_kv, other_kv), jnp.where(y == 0, other_kv, own_kv)], axis=0
    )

    local_lens = lax.dynamic_slice_in_dim(caption_lens, column * caps_local, caps_local)
    flat_states = caption_states.reshape(caps_local * cap_len, text_width).astype(F32)
    text_normed = rms_scale(flat_states, text_gain).astype(BF)
    local_heads = text_bias.shape[0]
    head_width = text_query.shape[1] // local_heads

    def heads_of(weight):
        return mm(text_normed, weight).astype(BF).reshape(
            caps_local, cap_len, local_heads, head_width
        )

    text_queries = heads_of(text_query)
    text_keys = heads_of(text_key)
    text_values = heads_of(text_value)
    text_scores = (
        jnp.einsum("cihd,cjhd->chij", text_queries, text_keys, preferred_element_type=F32)
        + text_bias[None]
    )
    key_valid = jnp.arange(cap_len, dtype=jnp.int32)[None, :] < local_lens[:, None]
    exp_scores = jnp.where(key_valid[:, None, None, :], jnp.exp(text_scores), 0.0)
    text_weights = (exp_scores / jnp.sum(exp_scores, axis=-1, keepdims=True)).astype(BF)
    text_mixed = jnp.einsum(
        "chij,cjhd->cihd", text_weights, text_values, preferred_element_type=F32
    )
    text_mixed = text_mixed.astype(BF).reshape(caps_local * cap_len, local_heads * head_width)
    partial_text = mm(text_mixed, text_out)
    text_rows = grp_scatter(partial_text, g, 0)
    encoded = rms_scale(quarter(flat_states, g) + text_rows, final_gain).astype(BF)

    part = text_width // pairs
    pieces = [
        lax.dynamic_slice_in_dim(encoded, ((z + far) % pairs) * part, part, 1)
        for far in range(pairs)
    ]
    mine = jnp.stack([fsend(p, far, 0) if far else p for far, p in enumerate(pieces)])
    over_x = jnp.concatenate([mine[:, None], gsend(mine, 2)[:, None]], axis=1)
    over_core = jnp.stack([over_x, gsend(over_x, 1)], axis=2)
    kv_partial = mm(over_core.reshape(-1, part), pair_kv).reshape(pairs, cap_len, 2 * width_local)
    kv_sum = kv_partial[0]
    for far in range(1, pairs):
        kv_sum += fsend(kv_partial[far].astype(BF), pairs - far, 0).astype(F32)
    kv_rows = kv_sum.astype(BF).reshape(4, cap_len // 4, 2 * width_local)
    order = jnp.arange(4, dtype=jnp.int32) ^ g
    cap_kv = jnp.concatenate(
        [lax.dynamic_slice_in_dim(kv_rows, order[k], 1, 0) for k in range(4)], axis=0
    ).reshape(cap_len, 2 * width_local)
    all_kv = jnp.stack(gather_direct(cap_kv))

    video = video_states.astype(F32)
    center = video - jnp.mean(video, axis=-1, keepdims=True)
    inverse = lax.rsqrt(jnp.mean(center * center, axis=-1, keepdims=True) + 1e-06)
    video_hat = center * inverse
    video_normed = video_hat.astype(BF)

    both = jnp.stack([quarter(video_normed, g), quarter(out_grad, g)])
    tiles = []
    for far in range(pairs):
        for side in range(2):
            tile = lax.dynamic_slice_in_dim(both, target(far, side) * query_rows, query_rows, 2)
            tiles.append(fsend(tile, far, side) if far or side else tile)
    tiles = jnp.stack(tiles)
    tiles_x = jnp.stack([tiles, gsend(tiles, 2)], axis=2)
    tiles_all = jnp.stack([tiles_x, gsend(tiles_x, 1)], axis=3)
    normed_tile = tiles_all[:, 0].reshape(-1, query_rows)
    grad_tile = tiles_all[:, 1].reshape(-1, query_rows)

    caption_total = all_kv.shape[0]
    positions = column * tokens + jnp.arange(tokens, dtype=jnp.int32)
    sample_end = jnp.cumsum(video_counts)
    token_sample = jnp.sum((sample_end[None, :] <= positions[:, None]).astype(jnp.int32), axis=1)
    slot_count = 3
    slot_sample = token_sample[0] + jnp.arange(slot_count, dtype=jnp.int32)
    slot_valid = slot_sample < caption_total
    slot_clipped = jnp.minimum(slot_sample, caption_total - 1)
    numbers = jnp.arange(caption_total, dtype=jnp.int32)
    slot_pick = slot_clipped[:, None] == numbers[None, :]
    slot_caption = jnp.sum(jnp.where(slot_pick, sample_caption[None, :], 0), axis=1)
    caption_pick = slot_caption[:, None] == numbers[None, :]
    slot_lens = jnp.sum(jnp.where(caption_pick, caption_lens[None, :], 0), axis=1)
    slot_member = token_sample[None, :] == slot_sample[:, None]
    member_float = slot_member.astype(F32)
    member_half = slot_member.astype(BF)
    slot_entry = ((z - slot_caption // 2) % pairs) * 2 + ((slot_caption % 2) ^ y)
    slot_kv = jnp.take(all_kv, slot_entry, axis=0)
    slot_keys = slot_kv[..., :width_local].reshape(slot_count, cap_len, cross_local, HEAD_SIZE)
    slot_values = slot_kv[..., width_local:].reshape(slot_count, cap_len, cross_local, HEAD_SIZE)
    token_lens = jnp.sum(jnp.where(slot_member, slot_lens[:, None], 0), axis=0)

    query_sum = mm(video_normed, full_query)
    queries = query_sum.astype(BF)
    d_attended = contract_last(out_grad, full_out).astype(BF).reshape(
        tokens, cross_local, HEAD_SIZE
    )
    score_scale = 1.0 / math.sqrt(HEAD_SIZE)
    query_heads = queries.reshape(tokens, cross_local, HEAD_SIZE)
    slot_scores = jnp.einsum("thd,kjhd->kthj", query_heads, slot_keys, preferred_element_type=F32)
    scores = jnp.sum(member_float[:, :, None, None] * slot_scores, axis=0) * score_scale
    token_valid = (jnp.arange(cap_len, dtype=jnp.int32)[None, :] < token_lens[:, None])[:, None, :]
    exp_video = jnp.where(token_valid, jnp.exp(scores), 0.0)
    weights = exp_video / jnp.sum(exp_video, axis=-1, keepdims=True)
    probs = weights.astype(BF)
    masked_probs = member_half[:, :, None, None] * probs[None]
    attended = jnp.einsum("kthj,kjhd->thd", masked_probs, slot_values, preferred_element_type=F32)
    attended = attended.astype(BF).reshape(tokens, width_local)

    def reorder(array):
        return jnp.concatenate([quarter(array, order[k]) for k in range(4)], axis=0)

    all_attended = jnp.concatenate(gather_direct(reorder(attended)), axis=0)
    out_weight_grad = contract_first(all_attended, grad_tile)

    out_share = grp_scatter(mm(attended, full_out), g, 1)
    updated = (quarter(video, g, 1) + out_share).astype(BF)

    slot_dprobs = jnp.einsum("thd,kjhd->kthj", d_attended, slot_values, preferred_element_type=F32)
    d_probs = jnp.sum(member_float[:, :, None, None] * slot_dprobs, axis=0)
    d_scores = (
        weights * (d_probs - jnp.sum(weights * d_probs, axis=-1, keepdims=True)) * score_scale
    ).astype(BF)
    masked_scores = member_half[:, :, None, None] * d_scores[None]
    d_queries = jnp.einsum("kthj,kjhd->thd", masked_scores, slot_keys, preferred_element_type=F32)
    d_queries = d_queries.astype(BF).reshape(tokens, width_local)
    all_d_queries = jnp.concatenate(gather_direct(reorder(d_queries)), axis=0)
    query_grad = contract_first(normed_tile, all_d_queries)

    key_slots = jnp.einsum("kthj,thd->kjhd", masked_scores, query_heads, preferred_element_type=F32)
    value_slots = jnp.einsum("kthj,thd->kjhd", masked_probs, d_attended, preferred_element_type=F32)
    slot_terms = jnp.concatenate(
        [
            key_slots.reshape(slot_count, cap_len, width_local),
            value_slots.reshape(slot_count, cap_len, width_local),
        ],
        axis=-1,
    )

    def caption_terms(far, side):
        picked = (slot_caption == target(far, side)) & slot_valid
        return jnp.sum(jnp.where(picked[:, None, None], slot_terms, 0.0), axis=0)

    away = jnp.stack([caption_terms(far, 1).astype(BF) for far in range(pairs)])
    got = fsend(away, 0, 1).astype(F32)
    kv_grads = caption_terms(0, 0) + got[0]
    for far in range(1, pairs):
        kv_grads += fsend((caption_terms(far, 0) + got[far]).astype(BF), far, 0).astype(F32)
    kv_grads = kv_grads.astype(BF)[None]
    key_grad = kv_grads[:, :, :width_local]
    value_grad = kv_grads[:, :, width_local:]

    d_wide = d_queries.astype(F32)
    column_sum = jnp.sum(full_query.astype(F32), axis=0)
    row_sums = jnp.stack(
        [jnp.sum(d_wide * column_sum, axis=-1), jnp.sum(d_wide * query_sum, axis=-1)]
    )
    row_sums = row_sums + gsend(row_sums, 1)
    row_sums = (row_sums + gsend(row_sums, 2)) / model_width
    d_share = grp_scatter(contract_last(d_queries, full_query), g, 1)
    input_grad = (
        quarter(out_grad, g, 1).astype(F32)
        + inverse
        * (d_share - row_sums[0][:, None] - quarter(video_hat, g, 1) * row_sums[1][:, None])
    ).astype(BF)
    return (updated, input_grad, query_grad, out_weight_grad, key_grad, value_grad)


def after(value, *others):
    return lax.optimization_barrier((value, *others))[0]


def call(body, out_shape, operands, scalars, scratch=()):
    specs = [pl.BlockSpec(memory_space=pltpu.SMEM)] * scalars
    specs += [pl.BlockSpec(memory_space=pltpu.VMEM)] * (len(operands) - scalars)
    held = (*operands[scalars:], *jax.tree.leaves(out_shape), *scratch)
    held_bytes = sum(math.prod(a.shape) * jnp.dtype(a.dtype).itemsize for a in held)
    return pl.pallas_call(
        body,
        out_shape=out_shape,
        in_specs=specs,
        out_specs=jax.tree.map(lambda _: pl.BlockSpec(memory_space=pltpu.VMEM), out_shape),
        scratch_shapes=list(scratch),
        compiler_params=pltpu.CompilerParams(vmem_limit_bytes=held_bytes + SPARE_BYTES),
        cost_estimate=SMALL,
    )(*operands)


def shaped(shape, dtype=BF):
    return jax.ShapeDtypeStruct(shape, dtype)


def aligned(start, unit):
    return pl.multiple_of(start, unit)


def project_text(states, gain, weights, steps=4):
    rows, depth = states.shape
    width = weights[0].shape[1]
    chunk = depth // steps

    def body(states_ref, gain_ref, wq_ref, wk_ref, wv_ref, out_ref, normed_ref, total_ref):
        step = pl.program_id(0)

        @pl.when(step == 0)
        def _():
            for at in range(0, rows, 16):
                values = states_ref[at : at + 16, :].astype(F32)
                normed_ref[at : at + 16, :] = rms_scale(values, gain_ref[...]).astype(BF)
            total_ref[...] = jnp.zeros_like(total_ref)

        here = normed_ref[:, pl.ds(aligned(step * chunk, chunk), chunk)]
        for k, weight_ref in enumerate((wq_ref, wk_ref, wv_ref)):
            total_ref[:, k * width : (k + 1) * width] += mm(here, weight_ref[...])

        @pl.when(step == steps - 1)
        def _():
            out_ref[...] = total_ref[...].astype(BF)

    whole = lambda shape: pl.BlockSpec(shape, lambda i: (0,) * len(shape))
    return pl.pallas_call(
        body,
        grid=(steps,),
        out_shape=shaped((rows, 3 * width)),
        in_specs=[whole((rows, depth)), whole((1, depth))]
        + [pl.BlockSpec((chunk, width), lambda i: (i, 0))] * 3,
        out_specs=whole((rows, 3 * width)),
        scratch_shapes=[pltpu.VMEM((rows, depth), BF), pltpu.VMEM((rows, 3 * width), F32)],
        compiler_params=pltpu.CompilerParams(vmem_limit_bytes=VMEM_BYTES),
        cost_estimate=SMALL,
    )(states, gain.reshape(1, -1), *weights)


def attend_text(projected, bias, text_out, place, lens, steps=4):
    rows = projected.shape[0]
    heads = bias.shape[0]
    inner, depth = text_out.shape
    size = inner // heads
    quarter_rows = rows // 4
    chunk = depth // steps

    def body(place_ref, len_ref, qkv_ref, bias_ref, out_ref, kept_ref, away_ref, held_ref, mixed_ref):
        @pl.when(pl.program_id(0) == 0)
        def _():
            g = place_ref[2]
            length = len_ref[place_ref[0] * 2 + place_ref[1]]
            live = lax.broadcasted_iota(jnp.int32, (rows, rows), 1) < length
            for head in range(heads):
                query, key, value = (
                    qkv_ref[:, k * inner + head * size : k * inner + (head + 1) * size]
                    for k in range(3)
                )
                grown = jnp.where(live, jnp.exp(contract_last(query, key) + bias_ref[head]), 0.0)
                weights = grown * (1.0 / jnp.sum(grown, axis=-1, keepdims=True))
                held_ref[:, head * size : (head + 1) * size] = mm(weights.astype(BF), value).astype(BF)
            for k, to in ((0, 0), (2, 1), (1, 2), (3, 3)):
                rows_from = pl.ds(aligned((g ^ k) * quarter_rows, quarter_rows), quarter_rows)
                mixed_ref[to * quarter_rows : (to + 1) * quarter_rows, :] = held_ref[rows_from, :]

        product = mm(mixed_ref[...], out_ref[...]).astype(BF)
        kept_ref[...] = product[: rows // 2]
        away_ref[...] = product[rows // 2 :]

    whole = lambda shape: pl.BlockSpec(shape, lambda i: (0,) * len(shape))
    return pl.pallas_call(
        body,
        grid=(steps,),
        out_shape=[shaped((rows // 2, depth))] * 2,
        in_specs=[pl.BlockSpec(memory_space=pltpu.SMEM)] * 2
        + [whole(projected.shape), whole(bias.shape)]
        + [pl.BlockSpec((inner, chunk), lambda i: (0, i))],
        out_specs=[pl.BlockSpec((rows // 2, chunk), lambda i: (0, i))] * 2,
        scratch_shapes=[pltpu.VMEM((rows, inner), BF), pltpu.VMEM((rows, inner), BF)],
        compiler_params=pltpu.CompilerParams(vmem_limit_bytes=VMEM_BYTES),
        cost_estimate=SMALL,
    )(place, lens, projected, bias, text_out)


def encode_rows(states, kept, got, far, gain, place, pairs):
    quarter_rows = states.shape[0] // 4
    width = states.shape[1]
    depth = width // pairs

    def body(place_ref, states_ref, kept_ref, got_ref, far_ref, gain_ref, *refs):
        piece_refs, encoded_ref = refs[:-1], refs[-1]
        z, g = place_ref[0], place_ref[2]
        mine = pl.ds(aligned(g * quarter_rows, quarter_rows), quarter_rows)
        total = states_ref[mine, :].astype(F32) + far_ref[...].astype(F32)
        total += kept_ref[:quarter_rows, :].astype(F32) + got_ref[:quarter_rows, :].astype(F32)
        encoded_ref[...] = rms_scale(total, gain_ref[...]).astype(BF)
        for far_by, piece in enumerate(piece_refs):
            to = lax.rem(z + far_by, pairs)
            piece[...] = encoded_ref[:, pl.ds(aligned(to * depth, 128), depth)]

    out = [shaped((quarter_rows, depth))] * pairs
    operands = (place, states, kept, got, far, gain.reshape(1, -1))
    return call(body, out, operands, 1, [pltpu.VMEM((quarter_rows, width), BF)])


def pieces_of(pairs_of_blocks):
    arrays, listed = [], []
    for entry in pairs_of_blocks:
        numbers = []
        for array, start in entry:
            if not any(array is held for held in arrays):
                arrays.append(array)
            numbers.append((next(k for k, held in enumerate(arrays) if held is array), start))
        listed.append(numbers)
    return arrays, listed


def prepare_video(video_states, out_grad, place, pairs, part):
    tokens, model_width = video_states.shape
    rows = tokens // 4

    def body(place_ref, video_ref, grad_ref, normed_ref, mean_ref, inverse_ref, *tile_refs):
        @pl.loop(0, tokens // 32)
        def _(step):
            here = pl.ds(aligned(step * 32, 32), 32)
            values = video_ref[here, :].astype(F32)
            mean = jnp.mean(values, axis=-1, keepdims=True)
            center = values - mean
            inverse = lax.rsqrt(jnp.mean(center * center, axis=-1, keepdims=True) + 1e-06)
            normed_ref[here, :] = (center * inverse).astype(BF)
            mean_ref[here, :] = mean
            inverse_ref[here, :] = inverse

        z, y, g = place_ref[0], place_ref[1], place_ref[2]
        mine = pl.ds(aligned(g * rows, rows), rows)
        for far in range(pairs):
            for side in range(2):
                to = lax.rem(z + far, pairs) * 2 + (y ^ side)
                columns = pl.ds(aligned(to * part, 128), part)
                tile_refs[side][far, 0] = normed_ref[mine, columns]
                tile_refs[side][far, 1] = grad_ref[mine, columns]

    out = [shaped((tokens, model_width)), shaped((tokens, 1), F32), shaped((tokens, 1), F32)]
    out += [shaped((pairs, 2, rows, part))] * 2
    return call(body, out, (place, video_states, out_grad), 1)


def project_rows(normed, out_grad, blocks, place, pairs, part):
    tokens = normed.shape[0]
    arrays, blocks = pieces_of(blocks)
    width = arrays[0].shape[1]

    def body(place_ref, normed_ref, grad_ref, *refs):
        block_refs, (query_ref, d_ref, sum_ref) = refs[:-3], refs[-3:]
        z, y = place_ref[0], place_ref[1]
        query = jnp.zeros((tokens, width), F32)
        d_attended = jnp.zeros((tokens, width), F32)
        total = jnp.zeros((1, width), F32)
        for far in range(pairs):
            for side in range(2):
                (of_query, query_at), (of_out, out_at) = blocks[2 * far + side]
                origin = lax.rem(z - far + pairs, pairs) * 2 + (y ^ side)
                columns = pl.ds(aligned(origin * part, 128), part)
                weight = block_refs[of_query][query_at : query_at + part, :]
                out_weight = block_refs[of_out][out_at : out_at + width, :]
                query += mm(normed_ref[:, columns], weight)
                d_attended += contract_last(grad_ref[:, columns], out_weight)
                total += jnp.sum(weight.astype(F32), axis=0, keepdims=True)
        query_ref[...] = query.astype(BF)
        d_ref[...] = d_attended.astype(BF)
        sum_ref[...] = total

    out = [shaped((tokens, width)), shaped((tokens, width)), shaped((1, width), F32)]
    return call(body, out, (place, normed, out_grad, *arrays), 1)


def project_captions(parts, own_key, own_value, side_key, side_value, place, pairs):
    quarter_rows, depth = parts[0].shape[1:]
    half = depth // 2
    width = own_key.shape[1]

    def body(place_ref, *refs):
        part_refs = refs[:4]
        key_ref, value_ref, side_key_ref, side_value_ref = refs[4:8]
        out_refs = refs[8:]
        y = place_ref[1]
        mine = pl.ds(aligned(y * half, 128), half)
        theirs = pl.ds(aligned((1 - y) * half, 128), half)
        own = jnp.concatenate([r[far, :, mine] for far in range(pairs) for r in part_refs], 0)
        other = jnp.concatenate([r[far, :, theirs] for far in range(pairs) for r in part_refs], 0)
        keys = mm(own, key_ref[...]) + mm(other, side_key_ref[...])
        values = mm(own, value_ref[...]) + mm(other, side_value_ref[...])
        for far in range(pairs):
            rows = slice(far * 4 * quarter_rows, (far + 1) * 4 * quarter_rows)
            out_refs[far][:, :width] = keys[rows].astype(BF)
            out_refs[far][:, width:] = values[rows].astype(BF)

    out = [shaped((4 * quarter_rows, 2 * width))] * pairs
    operands = (place, *parts, own_key, own_value, side_key, side_value)
    return call(body, out, operands, 1)


def slots_of(count_ref, caption_ref, base, captions):
    def find(sample, carry):
        total, first, start = carry
        total = total + count_ref[sample]
        past = total <= base
        return total, first + past.astype(jnp.int32), jnp.where(past, total, start)

    zero = jnp.int32(0)
    _, first, start = lax.fori_loop(0, captions, find, (zero, zero, zero))
    found, edge = [], start - base
    for slot in range(SLOTS):
        valid = first + slot < captions
        sample = jnp.minimum(first + slot, captions - 1)
        end = edge + jnp.where(valid, count_ref[sample], 0)
        found.append((edge, end, caption_ref[sample], valid))
        edge = end
    return found


def attend(queries, d_attended, column_sum, kv_blocks, place, counts, sample_caption, lens, pairs):
    tokens, width = queries.shape
    cap_len = kv_blocks[0].shape[0]
    heads = width // HEAD_SIZE
    captions = counts.shape[0]
    keys_wide = SLOTS * cap_len
    cap_quarter, row_quarter = cap_len // 4, tokens // 4
    scale = 1.0 / math.sqrt(HEAD_SIZE)

    def body(place_ref, count_ref, caption_ref, len_ref, q_ref, da_ref, sum_ref, *refs):
        block_refs = refs[: len(kv_blocks)]
        both_ref, att_ref, dq_ref, rows_ref, slot_ref, kv_ref = refs[len(kv_blocks) :]
        z, y, g = place_ref[0], place_ref[1], place_ref[2]
        low, high, length = [], [], []
        found = slots_of(count_ref, caption_ref, (z * 2 + y) * tokens, captions)
        for slot, (start, end, caption, _) in enumerate(found):
            low.append(start)
            high.append(end)
            length.append(len_ref[caption])
            entry = lax.rem(z - caption // 2 + pairs, pairs) * 2 + (lax.rem(caption, 2) ^ y)
            for number, block in enumerate(block_refs):

                @pl.when(entry == number)
                def _(slot=slot, block=block):
                    kv_ref[slot * cap_len : (slot + 1) * cap_len, :] = block[...]

        token = lax.broadcasted_iota(jnp.int32, (tokens, keys_wide), 0)
        column = lax.broadcasted_iota(jnp.int32, (tokens, keys_wide), 1)
        slot_of = column // cap_len
        inside = column % cap_len
        key = ((inside // cap_quarter) ^ g) * cap_quarter + inside % cap_quarter

        def of_slot(values):
            return jnp.where(slot_of == 0, values[0], jnp.where(slot_of == 1, values[1], values[2]))

        live = (token >= of_slot(low)) & (token < of_slot(high)) & (key < of_slot(length))
        first_sum = jnp.zeros((tokens, 1), F32)
        second_sum = jnp.zeros((tokens, 1), F32)
        for head in range(heads):
            at = slice(head * HEAD_SIZE, (head + 1) * HEAD_SIZE)
            at_value = slice(width + head * HEAD_SIZE, width + (head + 1) * HEAD_SIZE)
            query, d_att = q_ref[:, at], da_ref[:, at]
            keys, values = kv_ref[:, at], kv_ref[:, at_value]
            grown = jnp.where(live, jnp.exp(contract_last(query, keys) * scale), 0.0)
            weights = grown * (1.0 / jnp.sum(grown, axis=-1, keepdims=True))
            probs = weights.astype(BF)
            d_probs = contract_last(d_att, values)
            mixed = jnp.sum(weights * d_probs, axis=-1, keepdims=True)
            d_scores = (weights * (d_probs - mixed) * scale).astype(BF)
            att_ref[:, at] = mm(probs, values).astype(BF)
            d_query = mm(d_scores, keys).astype(BF)
            dq_ref[:, at] = d_query
            d_wide = d_query.astype(F32)
            first_sum += jnp.sum(d_wide * sum_ref[:, at], axis=-1, keepdims=True)
            second_sum += jnp.sum(d_wide * query.astype(F32), axis=-1, keepdims=True)
            key_grad = contract_first(d_scores, query).astype(BF)
            value_grad = contract_first(probs, d_att).astype(BF)
            for slot in range(SLOTS):
                for part in range(4):
                    held = slice(
                        slot * cap_len + part * cap_quarter, slot * cap_len + (part + 1) * cap_quarter
                    )
                    to = pl.ds(aligned((part ^ g) * cap_quarter, cap_quarter), cap_quarter)
                    slot_ref[slot, to, at] = key_grad[held]
                    slot_ref[slot, to, at_value] = value_grad[held]

        rows_ref[:, 0:1] = first_sum
        rows_ref[:, 1:2] = second_sum
        for part in range(4):
            rows = pl.ds(aligned((part ^ g) * row_quarter, row_quarter), row_quarter)
            to = slice(part * row_quarter, (part + 1) * row_quarter)
            both_ref[0, to, :] = att_ref[rows, :]
            both_ref[1, to, :] = dq_ref[rows, :]

    out = [
        shaped((2, tokens, width)),
        shaped((tokens, width)),
        shaped((tokens, width)),
        shaped((tokens, 2), F32),
        shaped((SLOTS, cap_len, 2 * width)),
    ]
    operands = (place, counts, sample_caption, lens, queries, d_attended, column_sum, *kv_blocks)
    scratch = [pltpu.VMEM((keys_wide, 2 * width), BF)]
    return call(body, out, operands, 4, scratch)


def caption_terms(slots, side_slots, place, counts, sample_caption, tokens, pairs):
    captions = counts.shape[0]
    shape = slots.shape[1:]

    def body(place_ref, count_ref, caption_ref, own_ref, side_ref, *refs):
        term_refs, total_ref = refs[:-1], refs[-1]
        z, y = place_ref[0], place_ref[1]
        total_ref[...] = jnp.zeros_like(total_ref)
        for side, slot_ref in enumerate((own_ref, side_ref)):
            base = (z * 2 + (y ^ side)) * tokens
            for slot, (_, _, caption, valid) in enumerate(
                slots_of(count_ref, caption_ref, base, captions)
            ):
                far = lax.rem(caption // 2 - z + pairs, pairs)

                @pl.when(valid & (lax.rem(caption, 2) == y))
                def _(slot=slot, far=far, slot_ref=slot_ref):
                    total_ref[far] += slot_ref[slot].astype(F32)

        for far, term_ref in enumerate(term_refs):
            term_ref[...] = total_ref[far].astype(term_ref.dtype)

    out = [shaped(shape, F32 if far == 0 else BF) for far in range(pairs)]
    operands = (place, counts, sample_caption, slots, side_slots)
    return call(body, out, operands, 3, [pltpu.VMEM((pairs, *shape), F32)])


def project_back(attended, d_queries, blocks, place, pairs, part):
    tokens, width = attended.shape
    arrays, blocks = pieces_of(blocks)
    model_width = 2 * pairs * part
    per_piece = 2 * pairs // 4
    piece = model_width // 4

    def body(place_ref, att_ref, dq_ref, *refs):
        block_refs = refs[: len(arrays)]
        own_ref, far_ref, away_ref = refs[len(arrays) :]
        z, y, g = place_ref[0], place_ref[1], place_ref[2]
        att, d_query = att_ref[...], dq_ref[...]
        for far in range(pairs):
            for side in range(2):
                (of_query, query_at), (of_out, out_at) = blocks[2 * far + side]
                weight = block_refs[of_query][query_at : query_at + part, :]
                out_weight = block_refs[of_out][out_at : out_at + width, :]
                origin = lax.rem(z - far + pairs, pairs) * 2 + (y ^ side)
                flip = (origin // per_piece) ^ g
                start = lax.rem(origin, per_piece) * part
                columns = pl.ds(aligned(start, 128), part)
                beyond = pl.ds(aligned(start + piece, 128), part)
                added = mm(att, out_weight).astype(BF)
                d_normed = contract_last(d_query, weight).astype(BF)
                places = ((own_ref, columns), (away_ref, columns), (far_ref, columns), (away_ref, beyond))
                for number, (target_ref, to) in enumerate(places):

                    @pl.when(flip == number)
                    def _(target_ref=target_ref, to=to, added=added, d_normed=d_normed):
                        target_ref[0, :, to] = added
                        target_ref[1, :, to] = d_normed

    out = [shaped((2, tokens, piece)), shaped((2, tokens, piece)), shaped((2, tokens, 2 * piece))]
    return call(body, out, (place, attended, d_queries, *arrays), 1)


def weight_grads(tiles, both_blocks, known, pairs):
    part = tiles[0].shape[-1]
    given = [k for k, block in enumerate(both_blocks) if block is not None]
    arrays, blocks = pieces_of([both_blocks[k] for k in given])
    width = arrays[0].shape[-1]
    known = known or []

    def body(*refs):
        tile_refs, known_refs = refs[:4], refs[4 : 4 + len(known)]
        block_refs, (query_ref, out_ref) = refs[4 + len(known) : -2], refs[-2:]
        query_grad = known_refs[0][...] if known else jnp.zeros((part, width), F32)
        out_grad = known_refs[1][...] if known else jnp.zeros((width, part), F32)
        for k, ((number, at),) in zip(given, blocks):
            side, far = divmod(k, pairs)
            block = block_refs[number]
            normed, grad = (
                jnp.concatenate([r[far, side, which] for r in tile_refs], axis=0)
                for which in range(2)
            )
            out_grad += contract_first(block[at], grad)
            query_grad += contract_first(normed, block[at + 1])
        query_ref[...] = query_grad
        out_ref[...] = out_grad

    out = [shaped((part, width), F32), shaped((width, part), F32)]
    return call(body, out, (*tiles, *known, *arrays), 0)


def local(
    caption_states,
    caption_lens,
    text_gain,
    text_query,
    text_key,
    text_value,
    text_bias,
    text_out,
    final_gain,
    cross_key,
    cross_value,
    video_states,
    video_counts,
    sample_caption,
    cross_query,
    cross_out,
    out_grad,
):
    column = lax.axis_index("fsdp")
    g = lax.axis_index("grp")
    pairs = lax.axis_size("fsdp") // 2
    z, y = column // 2, column % 2
    place = jnp.stack([z, y, g]).astype(jnp.int32)
    caps_local, cap_len, text_width = caption_states.shape
    tokens, model_width = video_states.shape
    width_local = cross_key.shape[1]
    part = cross_query.shape[0]

    states = caption_states.reshape(cap_len, text_width)
    quarter_rows = cap_len // 4

    first = [fsend(cross_query, 1, 0), fsend(cross_out, 1, 0)]
    side_key, side_value = fsend(cross_key, 0, 1), fsend(cross_value, 0, 1)
    projected = project_text(states, text_gain, (text_query, text_key, text_value))
    kept, away = attend_text(projected, text_bias, text_out, place, caption_lens)
    kept, away = after((kept, away), first, side_key, side_value)
    got = gsend(away, 1)
    ring = [None, jnp.concatenate(first, axis=0)]
    side_first = fsend(jnp.concatenate([cross_query, cross_out, *first], axis=0), 0, 1)
    ring.append(fsend(ring[1], 1, 0))
    sent = (kept[quarter_rows:].astype(F32) + got[quarter_rows:].astype(F32)).astype(BF)
    over_x = gsend(sent, 2)
    normed, mean, inverse, own_tiles, other_tiles = prepare_video(
        after(video_states, sent), out_grad, place, pairs, part
    )
    pieces = encode_rows(
        states, kept, got, after(over_x, normed), final_gain, place, pairs
    )

    mine = jnp.stack([fsend(p, far, 0) if far else p for far, p in enumerate(pieces)])
    mine = after(mine, ring[2])
    over_x = gsend(mine, 2)
    parts = [mine, gsend(mine, 1), over_x, gsend(over_x, 1)]
    current = after(ring[2], mine)
    for far in range(3, pairs):
        current = fsend(current, 1, 0)
        ring.append(current)
    parts[3] = after(parts[3], side_first)
    kv_partial = project_captions(
        parts, cross_key, cross_value, side_key, side_value, place, pairs
    )
    kv_partial = after(tuple(kv_partial), ring[-1])
    kv_sum = kv_partial[0].astype(F32)
    for far in range(1, pairs):
        kv_sum += fsend(kv_partial[far], pairs - far, 0).astype(F32)
    side_later = [fsend(w, 0, 1) for w in ring[2:]]
    other_tiles = fsend(other_tiles, 0, 1)
    kv_sum = after(kv_sum.astype(BF), side_later[0])
    kv_blocks = gather_direct(kv_sum)
    kv_blocks[4] = after(kv_blocks[4], side_later, other_tiles)

    step = part + width_local
    blocks = []
    for far, held in enumerate(ring):
        side, start = (side_first, far * step) if far < 2 else (side_later[far - 2], 0)
        here = ((held, 0), (held, part)) if far else ((cross_query, 0), (cross_out, 0))
        blocks += [here, ((side, start), (side, start + part))]
    queries, d_attended, column_sum = project_rows(
        normed, after(out_grad, kv_blocks[4]), blocks, place, pairs, part
    )

    tiles = jnp.stack([own_tiles, other_tiles], axis=1)
    over_z = [fsend(after(tiles[far], kv_blocks[4]), far, 0) for far in range(1, pairs)]
    over_z = [tiles[0]] + over_z

    both, attended, d_queries, row_sums, slots = attend(
        queries,
        d_attended,
        column_sum,
        kv_blocks,
        place,
        video_counts,
        sample_caption,
        caption_lens,
        pairs,
    )

    side_slots = fsend(slots, 0, 1)
    sides = [fsend(both, 0, 1)]
    first, over_z = after((both, over_z))
    tiles = jnp.stack(over_z)
    late = [both, fsend(first, 1, 0)]
    sides.append(fsend(after(late[1], side_slots), 0, 1))
    for far in range(2, pairs):
        late.append(fsend(after(late[-1], sides[0]) if far == pairs - 1 else late[-1], 1, 0))
    row_sums = row_sums + gsend(row_sums, 1)
    tiles = after(tiles, row_sums)
    tiles_x = gsend(tiles, 2)
    tiles_core = gsend(tiles, 1)
    own, far_piece, away = project_back(
        after(attended, row_sums), d_queries, blocks, place, pairs, part
    )
    tiles = [tiles, tiles_core, tiles_x, gsend(tiles_x, 1)]
    stage = (side_slots, sides, late, tiles, row_sums, away)
    side_slots, sides, late, tiles, row_sums, away = after(stage)

    joint = jnp.stack(late[2:]).reshape(-1, tokens, width_local)
    joint = fsend(joint, 0, 1)
    got = gsend(away, 1)
    sums_x = gsend(row_sums, 2)
    width = model_width // 4
    sent = (far_piece.astype(F32) + got[:, :, width:].astype(F32)).astype(BF)
    far_sum = gsend(after(sent, sums_x), 2)
    terms = caption_terms(
        slots, side_slots, place, video_counts, sample_caption, tokens, pairs
    )
    kv_parts = [fsend(terms[far], far, 0) for far in range(1, pairs)]
    kv_grads = (terms[0] + sum(p.astype(F32) for p in kv_parts)).astype(BF)[None]
    key_grad = kv_grads[:, :, :width_local]
    value_grad = kv_grads[:, :, width_local:]
    tiles = after(tiles, far_sum)
    here = [((block, 0),) for block in late]
    there = [((block, 0),) for block in sides]
    there += [((joint, 2 * k),) for k in range(pairs - 2)]
    known = weight_grads(tiles, here + there[:2], None, pairs)
    total = own.astype(F32) + got[:, :, :width].astype(F32) + far_sum.astype(F32)
    row_sums = (row_sums + sums_x) / model_width
    video = quarter(video_states, g, 1).astype(F32)
    updated = (video + total[0]).astype(BF)
    video_hat = (video - mean) * inverse
    input_grad = (
        quarter(out_grad, g, 1).astype(F32)
        + inverse * (total[1] - row_sums[:, 0:1] - video_hat * row_sums[:, 1:2])
    ).astype(BF)
    query_grad, out_weight_grad = weight_grads(
        tiles, [None] * (pairs + 2) + there[2:], known, pairs
    )
    return (updated, input_grad, query_grad, out_weight_grad, key_grad, value_grad)


def local_of(*arrays):
    whole_tiles = arrays[14].shape[0] % 128 == 0 and arrays[0].shape[0] == 1
    return local(*arrays) if whole_tiles else local_general(*arrays)


def solution(mesh):
    in_specs = (
        P("fsdp", None, None),
        P(),
        P(),
        P(None, "grp"),
        P(None, "grp"),
        P(None, "grp"),
        P("grp", None, None),
        P("grp", None),
        P(),
        P("fsdp", "grp"),
        P("fsdp", "grp"),
        P("fsdp", None),
        P(),
        P(),
        P("fsdp", "grp"),
        P("grp", "fsdp"),
        P("fsdp", None),
    )
    out_specs = (
        P("fsdp", "grp"),
        P("fsdp", "grp"),
        P("fsdp", "grp"),
        P("grp", "fsdp"),
        P("fsdp", None, "grp"),
        P("fsdp", None, "grp"),
    )
    return jax.shard_map(
        local_of, mesh=mesh, in_specs=in_specs, out_specs=out_specs, check_vma=False
    )
```

```python
import math

import jax
import jax.numpy as jnp
from jax import lax
from jax.experimental import pallas as pl
from jax.experimental.pallas import tpu as pltpu
from jax.sharding import PartitionSpec as P

HEAD_SIZE = 128
BF = jnp.bfloat16
F32 = jnp.float32
SLOTS = 3
VMEM_BYTES = 60 * 1024 * 1024
SPARE_BYTES = 8 * 1024 * 1024
SMALL = pl.CostEstimate(flops=1, bytes_accessed=1, transcendentals=0)


def rms_scale(values, gain):
    mean_square = jnp.mean(values * values, axis=-1, keepdims=True)
    return values * lax.rsqrt(mean_square + 1e-06) * gain


def mm(left, right):
    return jnp.dot(left, right, preferred_element_type=F32)


def contract_last(left, right):
    return lax.dot_general(left, right, (((1,), (1,)), ((), ())), preferred_element_type=F32)


def contract_first(left, right):
    return lax.dot_general(left, right, (((0,), (0,)), ((), ())), preferred_element_type=F32)


def fsend(block, far, side):
    size = lax.axis_size("fsdp")
    pairs = size // 2
    perm = [(s, ((s // 2 + far) % pairs) * 2 + ((s % 2) ^ side)) for s in range(size)]
    return lax.ppermute(block, "fsdp", perm)


def gsend(block, flip):
    return lax.ppermute(block, "grp", [(s, s ^ flip) for s in range(lax.axis_size("grp"))])


def gather_ring(block):
    blocks = []
    current = block
    for far in range(lax.axis_size("fsdp") // 2):
        if far:
            current = fsend(current, 1, 0)
        blocks += [current, fsend(current, 0, 1)]
    return blocks


def gather_direct(block):
    blocks = []
    for far in range(lax.axis_size("fsdp") // 2):
        current = fsend(block, far, 0) if far else block
        blocks += [current, fsend(current, 0, 1)]
    return blocks


def quarter(array, index, axis=0):
    size = array.shape[axis] // 4
    return lax.dynamic_slice_in_dim(array, index * size, size, axis)


def grp_scatter(partial, g, axis):
    away = [quarter(partial, g ^ 1, axis), quarter(partial, g ^ 3, axis)]
    kept = [quarter(partial, g, axis), quarter(partial, g ^ 2, axis)]
    got = gsend(jnp.stack(away).astype(BF), 1)
    far = gsend((kept[1] + got[1].astype(F32)).astype(BF), 2)
    return kept[0] + got[0].astype(F32) + far.astype(F32)


def local_general(
    caption_states,
    caption_lens,
    text_gain,
    text_query,
    text_key,
    text_value,
    text_bias,
    text_out,
    final_gain,
    cross_key,
    cross_value,
    video_states,
    video_counts,
    sample_caption,
    cross_query,
    cross_out,
    out_grad,
):
    column = lax.axis_index("fsdp")
    g = lax.axis_index("grp")
    fsdp = lax.axis_size("fsdp")
    pairs = fsdp // 2
    z, y = column // 2, column % 2
    caps_local, cap_len, text_width = caption_states.shape
    tokens, model_width = video_states.shape
    width_local = cross_key.shape[1]
    cross_local = width_local // HEAD_SIZE
    query_rows = cross_query.shape[0]

    def source(far, side):
        return ((z - far) % pairs) * 2 + (y ^ side)

    def target(far, side):
        return ((z + far) % pairs) * 2 + (y ^ side)

    query_blocks = gather_ring(cross_query)
    out_blocks = gather_ring(cross_out)
    full_query = jnp.zeros((model_width, width_local), BF)
    full_out = jnp.zeros((width_local, model_width), BF)
    for far in range(pairs):
        for side in range(2):
            start = source(far, side) * query_rows
            full_query = lax.dynamic_update_slice(
                full_query, query_blocks[2 * far + side], (start, jnp.int32(0))
            )
            full_out = lax.dynamic_update_slice(
                full_out, out_blocks[2 * far + side], (jnp.int32(0), start)
            )

    own_kv = jnp.concatenate([cross_key, cross_value], axis=1)
    other_kv = fsend(own_kv, 0, 1)
    pair_kv = jnp.concatenate(
        [jnp.where(y == 0, own_kv, other_kv), jnp.where(y == 0, other_kv, own_kv)], axis=0
    )

    local_lens = lax.dynamic_slice_in_dim(caption_lens, column * caps_local, caps_local)
    flat_states = caption_states.reshape(caps_local * cap_len, text_width).astype(F32)
    text_normed = rms_scale(flat_states, text_gain).astype(BF)
    local_heads = text_bias.shape[0]
    head_width = text_query.shape[1] // local_heads

    def heads_of(weight):
        return mm(text_normed, weight).astype(BF).reshape(
            caps_local, cap_len, local_heads, head_width
        )

    text_queries = heads_of(text_query)
    text_keys = heads_of(text_key)
    text_values = heads_of(text_value)
    text_scores = (
        jnp.einsum("cihd,cjhd->chij", text_queries, text_keys, preferred_element_type=F32)
        + text_bias[None]
    )
    key_valid = jnp.arange(cap_len, dtype=jnp.int32)[None, :] < local_lens[:, None]
    exp_scores = jnp.where(key_valid[:, None, None, :], jnp.exp(text_scores), 0.0)
    text_weights = (exp_scores / jnp.sum(exp_scores, axis=-1, keepdims=True)).astype(BF)
    text_mixed = jnp.einsum(
        "chij,cjhd->cihd", text_weights, text_values, preferred_element_type=F32
    )
    text_mixed = text_mixed.astype(BF).reshape(caps_local * cap_len, local_heads * head_width)
    partial_text = mm(text_mixed, text_out)
    text_rows = grp_scatter(partial_text, g, 0)
    encoded = rms_scale(quarter(flat_states, g) + text_rows, final_gain).astype(BF)

    part = text_width // pairs
    pieces = [
        lax.dynamic_slice_in_dim(encoded, ((z + far) % pairs) * part, part, 1)
        for far in range(pairs)
    ]
    mine = jnp.stack([fsend(p, far, 0) if far else p for far, p in enumerate(pieces)])
    over_x = jnp.concatenate([mine[:, None], gsend(mine, 2)[:, None]], axis=1)
    over_core = jnp.stack([over_x, gsend(over_x, 1)], axis=2)
    kv_partial = mm(over_core.reshape(-1, part), pair_kv).reshape(pairs, cap_len, 2 * width_local)
    kv_sum = kv_partial[0]
    for far in range(1, pairs):
        kv_sum += fsend(kv_partial[far].astype(BF), pairs - far, 0).astype(F32)
    kv_rows = kv_sum.astype(BF).reshape(4, cap_len // 4, 2 * width_local)
    order = jnp.arange(4, dtype=jnp.int32) ^ g
    cap_kv = jnp.concatenate(
        [lax.dynamic_slice_in_dim(kv_rows, order[k], 1, 0) for k in range(4)], axis=0
    ).reshape(cap_len, 2 * width_local)
    all_kv = jnp.stack(gather_direct(cap_kv))

    video = video_states.astype(F32)
    center = video - jnp.mean(video, axis=-1, keepdims=True)
    inverse = lax.rsqrt(jnp.mean(center * center, axis=-1, keepdims=True) + 1e-06)
    video_hat = center * inverse
    video_normed = video_hat.astype(BF)

    both = jnp.stack([quarter(video_normed, g), quarter(out_grad, g)])
    tiles = []
    for far in range(pairs):
        for side in range(2):
            tile = lax.dynamic_slice_in_dim(both, target(far, side) * query_rows, query_rows, 2)
            tiles.append(fsend(tile, far, side) if far or side else tile)
    tiles = jnp.stack(tiles)
    tiles_x = jnp.stack([tiles, gsend(tiles, 2)], axis=2)
    tiles_all = jnp.stack([tiles_x, gsend(tiles_x, 1)], axis=3)
    normed_tile = tiles_all[:, 0].reshape(-1, query_rows)
    grad_tile = tiles_all[:, 1].reshape(-1, query_rows)

    caption_total = all_kv.shape[0]
    positions = column * tokens + jnp.arange(tokens, dtype=jnp.int32)
    sample_end = jnp.cumsum(video_counts)
    token_sample = jnp.sum((sample_end[None, :] <= positions[:, None]).astype(jnp.int32), axis=1)
    slot_count = 3
    slot_sample = token_sample[0] + jnp.arange(slot_count, dtype=jnp.int32)
    slot_valid = slot_sample < caption_total
    slot_clipped = jnp.minimum(slot_sample, caption_total - 1)
    numbers = jnp.arange(caption_total, dtype=jnp.int32)
    slot_pick = slot_clipped[:, None] == numbers[None, :]
    slot_caption = jnp.sum(jnp.where(slot_pick, sample_caption[None, :], 0), axis=1)
    caption_pick = slot_caption[:, None] == numbers[None, :]
    slot_lens = jnp.sum(jnp.where(caption_pick, caption_lens[None, :], 0), axis=1)
    slot_member = token_sample[None, :] == slot_sample[:, None]
    member_float = slot_member.astype(F32)
    member_half = slot_member.astype(BF)
    slot_entry = ((z - slot_caption // 2) % pairs) * 2 + ((slot_caption % 2) ^ y)
    slot_kv = jnp.take(all_kv, slot_entry, axis=0)
    slot_keys = slot_kv[..., :width_local].reshape(slot_count, cap_len, cross_local, HEAD_SIZE)
    slot_values = slot_kv[..., width_local:].reshape(slot_count, cap_len, cross_local, HEAD_SIZE)
    token_lens = jnp.sum(jnp.where(slot_member, slot_lens[:, None], 0), axis=0)

    query_sum = mm(video_normed, full_query)
    queries = query_sum.astype(BF)
    d_attended = contract_last(out_grad, full_out).astype(BF).reshape(
        tokens, cross_local, HEAD_SIZE
    )
    score_scale = 1.0 / math.sqrt(HEAD_SIZE)
    query_heads = queries.reshape(tokens, cross_local, HEAD_SIZE)
    slot_scores = jnp.einsum("thd,kjhd->kthj", query_heads, slot_keys, preferred_element_type=F32)
    scores = jnp.sum(member_float[:, :, None, None] * slot_scores, axis=0) * score_scale
    token_valid = (jnp.arange(cap_len, dtype=jnp.int32)[None, :] < token_lens[:, None])[:, None, :]
    exp_video = jnp.where(token_valid, jnp.exp(scores), 0.0)
    weights = exp_video / jnp.sum(exp_video, axis=-1, keepdims=True)
    probs = weights.astype(BF)
    masked_probs = member_half[:, :, None, None] * probs[None]
    attended = jnp.einsum("kthj,kjhd->thd", masked_probs, slot_values, preferred_element_type=F32)
    attended = attended.astype(BF).reshape(tokens, width_local)

    def reorder(array):
        return jnp.concatenate([quarter(array, order[k]) for k in range(4)], axis=0)

    all_attended = jnp.concatenate(gather_direct(reorder(attended)), axis=0)
    out_weight_grad = contract_first(all_attended, grad_tile)

    out_share = grp_scatter(mm(attended, full_out), g, 1)
    updated = (quarter(video, g, 1) + out_share).astype(BF)

    slot_dprobs = jnp.einsum("thd,kjhd->kthj", d_attended, slot_values, preferred_element_type=F32)
    d_probs = jnp.sum(member_float[:, :, None, None] * slot_dprobs, axis=0)
    d_scores = (
        weights * (d_probs - jnp.sum(weights * d_probs, axis=-1, keepdims=True)) * score_scale
    ).astype(BF)
    masked_scores = member_half[:, :, None, None] * d_scores[None]
    d_queries = jnp.einsum("kthj,kjhd->thd", masked_scores, slot_keys, preferred_element_type=F32)
    d_queries = d_queries.astype(BF).reshape(tokens, width_local)
    all_d_queries = jnp.concatenate(gather_direct(reorder(d_queries)), axis=0)
    query_grad = contract_first(normed_tile, all_d_queries)

    key_slots = jnp.einsum("kthj,thd->kjhd", masked_scores, query_heads, preferred_element_type=F32)
    value_slots = jnp.einsum("kthj,thd->kjhd", masked_probs, d_attended, preferred_element_type=F32)
    slot_terms = jnp.concatenate(
        [
            key_slots.reshape(slot_count, cap_len, width_local),
            value_slots.reshape(slot_count, cap_len, width_local),
        ],
        axis=-1,
    )

    def caption_terms(far, side):
        picked = (slot_caption == target(far, side)) & slot_valid
        return jnp.sum(jnp.where(picked[:, None, None], slot_terms, 0.0), axis=0)

    away = jnp.stack([caption_terms(far, 1).astype(BF) for far in range(pairs)])
    got = fsend(away, 0, 1).astype(F32)
    kv_grads = caption_terms(0, 0) + got[0]
    for far in range(1, pairs):
        kv_grads += fsend((caption_terms(far, 0) + got[far]).astype(BF), far, 0).astype(F32)
    kv_grads = kv_grads.astype(BF)[None]
    key_grad = kv_grads[:, :, :width_local]
    value_grad = kv_grads[:, :, width_local:]

    d_wide = d_queries.astype(F32)
    column_sum = jnp.sum(full_query.astype(F32), axis=0)
    row_sums = jnp.stack(
        [jnp.sum(d_wide * column_sum, axis=-1), jnp.sum(d_wide * query_sum, axis=-1)]
    )
    row_sums = row_sums + gsend(row_sums, 1)
    row_sums = (row_sums + gsend(row_sums, 2)) / model_width
    d_share = grp_scatter(contract_last(d_queries, full_query), g, 1)
    input_grad = (
        quarter(out_grad, g, 1).astype(F32)
        + inverse
        * (d_share - row_sums[0][:, None] - quarter(video_hat, g, 1) * row_sums[1][:, None])
    ).astype(BF)
    return (updated, input_grad, query_grad, out_weight_grad, key_grad, value_grad)


def after(value, *others):
    return lax.optimization_barrier((value, *others))[0]


def call(body, out_shape, operands, scalars, scratch=()):
    specs = [pl.BlockSpec(memory_space=pltpu.SMEM)] * scalars
    specs += [pl.BlockSpec(memory_space=pltpu.VMEM)] * (len(operands) - scalars)
    held = (*operands[scalars:], *jax.tree.leaves(out_shape), *scratch)
    held_bytes = sum(math.prod(a.shape) * jnp.dtype(a.dtype).itemsize for a in held)
    return pl.pallas_call(
        body,
        out_shape=out_shape,
        in_specs=specs,
        out_specs=jax.tree.map(lambda _: pl.BlockSpec(memory_space=pltpu.VMEM), out_shape),
        scratch_shapes=list(scratch),
        compiler_params=pltpu.CompilerParams(vmem_limit_bytes=held_bytes + SPARE_BYTES),
        cost_estimate=SMALL,
    )(*operands)


def shaped(shape, dtype=BF):
    return jax.ShapeDtypeStruct(shape, dtype)


def aligned(start, unit):
    return pl.multiple_of(start, unit)


def project_text(states, gain, weights, steps=4):
    rows, depth = states.shape
    width = weights[0].shape[1]
    chunk = depth // steps

    def body(states_ref, gain_ref, wq_ref, wk_ref, wv_ref, out_ref, normed_ref, total_ref):
        step = pl.program_id(0)

        @pl.when(step == 0)
        def _():
            for at in range(0, rows, 16):
                values = states_ref[at : at + 16, :].astype(F32)
                normed_ref[at : at + 16, :] = rms_scale(values, gain_ref[...]).astype(BF)
            total_ref[...] = jnp.zeros_like(total_ref)

        here = normed_ref[:, pl.ds(aligned(step * chunk, chunk), chunk)]
        for k, weight_ref in enumerate((wq_ref, wk_ref, wv_ref)):
            total_ref[:, k * width : (k + 1) * width] += mm(here, weight_ref[...])

        @pl.when(step == steps - 1)
        def _():
            out_ref[...] = total_ref[...].astype(BF)

    whole = lambda shape: pl.BlockSpec(shape, lambda i: (0,) * len(shape))
    return pl.pallas_call(
        body,
        grid=(steps,),
        out_shape=shaped((rows, 3 * width)),
        in_specs=[whole((rows, depth)), whole((1, depth))]
        + [pl.BlockSpec((chunk, width), lambda i: (i, 0))] * 3,
        out_specs=whole((rows, 3 * width)),
        scratch_shapes=[pltpu.VMEM((rows, depth), BF), pltpu.VMEM((rows, 3 * width), F32)],
        compiler_params=pltpu.CompilerParams(vmem_limit_bytes=VMEM_BYTES),
        cost_estimate=SMALL,
    )(states, gain.reshape(1, -1), *weights)


def attend_text(projected, bias, text_out, place, lens, steps=4):
    rows = projected.shape[0]
    heads = bias.shape[0]
    inner, depth = text_out.shape
    size = inner // heads
    quarter_rows = rows // 4
    chunk = depth // steps

    def body(place_ref, len_ref, qkv_ref, bias_ref, out_ref, kept_ref, away_ref, held_ref, mixed_ref):
        @pl.when(pl.program_id(0) == 0)
        def _():
            g = place_ref[2]
            length = len_ref[place_ref[0] * 2 + place_ref[1]]
            live = lax.broadcasted_iota(jnp.int32, (rows, rows), 1) < length
            for head in range(heads):
                query, key, value = (
                    qkv_ref[:, k * inner + head * size : k * inner + (head + 1) * size]
                    for k in range(3)
                )
                grown = jnp.where(live, jnp.exp(contract_last(query, key) + bias_ref[head]), 0.0)
                weights = grown * (1.0 / jnp.sum(grown, axis=-1, keepdims=True))
                held_ref[:, head * size : (head + 1) * size] = mm(weights.astype(BF), value).astype(BF)
            for k, to in ((0, 0), (2, 1), (1, 2), (3, 3)):
                rows_from = pl.ds(aligned((g ^ k) * quarter_rows, quarter_rows), quarter_rows)
                mixed_ref[to * quarter_rows : (to + 1) * quarter_rows, :] = held_ref[rows_from, :]

        product = mm(mixed_ref[...], out_ref[...]).astype(BF)
        kept_ref[...] = product[: rows // 2]
        away_ref[...] = product[rows // 2 :]

    whole = lambda shape: pl.BlockSpec(shape, lambda i: (0,) * len(shape))
    return pl.pallas_call(
        body,
        grid=(steps,),
        out_shape=[shaped((rows // 2, depth))] * 2,
        in_specs=[pl.BlockSpec(memory_space=pltpu.SMEM)] * 2
        + [whole(projected.shape), whole(bias.shape)]
        + [pl.BlockSpec((inner, chunk), lambda i: (0, i))],
        out_specs=[pl.BlockSpec((rows // 2, chunk), lambda i: (0, i))] * 2,
        scratch_shapes=[pltpu.VMEM((rows, inner), BF), pltpu.VMEM((rows, inner), BF)],
        compiler_params=pltpu.CompilerParams(vmem_limit_bytes=VMEM_BYTES),
        cost_estimate=SMALL,
    )(place, lens, projected, bias, text_out)


def encode_rows(states, kept, got, far, gain, place, pairs):
    quarter_rows = states.shape[0] // 4
    width = states.shape[1]
    depth = width // pairs

    def body(place_ref, states_ref, kept_ref, got_ref, far_ref, gain_ref, *refs):
        piece_refs, encoded_ref = refs[:-1], refs[-1]
        z, g = place_ref[0], place_ref[2]
        mine = pl.ds(aligned(g * quarter_rows, quarter_rows), quarter_rows)
        total = states_ref[mine, :].astype(F32) + far_ref[...].astype(F32)
        total += kept_ref[:quarter_rows, :].astype(F32) + got_ref[:quarter_rows, :].astype(F32)
        encoded_ref[...] = rms_scale(total, gain_ref[...]).astype(BF)
        for far_by, piece in enumerate(piece_refs):
            to = lax.rem(z + far_by, pairs)
            piece[...] = encoded_ref[:, pl.ds(aligned(to * depth, 128), depth)]

    out = [shaped((quarter_rows, depth))] * pairs
    operands = (place, states, kept, got, far, gain.reshape(1, -1))
    return call(body, out, operands, 1, [pltpu.VMEM((quarter_rows, width), BF)])


def pieces_of(pairs_of_blocks):
    arrays, listed = [], []
    for entry in pairs_of_blocks:
        numbers = []
        for array, start in entry:
            if not any(array is held for held in arrays):
                arrays.append(array)
            numbers.append((next(k for k, held in enumerate(arrays) if held is array), start))
        listed.append(numbers)
    return arrays, listed


def prepare_video(video_states, out_grad, place, pairs, part):
    tokens, model_width = video_states.shape
    rows = tokens // 4

    def body(place_ref, video_ref, grad_ref, normed_ref, mean_ref, inverse_ref, *tile_refs):
        @pl.loop(0, tokens // 32)
        def _(step):
            here = pl.ds(aligned(step * 32, 32), 32)
            values = video_ref[here, :].astype(F32)
            mean = jnp.mean(values, axis=-1, keepdims=True)
            center = values - mean
            inverse = lax.rsqrt(jnp.mean(center * center, axis=-1, keepdims=True) + 1e-06)
            normed_ref[here, :] = (center * inverse).astype(BF)
            mean_ref[here, :] = mean
            inverse_ref[here, :] = inverse

        z, y, g = place_ref[0], place_ref[1], place_ref[2]
        mine = pl.ds(aligned(g * rows, rows), rows)
        for far in range(pairs):
            for side in range(2):
                to = lax.rem(z + far, pairs) * 2 + (y ^ side)
                columns = pl.ds(aligned(to * part, 128), part)
                tile_refs[side][far, 0] = normed_ref[mine, columns]
                tile_refs[side][far, 1] = grad_ref[mine, columns]

    out = [shaped((tokens, model_width)), shaped((tokens, 1), F32), shaped((tokens, 1), F32)]
    out += [shaped((pairs, 2, rows, part))] * 2
    return call(body, out, (place, video_states, out_grad), 1)


def project_rows(normed, out_grad, blocks, place, pairs, part):
    tokens = normed.shape[0]
    arrays, blocks = pieces_of(blocks)
    width = arrays[0].shape[1]

    def body(place_ref, normed_ref, grad_ref, *refs):
        block_refs, (query_ref, d_ref, sum_ref) = refs[:-3], refs[-3:]
        z, y = place_ref[0], place_ref[1]
        query = jnp.zeros((tokens, width), F32)
        d_attended = jnp.zeros((tokens, width), F32)
        total = jnp.zeros((1, width), F32)
        for far in range(pairs):
            for side in range(2):
                (of_query, query_at), (of_out, out_at) = blocks[2 * far + side]
                origin = lax.rem(z - far + pairs, pairs) * 2 + (y ^ side)
                columns = pl.ds(aligned(origin * part, 128), part)
                weight = block_refs[of_query][query_at : query_at + part, :]
                out_weight = block_refs[of_out][out_at : out_at + width, :]
                query += mm(normed_ref[:, columns], weight)
                d_attended += contract_last(grad_ref[:, columns], out_weight)
                total += jnp.sum(weight.astype(F32), axis=0, keepdims=True)
        query_ref[...] = query.astype(BF)
        d_ref[...] = d_attended.astype(BF)
        sum_ref[...] = total

    out = [shaped((tokens, width)), shaped((tokens, width)), shaped((1, width), F32)]
    return call(body, out, (place, normed, out_grad, *arrays), 1)


def project_captions(parts, own_key, own_value, side_key, side_value, place, pairs):
    quarter_rows, depth = parts[0].shape[1:]
    half = depth // 2
    width = own_key.shape[1]

    def body(place_ref, *refs):
        part_refs = refs[:4]
        key_ref, value_ref, side_key_ref, side_value_ref = refs[4:8]
        out_refs = refs[8:]
        y = place_ref[1]
        mine = pl.ds(aligned(y * half, 128), half)
        theirs = pl.ds(aligned((1 - y) * half, 128), half)
        own = jnp.concatenate([r[far, :, mine] for far in range(pairs) for r in part_refs], 0)
        other = jnp.concatenate([r[far, :, theirs] for far in range(pairs) for r in part_refs], 0)
        keys = mm(own, key_ref[...]) + mm(other, side_key_ref[...])
        values = mm(own, value_ref[...]) + mm(other, side_value_ref[...])
        for far in range(pairs):
            rows = slice(far * 4 * quarter_rows, (far + 1) * 4 * quarter_rows)
            out_refs[far][:, :width] = keys[rows].astype(BF)
            out_refs[far][:, width:] = values[rows].astype(BF)

    out = [shaped((4 * quarter_rows, 2 * width))] * pairs
    operands = (place, *parts, own_key, own_value, side_key, side_value)
    return call(body, out, operands, 1)


def slots_of(count_ref, caption_ref, base, captions):
    def find(sample, carry):
        total, first, start = carry
        total = total + count_ref[sample]
        past = total <= base
        return total, first + past.astype(jnp.int32), jnp.where(past, total, start)

    zero = jnp.int32(0)
    _, first, start = lax.fori_loop(0, captions, find, (zero, zero, zero))
    found, edge = [], start - base
    for slot in range(SLOTS):
        valid = first + slot < captions
        sample = jnp.minimum(first + slot, captions - 1)
        end = edge + jnp.where(valid, count_ref[sample], 0)
        found.append((edge, end, caption_ref[sample], valid))
        edge = end
    return found


def attend(queries, d_attended, column_sum, kv_blocks, place, counts, sample_caption, lens, pairs):
    tokens, width = queries.shape
    cap_len = kv_blocks[0].shape[0]
    heads = width // HEAD_SIZE
    captions = counts.shape[0]
    keys_wide = SLOTS * cap_len
    cap_quarter, row_quarter = cap_len // 4, tokens // 4
    scale = 1.0 / math.sqrt(HEAD_SIZE)

    def body(place_ref, count_ref, caption_ref, len_ref, q_ref, da_ref, sum_ref, *refs):
        block_refs = refs[: len(kv_blocks)]
        both_ref, att_ref, dq_ref, rows_ref, slot_ref, kv_ref = refs[len(kv_blocks) :]
        z, y, g = place_ref[0], place_ref[1], place_ref[2]
        low, high, length = [], [], []
        found = slots_of(count_ref, caption_ref, (z * 2 + y) * tokens, captions)
        for slot, (start, end, caption, _) in enumerate(found):
            low.append(start)
            high.append(end)
            length.append(len_ref[caption])
            entry = lax.rem(z - caption // 2 + pairs, pairs) * 2 + (lax.rem(caption, 2) ^ y)
            for number, block in enumerate(block_refs):

                @pl.when(entry == number)
                def _(slot=slot, block=block):
                    kv_ref[slot * cap_len : (slot + 1) * cap_len, :] = block[...]

        token = lax.broadcasted_iota(jnp.int32, (tokens, keys_wide), 0)
        column = lax.broadcasted_iota(jnp.int32, (tokens, keys_wide), 1)
        slot_of = column // cap_len
        inside = column % cap_len
        key = ((inside // cap_quarter) ^ g) * cap_quarter + inside % cap_quarter

        def of_slot(values):
            return jnp.where(slot_of == 0, values[0], jnp.where(slot_of == 1, values[1], values[2]))

        live = (token >= of_slot(low)) & (token < of_slot(high)) & (key < of_slot(length))
        first_sum = jnp.zeros((tokens, 1), F32)
        second_sum = jnp.zeros((tokens, 1), F32)
        for head in range(heads):
            at = slice(head * HEAD_SIZE, (head + 1) * HEAD_SIZE)
            at_value = slice(width + head * HEAD_SIZE, width + (head + 1) * HEAD_SIZE)
            query, d_att = q_ref[:, at], da_ref[:, at]
            keys, values = kv_ref[:, at], kv_ref[:, at_value]
            grown = jnp.where(live, jnp.exp(contract_last(query, keys) * scale), 0.0)
            weights = grown * (1.0 / jnp.sum(grown, axis=-1, keepdims=True))
            probs = weights.astype(BF)
            d_probs = contract_last(d_att, values)
            mixed = jnp.sum(weights * d_probs, axis=-1, keepdims=True)
            d_scores = (weights * (d_probs - mixed) * scale).astype(BF)
            att_ref[:, at] = mm(probs, values).astype(BF)
            d_query = mm(d_scores, keys).astype(BF)
            dq_ref[:, at] = d_query
            d_wide = d_query.astype(F32)
            first_sum += jnp.sum(d_wide * sum_ref[:, at], axis=-1, keepdims=True)
            second_sum += jnp.sum(d_wide * query.astype(F32), axis=-1, keepdims=True)
            key_grad = contract_first(d_scores, query).astype(BF)
            value_grad = contract_first(probs, d_att).astype(BF)
            for slot in range(SLOTS):
                for part in range(4):
                    held = slice(
                        slot * cap_len + part * cap_quarter, slot * cap_len + (part + 1) * cap_quarter
                    )
                    to = pl.ds(aligned((part ^ g) * cap_quarter, cap_quarter), cap_quarter)
                    slot_ref[slot, to, at] = key_grad[held]
                    slot_ref[slot, to, at_value] = value_grad[held]

        rows_ref[:, 0:1] = first_sum
        rows_ref[:, 1:2] = second_sum
        for part in range(4):
            rows = pl.ds(aligned((part ^ g) * row_quarter, row_quarter), row_quarter)
            to = slice(part * row_quarter, (part + 1) * row_quarter)
            both_ref[0, to, :] = att_ref[rows, :]
            both_ref[1, to, :] = dq_ref[rows, :]

    out = [
        shaped((2, tokens, width)),
        shaped((tokens, width)),
        shaped((tokens, width)),
        shaped((tokens, 2), F32),
        shaped((SLOTS, cap_len, 2 * width)),
    ]
    operands = (place, counts, sample_caption, lens, queries, d_attended, column_sum, *kv_blocks)
    scratch = [pltpu.VMEM((keys_wide, 2 * width), BF)]
    return call(body, out, operands, 4, scratch)


def caption_terms(slots, side_slots, place, counts, sample_caption, tokens, pairs):
    captions = counts.shape[0]
    shape = slots.shape[1:]

    def body(place_ref, count_ref, caption_ref, own_ref, side_ref, *refs):
        term_refs, total_ref = refs[:-1], refs[-1]
        z, y = place_ref[0], place_ref[1]
        total_ref[...] = jnp.zeros_like(total_ref)
        for side, slot_ref in enumerate((own_ref, side_ref)):
            base = (z * 2 + (y ^ side)) * tokens
            for slot, (_, _, caption, valid) in enumerate(
                slots_of(count_ref, caption_ref, base, captions)
            ):
                far = lax.rem(caption // 2 - z + pairs, pairs)

                @pl.when(valid & (lax.rem(caption, 2) == y))
                def _(slot=slot, far=far, slot_ref=slot_ref):
                    total_ref[far] += slot_ref[slot].astype(F32)

        for far, term_ref in enumerate(term_refs):
            term_ref[...] = total_ref[far].astype(term_ref.dtype)

    out = [shaped(shape, F32 if far == 0 else BF) for far in range(pairs)]
    operands = (place, counts, sample_caption, slots, side_slots)
    return call(body, out, operands, 3, [pltpu.VMEM((pairs, *shape), F32)])


def project_back(attended, d_queries, blocks, place, pairs, part):
    tokens, width = attended.shape
    arrays, blocks = pieces_of(blocks)
    model_width = 2 * pairs * part
    per_piece = 2 * pairs // 4
    piece = model_width // 4

    def body(place_ref, att_ref, dq_ref, *refs):
        block_refs = refs[: len(arrays)]
        own_ref, far_ref, away_ref = refs[len(arrays) :]
        z, y, g = place_ref[0], place_ref[1], place_ref[2]
        att, d_query = att_ref[...], dq_ref[...]
        for far in range(pairs):
            for side in range(2):
                (of_query, query_at), (of_out, out_at) = blocks[2 * far + side]
                weight = block_refs[of_query][query_at : query_at + part, :]
                out_weight = block_refs[of_out][out_at : out_at + width, :]
                origin = lax.rem(z - far + pairs, pairs) * 2 + (y ^ side)
                flip = (origin // per_piece) ^ g
                start = lax.rem(origin, per_piece) * part
                columns = pl.ds(aligned(start, 128), part)
                beyond = pl.ds(aligned(start + piece, 128), part)
                added = mm(att, out_weight).astype(BF)
                d_normed = contract_last(d_query, weight).astype(BF)
                places = ((own_ref, columns), (away_ref, columns), (far_ref, columns), (away_ref, beyond))
                for number, (target_ref, to) in enumerate(places):

                    @pl.when(flip == number)
                    def _(target_ref=target_ref, to=to, added=added, d_normed=d_normed):
                        target_ref[0, :, to] = added
                        target_ref[1, :, to] = d_normed

    out = [shaped((2, tokens, piece)), shaped((2, tokens, piece)), shaped((2, tokens, 2 * piece))]
    return call(body, out, (place, attended, d_queries, *arrays), 1)


def weight_grads(tiles, both_blocks, known, pairs):
    part = tiles[0].shape[-1]
    given = [k for k, block in enumerate(both_blocks) if block is not None]
    arrays, blocks = pieces_of([both_blocks[k] for k in given])
    width = arrays[0].shape[-1]
    known = known or []

    def body(*refs):
        tile_refs, known_refs = refs[:4], refs[4 : 4 + len(known)]
        block_refs, (query_ref, out_ref) = refs[4 + len(known) : -2], refs[-2:]
        query_grad = known_refs[0][...] if known else jnp.zeros((part, width), F32)
        out_grad = known_refs[1][...] if known else jnp.zeros((width, part), F32)
        for k, ((number, at),) in zip(given, blocks):
            side, far = divmod(k, pairs)
            block = block_refs[number]
            normed, grad = (
                jnp.concatenate([r[far, side, which] for r in tile_refs], axis=0)
                for which in range(2)
            )
            out_grad += contract_first(block[at], grad)
            query_grad += contract_first(normed, block[at + 1])
        query_ref[...] = query_grad
        out_ref[...] = out_grad

    out = [shaped((part, width), F32), shaped((width, part), F32)]
    return call(body, out, (*tiles, *known, *arrays), 0)


def local(
    caption_states,
    caption_lens,
    text_gain,
    text_query,
    text_key,
    text_value,
    text_bias,
    text_out,
    final_gain,
    cross_key,
    cross_value,
    video_states,
    video_counts,
    sample_caption,
    cross_query,
    cross_out,
    out_grad,
):
    column = lax.axis_index("fsdp")
    g = lax.axis_index("grp")
    pairs = lax.axis_size("fsdp") // 2
    z, y = column // 2, column % 2
    place = jnp.stack([z, y, g]).astype(jnp.int32)
    caps_local, cap_len, text_width = caption_states.shape
    tokens, model_width = video_states.shape
    width_local = cross_key.shape[1]
    part = cross_query.shape[0]

    states = caption_states.reshape(cap_len, text_width)
    quarter_rows = cap_len // 4

    first = [fsend(cross_query, 1, 0), fsend(cross_out, 1, 0)]
    side_key, side_value = fsend(cross_key, 0, 1), fsend(cross_value, 0, 1)
    projected = project_text(states, text_gain, (text_query, text_key, text_value))
    kept, away = attend_text(projected, text_bias, text_out, place, caption_lens)
    kept, away = after((kept, away), first, side_key, side_value)
    got = gsend(away, 1)
    ring = [None, jnp.concatenate(first, axis=0)]
    side_first = fsend(jnp.concatenate([cross_query, cross_out, *first], axis=0), 0, 1)
    ring.append(fsend(ring[1], 1, 0))
    sent = (kept[quarter_rows:].astype(F32) + got[quarter_rows:].astype(F32)).astype(BF)
    over_x = gsend(sent, 2)
    normed, mean, inverse, own_tiles, other_tiles = prepare_video(
        after(video_states, sent), out_grad, place, pairs, part
    )
    pieces = encode_rows(
        states, kept, got, after(over_x, normed), final_gain, place, pairs
    )

    mine = jnp.stack([fsend(p, far, 0) if far else p for far, p in enumerate(pieces)])
    mine = after(mine, ring[2])
    over_x = gsend(mine, 2)
    parts = [mine, gsend(mine, 1), over_x, gsend(over_x, 1)]
    current = after(ring[2], mine)
    for far in range(3, pairs):
        current = fsend(current, 1, 0)
        ring.append(current)
    parts[3] = after(parts[3], side_first)
    kv_partial = project_captions(
        parts, cross_key, cross_value, side_key, side_value, place, pairs
    )
    kv_partial = after(tuple(kv_partial), ring[-1])
    kv_sum = kv_partial[0].astype(F32)
    for far in range(1, pairs):
        kv_sum += fsend(kv_partial[far], pairs - far, 0).astype(F32)
    side_later = [fsend(w, 0, 1) for w in ring[2:]]
    other_tiles = fsend(other_tiles, 0, 1)
    kv_sum = after(kv_sum.astype(BF), side_later[0])
    kv_blocks = gather_direct(kv_sum)
    kv_blocks[4] = after(kv_blocks[4], side_later, other_tiles)

    step = part + width_local
    blocks = []
    for far, held in enumerate(ring):
        side, start = (side_first, far * step) if far < 2 else (side_later[far - 2], 0)
        here = ((held, 0), (held, part)) if far else ((cross_query, 0), (cross_out, 0))
        blocks += [here, ((side, start), (side, start + part))]
    queries, d_attended, column_sum = project_rows(
        normed, after(out_grad, kv_blocks[4]), blocks, place, pairs, part
    )

    tiles = jnp.stack([own_tiles, other_tiles], axis=1)
    over_z = [fsend(after(tiles[far], kv_blocks[4]), far, 0) for far in range(1, pairs)]
    over_z = [tiles[0]] + over_z

    both, attended, d_queries, row_sums, slots = attend(
        queries,
        d_attended,
        column_sum,
        kv_blocks,
        place,
        video_counts,
        sample_caption,
        caption_lens,
        pairs,
    )

    def chain(blocks, steps):
        for _ in range(steps):
            blocks.append(fsend(blocks[-1], 1, 0))
        return blocks

    side_slots = fsend(slots, 0, 1)
    side_mine = fsend(both, 0, 1)
    first, over_z = after((both, over_z))
    tiles = jnp.stack(over_z)
    late = chain([first], 2)
    sums_core = gsend(row_sums, 1)
    row_sums = row_sums + sums_core
    attended, tiles = after((attended, tiles), row_sums)
    tiles_x = gsend(tiles, 2)
    own, far_piece, away = project_back(attended, d_queries, blocks, place, pairs, part)
    tiles_core = gsend(tiles, 1)
    stage = (side_slots, side_mine, late, row_sums, tiles_x, tiles_core, away)
    side_slots, side_mine, late, row_sums, tiles_x, tiles_core, away = after(stage)

    joint = fsend(jnp.stack(late[1:3]).reshape(4, tokens, width_local), 0, 1)
    late = chain(list(late), pairs - 3)
    got = gsend(away, 1)
    width = model_width // 4
    sent = [
        (far_piece[k].astype(F32) + got[k, :, width:].astype(F32)).astype(BF) for k in range(2)
    ]
    sums_x = gsend(row_sums, 2)
    far_out = gsend(after(sent[0], sums_x), 2)
    terms = caption_terms(
        after(slots, sent[0]), side_slots, place, video_counts, sample_caption, tokens, pairs
    )
    kv_parts = [fsend(terms[far], far, 0) for far in range(1, pairs, 2)]
    stage = (joint, late, tiles_x, kv_parts, terms, far_out, sent[1])
    joint, late, tiles_x, kv_parts, terms, far_out, sent_d = after(stage)

    here = [((block, 0),) for block in late]
    tiles = [tiles, tiles_core, tiles_x, gsend(tiles_x, 1)]
    there = [((side_mine, 0),), ((joint, 0),), ((joint, 2),)]
    there += [((fsend(block, 0, 1), 0),) for block in late[3:]]
    known = weight_grads(tiles, here + there[:3], None, pairs)
    total = [
        own[k].astype(F32) + got[k, :, :width].astype(F32) + far.astype(F32)
        for k, far in enumerate((far_out, after(gsend(sent_d, 2), known)))
    ]
    row_sums = (row_sums + sums_x) / model_width
    video = quarter(video_states, g, 1).astype(F32)
    updated = (video + total[0]).astype(BF)
    video_hat = (video - mean) * inverse
    input_grad = (
        quarter(out_grad, g, 1).astype(F32)
        + inverse * (total[1] - row_sums[:, 0:1] - video_hat * row_sums[:, 1:2])
    ).astype(BF)
    kv_parts += [fsend(terms[far], far, 0) for far in range(2, pairs, 2)]
    kv_grads = (terms[0] + sum(p.astype(F32) for p in kv_parts)).astype(BF)[None]
    key_grad = kv_grads[:, :, :width_local]
    value_grad = kv_grads[:, :, width_local:]
    query_grad, out_weight_grad = weight_grads(
        tiles, [None] * (pairs + 3) + there[3:], known, pairs
    )
    return (updated, input_grad, query_grad, out_weight_grad, key_grad, value_grad)


def local_of(*arrays):
    whole_tiles = arrays[14].shape[0] % 128 == 0 and arrays[0].shape[0] == 1
    return local(*arrays) if whole_tiles else local_general(*arrays)


def solution(mesh):
    in_specs = (
        P("fsdp", None, None),
        P(),
        P(),
        P(None, "grp"),
        P(None, "grp"),
        P(None, "grp"),
        P("grp", None, None),
        P("grp", None),
        P(),
        P("fsdp", "grp"),
        P("fsdp", "grp"),
        P("fsdp", None),
        P(),
        P(),
        P("fsdp", "grp"),
        P("grp", "fsdp"),
        P("fsdp", None),
    )
    out_specs = (
        P("fsdp", "grp"),
        P("fsdp", "grp"),
        P("fsdp", "grp"),
        P("grp", "fsdp"),
        P("fsdp", None, "grp"),
        P("fsdp", None, "grp"),
    )
    return jax.shard_map(
        local_of, mesh=mesh, in_specs=in_specs, out_specs=out_specs, check_vma=False
    )
```

```python
import math

import jax
import jax.numpy as jnp
from jax import lax
from jax.experimental import pallas as pl
from jax.experimental.pallas import tpu as pltpu
from jax.sharding import PartitionSpec as P

HEAD_SIZE = 128
BF = jnp.bfloat16
F32 = jnp.float32
SLOTS = 3
VMEM_BYTES = 60 * 1024 * 1024
SPARE_BYTES = 8 * 1024 * 1024
SMALL = pl.CostEstimate(flops=1, bytes_accessed=1, transcendentals=0)


def rms_scale(values, gain):
    mean_square = jnp.mean(values * values, axis=-1, keepdims=True)
    return values * lax.rsqrt(mean_square + 1e-06) * gain


def mm(left, right):
    return jnp.dot(left, right, preferred_element_type=F32)


def contract_last(left, right):
    return lax.dot_general(left, right, (((1,), (1,)), ((), ())), preferred_element_type=F32)


def contract_first(left, right):
    return lax.dot_general(left, right, (((0,), (0,)), ((), ())), preferred_element_type=F32)


def fsend(block, far, side):
    size = lax.axis_size("fsdp")
    pairs = size // 2
    perm = [(s, ((s // 2 + far) % pairs) * 2 + ((s % 2) ^ side)) for s in range(size)]
    return lax.ppermute(block, "fsdp", perm)


def gsend(block, flip):
    return lax.ppermute(block, "grp", [(s, s ^ flip) for s in range(lax.axis_size("grp"))])


def gather_ring(block):
    blocks = []
    current = block
    for far in range(lax.axis_size("fsdp") // 2):
        if far:
            current = fsend(current, 1, 0)
        blocks += [current, fsend(current, 0, 1)]
    return blocks


def gather_direct(block):
    blocks = []
    for far in range(lax.axis_size("fsdp") // 2):
        current = fsend(block, far, 0) if far else block
        blocks += [current, fsend(current, 0, 1)]
    return blocks


def quarter(array, index, axis=0):
    size = array.shape[axis] // 4
    return lax.dynamic_slice_in_dim(array, index * size, size, axis)


def grp_scatter(partial, g, axis):
    away = [quarter(partial, g ^ 1, axis), quarter(partial, g ^ 3, axis)]
    kept = [quarter(partial, g, axis), quarter(partial, g ^ 2, axis)]
    got = gsend(jnp.stack(away).astype(BF), 1)
    far = gsend((kept[1] + got[1].astype(F32)).astype(BF), 2)
    return kept[0] + got[0].astype(F32) + far.astype(F32)


def local_general(
    caption_states,
    caption_lens,
    text_gain,
    text_query,
    text_key,
    text_value,
    text_bias,
    text_out,
    final_gain,
    cross_key,
    cross_value,
    video_states,
    video_counts,
    sample_caption,
    cross_query,
    cross_out,
    out_grad,
):
    column = lax.axis_index("fsdp")
    g = lax.axis_index("grp")
    fsdp = lax.axis_size("fsdp")
    pairs = fsdp // 2
    z, y = column // 2, column % 2
    caps_local, cap_len, text_width = caption_states.shape
    tokens, model_width = video_states.shape
    width_local = cross_key.shape[1]
    cross_local = width_local // HEAD_SIZE
    query_rows = cross_query.shape[0]

    def source(far, side):
        return ((z - far) % pairs) * 2 + (y ^ side)

    def target(far, side):
        return ((z + far) % pairs) * 2 + (y ^ side)

    query_blocks = gather_ring(cross_query)
    out_blocks = gather_ring(cross_out)
    full_query = jnp.zeros((model_width, width_local), BF)
    full_out = jnp.zeros((width_local, model_width), BF)
    for far in range(pairs):
        for side in range(2):
            start = source(far, side) * query_rows
            full_query = lax.dynamic_update_slice(
                full_query, query_blocks[2 * far + side], (start, jnp.int32(0))
            )
            full_out = lax.dynamic_update_slice(
                full_out, out_blocks[2 * far + side], (jnp.int32(0), start)
            )

    own_kv = jnp.concatenate([cross_key, cross_value], axis=1)
    other_kv = fsend(own_kv, 0, 1)
    pair_kv = jnp.concatenate(
        [jnp.where(y == 0, own_kv, other_kv), jnp.where(y == 0, other_kv, own_kv)], axis=0
    )

    local_lens = lax.dynamic_slice_in_dim(caption_lens, column * caps_local, caps_local)
    flat_states = caption_states.reshape(caps_local * cap_len, text_width).astype(F32)
    text_normed = rms_scale(flat_states, text_gain).astype(BF)
    local_heads = text_bias.shape[0]
    head_width = text_query.shape[1] // local_heads

    def heads_of(weight):
        return mm(text_normed, weight).astype(BF).reshape(
            caps_local, cap_len, local_heads, head_width
        )

    text_queries = heads_of(text_query)
    text_keys = heads_of(text_key)
    text_values = heads_of(text_value)
    text_scores = (
        jnp.einsum("cihd,cjhd->chij", text_queries, text_keys, preferred_element_type=F32)
        + text_bias[None]
    )
    key_valid = jnp.arange(cap_len, dtype=jnp.int32)[None, :] < local_lens[:, None]
    exp_scores = jnp.where(key_valid[:, None, None, :], jnp.exp(text_scores), 0.0)
    text_weights = (exp_scores / jnp.sum(exp_scores, axis=-1, keepdims=True)).astype(BF)
    text_mixed = jnp.einsum(
        "chij,cjhd->cihd", text_weights, text_values, preferred_element_type=F32
    )
    text_mixed = text_mixed.astype(BF).reshape(caps_local * cap_len, local_heads * head_width)
    partial_text = mm(text_mixed, text_out)
    text_rows = grp_scatter(partial_text, g, 0)
    encoded = rms_scale(quarter(flat_states, g) + text_rows, final_gain).astype(BF)

    part = text_width // pairs
    pieces = [
        lax.dynamic_slice_in_dim(encoded, ((z + far) % pairs) * part, part, 1)
        for far in range(pairs)
    ]
    mine = jnp.stack([fsend(p, far, 0) if far else p for far, p in enumerate(pieces)])
    over_x = jnp.concatenate([mine[:, None], gsend(mine, 2)[:, None]], axis=1)
    over_core = jnp.stack([over_x, gsend(over_x, 1)], axis=2)
    kv_partial = mm(over_core.reshape(-1, part), pair_kv).reshape(pairs, cap_len, 2 * width_local)
    kv_sum = kv_partial[0]
    for far in range(1, pairs):
        kv_sum += fsend(kv_partial[far].astype(BF), pairs - far, 0).astype(F32)
    kv_rows = kv_sum.astype(BF).reshape(4, cap_len // 4, 2 * width_local)
    order = jnp.arange(4, dtype=jnp.int32) ^ g
    cap_kv = jnp.concatenate(
        [lax.dynamic_slice_in_dim(kv_rows, order[k], 1, 0) for k in range(4)], axis=0
    ).reshape(cap_len, 2 * width_local)
    all_kv = jnp.stack(gather_direct(cap_kv))

    video = video_states.astype(F32)
    center = video - jnp.mean(video, axis=-1, keepdims=True)
    inverse = lax.rsqrt(jnp.mean(center * center, axis=-1, keepdims=True) + 1e-06)
    video_hat = center * inverse
    video_normed = video_hat.astype(BF)

    both = jnp.stack([quarter(video_normed, g), quarter(out_grad, g)])
    tiles = []
    for far in range(pairs):
        for side in range(2):
            tile = lax.dynamic_slice_in_dim(both, target(far, side) * query_rows, query_rows, 2)
            tiles.append(fsend(tile, far, side) if far or side else tile)
    tiles = jnp.stack(tiles)
    tiles_x = jnp.stack([tiles, gsend(tiles, 2)], axis=2)
    tiles_all = jnp.stack([tiles_x, gsend(tiles_x, 1)], axis=3)
    normed_tile = tiles_all[:, 0].reshape(-1, query_rows)
    grad_tile = tiles_all[:, 1].reshape(-1, query_rows)

    caption_total = all_kv.shape[0]
    positions = column * tokens + jnp.arange(tokens, dtype=jnp.int32)
    sample_end = jnp.cumsum(video_counts)
    token_sample = jnp.sum((sample_end[None, :] <= positions[:, None]).astype(jnp.int32), axis=1)
    slot_count = 3
    slot_sample = token_sample[0] + jnp.arange(slot_count, dtype=jnp.int32)
    slot_valid = slot_sample < caption_total
    slot_clipped = jnp.minimum(slot_sample, caption_total - 1)
    numbers = jnp.arange(caption_total, dtype=jnp.int32)
    slot_pick = slot_clipped[:, None] == numbers[None, :]
    slot_caption = jnp.sum(jnp.where(slot_pick, sample_caption[None, :], 0), axis=1)
    caption_pick = slot_caption[:, None] == numbers[None, :]
    slot_lens = jnp.sum(jnp.where(caption_pick, caption_lens[None, :], 0), axis=1)
    slot_member = token_sample[None, :] == slot_sample[:, None]
    member_float = slot_member.astype(F32)
    member_half = slot_member.astype(BF)
    slot_entry = ((z - slot_caption // 2) % pairs) * 2 + ((slot_caption % 2) ^ y)
    slot_kv = jnp.take(all_kv, slot_entry, axis=0)
    slot_keys = slot_kv[..., :width_local].reshape(slot_count, cap_len, cross_local, HEAD_SIZE)
    slot_values = slot_kv[..., width_local:].reshape(slot_count, cap_len, cross_local, HEAD_SIZE)
    token_lens = jnp.sum(jnp.where(slot_member, slot_lens[:, None], 0), axis=0)

    query_sum = mm(video_normed, full_query)
    queries = query_sum.astype(BF)
    d_attended = contract_last(out_grad, full_out).astype(BF).reshape(
        tokens, cross_local, HEAD_SIZE
    )
    score_scale = 1.0 / math.sqrt(HEAD_SIZE)
    query_heads = queries.reshape(tokens, cross_local, HEAD_SIZE)
    slot_scores = jnp.einsum("thd,kjhd->kthj", query_heads, slot_keys, preferred_element_type=F32)
    scores = jnp.sum(member_float[:, :, None, None] * slot_scores, axis=0) * score_scale
    token_valid = (jnp.arange(cap_len, dtype=jnp.int32)[None, :] < token_lens[:, None])[:, None, :]
    exp_video = jnp.where(token_valid, jnp.exp(scores), 0.0)
    weights = exp_video / jnp.sum(exp_video, axis=-1, keepdims=True)
    probs = weights.astype(BF)
    masked_probs = member_half[:, :, None, None] * probs[None]
    attended = jnp.einsum("kthj,kjhd->thd", masked_probs, slot_values, preferred_element_type=F32)
    attended = attended.astype(BF).reshape(tokens, width_local)

    def reorder(array):
        return jnp.concatenate([quarter(array, order[k]) for k in range(4)], axis=0)

    all_attended = jnp.concatenate(gather_direct(reorder(attended)), axis=0)
    out_weight_grad = contract_first(all_attended, grad_tile)

    out_share = grp_scatter(mm(attended, full_out), g, 1)
    updated = (quarter(video, g, 1) + out_share).astype(BF)

    slot_dprobs = jnp.einsum("thd,kjhd->kthj", d_attended, slot_values, preferred_element_type=F32)
    d_probs = jnp.sum(member_float[:, :, None, None] * slot_dprobs, axis=0)
    d_scores = (
        weights * (d_probs - jnp.sum(weights * d_probs, axis=-1, keepdims=True)) * score_scale
    ).astype(BF)
    masked_scores = member_half[:, :, None, None] * d_scores[None]
    d_queries = jnp.einsum("kthj,kjhd->thd", masked_scores, slot_keys, preferred_element_type=F32)
    d_queries = d_queries.astype(BF).reshape(tokens, width_local)
    all_d_queries = jnp.concatenate(gather_direct(reorder(d_queries)), axis=0)
    query_grad = contract_first(normed_tile, all_d_queries)

    key_slots = jnp.einsum("kthj,thd->kjhd", masked_scores, query_heads, preferred_element_type=F32)
    value_slots = jnp.einsum("kthj,thd->kjhd", masked_probs, d_attended, preferred_element_type=F32)
    slot_terms = jnp.concatenate(
        [
            key_slots.reshape(slot_count, cap_len, width_local),
            value_slots.reshape(slot_count, cap_len, width_local),
        ],
        axis=-1,
    )

    def caption_terms(far, side):
        picked = (slot_caption == target(far, side)) & slot_valid
        return jnp.sum(jnp.where(picked[:, None, None], slot_terms, 0.0), axis=0)

    away = jnp.stack([caption_terms(far, 1).astype(BF) for far in range(pairs)])
    got = fsend(away, 0, 1).astype(F32)
    kv_grads = caption_terms(0, 0) + got[0]
    for far in range(1, pairs):
        kv_grads += fsend((caption_terms(far, 0) + got[far]).astype(BF), far, 0).astype(F32)
    kv_grads = kv_grads.astype(BF)[None]
    key_grad = kv_grads[:, :, :width_local]
    value_grad = kv_grads[:, :, width_local:]

    d_wide = d_queries.astype(F32)
    column_sum = jnp.sum(full_query.astype(F32), axis=0)
    row_sums = jnp.stack(
        [jnp.sum(d_wide * column_sum, axis=-1), jnp.sum(d_wide * query_sum, axis=-1)]
    )
    row_sums = row_sums + gsend(row_sums, 1)
    row_sums = (row_sums + gsend(row_sums, 2)) / model_width
    d_share = grp_scatter(contract_last(d_queries, full_query), g, 1)
    input_grad = (
        quarter(out_grad, g, 1).astype(F32)
        + inverse
        * (d_share - row_sums[0][:, None] - quarter(video_hat, g, 1) * row_sums[1][:, None])
    ).astype(BF)
    return (updated, input_grad, query_grad, out_weight_grad, key_grad, value_grad)


def after(value, *others):
    return lax.optimization_barrier((value, *others))[0]


def call(body, out_shape, operands, scalars, scratch=()):
    specs = [pl.BlockSpec(memory_space=pltpu.SMEM)] * scalars
    specs += [pl.BlockSpec(memory_space=pltpu.VMEM)] * (len(operands) - scalars)
    held = (*operands[scalars:], *jax.tree.leaves(out_shape), *scratch)
    held_bytes = sum(math.prod(a.shape) * jnp.dtype(a.dtype).itemsize for a in held)
    return pl.pallas_call(
        body,
        out_shape=out_shape,
        in_specs=specs,
        out_specs=jax.tree.map(lambda _: pl.BlockSpec(memory_space=pltpu.VMEM), out_shape),
        scratch_shapes=list(scratch),
        compiler_params=pltpu.CompilerParams(vmem_limit_bytes=held_bytes + SPARE_BYTES),
        cost_estimate=SMALL,
    )(*operands)


def shaped(shape, dtype=BF):
    return jax.ShapeDtypeStruct(shape, dtype)


def aligned(start, unit):
    return pl.multiple_of(start, unit)


def project_text(states, gain, weights, steps=4):
    rows, depth = states.shape
    width = weights[0].shape[1]
    chunk = depth // steps

    def body(states_ref, gain_ref, wq_ref, wk_ref, wv_ref, out_ref, normed_ref, total_ref):
        step = pl.program_id(0)

        @pl.when(step == 0)
        def _():
            for at in range(0, rows, 16):
                values = states_ref[at : at + 16, :].astype(F32)
                normed_ref[at : at + 16, :] = rms_scale(values, gain_ref[...]).astype(BF)
            total_ref[...] = jnp.zeros_like(total_ref)

        here = normed_ref[:, pl.ds(aligned(step * chunk, chunk), chunk)]
        for k, weight_ref in enumerate((wq_ref, wk_ref, wv_ref)):
            total_ref[:, k * width : (k + 1) * width] += mm(here, weight_ref[...])

        @pl.when(step == steps - 1)
        def _():
            out_ref[...] = total_ref[...].astype(BF)

    whole = lambda shape: pl.BlockSpec(shape, lambda i: (0,) * len(shape))
    return pl.pallas_call(
        body,
        grid=(steps,),
        out_shape=shaped((rows, 3 * width)),
        in_specs=[whole((rows, depth)), whole((1, depth))]
        + [pl.BlockSpec((chunk, width), lambda i: (i, 0))] * 3,
        out_specs=whole((rows, 3 * width)),
        scratch_shapes=[pltpu.VMEM((rows, depth), BF), pltpu.VMEM((rows, 3 * width), F32)],
        compiler_params=pltpu.CompilerParams(vmem_limit_bytes=VMEM_BYTES),
        cost_estimate=SMALL,
    )(states, gain.reshape(1, -1), *weights)


def attend_text(projected, bias, text_out, place, lens, steps=4):
    rows = projected.shape[0]
    heads = bias.shape[0]
    inner, depth = text_out.shape
    size = inner // heads
    quarter_rows = rows // 4
    chunk = depth // steps

    def body(place_ref, len_ref, qkv_ref, bias_ref, out_ref, kept_ref, away_ref, held_ref, mixed_ref):
        @pl.when(pl.program_id(0) == 0)
        def _():
            g = place_ref[2]
            length = len_ref[place_ref[0] * 2 + place_ref[1]]
            live = lax.broadcasted_iota(jnp.int32, (rows, rows), 1) < length
            for head in range(heads):
                query, key, value = (
                    qkv_ref[:, k * inner + head * size : k * inner + (head + 1) * size]
                    for k in range(3)
                )
                grown = jnp.where(live, jnp.exp(contract_last(query, key) + bias_ref[head]), 0.0)
                weights = grown * (1.0 / jnp.sum(grown, axis=-1, keepdims=True))
                held_ref[:, head * size : (head + 1) * size] = mm(weights.astype(BF), value).astype(BF)
            for k, to in ((0, 0), (2, 1), (1, 2), (3, 3)):
                rows_from = pl.ds(aligned((g ^ k) * quarter_rows, quarter_rows), quarter_rows)
                mixed_ref[to * quarter_rows : (to + 1) * quarter_rows, :] = held_ref[rows_from, :]

        product = mm(mixed_ref[...], out_ref[...]).astype(BF)
        kept_ref[...] = product[: rows // 2]
        away_ref[...] = product[rows // 2 :]

    whole = lambda shape: pl.BlockSpec(shape, lambda i: (0,) * len(shape))
    return pl.pallas_call(
        body,
        grid=(steps,),
        out_shape=[shaped((rows // 2, depth))] * 2,
        in_specs=[pl.BlockSpec(memory_space=pltpu.SMEM)] * 2
        + [whole(projected.shape), whole(bias.shape)]
        + [pl.BlockSpec((inner, chunk), lambda i: (0, i))],
        out_specs=[pl.BlockSpec((rows // 2, chunk), lambda i: (0, i))] * 2,
        scratch_shapes=[pltpu.VMEM((rows, inner), BF), pltpu.VMEM((rows, inner), BF)],
        compiler_params=pltpu.CompilerParams(vmem_limit_bytes=VMEM_BYTES),
        cost_estimate=SMALL,
    )(place, lens, projected, bias, text_out)


def encode_rows(states, kept, got, far, gain, place, pairs):
    quarter_rows = states.shape[0] // 4
    width = states.shape[1]
    depth = width // pairs

    def body(place_ref, states_ref, kept_ref, got_ref, far_ref, gain_ref, *refs):
        piece_refs, encoded_ref = refs[:-1], refs[-1]
        z, g = place_ref[0], place_ref[2]
        mine = pl.ds(aligned(g * quarter_rows, quarter_rows), quarter_rows)
        total = states_ref[mine, :].astype(F32) + far_ref[...].astype(F32)
        total += kept_ref[:quarter_rows, :].astype(F32) + got_ref[:quarter_rows, :].astype(F32)
        encoded_ref[...] = rms_scale(total, gain_ref[...]).astype(BF)
        for far_by, piece in enumerate(piece_refs):
            to = lax.rem(z + far_by, pairs)
            piece[...] = encoded_ref[:, pl.ds(aligned(to * depth, 128), depth)]

    out = [shaped((quarter_rows, depth))] * pairs
    operands = (place, states, kept, got, far, gain.reshape(1, -1))
    return call(body, out, operands, 1, [pltpu.VMEM((quarter_rows, width), BF)])


def pieces_of(pairs_of_blocks):
    arrays, listed = [], []
    for entry in pairs_of_blocks:
        numbers = []
        for array, start in entry:
            if not any(array is held for held in arrays):
                arrays.append(array)
            numbers.append((next(k for k, held in enumerate(arrays) if held is array), start))
        listed.append(numbers)
    return arrays, listed


def prepare_video(video_states, out_grad, place, pairs, part):
    tokens, model_width = video_states.shape
    rows = tokens // 4

    def body(place_ref, video_ref, grad_ref, normed_ref, mean_ref, inverse_ref, *tile_refs):
        @pl.loop(0, tokens // 32)
        def _(step):
            here = pl.ds(aligned(step * 32, 32), 32)
            values = video_ref[here, :].astype(F32)
            mean = jnp.mean(values, axis=-1, keepdims=True)
            center = values - mean
            inverse = lax.rsqrt(jnp.mean(center * center, axis=-1, keepdims=True) + 1e-06)
            normed_ref[here, :] = (center * inverse).astype(BF)
            mean_ref[here, :] = mean
            inverse_ref[here, :] = inverse

        z, y, g = place_ref[0], place_ref[1], place_ref[2]
        mine = pl.ds(aligned(g * rows, rows), rows)
        for far in range(pairs):
            for side in range(2):
                to = lax.rem(z + far, pairs) * 2 + (y ^ side)
                columns = pl.ds(aligned(to * part, 128), part)
                tile_refs[side][far, 0] = normed_ref[mine, columns]
                tile_refs[side][far, 1] = grad_ref[mine, columns]

    out = [shaped((tokens, model_width)), shaped((tokens, 1), F32), shaped((tokens, 1), F32)]
    out += [shaped((pairs, 2, rows, part))] * 2
    return call(body, out, (place, video_states, out_grad), 1)


def project_rows(normed, out_grad, blocks, place, pairs, part):
    tokens = normed.shape[0]
    arrays, blocks = pieces_of(blocks)
    width = arrays[0].shape[1]

    def body(place_ref, normed_ref, grad_ref, *refs):
        block_refs, (query_ref, d_ref, sum_ref) = refs[:-3], refs[-3:]
        z, y = place_ref[0], place_ref[1]
        query = jnp.zeros((tokens, width), F32)
        d_attended = jnp.zeros((tokens, width), F32)
        total = jnp.zeros((1, width), F32)
        for far in range(pairs):
            for side in range(2):
                (of_query, query_at), (of_out, out_at) = blocks[2 * far + side]
                origin = lax.rem(z - far + pairs, pairs) * 2 + (y ^ side)
                columns = pl.ds(aligned(origin * part, 128), part)
                weight = block_refs[of_query][query_at : query_at + part, :]
                out_weight = block_refs[of_out][out_at : out_at + width, :]
                query += mm(normed_ref[:, columns], weight)
                d_attended += contract_last(grad_ref[:, columns], out_weight)
                total += jnp.sum(weight.astype(F32), axis=0, keepdims=True)
        query_ref[...] = query.astype(BF)
        d_ref[...] = d_attended.astype(BF)
        sum_ref[...] = total

    out = [shaped((tokens, width)), shaped((tokens, width)), shaped((1, width), F32)]
    return call(body, out, (place, normed, out_grad, *arrays), 1)


def project_captions(parts, own_key, own_value, side_key, side_value, place, pairs):
    quarter_rows, depth = parts[0].shape[1:]
    half = depth // 2
    width = own_key.shape[1]

    def body(place_ref, *refs):
        part_refs = refs[:4]
        key_ref, value_ref, side_key_ref, side_value_ref = refs[4:8]
        out_refs = refs[8:]
        y = place_ref[1]
        mine = pl.ds(aligned(y * half, 128), half)
        theirs = pl.ds(aligned((1 - y) * half, 128), half)
        own = jnp.concatenate([r[far, :, mine] for far in range(pairs) for r in part_refs], 0)
        other = jnp.concatenate([r[far, :, theirs] for far in range(pairs) for r in part_refs], 0)
        keys = mm(own, key_ref[...]) + mm(other, side_key_ref[...])
        values = mm(own, value_ref[...]) + mm(other, side_value_ref[...])
        for far in range(pairs):
            rows = slice(far * 4 * quarter_rows, (far + 1) * 4 * quarter_rows)
            out_refs[far][:, :width] = keys[rows].astype(BF)
            out_refs[far][:, width:] = values[rows].astype(BF)

    out = [shaped((4 * quarter_rows, 2 * width))] * pairs
    operands = (place, *parts, own_key, own_value, side_key, side_value)
    return call(body, out, operands, 1)


def slots_of(count_ref, caption_ref, base, captions):
    def find(sample, carry):
        total, first, start = carry
        total = total + count_ref[sample]
        past = total <= base
        return total, first + past.astype(jnp.int32), jnp.where(past, total, start)

    zero = jnp.int32(0)
    _, first, start = lax.fori_loop(0, captions, find, (zero, zero, zero))
    found, edge = [], start - base
    for slot in range(SLOTS):
        valid = first + slot < captions
        sample = jnp.minimum(first + slot, captions - 1)
        end = edge + jnp.where(valid, count_ref[sample], 0)
        found.append((edge, end, caption_ref[sample], valid))
        edge = end
    return found


def attend(queries, d_attended, column_sum, kv_blocks, place, counts, sample_caption, lens, pairs):
    tokens, width = queries.shape
    cap_len = kv_blocks[0].shape[0]
    heads = width // HEAD_SIZE
    captions = counts.shape[0]
    keys_wide = SLOTS * cap_len
    cap_quarter, row_quarter = cap_len // 4, tokens // 4
    scale = 1.0 / math.sqrt(HEAD_SIZE)

    def body(place_ref, count_ref, caption_ref, len_ref, q_ref, da_ref, sum_ref, *refs):
        block_refs = refs[: len(kv_blocks)]
        both_ref, att_ref, dq_ref, rows_ref, slot_ref, kv_ref = refs[len(kv_blocks) :]
        z, y, g = place_ref[0], place_ref[1], place_ref[2]
        low, high, length = [], [], []
        found = slots_of(count_ref, caption_ref, (z * 2 + y) * tokens, captions)
        for slot, (start, end, caption, _) in enumerate(found):
            low.append(start)
            high.append(end)
            length.append(len_ref[caption])
            entry = lax.rem(z - caption // 2 + pairs, pairs) * 2 + (lax.rem(caption, 2) ^ y)
            for number, block in enumerate(block_refs):

                @pl.when(entry == number)
                def _(slot=slot, block=block):
                    kv_ref[slot * cap_len : (slot + 1) * cap_len, :] = block[...]

        token = lax.broadcasted_iota(jnp.int32, (tokens, keys_wide), 0)
        column = lax.broadcasted_iota(jnp.int32, (tokens, keys_wide), 1)
        slot_of = column // cap_len
        inside = column % cap_len
        key = ((inside // cap_quarter) ^ g) * cap_quarter + inside % cap_quarter

        def of_slot(values):
            return jnp.where(slot_of == 0, values[0], jnp.where(slot_of == 1, values[1], values[2]))

        live = (token >= of_slot(low)) & (token < of_slot(high)) & (key < of_slot(length))
        first_sum = jnp.zeros((tokens, 1), F32)
        second_sum = jnp.zeros((tokens, 1), F32)
        for head in range(heads):
            at = slice(head * HEAD_SIZE, (head + 1) * HEAD_SIZE)
            at_value = slice(width + head * HEAD_SIZE, width + (head + 1) * HEAD_SIZE)
            query, d_att = q_ref[:, at], da_ref[:, at]
            keys, values = kv_ref[:, at], kv_ref[:, at_value]
            grown = jnp.where(live, jnp.exp(contract_last(query, keys) * scale), 0.0)
            weights = grown * (1.0 / jnp.sum(grown, axis=-1, keepdims=True))
            probs = weights.astype(BF)
            d_probs = contract_last(d_att, values)
            mixed = jnp.sum(weights * d_probs, axis=-1, keepdims=True)
            d_scores = (weights * (d_probs - mixed) * scale).astype(BF)
            att_ref[:, at] = mm(probs, values).astype(BF)
            d_query = mm(d_scores, keys).astype(BF)
            dq_ref[:, at] = d_query
            d_wide = d_query.astype(F32)
            first_sum += jnp.sum(d_wide * sum_ref[:, at], axis=-1, keepdims=True)
            second_sum += jnp.sum(d_wide * query.astype(F32), axis=-1, keepdims=True)
            key_grad = contract_first(d_scores, query).astype(BF)
            value_grad = contract_first(probs, d_att).astype(BF)
            for slot in range(SLOTS):
                for part in range(4):
                    held = slice(
                        slot * cap_len + part * cap_quarter, slot * cap_len + (part + 1) * cap_quarter
                    )
                    to = pl.ds(aligned((part ^ g) * cap_quarter, cap_quarter), cap_quarter)
                    slot_ref[slot, to, at] = key_grad[held]
                    slot_ref[slot, to, at_value] = value_grad[held]

        rows_ref[:, 0:1] = first_sum
        rows_ref[:, 1:2] = second_sum
        for part in range(4):
            rows = pl.ds(aligned((part ^ g) * row_quarter, row_quarter), row_quarter)
            to = slice(part * row_quarter, (part + 1) * row_quarter)
            both_ref[0, to, :] = att_ref[rows, :]
            both_ref[1, to, :] = dq_ref[rows, :]

    out = [
        shaped((2, tokens, width)),
        shaped((tokens, width)),
        shaped((tokens, width)),
        shaped((tokens, 2), F32),
        shaped((SLOTS, cap_len, 2 * width)),
    ]
    operands = (place, counts, sample_caption, lens, queries, d_attended, column_sum, *kv_blocks)
    scratch = [pltpu.VMEM((keys_wide, 2 * width), BF)]
    return call(body, out, operands, 4, scratch)


def caption_terms(slots, side_slots, place, counts, sample_caption, tokens, pairs):
    captions = counts.shape[0]
    shape = slots.shape[1:]

    def body(place_ref, count_ref, caption_ref, own_ref, side_ref, *refs):
        term_refs, total_ref = refs[:-1], refs[-1]
        z, y = place_ref[0], place_ref[1]
        total_ref[...] = jnp.zeros_like(total_ref)
        for side, slot_ref in enumerate((own_ref, side_ref)):
            base = (z * 2 + (y ^ side)) * tokens
            for slot, (_, _, caption, valid) in enumerate(
                slots_of(count_ref, caption_ref, base, captions)
            ):
                far = lax.rem(caption // 2 - z + pairs, pairs)

                @pl.when(valid & (lax.rem(caption, 2) == y))
                def _(slot=slot, far=far, slot_ref=slot_ref):
                    total_ref[far] += slot_ref[slot].astype(F32)

        for far, term_ref in enumerate(term_refs):
            term_ref[...] = total_ref[far].astype(term_ref.dtype)

    out = [shaped(shape, F32 if far == 0 else BF) for far in range(pairs)]
    operands = (place, counts, sample_caption, slots, side_slots)
    return call(body, out, operands, 3, [pltpu.VMEM((pairs, *shape), F32)])


def project_back(attended, d_queries, blocks, place, pairs, part):
    tokens, width = attended.shape
    arrays, blocks = pieces_of(blocks)
    model_width = 2 * pairs * part
    per_piece = 2 * pairs // 4
    piece = model_width // 4

    def body(place_ref, att_ref, dq_ref, *refs):
        block_refs = refs[: len(arrays)]
        own_ref, far_ref, away_ref = refs[len(arrays) :]
        z, y, g = place_ref[0], place_ref[1], place_ref[2]
        att, d_query = att_ref[...], dq_ref[...]
        for far in range(pairs):
            for side in range(2):
                (of_query, query_at), (of_out, out_at) = blocks[2 * far + side]
                weight = block_refs[of_query][query_at : query_at + part, :]
                out_weight = block_refs[of_out][out_at : out_at + width, :]
                origin = lax.rem(z - far + pairs, pairs) * 2 + (y ^ side)
                flip = (origin // per_piece) ^ g
                start = lax.rem(origin, per_piece) * part
                columns = pl.ds(aligned(start, 128), part)
                beyond = pl.ds(aligned(start + piece, 128), part)
                added = mm(att, out_weight).astype(BF)
                d_normed = contract_last(d_query, weight).astype(BF)
                places = ((own_ref, columns), (away_ref, columns), (far_ref, columns), (away_ref, beyond))
                for number, (target_ref, to) in enumerate(places):

                    @pl.when(flip == number)
                    def _(target_ref=target_ref, to=to, added=added, d_normed=d_normed):
                        target_ref[0, :, to] = added
                        target_ref[1, :, to] = d_normed

    out = [shaped((2, tokens, piece)), shaped((2, tokens, piece)), shaped((2, tokens, 2 * piece))]
    return call(body, out, (place, attended, d_queries, *arrays), 1)


def weight_grads(tiles, both_blocks, known, pairs):
    part = tiles[0].shape[-1]
    given = [k for k, block in enumerate(both_blocks) if block is not None]
    arrays, blocks = pieces_of([both_blocks[k] for k in given])
    width = arrays[0].shape[-1]
    known = known or []

    def body(*refs):
        tile_refs, known_refs = refs[:4], refs[4 : 4 + len(known)]
        block_refs, (query_ref, out_ref) = refs[4 + len(known) : -2], refs[-2:]
        query_grad = known_refs[0][...] if known else jnp.zeros((part, width), F32)
        out_grad = known_refs[1][...] if known else jnp.zeros((width, part), F32)
        for k, ((number, at),) in zip(given, blocks):
            side, far = divmod(k, pairs)
            block = block_refs[number]
            normed, grad = (
                jnp.concatenate([r[far, side, which] for r in tile_refs], axis=0)
                for which in range(2)
            )
            out_grad += contract_first(block[at], grad)
            query_grad += contract_first(normed, block[at + 1])
        query_ref[...] = query_grad
        out_ref[...] = out_grad

    out = [shaped((part, width), F32), shaped((width, part), F32)]
    return call(body, out, (*tiles, *known, *arrays), 0)


def local(
    caption_states,
    caption_lens,
    text_gain,
    text_query,
    text_key,
    text_value,
    text_bias,
    text_out,
    final_gain,
    cross_key,
    cross_value,
    video_states,
    video_counts,
    sample_caption,
    cross_query,
    cross_out,
    out_grad,
):
    column = lax.axis_index("fsdp")
    g = lax.axis_index("grp")
    pairs = lax.axis_size("fsdp") // 2
    z, y = column // 2, column % 2
    place = jnp.stack([z, y, g]).astype(jnp.int32)
    caps_local, cap_len, text_width = caption_states.shape
    tokens, model_width = video_states.shape
    width_local = cross_key.shape[1]
    part = cross_query.shape[0]

    states = caption_states.reshape(cap_len, text_width)
    quarter_rows = cap_len // 4

    first = [fsend(cross_query, 1, 0), fsend(cross_out, 1, 0)]
    side_key, side_value = fsend(cross_key, 0, 1), fsend(cross_value, 0, 1)
    projected = project_text(states, text_gain, (text_query, text_key, text_value))
    kept, away = attend_text(projected, text_bias, text_out, place, caption_lens)
    kept, away = after((kept, away), first, side_key, side_value)
    got = gsend(away, 1)
    ring = [None, jnp.concatenate(first, axis=0)]
    side_first = fsend(jnp.concatenate([cross_query, cross_out, *first], axis=0), 0, 1)
    ring.append(fsend(ring[1], 1, 0))
    sent = (kept[quarter_rows:].astype(F32) + got[quarter_rows:].astype(F32)).astype(BF)
    over_x = gsend(sent, 2)
    normed, mean, inverse, own_tiles, other_tiles = prepare_video(
        after(video_states, sent), out_grad, place, pairs, part
    )
    pieces = encode_rows(
        states, kept, got, after(over_x, normed), final_gain, place, pairs
    )

    mine = jnp.stack([fsend(p, far, 0) if far else p for far, p in enumerate(pieces)])
    mine = after(mine, ring[2])
    over_x = gsend(mine, 2)
    parts = [mine, gsend(mine, 1), over_x, gsend(over_x, 1)]
    current = after(ring[2], mine)
    for far in range(3, pairs):
        current = fsend(current, 1, 0)
        ring.append(current)
    parts[3] = after(parts[3], side_first)
    kv_partial = project_captions(
        parts, cross_key, cross_value, side_key, side_value, place, pairs
    )
    kv_partial = after(tuple(kv_partial), ring[-1])
    kv_sum = kv_partial[0].astype(F32)
    for far in range(1, pairs):
        kv_sum += fsend(kv_partial[far], pairs - far, 0).astype(F32)
    side_later = [fsend(w, 0, 1) for w in ring[2:]]
    other_tiles = fsend(other_tiles, 0, 1)
    kv_sum = after(kv_sum.astype(BF), side_later[0])
    kv_blocks = gather_direct(kv_sum)
    kv_blocks[4] = after(kv_blocks[4], side_later, other_tiles)

    step = part + width_local
    blocks = []
    for far, held in enumerate(ring):
        side, start = (side_first, far * step) if far < 2 else (side_later[far - 2], 0)
        here = ((held, 0), (held, part)) if far else ((cross_query, 0), (cross_out, 0))
        blocks += [here, ((side, start), (side, start + part))]
    queries, d_attended, column_sum = project_rows(
        normed, after(out_grad, kv_blocks[4]), blocks, place, pairs, part
    )

    tiles = jnp.stack([own_tiles, other_tiles], axis=1)
    over_z = [fsend(after(tiles[far], kv_blocks[4]), far, 0) for far in range(1, pairs)]
    over_z = [tiles[0]] + over_z

    both, attended, d_queries, row_sums, slots = attend(
        queries,
        d_attended,
        column_sum,
        kv_blocks,
        place,
        video_counts,
        sample_caption,
        caption_lens,
        pairs,
    )

    def chain(blocks, steps):
        for _ in range(steps):
            blocks.append(fsend(blocks[-1], 1, 0))
        return blocks

    side_slots = fsend(slots, 0, 1)
    side_mine = fsend(both, 0, 1)
    first, over_z = after((both, over_z))
    tiles = jnp.stack(over_z)
    late = chain([first], 2)
    sums_core = gsend(row_sums, 1)
    row_sums = row_sums + sums_core
    attended, tiles = after((attended, tiles), row_sums)
    tiles_x = gsend(tiles, 2)
    own, far_piece, away = project_back(attended, d_queries, blocks, place, pairs, part)
    tiles_core = gsend(tiles, 1)
    stage = (side_slots, side_mine, late, row_sums, tiles_x, tiles_core, away)
    side_slots, side_mine, late, row_sums, tiles_x, tiles_core, away = after(stage)

    sides = [fsend(block, 0, 1) for block in late[1:3]]
    late = chain(list(late), pairs - 3)
    got = gsend(away, 1)
    width = model_width // 4
    sent = [
        (far_piece[k].astype(F32) + got[k, :, width:].astype(F32)).astype(BF) for k in range(2)
    ]
    sums_x = gsend(row_sums, 2)
    far_out = gsend(after(sent[0], sums_x), 2)
    terms = caption_terms(
        after(slots, sent[0]), side_slots, place, video_counts, sample_caption, tokens, pairs
    )
    kv_parts = [fsend(terms[1], 1, 0)]
    stage = (sides, late, tiles_x, kv_parts, terms, far_out, sent[1])
    sides, late, tiles_x, kv_parts, terms, far_out, sent_d = after(stage)

    here = [((block, 0),) for block in late]
    tiles = [tiles, tiles_core, tiles_x, gsend(tiles_x, 1)]
    there = [((block, 0),) for block in (side_mine, *sides)]
    there += [((fsend(block, 0, 1), 0),) for block in late[3:]]
    known = weight_grads(tiles, here + there[:3], None, pairs)
    total = [
        own[k].astype(F32) + got[k, :, :width].astype(F32) + far.astype(F32)
        for k, far in enumerate((far_out, after(gsend(sent_d, 2), known)))
    ]
    row_sums = (row_sums + sums_x) / model_width
    video = quarter(video_states, g, 1).astype(F32)
    updated = (video + total[0]).astype(BF)
    video_hat = (video - mean) * inverse
    input_grad = (
        quarter(out_grad, g, 1).astype(F32)
        + inverse * (total[1] - row_sums[:, 0:1] - video_hat * row_sums[:, 1:2])
    ).astype(BF)
    kv_parts += [fsend(terms[far], far, 0) for far in range(2, pairs)]
    kv_grads = (terms[0] + sum(p.astype(F32) for p in kv_parts)).astype(BF)[None]
    key_grad = kv_grads[:, :, :width_local]
    value_grad = kv_grads[:, :, width_local:]
    query_grad, out_weight_grad = weight_grads(
        tiles, [None] * (pairs + 3) + there[3:], known, pairs
    )
    return (updated, input_grad, query_grad, out_weight_grad, key_grad, value_grad)


def local_of(*arrays):
    whole_tiles = arrays[14].shape[0] % 128 == 0 and arrays[0].shape[0] == 1
    return local(*arrays) if whole_tiles else local_general(*arrays)


def solution(mesh):
    in_specs = (
        P("fsdp", None, None),
        P(),
        P(),
        P(None, "grp"),
        P(None, "grp"),
        P(None, "grp"),
        P("grp", None, None),
        P("grp", None),
        P(),
        P("fsdp", "grp"),
        P("fsdp", "grp"),
        P("fsdp", None),
        P(),
        P(),
        P("fsdp", "grp"),
        P("grp", "fsdp"),
        P("fsdp", None),
    )
    out_specs = (
        P("fsdp", "grp"),
        P("fsdp", "grp"),
        P("fsdp", "grp"),
        P("grp", "fsdp"),
        P("fsdp", None, "grp"),
        P("fsdp", None, "grp"),
    )
    return jax.shard_map(
        local_of, mesh=mesh, in_specs=in_specs, out_specs=out_specs, check_vma=False
    )
```

```python
import math

import jax
import jax.numpy as jnp
from jax import lax
from jax.experimental import pallas as pl
from jax.experimental.pallas import tpu as pltpu
from jax.sharding import PartitionSpec as P

HEAD_SIZE = 128
BF = jnp.bfloat16
F32 = jnp.float32
SLOTS = 3
VMEM_BYTES = 60 * 1024 * 1024
SPARE_BYTES = 8 * 1024 * 1024
SMALL = pl.CostEstimate(flops=1, bytes_accessed=1, transcendentals=0)


def rms_scale(values, gain):
    mean_square = jnp.mean(values * values, axis=-1, keepdims=True)
    return values * lax.rsqrt(mean_square + 1e-06) * gain


def mm(left, right):
    return jnp.dot(left, right, preferred_element_type=F32)


def contract_last(left, right):
    return lax.dot_general(left, right, (((1,), (1,)), ((), ())), preferred_element_type=F32)


def contract_first(left, right):
    return lax.dot_general(left, right, (((0,), (0,)), ((), ())), preferred_element_type=F32)


def fsend(block, far, side):
    size = lax.axis_size("fsdp")
    pairs = size // 2
    perm = [(s, ((s // 2 + far) % pairs) * 2 + ((s % 2) ^ side)) for s in range(size)]
    return lax.ppermute(block, "fsdp", perm)


def gsend(block, flip):
    return lax.ppermute(block, "grp", [(s, s ^ flip) for s in range(lax.axis_size("grp"))])


def gather_ring(block):
    blocks = []
    current = block
    for far in range(lax.axis_size("fsdp") // 2):
        if far:
            current = fsend(current, 1, 0)
        blocks += [current, fsend(current, 0, 1)]
    return blocks


def gather_direct(block):
    blocks = []
    for far in range(lax.axis_size("fsdp") // 2):
        current = fsend(block, far, 0) if far else block
        blocks += [current, fsend(current, 0, 1)]
    return blocks


def quarter(array, index, axis=0):
    size = array.shape[axis] // 4
    return lax.dynamic_slice_in_dim(array, index * size, size, axis)


def grp_scatter(partial, g, axis):
    away = [quarter(partial, g ^ 1, axis), quarter(partial, g ^ 3, axis)]
    kept = [quarter(partial, g, axis), quarter(partial, g ^ 2, axis)]
    got = gsend(jnp.stack(away).astype(BF), 1)
    far = gsend((kept[1] + got[1].astype(F32)).astype(BF), 2)
    return kept[0] + got[0].astype(F32) + far.astype(F32)


def local_general(
    caption_states,
    caption_lens,
    text_gain,
    text_query,
    text_key,
    text_value,
    text_bias,
    text_out,
    final_gain,
    cross_key,
    cross_value,
    video_states,
    video_counts,
    sample_caption,
    cross_query,
    cross_out,
    out_grad,
):
    column = lax.axis_index("fsdp")
    g = lax.axis_index("grp")
    fsdp = lax.axis_size("fsdp")
    pairs = fsdp // 2
    z, y = column // 2, column % 2
    caps_local, cap_len, text_width = caption_states.shape
    tokens, model_width = video_states.shape
    width_local = cross_key.shape[1]
    cross_local = width_local // HEAD_SIZE
    query_rows = cross_query.shape[0]

    def source(far, side):
        return ((z - far) % pairs) * 2 + (y ^ side)

    def target(far, side):
        return ((z + far) % pairs) * 2 + (y ^ side)

    query_blocks = gather_ring(cross_query)
    out_blocks = gather_ring(cross_out)
    full_query = jnp.zeros((model_width, width_local), BF)
    full_out = jnp.zeros((width_local, model_width), BF)
    for far in range(pairs):
        for side in range(2):
            start = source(far, side) * query_rows
            full_query = lax.dynamic_update_slice(
                full_query, query_blocks[2 * far + side], (start, jnp.int32(0))
            )
            full_out = lax.dynamic_update_slice(
                full_out, out_blocks[2 * far + side], (jnp.int32(0), start)
            )

    own_kv = jnp.concatenate([cross_key, cross_value], axis=1)
    other_kv = fsend(own_kv, 0, 1)
    pair_kv = jnp.concatenate(
        [jnp.where(y == 0, own_kv, other_kv), jnp.where(y == 0, other_kv, own_kv)], axis=0
    )

    local_lens = lax.dynamic_slice_in_dim(caption_lens, column * caps_local, caps_local)
    flat_states = caption_states.reshape(caps_local * cap_len, text_width).astype(F32)
    text_normed = rms_scale(flat_states, text_gain).astype(BF)
    local_heads = text_bias.shape[0]
    head_width = text_query.shape[1] // local_heads

    def heads_of(weight):
        return mm(text_normed, weight).astype(BF).reshape(
            caps_local, cap_len, local_heads, head_width
        )

    text_queries = heads_of(text_query)
    text_keys = heads_of(text_key)
    text_values = heads_of(text_value)
    text_scores = (
        jnp.einsum("cihd,cjhd->chij", text_queries, text_keys, preferred_element_type=F32)
        + text_bias[None]
    )
    key_valid = jnp.arange(cap_len, dtype=jnp.int32)[None, :] < local_lens[:, None]
    exp_scores = jnp.where(key_valid[:, None, None, :], jnp.exp(text_scores), 0.0)
    text_weights = (exp_scores / jnp.sum(exp_scores, axis=-1, keepdims=True)).astype(BF)
    text_mixed = jnp.einsum(
        "chij,cjhd->cihd", text_weights, text_values, preferred_element_type=F32
    )
    text_mixed = text_mixed.astype(BF).reshape(caps_local * cap_len, local_heads * head_width)
    partial_text = mm(text_mixed, text_out)
    text_rows = grp_scatter(partial_text, g, 0)
    encoded = rms_scale(quarter(flat_states, g) + text_rows, final_gain).astype(BF)

    part = text_width // pairs
    pieces = [
        lax.dynamic_slice_in_dim(encoded, ((z + far) % pairs) * part, part, 1)
        for far in range(pairs)
    ]
    mine = jnp.stack([fsend(p, far, 0) if far else p for far, p in enumerate(pieces)])
    over_x = jnp.concatenate([mine[:, None], gsend(mine, 2)[:, None]], axis=1)
    over_core = jnp.stack([over_x, gsend(over_x, 1)], axis=2)
    kv_partial = mm(over_core.reshape(-1, part), pair_kv).reshape(pairs, cap_len, 2 * width_local)
    kv_sum = kv_partial[0]
    for far in range(1, pairs):
        kv_sum += fsend(kv_partial[far].astype(BF), pairs - far, 0).astype(F32)
    kv_rows = kv_sum.astype(BF).reshape(4, cap_len // 4, 2 * width_local)
    order = jnp.arange(4, dtype=jnp.int32) ^ g
    cap_kv = jnp.concatenate(
        [lax.dynamic_slice_in_dim(kv_rows, order[k], 1, 0) for k in range(4)], axis=0
    ).reshape(cap_len, 2 * width_local)
    all_kv = jnp.stack(gather_direct(cap_kv))

    video = video_states.astype(F32)
    center = video - jnp.mean(video, axis=-1, keepdims=True)
    inverse = lax.rsqrt(jnp.mean(center * center, axis=-1, keepdims=True) + 1e-06)
    video_hat = center * inverse
    video_normed = video_hat.astype(BF)

    both = jnp.stack([quarter(video_normed, g), quarter(out_grad, g)])
    tiles = []
    for far in range(pairs):
        for side in range(2):
            tile = lax.dynamic_slice_in_dim(both, target(far, side) * query_rows, query_rows, 2)
            tiles.append(fsend(tile, far, side) if far or side else tile)
    tiles = jnp.stack(tiles)
    tiles_x = jnp.stack([tiles, gsend(tiles, 2)], axis=2)
    tiles_all = jnp.stack([tiles_x, gsend(tiles_x, 1)], axis=3)
    normed_tile = tiles_all[:, 0].reshape(-1, query_rows)
    grad_tile = tiles_all[:, 1].reshape(-1, query_rows)

    caption_total = all_kv.shape[0]
    positions = column * tokens + jnp.arange(tokens, dtype=jnp.int32)
    sample_end = jnp.cumsum(video_counts)
    token_sample = jnp.sum((sample_end[None, :] <= positions[:, None]).astype(jnp.int32), axis=1)
    slot_count = 3
    slot_sample = token_sample[0] + jnp.arange(slot_count, dtype=jnp.int32)
    slot_valid = slot_sample < caption_total
    slot_clipped = jnp.minimum(slot_sample, caption_total - 1)
    numbers = jnp.arange(caption_total, dtype=jnp.int32)
    slot_pick = slot_clipped[:, None] == numbers[None, :]
    slot_caption = jnp.sum(jnp.where(slot_pick, sample_caption[None, :], 0), axis=1)
    caption_pick = slot_caption[:, None] == numbers[None, :]
    slot_lens = jnp.sum(jnp.where(caption_pick, caption_lens[None, :], 0), axis=1)
    slot_member = token_sample[None, :] == slot_sample[:, None]
    member_float = slot_member.astype(F32)
    member_half = slot_member.astype(BF)
    slot_entry = ((z - slot_caption // 2) % pairs) * 2 + ((slot_caption % 2) ^ y)
    slot_kv = jnp.take(all_kv, slot_entry, axis=0)
    slot_keys = slot_kv[..., :width_local].reshape(slot_count, cap_len, cross_local, HEAD_SIZE)
    slot_values = slot_kv[..., width_local:].reshape(slot_count, cap_len, cross_local, HEAD_SIZE)
    token_lens = jnp.sum(jnp.where(slot_member, slot_lens[:, None], 0), axis=0)

    query_sum = mm(video_normed, full_query)
    queries = query_sum.astype(BF)
    d_attended = contract_last(out_grad, full_out).astype(BF).reshape(
        tokens, cross_local, HEAD_SIZE
    )
    score_scale = 1.0 / math.sqrt(HEAD_SIZE)
    query_heads = queries.reshape(tokens, cross_local, HEAD_SIZE)
    slot_scores = jnp.einsum("thd,kjhd->kthj", query_heads, slot_keys, preferred_element_type=F32)
    scores = jnp.sum(member_float[:, :, None, None] * slot_scores, axis=0) * score_scale
    token_valid = (jnp.arange(cap_len, dtype=jnp.int32)[None, :] < token_lens[:, None])[:, None, :]
    exp_video = jnp.where(token_valid, jnp.exp(scores), 0.0)
    weights = exp_video / jnp.sum(exp_video, axis=-1, keepdims=True)
    probs = weights.astype(BF)
    masked_probs = member_half[:, :, None, None] * probs[None]
    attended = jnp.einsum("kthj,kjhd->thd", masked_probs, slot_values, preferred_element_type=F32)
    attended = attended.astype(BF).reshape(tokens, width_local)

    def reorder(array):
        return jnp.concatenate([quarter(array, order[k]) for k in range(4)], axis=0)

    all_attended = jnp.concatenate(gather_direct(reorder(attended)), axis=0)
    out_weight_grad = contract_first(all_attended, grad_tile)

    out_share = grp_scatter(mm(attended, full_out), g, 1)
    updated = (quarter(video, g, 1) + out_share).astype(BF)

    slot_dprobs = jnp.einsum("thd,kjhd->kthj", d_attended, slot_values, preferred_element_type=F32)
    d_probs = jnp.sum(member_float[:, :, None, None] * slot_dprobs, axis=0)
    d_scores = (
        weights * (d_probs - jnp.sum(weights * d_probs, axis=-1, keepdims=True)) * score_scale
    ).astype(BF)
    masked_scores = member_half[:, :, None, None] * d_scores[None]
    d_queries = jnp.einsum("kthj,kjhd->thd", masked_scores, slot_keys, preferred_element_type=F32)
    d_queries = d_queries.astype(BF).reshape(tokens, width_local)
    all_d_queries = jnp.concatenate(gather_direct(reorder(d_queries)), axis=0)
    query_grad = contract_first(normed_tile, all_d_queries)

    key_slots = jnp.einsum("kthj,thd->kjhd", masked_scores, query_heads, preferred_element_type=F32)
    value_slots = jnp.einsum("kthj,thd->kjhd", masked_probs, d_attended, preferred_element_type=F32)
    slot_terms = jnp.concatenate(
        [
            key_slots.reshape(slot_count, cap_len, width_local),
            value_slots.reshape(slot_count, cap_len, width_local),
        ],
        axis=-1,
    )

    def caption_terms(far, side):
        picked = (slot_caption == target(far, side)) & slot_valid
        return jnp.sum(jnp.where(picked[:, None, None], slot_terms, 0.0), axis=0)

    away = jnp.stack([caption_terms(far, 1).astype(BF) for far in range(pairs)])
    got = fsend(away, 0, 1).astype(F32)
    kv_grads = caption_terms(0, 0) + got[0]
    for far in range(1, pairs):
        kv_grads += fsend((caption_terms(far, 0) + got[far]).astype(BF), far, 0).astype(F32)
    kv_grads = kv_grads.astype(BF)[None]
    key_grad = kv_grads[:, :, :width_local]
    value_grad = kv_grads[:, :, width_local:]

    d_wide = d_queries.astype(F32)
    column_sum = jnp.sum(full_query.astype(F32), axis=0)
    row_sums = jnp.stack(
        [jnp.sum(d_wide * column_sum, axis=-1), jnp.sum(d_wide * query_sum, axis=-1)]
    )
    row_sums = row_sums + gsend(row_sums, 1)
    row_sums = (row_sums + gsend(row_sums, 2)) / model_width
    d_share = grp_scatter(contract_last(d_queries, full_query), g, 1)
    input_grad = (
        quarter(out_grad, g, 1).astype(F32)
        + inverse
        * (d_share - row_sums[0][:, None] - quarter(video_hat, g, 1) * row_sums[1][:, None])
    ).astype(BF)
    return (updated, input_grad, query_grad, out_weight_grad, key_grad, value_grad)


def after(value, *others):
    return lax.optimization_barrier((value, *others))[0]


def call(body, out_shape, operands, scalars, scratch=()):
    specs = [pl.BlockSpec(memory_space=pltpu.SMEM)] * scalars
    specs += [pl.BlockSpec(memory_space=pltpu.VMEM)] * (len(operands) - scalars)
    held = (*operands[scalars:], *jax.tree.leaves(out_shape), *scratch)
    held_bytes = sum(math.prod(a.shape) * jnp.dtype(a.dtype).itemsize for a in held)
    return pl.pallas_call(
        body,
        out_shape=out_shape,
        in_specs=specs,
        out_specs=jax.tree.map(lambda _: pl.BlockSpec(memory_space=pltpu.VMEM), out_shape),
        scratch_shapes=list(scratch),
        compiler_params=pltpu.CompilerParams(vmem_limit_bytes=held_bytes + SPARE_BYTES),
        cost_estimate=SMALL,
    )(*operands)


def shaped(shape, dtype=BF):
    return jax.ShapeDtypeStruct(shape, dtype)


def aligned(start, unit):
    return pl.multiple_of(start, unit)


def project_text(states, gain, weights, steps=4):
    rows, depth = states.shape
    width = weights[0].shape[1]
    chunk = depth // steps

    def body(states_ref, gain_ref, wq_ref, wk_ref, wv_ref, out_ref, normed_ref, total_ref):
        step = pl.program_id(0)

        @pl.when(step == 0)
        def _():
            for at in range(0, rows, 16):
                values = states_ref[at : at + 16, :].astype(F32)
                normed_ref[at : at + 16, :] = rms_scale(values, gain_ref[...]).astype(BF)
            total_ref[...] = jnp.zeros_like(total_ref)

        here = normed_ref[:, pl.ds(aligned(step * chunk, chunk), chunk)]
        for k, weight_ref in enumerate((wq_ref, wk_ref, wv_ref)):
            total_ref[:, k * width : (k + 1) * width] += mm(here, weight_ref[...])

        @pl.when(step == steps - 1)
        def _():
            out_ref[...] = total_ref[...].astype(BF)

    whole = lambda shape: pl.BlockSpec(shape, lambda i: (0,) * len(shape))
    return pl.pallas_call(
        body,
        grid=(steps,),
        out_shape=shaped((rows, 3 * width)),
        in_specs=[whole((rows, depth)), whole((1, depth))]
        + [pl.BlockSpec((chunk, width), lambda i: (i, 0))] * 3,
        out_specs=whole((rows, 3 * width)),
        scratch_shapes=[pltpu.VMEM((rows, depth), BF), pltpu.VMEM((rows, 3 * width), F32)],
        compiler_params=pltpu.CompilerParams(vmem_limit_bytes=VMEM_BYTES),
        cost_estimate=SMALL,
    )(states, gain.reshape(1, -1), *weights)


def attend_text(projected, bias, text_out, place, lens, steps=4):
    rows = projected.shape[0]
    heads = bias.shape[0]
    inner, depth = text_out.shape
    size = inner // heads
    quarter_rows = rows // 4
    chunk = depth // steps

    def body(place_ref, len_ref, qkv_ref, bias_ref, out_ref, kept_ref, away_ref, held_ref, mixed_ref):
        @pl.when(pl.program_id(0) == 0)
        def _():
            g = place_ref[2]
            length = len_ref[place_ref[0] * 2 + place_ref[1]]
            live = lax.broadcasted_iota(jnp.int32, (rows, rows), 1) < length
            for head in range(heads):
                query, key, value = (
                    qkv_ref[:, k * inner + head * size : k * inner + (head + 1) * size]
                    for k in range(3)
                )
                grown = jnp.where(live, jnp.exp(contract_last(query, key) + bias_ref[head]), 0.0)
                weights = grown * (1.0 / jnp.sum(grown, axis=-1, keepdims=True))
                held_ref[:, head * size : (head + 1) * size] = mm(weights.astype(BF), value).astype(BF)
            for k, to in ((0, 0), (2, 1), (1, 2), (3, 3)):
                rows_from = pl.ds(aligned((g ^ k) * quarter_rows, quarter_rows), quarter_rows)
                mixed_ref[to * quarter_rows : (to + 1) * quarter_rows, :] = held_ref[rows_from, :]

        product = mm(mixed_ref[...], out_ref[...]).astype(BF)
        kept_ref[...] = product[: rows // 2]
        away_ref[...] = product[rows // 2 :]

    whole = lambda shape: pl.BlockSpec(shape, lambda i: (0,) * len(shape))
    return pl.pallas_call(
        body,
        grid=(steps,),
        out_shape=[shaped((rows // 2, depth))] * 2,
        in_specs=[pl.BlockSpec(memory_space=pltpu.SMEM)] * 2
        + [whole(projected.shape), whole(bias.shape)]
        + [pl.BlockSpec((inner, chunk), lambda i: (0, i))],
        out_specs=[pl.BlockSpec((rows // 2, chunk), lambda i: (0, i))] * 2,
        scratch_shapes=[pltpu.VMEM((rows, inner), BF), pltpu.VMEM((rows, inner), BF)],
        compiler_params=pltpu.CompilerParams(vmem_limit_bytes=VMEM_BYTES),
        cost_estimate=SMALL,
    )(place, lens, projected, bias, text_out)


def encode_rows(states, kept, got, far, gain, place, pairs):
    quarter_rows = states.shape[0] // 4
    width = states.shape[1]
    depth = width // pairs

    def body(place_ref, states_ref, kept_ref, got_ref, far_ref, gain_ref, *refs):
        piece_refs, encoded_ref = refs[:-1], refs[-1]
        z, g = place_ref[0], place_ref[2]
        mine = pl.ds(aligned(g * quarter_rows, quarter_rows), quarter_rows)
        total = states_ref[mine, :].astype(F32) + far_ref[...].astype(F32)
        total += kept_ref[:quarter_rows, :].astype(F32) + got_ref[:quarter_rows, :].astype(F32)
        encoded_ref[...] = rms_scale(total, gain_ref[...]).astype(BF)
        for far_by, piece in enumerate(piece_refs):
            to = lax.rem(z + far_by, pairs)
            piece[...] = encoded_ref[:, pl.ds(aligned(to * depth, 128), depth)]

    out = [shaped((quarter_rows, depth))] * pairs
    operands = (place, states, kept, got, far, gain.reshape(1, -1))
    return call(body, out, operands, 1, [pltpu.VMEM((quarter_rows, width), BF)])


def pieces_of(pairs_of_blocks):
    arrays, listed = [], []
    for entry in pairs_of_blocks:
        numbers = []
        for array, start in entry:
            if not any(array is held for held in arrays):
                arrays.append(array)
            numbers.append((next(k for k, held in enumerate(arrays) if held is array), start))
        listed.append(numbers)
    return arrays, listed


def prepare_video(video_states, out_grad, place, pairs, part):
    tokens, model_width = video_states.shape
    rows = tokens // 4

    def body(place_ref, video_ref, grad_ref, normed_ref, mean_ref, inverse_ref, *tile_refs):
        @pl.loop(0, tokens // 32)
        def _(step):
            here = pl.ds(aligned(step * 32, 32), 32)
            values = video_ref[here, :].astype(F32)
            mean = jnp.mean(values, axis=-1, keepdims=True)
            center = values - mean
            inverse = lax.rsqrt(jnp.mean(center * center, axis=-1, keepdims=True) + 1e-06)
            normed_ref[here, :] = (center * inverse).astype(BF)
            mean_ref[here, :] = mean
            inverse_ref[here, :] = inverse

        z, y, g = place_ref[0], place_ref[1], place_ref[2]
        mine = pl.ds(aligned(g * rows, rows), rows)
        for far in range(pairs):
            for side in range(2):
                to = lax.rem(z + far, pairs) * 2 + (y ^ side)
                columns = pl.ds(aligned(to * part, 128), part)
                tile_refs[side][far, 0] = normed_ref[mine, columns]
                tile_refs[side][far, 1] = grad_ref[mine, columns]

    out = [shaped((tokens, model_width)), shaped((tokens, 1), F32), shaped((tokens, 1), F32)]
    out += [shaped((pairs, 2, rows, part))] * 2
    return call(body, out, (place, video_states, out_grad), 1)


def project_rows(normed, out_grad, blocks, place, pairs, part):
    tokens = normed.shape[0]
    arrays, blocks = pieces_of(blocks)
    width = arrays[0].shape[1]

    def body(place_ref, normed_ref, grad_ref, *refs):
        block_refs, (query_ref, d_ref, sum_ref) = refs[:-3], refs[-3:]
        z, y = place_ref[0], place_ref[1]
        query = jnp.zeros((tokens, width), F32)
        d_attended = jnp.zeros((tokens, width), F32)
        total = jnp.zeros((1, width), F32)
        for far in range(pairs):
            for side in range(2):
                (of_query, query_at), (of_out, out_at) = blocks[2 * far + side]
                origin = lax.rem(z - far + pairs, pairs) * 2 + (y ^ side)
                columns = pl.ds(aligned(origin * part, 128), part)
                weight = block_refs[of_query][query_at : query_at + part, :]
                out_weight = block_refs[of_out][out_at : out_at + width, :]
                query += mm(normed_ref[:, columns], weight)
                d_attended += contract_last(grad_ref[:, columns], out_weight)
                total += jnp.sum(weight.astype(F32), axis=0, keepdims=True)
        query_ref[...] = query.astype(BF)
        d_ref[...] = d_attended.astype(BF)
        sum_ref[...] = total

    out = [shaped((tokens, width)), shaped((tokens, width)), shaped((1, width), F32)]
    return call(body, out, (place, normed, out_grad, *arrays), 1)


def project_captions(parts, own_key, own_value, side_key, side_value, place, pairs):
    quarter_rows, depth = parts[0].shape[1:]
    half = depth // 2
    width = own_key.shape[1]

    def body(place_ref, *refs):
        part_refs = refs[:4]
        key_ref, value_ref, side_key_ref, side_value_ref = refs[4:8]
        out_refs = refs[8:]
        y = place_ref[1]
        mine = pl.ds(aligned(y * half, 128), half)
        theirs = pl.ds(aligned((1 - y) * half, 128), half)
        own = jnp.concatenate([r[far, :, mine] for far in range(pairs) for r in part_refs], 0)
        other = jnp.concatenate([r[far, :, theirs] for far in range(pairs) for r in part_refs], 0)
        keys = mm(own, key_ref[...]) + mm(other, side_key_ref[...])
        values = mm(own, value_ref[...]) + mm(other, side_value_ref[...])
        for far in range(pairs):
            rows = slice(far * 4 * quarter_rows, (far + 1) * 4 * quarter_rows)
            out_refs[far][:, :width] = keys[rows].astype(BF)
            out_refs[far][:, width:] = values[rows].astype(BF)

    out = [shaped((4 * quarter_rows, 2 * width))] * pairs
    operands = (place, *parts, own_key, own_value, side_key, side_value)
    return call(body, out, operands, 1)


def slots_of(count_ref, caption_ref, base, captions):
    def find(sample, carry):
        total, first, start = carry
        total = total + count_ref[sample]
        past = total <= base
        return total, first + past.astype(jnp.int32), jnp.where(past, total, start)

    zero = jnp.int32(0)
    _, first, start = lax.fori_loop(0, captions, find, (zero, zero, zero))
    found, edge = [], start - base
    for slot in range(SLOTS):
        valid = first + slot < captions
        sample = jnp.minimum(first + slot, captions - 1)
        end = edge + jnp.where(valid, count_ref[sample], 0)
        found.append((edge, end, caption_ref[sample], valid))
        edge = end
    return found


def attend(queries, d_attended, column_sum, kv_blocks, place, counts, sample_caption, lens, pairs):
    tokens, width = queries.shape
    cap_len = kv_blocks[0].shape[0]
    heads = width // HEAD_SIZE
    captions = counts.shape[0]
    keys_wide = SLOTS * cap_len
    cap_quarter, row_quarter = cap_len // 4, tokens // 4
    scale = 1.0 / math.sqrt(HEAD_SIZE)

    def body(place_ref, count_ref, caption_ref, len_ref, q_ref, da_ref, sum_ref, *refs):
        block_refs = refs[: len(kv_blocks)]
        both_ref, att_ref, dq_ref, rows_ref, slot_ref, kv_ref = refs[len(kv_blocks) :]
        z, y, g = place_ref[0], place_ref[1], place_ref[2]
        low, high, length = [], [], []
        found = slots_of(count_ref, caption_ref, (z * 2 + y) * tokens, captions)
        for slot, (start, end, caption, _) in enumerate(found):
            low.append(start)
            high.append(end)
            length.append(len_ref[caption])
            entry = lax.rem(z - caption // 2 + pairs, pairs) * 2 + (lax.rem(caption, 2) ^ y)
            for number, block in enumerate(block_refs):

                @pl.when(entry == number)
                def _(slot=slot, block=block):
                    kv_ref[slot * cap_len : (slot + 1) * cap_len, :] = block[...]

        token = lax.broadcasted_iota(jnp.int32, (tokens, keys_wide), 0)
        column = lax.broadcasted_iota(jnp.int32, (tokens, keys_wide), 1)
        slot_of = column // cap_len
        inside = column % cap_len
        key = ((inside // cap_quarter) ^ g) * cap_quarter + inside % cap_quarter

        def of_slot(values):
            return jnp.where(slot_of == 0, values[0], jnp.where(slot_of == 1, values[1], values[2]))

        live = (token >= of_slot(low)) & (token < of_slot(high)) & (key < of_slot(length))
        first_sum = jnp.zeros((tokens, 1), F32)
        second_sum = jnp.zeros((tokens, 1), F32)
        for head in range(heads):
            at = slice(head * HEAD_SIZE, (head + 1) * HEAD_SIZE)
            at_value = slice(width + head * HEAD_SIZE, width + (head + 1) * HEAD_SIZE)
            query, d_att = q_ref[:, at], da_ref[:, at]
            keys, values = kv_ref[:, at], kv_ref[:, at_value]
            grown = jnp.where(live, jnp.exp(contract_last(query, keys) * scale), 0.0)
            weights = grown * (1.0 / jnp.sum(grown, axis=-1, keepdims=True))
            probs = weights.astype(BF)
            d_probs = contract_last(d_att, values)
            mixed = jnp.sum(weights * d_probs, axis=-1, keepdims=True)
            d_scores = (weights * (d_probs - mixed) * scale).astype(BF)
            att_ref[:, at] = mm(probs, values).astype(BF)
            d_query = mm(d_scores, keys).astype(BF)
            dq_ref[:, at] = d_query
            d_wide = d_query.astype(F32)
            first_sum += jnp.sum(d_wide * sum_ref[:, at], axis=-1, keepdims=True)
            second_sum += jnp.sum(d_wide * query.astype(F32), axis=-1, keepdims=True)
            key_grad = contract_first(d_scores, query).astype(BF)
            value_grad = contract_first(probs, d_att).astype(BF)
            for slot in range(SLOTS):
                for part in range(4):
                    held = slice(
                        slot * cap_len + part * cap_quarter, slot * cap_len + (part + 1) * cap_quarter
                    )
                    to = pl.ds(aligned((part ^ g) * cap_quarter, cap_quarter), cap_quarter)
                    slot_ref[slot, to, at] = key_grad[held]
                    slot_ref[slot, to, at_value] = value_grad[held]

        rows_ref[:, 0:1] = first_sum
        rows_ref[:, 1:2] = second_sum
        for part in range(4):
            rows = pl.ds(aligned((part ^ g) * row_quarter, row_quarter), row_quarter)
            to = slice(part * row_quarter, (part + 1) * row_quarter)
            both_ref[0, to, :] = att_ref[rows, :]
            both_ref[1, to, :] = dq_ref[rows, :]

    out = [
        shaped((2, tokens, width)),
        shaped((tokens, width)),
        shaped((tokens, width)),
        shaped((tokens, 2), F32),
        shaped((SLOTS, cap_len, 2 * width)),
    ]
    operands = (place, counts, sample_caption, lens, queries, d_attended, column_sum, *kv_blocks)
    scratch = [pltpu.VMEM((keys_wide, 2 * width), BF)]
    return call(body, out, operands, 4, scratch)


def caption_terms(slots, side_slots, place, counts, sample_caption, tokens, pairs):
    captions = counts.shape[0]
    shape = slots.shape[1:]

    def body(place_ref, count_ref, caption_ref, own_ref, side_ref, *refs):
        term_refs, total_ref = refs[:-1], refs[-1]
        z, y = place_ref[0], place_ref[1]
        total_ref[...] = jnp.zeros_like(total_ref)
        for side, slot_ref in enumerate((own_ref, side_ref)):
            base = (z * 2 + (y ^ side)) * tokens
            for slot, (_, _, caption, valid) in enumerate(
                slots_of(count_ref, caption_ref, base, captions)
            ):
                far = lax.rem(caption // 2 - z + pairs, pairs)

                @pl.when(valid & (lax.rem(caption, 2) == y))
                def _(slot=slot, far=far, slot_ref=slot_ref):
                    total_ref[far] += slot_ref[slot].astype(F32)

        for far, term_ref in enumerate(term_refs):
            term_ref[...] = total_ref[far].astype(term_ref.dtype)

    out = [shaped(shape, F32 if far == 0 else BF) for far in range(pairs)]
    operands = (place, counts, sample_caption, slots, side_slots)
    return call(body, out, operands, 3, [pltpu.VMEM((pairs, *shape), F32)])


def project_back(attended, d_queries, blocks, place, pairs, part):
    tokens, width = attended.shape
    arrays, blocks = pieces_of(blocks)
    model_width = 2 * pairs * part
    per_piece = 2 * pairs // 4
    piece = model_width // 4

    def body(place_ref, att_ref, dq_ref, *refs):
        block_refs = refs[: len(arrays)]
        own_ref, far_ref, away_ref = refs[len(arrays) :]
        z, y, g = place_ref[0], place_ref[1], place_ref[2]
        att, d_query = att_ref[...], dq_ref[...]
        for far in range(pairs):
            for side in range(2):
                (of_query, query_at), (of_out, out_at) = blocks[2 * far + side]
                weight = block_refs[of_query][query_at : query_at + part, :]
                out_weight = block_refs[of_out][out_at : out_at + width, :]
                origin = lax.rem(z - far + pairs, pairs) * 2 + (y ^ side)
                flip = (origin // per_piece) ^ g
                start = lax.rem(origin, per_piece) * part
                columns = pl.ds(aligned(start, 128), part)
                beyond = pl.ds(aligned(start + piece, 128), part)
                added = mm(att, out_weight).astype(BF)
                d_normed = contract_last(d_query, weight).astype(BF)
                places = ((own_ref, columns), (away_ref, columns), (far_ref, columns), (away_ref, beyond))
                for number, (target_ref, to) in enumerate(places):

                    @pl.when(flip == number)
                    def _(target_ref=target_ref, to=to, added=added, d_normed=d_normed):
                        target_ref[0, :, to] = added
                        target_ref[1, :, to] = d_normed

    out = [shaped((2, tokens, piece)), shaped((2, tokens, piece)), shaped((2, tokens, 2 * piece))]
    return call(body, out, (place, attended, d_queries, *arrays), 1)


def weight_grads(tiles, both_blocks, known, pairs):
    part = tiles[0].shape[-1]
    given = [k for k, block in enumerate(both_blocks) if block is not None]
    arrays, blocks = pieces_of([both_blocks[k] for k in given])
    width = arrays[0].shape[-1]
    known = known or []

    def body(*refs):
        tile_refs, known_refs = refs[:4], refs[4 : 4 + len(known)]
        block_refs, (query_ref, out_ref) = refs[4 + len(known) : -2], refs[-2:]
        query_grad = known_refs[0][...] if known else jnp.zeros((part, width), F32)
        out_grad = known_refs[1][...] if known else jnp.zeros((width, part), F32)
        for k, ((number, at),) in zip(given, blocks):
            side, far = divmod(k, pairs)
            block = block_refs[number]
            normed, grad = (
                jnp.concatenate([r[far, side, which] for r in tile_refs], axis=0)
                for which in range(2)
            )
            out_grad += contract_first(block[at], grad)
            query_grad += contract_first(normed, block[at + 1])
        query_ref[...] = query_grad
        out_ref[...] = out_grad

    out = [shaped((part, width), F32), shaped((width, part), F32)]
    return call(body, out, (*tiles, *known, *arrays), 0)


def local(
    caption_states,
    caption_lens,
    text_gain,
    text_query,
    text_key,
    text_value,
    text_bias,
    text_out,
    final_gain,
    cross_key,
    cross_value,
    video_states,
    video_counts,
    sample_caption,
    cross_query,
    cross_out,
    out_grad,
):
    column = lax.axis_index("fsdp")
    g = lax.axis_index("grp")
    pairs = lax.axis_size("fsdp") // 2
    z, y = column // 2, column % 2
    place = jnp.stack([z, y, g]).astype(jnp.int32)
    caps_local, cap_len, text_width = caption_states.shape
    tokens, model_width = video_states.shape
    width_local = cross_key.shape[1]
    part = cross_query.shape[0]

    states = caption_states.reshape(cap_len, text_width)
    quarter_rows = cap_len // 4

    first = [fsend(cross_query, 1, 0), fsend(cross_out, 1, 0)]
    side_key, side_value = fsend(cross_key, 0, 1), fsend(cross_value, 0, 1)
    projected = project_text(states, text_gain, (text_query, text_key, text_value))
    kept, away = attend_text(projected, text_bias, text_out, place, caption_lens)
    kept, away = after((kept, away), first, side_key, side_value)
    got = gsend(away, 1)
    ring = [None, jnp.concatenate(first, axis=0)]
    side_own = [fsend(w, 0, 1) for w in (cross_query, cross_out)]
    side_first = fsend(ring[1], 0, 1)
    ring.append(fsend(ring[1], 1, 0))
    sent = (kept[quarter_rows:].astype(F32) + got[quarter_rows:].astype(F32)).astype(BF)
    over_x = gsend(sent, 2)
    normed, mean, inverse, own_tiles, other_tiles = prepare_video(
        after(video_states, sent), out_grad, place, pairs, part
    )
    pieces = encode_rows(
        states, kept, got, after(over_x, normed, *side_own), final_gain, place, pairs
    )

    mine = jnp.stack([fsend(p, far, 0) if far else p for far, p in enumerate(pieces)])
    mine = after(mine, ring[2], side_first)
    over_x = gsend(mine, 2)
    parts = [mine, gsend(mine, 1), over_x, gsend(over_x, 1)]
    current = after(ring[2], mine)
    for far in range(3, pairs):
        current = fsend(current, 1, 0)
        ring.append(current)
    kv_partial = project_captions(
        parts, cross_key, cross_value, side_key, side_value, place, pairs
    )
    kv_partial = after(tuple(kv_partial), ring[-1])
    kv_sum = kv_partial[0].astype(F32)
    for far in range(1, pairs):
        kv_sum += fsend(kv_partial[far], pairs - far, 0).astype(F32)
    side_later = [fsend(w, 0, 1) for w in ring[2:]]
    other_tiles = fsend(other_tiles, 0, 1)
    kv_sum = after(kv_sum.astype(BF), side_later[0])
    kv_blocks = gather_direct(kv_sum)
    kv_blocks[4] = after(kv_blocks[4], side_later, other_tiles)

    blocks = [((cross_query, 0), (cross_out, 0)), ((side_own[0], 0), (side_own[1], 0))]
    for held, side in zip(ring[1:], [side_first, *side_later]):
        blocks += [((held, 0), (held, part)), ((side, 0), (side, part))]
    queries, d_attended, column_sum = project_rows(
        normed, after(out_grad, kv_blocks[4]), blocks, place, pairs, part
    )

    tiles = jnp.stack([own_tiles, other_tiles], axis=1)
    over_z = [fsend(after(tiles[far], kv_blocks[4]), far, 0) for far in range(1, pairs)]
    over_z = [tiles[0]] + over_z

    both, attended, d_queries, row_sums, slots = attend(
        queries,
        d_attended,
        column_sum,
        kv_blocks,
        place,
        video_counts,
        sample_caption,
        caption_lens,
        pairs,
    )

    def chain(blocks, steps):
        for _ in range(steps):
            blocks.append(fsend(blocks[-1], 1, 0))
        return blocks

    side_slots = fsend(slots, 0, 1)
    side_mine = fsend(both, 0, 1)
    first, over_z = after((both, over_z))
    tiles = jnp.stack(over_z)
    late = chain([first], 2)
    sums_core = gsend(row_sums, 1)
    row_sums = row_sums + sums_core
    attended, tiles = after((attended, tiles), row_sums)
    tiles_x = gsend(tiles, 2)
    own, far_piece, away = project_back(attended, d_queries, blocks, place, pairs, part)
    tiles_core = gsend(tiles, 1)
    stage = (side_slots, side_mine, late, row_sums, tiles_x, tiles_core, away)
    side_slots, side_mine, late, row_sums, tiles_x, tiles_core, away = after(stage)

    sides = [fsend(block, 0, 1) for block in late[1:3]]
    late = chain(list(late), pairs - 3)
    got = gsend(away, 1)
    width = model_width // 4
    sent = [
        (far_piece[k].astype(F32) + got[k, :, width:].astype(F32)).astype(BF) for k in range(2)
    ]
    sums_x = gsend(row_sums, 2)
    far_out = gsend(after(sent[0], sums_x), 2)
    terms = caption_terms(
        after(slots, sent[0]), side_slots, place, video_counts, sample_caption, tokens, pairs
    )
    kv_parts = [fsend(terms[1], 1, 0)]
    stage = (sides, late, tiles_x, kv_parts, terms, far_out, sent[1])
    sides, late, tiles_x, kv_parts, terms, far_out, sent_d = after(stage)

    here = [((block, 0),) for block in late]
    tiles = [tiles, tiles_core, tiles_x, gsend(tiles_x, 1)]
    there = [((block, 0),) for block in (side_mine, *sides)]
    there += [((fsend(block, 0, 1), 0),) for block in late[3:]]
    known = weight_grads(tiles, here + there[:3], None, pairs)
    total = [
        own[k].astype(F32) + got[k, :, :width].astype(F32) + far.astype(F32)
        for k, far in enumerate((far_out, after(gsend(sent_d, 2), known)))
    ]
    row_sums = (row_sums + sums_x) / model_width
    video = quarter(video_states, g, 1).astype(F32)
    updated = (video + total[0]).astype(BF)
    video_hat = (video - mean) * inverse
    input_grad = (
        quarter(out_grad, g, 1).astype(F32)
        + inverse * (total[1] - row_sums[:, 0:1] - video_hat * row_sums[:, 1:2])
    ).astype(BF)
    kv_parts += [fsend(terms[far], far, 0) for far in range(2, pairs)]
    kv_parts = after(kv_parts, known)
    kv_grads = (terms[0] + sum(p.astype(F32) for p in kv_parts)).astype(BF)[None]
    key_grad = kv_grads[:, :, :width_local]
    value_grad = kv_grads[:, :, width_local:]
    known = after(known, updated, input_grad)
    query_grad, out_weight_grad = weight_grads(
        tiles, [None] * (pairs + 3) + there[3:], known, pairs
    )
    return (updated, input_grad, query_grad, out_weight_grad, key_grad, value_grad)


def local_of(*arrays):
    whole_tiles = arrays[14].shape[0] % 128 == 0 and arrays[0].shape[0] == 1
    return local(*arrays) if whole_tiles else local_general(*arrays)


def solution(mesh):
    in_specs = (
        P("fsdp", None, None),
        P(),
        P(),
        P(None, "grp"),
        P(None, "grp"),
        P(None, "grp"),
        P("grp", None, None),
        P("grp", None),
        P(),
        P("fsdp", "grp"),
        P("fsdp", "grp"),
        P("fsdp", None),
        P(),
        P(),
        P("fsdp", "grp"),
        P("grp", "fsdp"),
        P("fsdp", None),
    )
    out_specs = (
        P("fsdp", "grp"),
        P("fsdp", "grp"),
        P("fsdp", "grp"),
        P("grp", "fsdp"),
        P("fsdp", None, "grp"),
        P("fsdp", None, "grp"),
    )
    return jax.shard_map(
        local_of, mesh=mesh, in_specs=in_specs, out_specs=out_specs, check_vma=False
    )
```

```python
import math

import jax
import jax.numpy as jnp
from jax import lax
from jax.experimental import pallas as pl
from jax.experimental.pallas import tpu as pltpu
from jax.sharding import PartitionSpec as P

HEAD_SIZE = 128
BF = jnp.bfloat16
F32 = jnp.float32
SLOTS = 3
VMEM_BYTES = 60 * 1024 * 1024
SPARE_BYTES = 8 * 1024 * 1024
SMALL = pl.CostEstimate(flops=1, bytes_accessed=1, transcendentals=0)


def rms_scale(values, gain):
    mean_square = jnp.mean(values * values, axis=-1, keepdims=True)
    return values * lax.rsqrt(mean_square + 1e-06) * gain


def mm(left, right):
    return jnp.dot(left, right, preferred_element_type=F32)


def contract_last(left, right):
    return lax.dot_general(left, right, (((1,), (1,)), ((), ())), preferred_element_type=F32)


def contract_first(left, right):
    return lax.dot_general(left, right, (((0,), (0,)), ((), ())), preferred_element_type=F32)


def fsend(block, far, side):
    size = lax.axis_size("fsdp")
    pairs = size // 2
    perm = [(s, ((s // 2 + far) % pairs) * 2 + ((s % 2) ^ side)) for s in range(size)]
    return lax.ppermute(block, "fsdp", perm)


def gsend(block, flip):
    return lax.ppermute(block, "grp", [(s, s ^ flip) for s in range(lax.axis_size("grp"))])


def gather_ring(block):
    blocks = []
    current = block
    for far in range(lax.axis_size("fsdp") // 2):
        if far:
            current = fsend(current, 1, 0)
        blocks += [current, fsend(current, 0, 1)]
    return blocks


def gather_direct(block):
    blocks = []
    for far in range(lax.axis_size("fsdp") // 2):
        current = fsend(block, far, 0) if far else block
        blocks += [current, fsend(current, 0, 1)]
    return blocks


def quarter(array, index, axis=0):
    size = array.shape[axis] // 4
    return lax.dynamic_slice_in_dim(array, index * size, size, axis)


def grp_scatter(partial, g, axis):
    away = [quarter(partial, g ^ 1, axis), quarter(partial, g ^ 3, axis)]
    kept = [quarter(partial, g, axis), quarter(partial, g ^ 2, axis)]
    got = gsend(jnp.stack(away).astype(BF), 1)
    far = gsend((kept[1] + got[1].astype(F32)).astype(BF), 2)
    return kept[0] + got[0].astype(F32) + far.astype(F32)


def local_general(
    caption_states,
    caption_lens,
    text_gain,
    text_query,
    text_key,
    text_value,
    text_bias,
    text_out,
    final_gain,
    cross_key,
    cross_value,
    video_states,
    video_counts,
    sample_caption,
    cross_query,
    cross_out,
    out_grad,
):
    column = lax.axis_index("fsdp")
    g = lax.axis_index("grp")
    fsdp = lax.axis_size("fsdp")
    pairs = fsdp // 2
    z, y = column // 2, column % 2
    caps_local, cap_len, text_width = caption_states.shape
    tokens, model_width = video_states.shape
    width_local = cross_key.shape[1]
    cross_local = width_local // HEAD_SIZE
    query_rows = cross_query.shape[0]

    def source(far, side):
        return ((z - far) % pairs) * 2 + (y ^ side)

    def target(far, side):
        return ((z + far) % pairs) * 2 + (y ^ side)

    query_blocks = gather_ring(cross_query)
    out_blocks = gather_ring(cross_out)
    full_query = jnp.zeros((model_width, width_local), BF)
    full_out = jnp.zeros((width_local, model_width), BF)
    for far in range(pairs):
        for side in range(2):
            start = source(far, side) * query_rows
            full_query = lax.dynamic_update_slice(
                full_query, query_blocks[2 * far + side], (start, jnp.int32(0))
            )
            full_out = lax.dynamic_update_slice(
                full_out, out_blocks[2 * far + side], (jnp.int32(0), start)
            )

    own_kv = jnp.concatenate([cross_key, cross_value], axis=1)
    other_kv = fsend(own_kv, 0, 1)
    pair_kv = jnp.concatenate(
        [jnp.where(y == 0, own_kv, other_kv), jnp.where(y == 0, other_kv, own_kv)], axis=0
    )

    local_lens = lax.dynamic_slice_in_dim(caption_lens, column * caps_local, caps_local)
    flat_states = caption_states.reshape(caps_local * cap_len, text_width).astype(F32)
    text_normed = rms_scale(flat_states, text_gain).astype(BF)
    local_heads = text_bias.shape[0]
    head_width = text_query.shape[1] // local_heads

    def heads_of(weight):
        return mm(text_normed, weight).astype(BF).reshape(
            caps_local, cap_len, local_heads, head_width
        )

    text_queries = heads_of(text_query)
    text_keys = heads_of(text_key)
    text_values = heads_of(text_value)
    text_scores = (
        jnp.einsum("cihd,cjhd->chij", text_queries, text_keys, preferred_element_type=F32)
        + text_bias[None]
    )
    key_valid = jnp.arange(cap_len, dtype=jnp.int32)[None, :] < local_lens[:, None]
    exp_scores = jnp.where(key_valid[:, None, None, :], jnp.exp(text_scores), 0.0)
    text_weights = (exp_scores / jnp.sum(exp_scores, axis=-1, keepdims=True)).astype(BF)
    text_mixed = jnp.einsum(
        "chij,cjhd->cihd", text_weights, text_values, preferred_element_type=F32
    )
    text_mixed = text_mixed.astype(BF).reshape(caps_local * cap_len, local_heads * head_width)
    partial_text = mm(text_mixed, text_out)
    text_rows = grp_scatter(partial_text, g, 0)
    encoded = rms_scale(quarter(flat_states, g) + text_rows, final_gain).astype(BF)

    part = text_width // pairs
    pieces = [
        lax.dynamic_slice_in_dim(encoded, ((z + far) % pairs) * part, part, 1)
        for far in range(pairs)
    ]
    mine = jnp.stack([fsend(p, far, 0) if far else p for far, p in enumerate(pieces)])
    over_x = jnp.concatenate([mine[:, None], gsend(mine, 2)[:, None]], axis=1)
    over_core = jnp.stack([over_x, gsend(over_x, 1)], axis=2)
    kv_partial = mm(over_core.reshape(-1, part), pair_kv).reshape(pairs, cap_len, 2 * width_local)
    kv_sum = kv_partial[0]
    for far in range(1, pairs):
        kv_sum += fsend(kv_partial[far].astype(BF), pairs - far, 0).astype(F32)
    kv_rows = kv_sum.astype(BF).reshape(4, cap_len // 4, 2 * width_local)
    order = jnp.arange(4, dtype=jnp.int32) ^ g
    cap_kv = jnp.concatenate(
        [lax.dynamic_slice_in_dim(kv_rows, order[k], 1, 0) for k in range(4)], axis=0
    ).reshape(cap_len, 2 * width_local)
    all_kv = jnp.stack(gather_direct(cap_kv))

    video = video_states.astype(F32)
    center = video - jnp.mean(video, axis=-1, keepdims=True)
    inverse = lax.rsqrt(jnp.mean(center * center, axis=-1, keepdims=True) + 1e-06)
    video_hat = center * inverse
    video_normed = video_hat.astype(BF)

    both = jnp.stack([quarter(video_normed, g), quarter(out_grad, g)])
    tiles = []
    for far in range(pairs):
        for side in range(2):
            tile = lax.dynamic_slice_in_dim(both, target(far, side) * query_rows, query_rows, 2)
            tiles.append(fsend(tile, far, side) if far or side else tile)
    tiles = jnp.stack(tiles)
    tiles_x = jnp.stack([tiles, gsend(tiles, 2)], axis=2)
    tiles_all = jnp.stack([tiles_x, gsend(tiles_x, 1)], axis=3)
    normed_tile = tiles_all[:, 0].reshape(-1, query_rows)
    grad_tile = tiles_all[:, 1].reshape(-1, query_rows)

    caption_total = all_kv.shape[0]
    positions = column * tokens + jnp.arange(tokens, dtype=jnp.int32)
    sample_end = jnp.cumsum(video_counts)
    token_sample = jnp.sum((sample_end[None, :] <= positions[:, None]).astype(jnp.int32), axis=1)
    slot_count = 3
    slot_sample = token_sample[0] + jnp.arange(slot_count, dtype=jnp.int32)
    slot_valid = slot_sample < caption_total
    slot_clipped = jnp.minimum(slot_sample, caption_total - 1)
    numbers = jnp.arange(caption_total, dtype=jnp.int32)
    slot_pick = slot_clipped[:, None] == numbers[None, :]
    slot_caption = jnp.sum(jnp.where(slot_pick, sample_caption[None, :], 0), axis=1)
    caption_pick = slot_caption[:, None] == numbers[None, :]
    slot_lens = jnp.sum(jnp.where(caption_pick, caption_lens[None, :], 0), axis=1)
    slot_member = token_sample[None, :] == slot_sample[:, None]
    member_float = slot_member.astype(F32)
    member_half = slot_member.astype(BF)
    slot_entry = ((z - slot_caption // 2) % pairs) * 2 + ((slot_caption % 2) ^ y)
    slot_kv = jnp.take(all_kv, slot_entry, axis=0)
    slot_keys = slot_kv[..., :width_local].reshape(slot_count, cap_len, cross_local, HEAD_SIZE)
    slot_values = slot_kv[..., width_local:].reshape(slot_count, cap_len, cross_local, HEAD_SIZE)
    token_lens = jnp.sum(jnp.where(slot_member, slot_lens[:, None], 0), axis=0)

    query_sum = mm(video_normed, full_query)
    queries = query_sum.astype(BF)
    d_attended = contract_last(out_grad, full_out).astype(BF).reshape(
        tokens, cross_local, HEAD_SIZE
    )
    score_scale = 1.0 / math.sqrt(HEAD_SIZE)
    query_heads = queries.reshape(tokens, cross_local, HEAD_SIZE)
    slot_scores = jnp.einsum("thd,kjhd->kthj", query_heads, slot_keys, preferred_element_type=F32)
    scores = jnp.sum(member_float[:, :, None, None] * slot_scores, axis=0) * score_scale
    token_valid = (jnp.arange(cap_len, dtype=jnp.int32)[None, :] < token_lens[:, None])[:, None, :]
    exp_video = jnp.where(token_valid, jnp.exp(scores), 0.0)
    weights = exp_video / jnp.sum(exp_video, axis=-1, keepdims=True)
    probs = weights.astype(BF)
    masked_probs = member_half[:, :, None, None] * probs[None]
    attended = jnp.einsum("kthj,kjhd->thd", masked_probs, slot_values, preferred_element_type=F32)
    attended = attended.astype(BF).reshape(tokens, width_local)

    def reorder(array):
        return jnp.concatenate([quarter(array, order[k]) for k in range(4)], axis=0)

    all_attended = jnp.concatenate(gather_direct(reorder(attended)), axis=0)
    out_weight_grad = contract_first(all_attended, grad_tile)

    out_share = grp_scatter(mm(attended, full_out), g, 1)
    updated = (quarter(video, g, 1) + out_share).astype(BF)

    slot_dprobs = jnp.einsum("thd,kjhd->kthj", d_attended, slot_values, preferred_element_type=F32)
    d_probs = jnp.sum(member_float[:, :, None, None] * slot_dprobs, axis=0)
    d_scores = (
        weights * (d_probs - jnp.sum(weights * d_probs, axis=-1, keepdims=True)) * score_scale
    ).astype(BF)
    masked_scores = member_half[:, :, None, None] * d_scores[None]
    d_queries = jnp.einsum("kthj,kjhd->thd", masked_scores, slot_keys, preferred_element_type=F32)
    d_queries = d_queries.astype(BF).reshape(tokens, width_local)
    all_d_queries = jnp.concatenate(gather_direct(reorder(d_queries)), axis=0)
    query_grad = contract_first(normed_tile, all_d_queries)

    key_slots = jnp.einsum("kthj,thd->kjhd", masked_scores, query_heads, preferred_element_type=F32)
    value_slots = jnp.einsum("kthj,thd->kjhd", masked_probs, d_attended, preferred_element_type=F32)
    slot_terms = jnp.concatenate(
        [
            key_slots.reshape(slot_count, cap_len, width_local),
            value_slots.reshape(slot_count, cap_len, width_local),
        ],
        axis=-1,
    )

    def caption_terms(far, side):
        picked = (slot_caption == target(far, side)) & slot_valid
        return jnp.sum(jnp.where(picked[:, None, None], slot_terms, 0.0), axis=0)

    away = jnp.stack([caption_terms(far, 1).astype(BF) for far in range(pairs)])
    got = fsend(away, 0, 1).astype(F32)
    kv_grads = caption_terms(0, 0) + got[0]
    for far in range(1, pairs):
        kv_grads += fsend((caption_terms(far, 0) + got[far]).astype(BF), far, 0).astype(F32)
    kv_grads = kv_grads.astype(BF)[None]
    key_grad = kv_grads[:, :, :width_local]
    value_grad = kv_grads[:, :, width_local:]

    d_wide = d_queries.astype(F32)
    column_sum = jnp.sum(full_query.astype(F32), axis=0)
    row_sums = jnp.stack(
        [jnp.sum(d_wide * column_sum, axis=-1), jnp.sum(d_wide * query_sum, axis=-1)]
    )
    row_sums = row_sums + gsend(row_sums, 1)
    row_sums = (row_sums + gsend(row_sums, 2)) / model_width
    d_share = grp_scatter(contract_last(d_queries, full_query), g, 1)
    input_grad = (
        quarter(out_grad, g, 1).astype(F32)
        + inverse
        * (d_share - row_sums[0][:, None] - quarter(video_hat, g, 1) * row_sums[1][:, None])
    ).astype(BF)
    return (updated, input_grad, query_grad, out_weight_grad, key_grad, value_grad)


def after(value, *others):
    return lax.optimization_barrier((value, *others))[0]


def call(body, out_shape, operands, scalars, scratch=()):
    specs = [pl.BlockSpec(memory_space=pltpu.SMEM)] * scalars
    specs += [pl.BlockSpec(memory_space=pltpu.VMEM)] * (len(operands) - scalars)
    held = (*operands[scalars:], *jax.tree.leaves(out_shape), *scratch)
    held_bytes = sum(math.prod(a.shape) * jnp.dtype(a.dtype).itemsize for a in held)
    return pl.pallas_call(
        body,
        out_shape=out_shape,
        in_specs=specs,
        out_specs=jax.tree.map(lambda _: pl.BlockSpec(memory_space=pltpu.VMEM), out_shape),
        scratch_shapes=list(scratch),
        compiler_params=pltpu.CompilerParams(vmem_limit_bytes=held_bytes + SPARE_BYTES),
        cost_estimate=SMALL,
    )(*operands)


def shaped(shape, dtype=BF):
    return jax.ShapeDtypeStruct(shape, dtype)


def aligned(start, unit):
    return pl.multiple_of(start, unit)


def project_text(states, gain, weights, steps=4):
    rows, depth = states.shape
    width = weights[0].shape[1]
    chunk = depth // steps

    def body(states_ref, gain_ref, wq_ref, wk_ref, wv_ref, out_ref, normed_ref, total_ref):
        step = pl.program_id(0)

        @pl.when(step == 0)
        def _():
            for at in range(0, rows, 16):
                values = states_ref[at : at + 16, :].astype(F32)
                normed_ref[at : at + 16, :] = rms_scale(values, gain_ref[...]).astype(BF)
            total_ref[...] = jnp.zeros_like(total_ref)

        here = normed_ref[:, pl.ds(aligned(step * chunk, chunk), chunk)]
        for k, weight_ref in enumerate((wq_ref, wk_ref, wv_ref)):
            total_ref[:, k * width : (k + 1) * width] += mm(here, weight_ref[...])

        @pl.when(step == steps - 1)
        def _():
            out_ref[...] = total_ref[...].astype(BF)

    whole = lambda shape: pl.BlockSpec(shape, lambda i: (0,) * len(shape))
    return pl.pallas_call(
        body,
        grid=(steps,),
        out_shape=shaped((rows, 3 * width)),
        in_specs=[whole((rows, depth)), whole((1, depth))]
        + [pl.BlockSpec((chunk, width), lambda i: (i, 0))] * 3,
        out_specs=whole((rows, 3 * width)),
        scratch_shapes=[pltpu.VMEM((rows, depth), BF), pltpu.VMEM((rows, 3 * width), F32)],
        compiler_params=pltpu.CompilerParams(vmem_limit_bytes=VMEM_BYTES),
        cost_estimate=SMALL,
    )(states, gain.reshape(1, -1), *weights)


def attend_text(projected, bias, text_out, place, lens, steps=4):
    rows = projected.shape[0]
    heads = bias.shape[0]
    inner, depth = text_out.shape
    size = inner // heads
    quarter_rows = rows // 4
    chunk = depth // steps

    def body(place_ref, len_ref, qkv_ref, bias_ref, out_ref, kept_ref, away_ref, held_ref, mixed_ref):
        @pl.when(pl.program_id(0) == 0)
        def _():
            g = place_ref[2]
            length = len_ref[place_ref[0] * 2 + place_ref[1]]
            live = lax.broadcasted_iota(jnp.int32, (rows, rows), 1) < length
            for head in range(heads):
                query, key, value = (
                    qkv_ref[:, k * inner + head * size : k * inner + (head + 1) * size]
                    for k in range(3)
                )
                grown = jnp.where(live, jnp.exp(contract_last(query, key) + bias_ref[head]), 0.0)
                weights = grown * (1.0 / jnp.sum(grown, axis=-1, keepdims=True))
                held_ref[:, head * size : (head + 1) * size] = mm(weights.astype(BF), value).astype(BF)
            for k, to in ((0, 0), (2, 1), (1, 2), (3, 3)):
                rows_from = pl.ds(aligned((g ^ k) * quarter_rows, quarter_rows), quarter_rows)
                mixed_ref[to * quarter_rows : (to + 1) * quarter_rows, :] = held_ref[rows_from, :]

        product = mm(mixed_ref[...], out_ref[...]).astype(BF)
        kept_ref[...] = product[: rows // 2]
        away_ref[...] = product[rows // 2 :]

    whole = lambda shape: pl.BlockSpec(shape, lambda i: (0,) * len(shape))
    return pl.pallas_call(
        body,
        grid=(steps,),
        out_shape=[shaped((rows // 2, depth))] * 2,
        in_specs=[pl.BlockSpec(memory_space=pltpu.SMEM)] * 2
        + [whole(projected.shape), whole(bias.shape)]
        + [pl.BlockSpec((inner, chunk), lambda i: (0, i))],
        out_specs=[pl.BlockSpec((rows // 2, chunk), lambda i: (0, i))] * 2,
        scratch_shapes=[pltpu.VMEM((rows, inner), BF), pltpu.VMEM((rows, inner), BF)],
        compiler_params=pltpu.CompilerParams(vmem_limit_bytes=VMEM_BYTES),
        cost_estimate=SMALL,
    )(place, lens, projected, bias, text_out)


def encode_rows(states, kept, got, far, gain, place, pairs):
    quarter_rows = states.shape[0] // 4
    width = states.shape[1]
    depth = width // pairs

    def body(place_ref, states_ref, kept_ref, got_ref, far_ref, gain_ref, *refs):
        piece_refs, encoded_ref = refs[:-1], refs[-1]
        z, g = place_ref[0], place_ref[2]
        mine = pl.ds(aligned(g * quarter_rows, quarter_rows), quarter_rows)
        total = states_ref[mine, :].astype(F32) + far_ref[...].astype(F32)
        total += kept_ref[:quarter_rows, :].astype(F32) + got_ref[:quarter_rows, :].astype(F32)
        encoded_ref[...] = rms_scale(total, gain_ref[...]).astype(BF)
        for far_by, piece in enumerate(piece_refs):
            to = lax.rem(z + far_by, pairs)
            piece[...] = encoded_ref[:, pl.ds(aligned(to * depth, 128), depth)]

    out = [shaped((quarter_rows, depth))] * pairs
    operands = (place, states, kept, got, far, gain.reshape(1, -1))
    return call(body, out, operands, 1, [pltpu.VMEM((quarter_rows, width), BF)])


def pieces_of(pairs_of_blocks):
    arrays, listed = [], []
    for entry in pairs_of_blocks:
        numbers = []
        for array, start in entry:
            if not any(array is held for held in arrays):
                arrays.append(array)
            numbers.append((next(k for k, held in enumerate(arrays) if held is array), start))
        listed.append(numbers)
    return arrays, listed


def prepare_video(video_states, out_grad, place, pairs, part):
    tokens, model_width = video_states.shape
    rows = tokens // 4

    def body(place_ref, video_ref, grad_ref, normed_ref, mean_ref, inverse_ref, *tile_refs):
        @pl.loop(0, tokens // 32)
        def _(step):
            here = pl.ds(aligned(step * 32, 32), 32)
            values = video_ref[here, :].astype(F32)
            mean = jnp.mean(values, axis=-1, keepdims=True)
            center = values - mean
            inverse = lax.rsqrt(jnp.mean(center * center, axis=-1, keepdims=True) + 1e-06)
            normed_ref[here, :] = (center * inverse).astype(BF)
            mean_ref[here, :] = mean
            inverse_ref[here, :] = inverse

        z, y, g = place_ref[0], place_ref[1], place_ref[2]
        mine = pl.ds(aligned(g * rows, rows), rows)
        for far in range(pairs):
            for side in range(2):
                to = lax.rem(z + far, pairs) * 2 + (y ^ side)
                columns = pl.ds(aligned(to * part, 128), part)
                tile_refs[side][far, 0] = normed_ref[mine, columns]
                tile_refs[side][far, 1] = grad_ref[mine, columns]

    out = [shaped((tokens, model_width)), shaped((tokens, 1), F32), shaped((tokens, 1), F32)]
    out += [shaped((pairs, 2, rows, part))] * 2
    return call(body, out, (place, video_states, out_grad), 1)


def project_rows(normed, out_grad, blocks, place, pairs, part):
    tokens = normed.shape[0]
    arrays, blocks = pieces_of(blocks)
    width = arrays[0].shape[1]

    def body(place_ref, normed_ref, grad_ref, *refs):
        block_refs, (query_ref, d_ref, sum_ref) = refs[:-3], refs[-3:]
        z, y = place_ref[0], place_ref[1]
        query = jnp.zeros((tokens, width), F32)
        d_attended = jnp.zeros((tokens, width), F32)
        total = jnp.zeros((1, width), F32)
        for far in range(pairs):
            for side in range(2):
                (of_query, query_at), (of_out, out_at) = blocks[2 * far + side]
                origin = lax.rem(z - far + pairs, pairs) * 2 + (y ^ side)
                columns = pl.ds(aligned(origin * part, 128), part)
                weight = block_refs[of_query][query_at : query_at + part, :]
                out_weight = block_refs[of_out][out_at : out_at + width, :]
                query += mm(normed_ref[:, columns], weight)
                d_attended += contract_last(grad_ref[:, columns], out_weight)
                total += jnp.sum(weight.astype(F32), axis=0, keepdims=True)
        query_ref[...] = query.astype(BF)
        d_ref[...] = d_attended.astype(BF)
        sum_ref[...] = total

    out = [shaped((tokens, width)), shaped((tokens, width)), shaped((1, width), F32)]
    return call(body, out, (place, normed, out_grad, *arrays), 1)


def project_captions(parts, own_key, own_value, side_key, side_value, place, pairs):
    quarter_rows, depth = parts[0].shape[1:]
    half = depth // 2
    width = own_key.shape[1]

    def body(place_ref, *refs):
        part_refs = refs[:4]
        key_ref, value_ref, side_key_ref, side_value_ref = refs[4:8]
        out_refs = refs[8:]
        y = place_ref[1]
        mine = pl.ds(aligned(y * half, 128), half)
        theirs = pl.ds(aligned((1 - y) * half, 128), half)
        own = jnp.concatenate([r[far, :, mine] for far in range(pairs) for r in part_refs], 0)
        other = jnp.concatenate([r[far, :, theirs] for far in range(pairs) for r in part_refs], 0)
        keys = mm(own, key_ref[...]) + mm(other, side_key_ref[...])
        values = mm(own, value_ref[...]) + mm(other, side_value_ref[...])
        for far in range(pairs):
            rows = slice(far * 4 * quarter_rows, (far + 1) * 4 * quarter_rows)
            out_refs[far][:, :width] = keys[rows].astype(BF)
            out_refs[far][:, width:] = values[rows].astype(BF)

    out = [shaped((4 * quarter_rows, 2 * width))] * pairs
    operands = (place, *parts, own_key, own_value, side_key, side_value)
    return call(body, out, operands, 1)


def slots_of(count_ref, caption_ref, base, captions):
    def find(sample, carry):
        total, first, start = carry
        total = total + count_ref[sample]
        past = total <= base
        return total, first + past.astype(jnp.int32), jnp.where(past, total, start)

    zero = jnp.int32(0)
    _, first, start = lax.fori_loop(0, captions, find, (zero, zero, zero))
    found, edge = [], start - base
    for slot in range(SLOTS):
        valid = first + slot < captions
        sample = jnp.minimum(first + slot, captions - 1)
        end = edge + jnp.where(valid, count_ref[sample], 0)
        found.append((edge, end, caption_ref[sample], valid))
        edge = end
    return found


def attend(queries, d_attended, column_sum, kv_blocks, place, counts, sample_caption, lens, pairs):
    tokens, width = queries.shape
    cap_len = kv_blocks[0].shape[0]
    heads = width // HEAD_SIZE
    captions = counts.shape[0]
    keys_wide = SLOTS * cap_len
    cap_quarter, row_quarter = cap_len // 4, tokens // 4
    scale = 1.0 / math.sqrt(HEAD_SIZE)

    def body(place_ref, count_ref, caption_ref, len_ref, q_ref, da_ref, sum_ref, *refs):
        block_refs = refs[: len(kv_blocks)]
        both_ref, att_ref, dq_ref, rows_ref, slot_ref, kv_ref = refs[len(kv_blocks) :]
        z, y, g = place_ref[0], place_ref[1], place_ref[2]
        low, high, length = [], [], []
        found = slots_of(count_ref, caption_ref, (z * 2 + y) * tokens, captions)
        for slot, (start, end, caption, _) in enumerate(found):
            low.append(start)
            high.append(end)
            length.append(len_ref[caption])
            entry = lax.rem(z - caption // 2 + pairs, pairs) * 2 + (lax.rem(caption, 2) ^ y)
            for number, block in enumerate(block_refs):

                @pl.when(entry == number)
                def _(slot=slot, block=block):
                    kv_ref[slot * cap_len : (slot + 1) * cap_len, :] = block[...]

        token = lax.broadcasted_iota(jnp.int32, (tokens, keys_wide), 0)
        column = lax.broadcasted_iota(jnp.int32, (tokens, keys_wide), 1)
        slot_of = column // cap_len
        inside = column % cap_len
        key = ((inside // cap_quarter) ^ g) * cap_quarter + inside % cap_quarter

        def of_slot(values):
            return jnp.where(slot_of == 0, values[0], jnp.where(slot_of == 1, values[1], values[2]))

        live = (token >= of_slot(low)) & (token < of_slot(high)) & (key < of_slot(length))
        first_sum = jnp.zeros((tokens, 1), F32)
        second_sum = jnp.zeros((tokens, 1), F32)
        for head in range(heads):
            at = slice(head * HEAD_SIZE, (head + 1) * HEAD_SIZE)
            at_value = slice(width + head * HEAD_SIZE, width + (head + 1) * HEAD_SIZE)
            query, d_att = q_ref[:, at], da_ref[:, at]
            keys, values = kv_ref[:, at], kv_ref[:, at_value]
            grown = jnp.where(live, jnp.exp(contract_last(query, keys) * scale), 0.0)
            weights = grown * (1.0 / jnp.sum(grown, axis=-1, keepdims=True))
            probs = weights.astype(BF)
            d_probs = contract_last(d_att, values)
            mixed = jnp.sum(weights * d_probs, axis=-1, keepdims=True)
            d_scores = (weights * (d_probs - mixed) * scale).astype(BF)
            att_ref[:, at] = mm(probs, values).astype(BF)
            d_query = mm(d_scores, keys).astype(BF)
            dq_ref[:, at] = d_query
            d_wide = d_query.astype(F32)
            first_sum += jnp.sum(d_wide * sum_ref[:, at], axis=-1, keepdims=True)
            second_sum += jnp.sum(d_wide * query.astype(F32), axis=-1, keepdims=True)
            key_grad = contract_first(d_scores, query).astype(BF)
            value_grad = contract_first(probs, d_att).astype(BF)
            for slot in range(SLOTS):
                for part in range(4):
                    held = slice(
                        slot * cap_len + part * cap_quarter, slot * cap_len + (part + 1) * cap_quarter
                    )
                    to = pl.ds(aligned((part ^ g) * cap_quarter, cap_quarter), cap_quarter)
                    slot_ref[slot, to, at] = key_grad[held]
                    slot_ref[slot, to, at_value] = value_grad[held]

        rows_ref[:, 0:1] = first_sum
        rows_ref[:, 1:2] = second_sum
        for part in range(4):
            rows = pl.ds(aligned((part ^ g) * row_quarter, row_quarter), row_quarter)
            to = slice(part * row_quarter, (part + 1) * row_quarter)
            both_ref[0, to, :] = att_ref[rows, :]
            both_ref[1, to, :] = dq_ref[rows, :]

    out = [
        shaped((2, tokens, width)),
        shaped((tokens, width)),
        shaped((tokens, width)),
        shaped((tokens, 2), F32),
        shaped((SLOTS, cap_len, 2 * width)),
    ]
    operands = (place, counts, sample_caption, lens, queries, d_attended, column_sum, *kv_blocks)
    scratch = [pltpu.VMEM((keys_wide, 2 * width), BF)]
    return call(body, out, operands, 4, scratch)


def caption_terms(slots, side_slots, place, counts, sample_caption, tokens, pairs):
    captions = counts.shape[0]
    shape = slots.shape[1:]

    def body(place_ref, count_ref, caption_ref, own_ref, side_ref, *refs):
        term_refs, total_ref = refs[:-1], refs[-1]
        z, y = place_ref[0], place_ref[1]
        total_ref[...] = jnp.zeros_like(total_ref)
        for side, slot_ref in enumerate((own_ref, side_ref)):
            base = (z * 2 + (y ^ side)) * tokens
            for slot, (_, _, caption, valid) in enumerate(
                slots_of(count_ref, caption_ref, base, captions)
            ):
                far = lax.rem(caption // 2 - z + pairs, pairs)

                @pl.when(valid & (lax.rem(caption, 2) == y))
                def _(slot=slot, far=far, slot_ref=slot_ref):
                    total_ref[far] += slot_ref[slot].astype(F32)

        for far, term_ref in enumerate(term_refs):
            term_ref[...] = total_ref[far].astype(term_ref.dtype)

    out = [shaped(shape, F32 if far == 0 else BF) for far in range(pairs)]
    operands = (place, counts, sample_caption, slots, side_slots)
    return call(body, out, operands, 3, [pltpu.VMEM((pairs, *shape), F32)])


def project_back(attended, d_queries, blocks, place, pairs, part):
    tokens, width = attended.shape
    arrays, blocks = pieces_of(blocks)
    model_width = 2 * pairs * part
    per_piece = 2 * pairs // 4
    piece = model_width // 4

    def body(place_ref, att_ref, dq_ref, *refs):
        block_refs = refs[: len(arrays)]
        own_ref, far_ref, away_ref = refs[len(arrays) :]
        z, y, g = place_ref[0], place_ref[1], place_ref[2]
        att, d_query = att_ref[...], dq_ref[...]
        for far in range(pairs):
            for side in range(2):
                (of_query, query_at), (of_out, out_at) = blocks[2 * far + side]
                weight = block_refs[of_query][query_at : query_at + part, :]
                out_weight = block_refs[of_out][out_at : out_at + width, :]
                origin = lax.rem(z - far + pairs, pairs) * 2 + (y ^ side)
                flip = (origin // per_piece) ^ g
                start = lax.rem(origin, per_piece) * part
                columns = pl.ds(aligned(start, 128), part)
                beyond = pl.ds(aligned(start + piece, 128), part)
                added = mm(att, out_weight).astype(BF)
                d_normed = contract_last(d_query, weight).astype(BF)
                places = ((own_ref, columns), (away_ref, columns), (far_ref, columns), (away_ref, beyond))
                for number, (target_ref, to) in enumerate(places):

                    @pl.when(flip == number)
                    def _(target_ref=target_ref, to=to, added=added, d_normed=d_normed):
                        target_ref[0, :, to] = added
                        target_ref[1, :, to] = d_normed

    out = [shaped((2, tokens, piece)), shaped((2, tokens, piece)), shaped((2, tokens, 2 * piece))]
    return call(body, out, (place, attended, d_queries, *arrays), 1)


def weight_grads(tiles, both_blocks, known, pairs):
    part = tiles[0].shape[-1]
    given = [k for k, block in enumerate(both_blocks) if block is not None]
    arrays, blocks = pieces_of([both_blocks[k] for k in given])
    width = arrays[0].shape[-1]
    known = known or []

    def body(*refs):
        tile_refs, known_refs = refs[:4], refs[4 : 4 + len(known)]
        block_refs, (query_ref, out_ref) = refs[4 + len(known) : -2], refs[-2:]
        query_grad = known_refs[0][...] if known else jnp.zeros((part, width), F32)
        out_grad = known_refs[1][...] if known else jnp.zeros((width, part), F32)
        for k, ((number, at),) in zip(given, blocks):
            side, far = divmod(k, pairs)
            block = block_refs[number]
            normed, grad = (
                jnp.concatenate([r[far, side, which] for r in tile_refs], axis=0)
                for which in range(2)
            )
            out_grad += contract_first(block[at], grad)
            query_grad += contract_first(normed, block[at + 1])
        query_ref[...] = query_grad
        out_ref[...] = out_grad

    out = [shaped((part, width), F32), shaped((width, part), F32)]
    return call(body, out, (*tiles, *known, *arrays), 0)


def local(
    caption_states,
    caption_lens,
    text_gain,
    text_query,
    text_key,
    text_value,
    text_bias,
    text_out,
    final_gain,
    cross_key,
    cross_value,
    video_states,
    video_counts,
    sample_caption,
    cross_query,
    cross_out,
    out_grad,
):
    column = lax.axis_index("fsdp")
    g = lax.axis_index("grp")
    pairs = lax.axis_size("fsdp") // 2
    z, y = column // 2, column % 2
    place = jnp.stack([z, y, g]).astype(jnp.int32)
    caps_local, cap_len, text_width = caption_states.shape
    tokens, model_width = video_states.shape
    width_local = cross_key.shape[1]
    part = cross_query.shape[0]

    states = caption_states.reshape(cap_len, text_width)
    quarter_rows = cap_len // 4

    first = [fsend(cross_query, 1, 0), fsend(cross_out, 1, 0)]
    side_key, side_value = fsend(cross_key, 0, 1), fsend(cross_value, 0, 1)
    projected = project_text(states, text_gain, (text_query, text_key, text_value))
    kept, away = attend_text(projected, text_bias, text_out, place, caption_lens)
    kept, away = after((kept, away), first, side_key, side_value)
    got = gsend(away, 1)
    ring = [None, jnp.concatenate(first, axis=0)]
    side_first = fsend(jnp.concatenate([cross_query, cross_out, *first], axis=0), 0, 1)
    ring.append(fsend(ring[1], 1, 0))
    sent = (kept[quarter_rows:].astype(F32) + got[quarter_rows:].astype(F32)).astype(BF)
    over_x = gsend(sent, 2)
    normed, mean, inverse, own_tiles, other_tiles = prepare_video(
        after(video_states, sent), out_grad, place, pairs, part
    )
    pieces = encode_rows(
        states, kept, got, after(over_x, normed), final_gain, place, pairs
    )

    mine = jnp.stack([fsend(p, far, 0) if far else p for far, p in enumerate(pieces)])
    mine = after(mine, ring[2])
    over_x = gsend(mine, 2)
    parts = [mine, gsend(mine, 1), over_x, gsend(over_x, 1)]
    current = after(ring[2], mine)
    for far in range(3, pairs):
        current = fsend(current, 1, 0)
        ring.append(current)
    parts[3] = after(parts[3], side_first)
    kv_partial = project_captions(
        parts, cross_key, cross_value, side_key, side_value, place, pairs
    )
    kv_partial = after(tuple(kv_partial), ring[-1])
    kv_sum = kv_partial[0].astype(F32)
    for far in range(1, pairs):
        kv_sum += fsend(kv_partial[far], pairs - far, 0).astype(F32)
    side_later = [fsend(w, 0, 1) for w in ring[2:]]
    other_tiles = fsend(other_tiles, 0, 1)
    kv_sum = after(kv_sum.astype(BF), side_later[0])
    kv_blocks = gather_direct(kv_sum)
    kv_blocks[4] = after(kv_blocks[4], side_later, other_tiles)

    step = part + width_local
    blocks = []
    for far, held in enumerate(ring):
        side, start = (side_first, far * step) if far < 2 else (side_later[far - 2], 0)
        here = ((held, 0), (held, part)) if far else ((cross_query, 0), (cross_out, 0))
        blocks += [here, ((side, start), (side, start + part))]
    queries, d_attended, column_sum = project_rows(
        normed, after(out_grad, kv_blocks[4]), blocks, place, pairs, part
    )

    tiles = jnp.stack([own_tiles, other_tiles], axis=1)
    over_z = [fsend(after(tiles[far], kv_blocks[4]), far, 0) for far in range(1, pairs)]
    over_z = [tiles[0]] + over_z

    both, attended, d_queries, row_sums, slots = attend(
        queries,
        d_attended,
        column_sum,
        kv_blocks,
        place,
        video_counts,
        sample_caption,
        caption_lens,
        pairs,
    )

    def chain(blocks, steps):
        for _ in range(steps):
            blocks.append(fsend(blocks[-1], 1, 0))
        return blocks

    side_slots = fsend(slots, 0, 1)
    side_mine = fsend(both, 0, 1)
    first, over_z = after((both, over_z))
    tiles = jnp.stack(over_z)
    late = chain([first], 2)
    sums_core = gsend(row_sums, 1)
    row_sums = row_sums + sums_core
    attended, tiles = after((attended, tiles), row_sums)
    tiles_x = gsend(tiles, 2)
    own, far_piece, away = project_back(attended, d_queries, blocks, place, pairs, part)
    tiles_core = gsend(tiles, 1)
    stage = (side_slots, side_mine, late, row_sums, tiles_x, tiles_core, away)
    side_slots, side_mine, late, row_sums, tiles_x, tiles_core, away = after(stage)

    sides = [fsend(block, 0, 1) for block in late[1:3]]
    late = chain(list(late), pairs - 3)
    got = gsend(away, 1)
    width = model_width // 4
    sent = [
        (far_piece[k].astype(F32) + got[k, :, width:].astype(F32)).astype(BF) for k in range(2)
    ]
    sums_x = gsend(row_sums, 2)
    far_out = gsend(after(sent[0], sums_x), 2)
    terms = caption_terms(
        after(slots, sent[0]), side_slots, place, video_counts, sample_caption, tokens, pairs
    )
    kv_parts = [fsend(terms[1], 1, 0)]
    stage = (sides, late, tiles_x, kv_parts, terms, far_out, sent[1])
    sides, late, tiles_x, kv_parts, terms, far_out, sent_d = after(stage)

    here = [((block, 0),) for block in late]
    tiles = [tiles, tiles_core, tiles_x, gsend(tiles_x, 1)]
    there = [((block, 0),) for block in (side_mine, *sides)]
    there += [((fsend(block, 0, 1), 0),) for block in late[3:]]
    known = weight_grads(tiles, here + there[:3], None, pairs)
    total = [
        own[k].astype(F32) + got[k, :, :width].astype(F32) + far.astype(F32)
        for k, far in enumerate((far_out, after(gsend(sent_d, 2), known)))
    ]
    row_sums = (row_sums + sums_x) / model_width
    video = quarter(video_states, g, 1).astype(F32)
    updated = (video + total[0]).astype(BF)
    video_hat = (video - mean) * inverse
    input_grad = (
        quarter(out_grad, g, 1).astype(F32)
        + inverse * (total[1] - row_sums[:, 0:1] - video_hat * row_sums[:, 1:2])
    ).astype(BF)
    kv_parts += [fsend(terms[far], far, 0) for far in range(2, pairs)]
    known = after(known, updated, input_grad)
    query_grad, out_weight_grad = weight_grads(
        tiles, [None] * (pairs + 3) + there[3:], known, pairs
    )
    kv_parts = after(kv_parts, query_grad)
    kv_grads = (terms[0] + sum(p.astype(F32) for p in kv_parts)).astype(BF)[None]
    key_grad = kv_grads[:, :, :width_local]
    value_grad = kv_grads[:, :, width_local:]
    return (updated, input_grad, query_grad, out_weight_grad, key_grad, value_grad)


def local_of(*arrays):
    whole_tiles = arrays[14].shape[0] % 128 == 0 and arrays[0].shape[0] == 1
    return local(*arrays) if whole_tiles else local_general(*arrays)


def solution(mesh):
    in_specs = (
        P("fsdp", None, None),
        P(),
        P(),
        P(None, "grp"),
        P(None, "grp"),
        P(None, "grp"),
        P("grp", None, None),
        P("grp", None),
        P(),
        P("fsdp", "grp"),
        P("fsdp", "grp"),
        P("fsdp", None),
        P(),
        P(),
        P("fsdp", "grp"),
        P("grp", "fsdp"),
        P("fsdp", None),
    )
    out_specs = (
        P("fsdp", "grp"),
        P("fsdp", "grp"),
        P("fsdp", "grp"),
        P("grp", "fsdp"),
        P("fsdp", None, "grp"),
        P("fsdp", None, "grp"),
    )
    return jax.shard_map(
        local_of, mesh=mesh, in_specs=in_specs, out_specs=out_specs, check_vma=False
    )
```
